128 devices in a mesh: ctx: 16 (over x_hi, z, core), tp: 8 (over y, x_lo).
Axes of the slice: x: 4 (x_hi: 2, x_lo: 2; x = x_hi * 2 + x_lo), y: 4, z: 4, core: 2. Of those that a mesh axis runs over, the one named last changes fastest.
Arguments:
- tokens: bfloat16 [8192, 2048], P('ctx'), may hold values from -6 to 6
- cotangent: bfloat16 [8192, 2048], P('ctx'), may hold values from -6 to 6
- segment_ids: int32 [8192], replicated, may hold values from 0 to 2, as said below
- first_gain: float32 [2048], replicated, may hold values from 0.25 to 1.75
- first_shift: float32 [2048], replicated, may hold values from -3 to 3
- second_gain: float32 [2048], replicated, may hold values from 0.25 to 1.75
- second_shift: float32 [2048], replicated, may hold values from -3 to 3
- w_qkv: bfloat16 [2048, 3, 2048], P(None, None, 'tp'), may hold values from -0.125 to 0.125
- qkv_bias: float32 [3, 2048], P(None, 'tp'), may hold values from -3 to 3
- w_out: bfloat16 [2048, 2048], P('tp'), may hold values from -2 to 2
- w_gate_up: bfloat16 [2048, 2, 5632], P(None, None, 'tp'), may hold values from -0.125 to 0.125
- w_down: bfloat16 [5632, 2048], P('tp'), may hold values from -0.078125 to 0.078125
Outputs:
- layer_out: bfloat16 [8192, 2048], P('ctx')
- grad_tokens: bfloat16 [8192, 2048], P('ctx')
- grad_first_gain: float32 [2048], replicated
- grad_first_shift: float32 [2048], replicated
- grad_second_gain: float32 [2048], replicated
- grad_second_shift: float32 [2048], replicated
- grad_w_qkv: float32 [2048, 3, 2048], P('ctx', None, 'tp')
- grad_qkv_bias: float32 [3, 2048], P(None, 'tp')
- grad_w_out: float32 [2048, 2048], P('tp', 'ctx')
- grad_w_gate_up: float32 [2048, 2, 5632], P('ctx', None, 'tp')
- grad_w_down: float32 [5632, 2048], P('tp', 'ctx')
The draws below stay inside these ranges and needn't reach their ends.
Inputs may be any that keep to these rules, and one draw needn't show every extreme that they name: `segment_ids`: ids never fall from one token to the next, every id appears, document 0 ends within the first 512 tokens and document 2 begins within the last 512 tokens.
All inputs are finite; a program needn't handle non-finite values.
Results may differ from the reference program's by a relative error of at most 0.029.
Values may be sent and summed in bfloat16 or wider, within the bound.
No kernel may reach another device: no remote copies, remote signals or barrier semaphores. Data moves between devices by JAX's collectives and lax.ppermute only.
A program may use at most 192 MiB of HBM per device.

```python
import jax
import jax.numpy as jnp
from jax import lax

D = 2048
HEADS = 32
HDIM = 64
FF = 5632
DOCS = 3
TOK_DEV = 512
TOKENS = 8192


def draw_segment_ids(key, part):
    key = jax.random.fold_in(key, 7)
    opening_key, closing_key = jax.random.split(key)
    opening = jax.random.randint(opening_key, (), 1, TOK_DEV)
    closing = jax.random.randint(closing_key, (), 1, TOK_DEV)
    places = jnp.arange(TOKENS, dtype=jnp.int32)
    return (places >= opening).astype(jnp.int32) + (places >= TOKENS - closing).astype(jnp.int32)


def with_spikes(values, stream_key, source, target, shards_of, factor):
    owner, partner = [(jnp.arange(values.shape[axis_at]) // (values.shape[axis_at] // shards_of)).reshape([-1 if axis == axis_at else 1 for axis in range(values.ndim)]) for axis_at in (source, target)]
    chosen = jax.random.permutation(stream_key, shards_of)[partner]
    strong = (owner == chosen) | (owner == (partner + shards_of // 2) % shards_of)
    return jnp.where(strong, factor * values, values)


def levels(own_key, shape, pieces, low, largest):
    loudness = 1.0
    for position, shards_of in pieces:
        heights = jax.random.uniform(jax.random.fold_in(jax.random.fold_in(own_key, 6), position), (shards_of,), jnp.float32, low / len(pieces), largest / len(pieces))
        loudness = loudness * jnp.repeat(jnp.exp(heights), shape[position] // shards_of).reshape((-1,) + (1,) * (len(shape) - 1 - position))
    return loudness


def bell_draw(rng, extent, deviation, most, cuts=(), kind=jnp.bfloat16):
    values = deviation * jax.random.normal(rng, extent, jnp.float32)
    if cuts:
        values = values * levels(rng, extent, cuts, -0.22, 0.18)
    return jnp.clip(values, -most, most).astype(kind)


def noise_with(key, dims, scale, limit, pieces, heavy, kind=jnp.bfloat16):
    values = scale * jax.random.normal(key, dims, jnp.float32)
    if pieces:
        values = values * levels(key, dims, pieces, -0.22, 0.18)
    return jnp.clip(with_spikes(values, jax.random.fold_in(key, 3), *heavy), -limit, limit).astype(kind)


def setup_inputs(seed: int = 0) -> dict:
    seeds = jax.random.split(jax.random.key(seed), 13)
    return {
        "tokens": noise_with(seeds[0], (TOKENS, D), 1.0, 6.0, ((0, 16),), (0, 1, 16, 2.0)),
        "cotangent": noise_with(seeds[1], (TOKENS, D), 1.0, 6.0, ((0, 16),), (0, 1, 16, 2.0)),
        "segment_ids": draw_segment_ids(jax.random.fold_in(seeds[12], 71), 0),
        "first_gain": jnp.clip(1.0 + 0.15 * jax.random.normal(seeds[3], (D,), jnp.float32), 0.25, 1.75),
        "first_shift": bell_draw(seeds[4], (D,), 0.5, 3.0, (), jnp.float32),
        "second_gain": jnp.clip(1.0 + 0.15 * jax.random.normal(seeds[5], (D,), jnp.float32), 0.25, 1.75),
        "second_shift": bell_draw(seeds[6], (D,), 0.5, 3.0, (), jnp.float32),
        "w_qkv": bell_draw(seeds[7], (D, 3, HEADS * HDIM), D ** -0.5, 0.125, ((2, 8),)),
        "qkv_bias": bell_draw(seeds[8], (3, HEADS * HDIM), 0.5, 3.0, ((1, 8),), jnp.float32),
        "w_out": bell_draw(seeds[9], (HEADS * HDIM, D), (max(1, HEADS * HDIM * 32 // TOKENS)) ** -0.5, 2.0, ((0, 8),)),
        "w_gate_up": bell_draw(seeds[10], (D, 2, FF), D ** -0.5, 0.125, ((2, 8),)),
        "w_down": bell_draw(seeds[11], (FF, D), FF ** -0.5, 0.078125, ((0, 8),)),
    }


@jax.custom_vjp
def low(v):
    return lax.optimization_barrier(v.astype(jnp.bfloat16)).astype(jnp.float32)

@jax.custom_vjp
def low_back(v):
    return v

def low_keep(v):
    return (low(v), None)

def low_pass(kept, grad):
    return (grad,)

def back_keep(v):
    return (v, None)

def back_low(kept, grad):
    return (low(grad),)
low.defvjp(low_keep, low_pass)
low_back.defvjp(back_keep, back_low)

def layer_norm(values, gain, shift):
    center = values - lax.optimization_barrier(jnp.mean(values, axis=-1, keepdims=True))
    spread = lax.optimization_barrier(jnp.mean(center * center, axis=-1, keepdims=True))
    return center * lax.rsqrt(spread + 1e-05) * gain + shift

def doc_positions(segment_ids):
    places = jnp.arange(segment_ids.shape[0], dtype=jnp.int32)
    labels = jnp.arange(DOCS, dtype=jnp.int32)
    starts = lax.optimization_barrier(jnp.sum((segment_ids[:, None] < labels[None, :]).astype(jnp.int32), axis=0))
    begins = lax.optimization_barrier(jnp.sum(jnp.where(segment_ids[:, None] == labels[None, :], starts[None, :], 0), axis=1))
    return places - begins

def rotary(values, places, turning):
    frequency = 10000.0 ** (-jnp.arange(8, dtype=jnp.float32) / 8.0)
    angles = places.astype(jnp.float32)[:, None] * frequency[None, :]
    cosine = jnp.cos(angles)[:, None, :]
    sine_part = turning * jnp.sin(angles)[:, None, :]
    front_half = values[..., :8]
    back_half = values[..., 8:16]
    return jnp.concatenate([front_half * cosine - back_half * sine_part, back_half * cosine + front_half * sine_part, values[..., 16:]], axis=-1)

def attention(queries, key_rows, values, segment_ids):
    stream_places = jnp.arange(TOKENS, dtype=jnp.int32)
    span_rows = TOK_DEV // 2
    block_count = TOKENS // span_rows

    @jax.checkpoint
    def one_block(inputs):
        query_block, block_segment, block_places = inputs
        scores = low_back(jnp.einsum('qhd,khd->hqk', query_block, key_rows, precision=lax.Precision.HIGHEST))
        allowed = (block_segment[:, None] == segment_ids[None, :]) & (block_places[:, None] >= stream_places[None, :])
        scores = jnp.where(allowed[None], scores, -1e+30)
        row_max = lax.optimization_barrier(jnp.max(scores, axis=-1, keepdims=True))
        weights = jnp.exp(scores - row_max)
        probs = weights / lax.optimization_barrier(jnp.sum(weights, axis=-1, keepdims=True))
        return jnp.einsum('hqk,khd->qhd', low(probs), values, precision=lax.Precision.HIGHEST)
    outputs = lax.map(one_block, (queries.reshape(block_count, span_rows, HEADS, HDIM), segment_ids.reshape(block_count, span_rows), stream_places.reshape(block_count, span_rows)))
    return outputs.reshape(TOKENS, HEADS, HDIM)

def forward(tokens, first_gain, first_shift, second_gain, second_shift, w_qkv, qkv_bias, w_out, w_gate_up, w_down, segment_ids, places):
    normed = low(layer_norm(tokens, first_gain, first_shift))
    mixed = low_back(jnp.einsum('td,dch->tch', normed, w_qkv, precision=lax.Precision.HIGHEST) + qkv_bias[None])
    head_shape = (TOKENS, HEADS, HDIM)
    queries = low(rotary(mixed[:, 0].reshape(head_shape), places, 1.0) * 0.125)
    key_rows = low(rotary(mixed[:, 1].reshape(head_shape), places, 1.0))
    values = low(mixed[:, 2].reshape(head_shape))
    attended = low_back(low(attention(queries, key_rows, values, segment_ids))).reshape(TOKENS, HEADS * HDIM)
    branch = low_back(jnp.dot(attended, w_out, precision=lax.Precision.HIGHEST))
    middle = tokens + branch
    second = low(layer_norm(middle, second_gain, second_shift))
    gate_up = low_back(jnp.einsum('td,dcf->tcf', second, w_gate_up, precision=lax.Precision.HIGHEST))
    hidden = low(jax.nn.silu(gate_up[:, 0]) * gate_up[:, 1])
    return middle + jnp.dot(hidden, w_down, precision=lax.Precision.HIGHEST)

def reference(tokens, cotangent, segment_ids, first_gain, first_shift, second_gain, second_shift, w_qkv, qkv_bias, w_out, w_gate_up, w_down):
    places = doc_positions(segment_ids)
    inputs = tuple((element.astype(jnp.float32) for element in (tokens, first_gain, first_shift, second_gain, second_shift, w_qkv, qkv_bias, w_out, w_gate_up, w_down)))

    def forward_call(*params):
        return forward(*params, segment_ids, places)
    result, pullback = jax.vjp(forward_call, *inputs)
    gradients = pullback(cotangent.astype(jnp.float32))
    return (result.astype(jnp.bfloat16), gradients[0].astype(jnp.bfloat16), gradients[1], gradients[2], gradients[3], gradients[4], gradients[5], gradients[6], gradients[7], gradients[8], gradients[9])
```

```python
import functools

import jax
import jax.numpy as jnp
from jax import lax
from jax.experimental import pallas as pl
from jax.experimental.pallas import tpu as pltpu
from jax.sharding import Mesh
from jax.sharding import PartitionSpec as P

HDIM = 64
DOCS = 3
BLOCK = 512
HALF = 256
LOW = jnp.bfloat16
WIDE = jnp.float32
CTX = ("xh", "zh", "zl", "core")
TP = ("y", "xl")
SPREAD = ("xh", "zh")
Z = ("zh", "zl")
VMEM_BYTES = 48 * 1024 * 1024


def kernel_call(body, out_shape, inputs, scalars=(), scratch=(), flops=0, exps=0):
    moved = sum(a.size * a.dtype.itemsize for a in (*inputs, *jax.tree.leaves(out_shape)))
    in_specs = [pl.BlockSpec(memory_space=pltpu.SMEM)] * len(scalars)
    in_specs += [pl.BlockSpec(memory_space=pltpu.VMEM)] * len(inputs)
    return pl.pallas_call(
        body,
        out_shape=out_shape,
        in_specs=in_specs,
        out_specs=jax.tree.map(lambda _: pl.BlockSpec(memory_space=pltpu.VMEM), out_shape),
        scratch_shapes=list(scratch),
        compiler_params=pltpu.CompilerParams(vmem_limit_bytes=VMEM_BYTES),
        cost_estimate=pl.CostEstimate(flops=flops, bytes_accessed=moved, transcendentals=exps),
    )(*scalars, *inputs)


def lane_of(shape):
    return lax.broadcasted_iota(jnp.int32, shape, len(shape) - 1)


def exchange_halves(a, b):
    front = lane_of(a.shape) < HDIM
    return (
        jnp.where(front, a, pltpu.roll(b, HDIM, 1)),
        jnp.where(front, pltpu.roll(a, HDIM, 1), b),
    )


def nt(a, b):
    return lax.dot_general(a, b, (((1,), (1,)), ((), ())), preferred_element_type=WIDE)


def nn(a, b):
    return lax.dot_general(a, b, (((1,), (0,)), ((), ())), preferred_element_type=WIDE)


def turn(x, cosine, sine, sign):
    lane = lax.rem(lane_of(x.shape), HDIM)
    ahead = pltpu.roll(x, x.shape[1] - 8, 1)
    behind = pltpu.roll(x, 8, 1)
    swapped = jnp.where(lane < 8, -ahead, behind) * sign
    return x * cosine + swapped * sine


def project_kernel(tok, gain, shift, w, bias, cosine, sine, normed, mean_out, scale_out, packed):
    rows = 64

    def norm_rows(i, carry):
        at = pl.ds(pl.multiple_of(i * rows, rows), rows)
        x = tok[at, :].astype(WIDE)
        mean = jnp.mean(x, axis=-1, keepdims=True)
        center = x - mean
        scale = lax.rsqrt(jnp.mean(center * center, axis=-1, keepdims=True) + 1e-05)
        normed[at, :] = (center * scale * gain[...] + shift[...]).astype(LOW)
        mean_out[at, :] = mean
        scale_out[at, :] = scale
        return carry

    lax.fori_loop(0, BLOCK // rows, norm_rows, 0)
    mixed = [nn(normed[...], w[c]) + bias[c : c + 1, :] for c in range(3)]
    for pair in range(2):
        lanes = slice(pair * 128, pair * 128 + 128)
        q = turn(mixed[0][:, lanes], cosine[...], sine[...], 1.0) * 0.125
        k = turn(mixed[1][:, lanes], cosine[...], sine[...], 1.0)
        kv = exchange_halves(k, mixed[2][:, lanes])
        qq = exchange_halves(q[:HALF], q[HALF:])
        for one in range(2):
            packed[2 * pair + one, :BLOCK, :] = kv[one].astype(LOW)
            packed[2 * pair + one, BLOCK:, :] = qq[one].astype(LOW)


def padded_queries(q2):
    x = q2.astype(WIDE)
    front = lane_of(x.shape) < HDIM
    return (
        jnp.where(front, x, 0.0).astype(LOW),
        jnp.where(front, pltpu.roll(x, HDIM, 1), 0.0).astype(LOW),
    )


def padded_behind(d2):
    x = d2.astype(WIDE)
    front = lane_of(x.shape) < HDIM
    return (
        jnp.where(front, 0.0, pltpu.roll(x, HDIM, 1)).astype(LOW),
        jnp.where(front, 0.0, x).astype(LOW),
    )


def allowed_keys(key_block, query_block, half, begin):
    shape = (BLOCK, HALF)
    key_at = key_block * BLOCK + lax.broadcasted_iota(jnp.int32, shape, 0)
    query_at = query_block * BLOCK + half * HALF + lax.broadcasted_iota(jnp.int32, shape, 1)
    return (key_at <= query_at) & (key_at >= begin)


def for_key_blocks(query_block, blocks, work):
    def one(key_block, carry):
        edge = (key_block == query_block) | (key_block == 0) | (query_block == blocks - 1)

        @pl.when(edge)
        def _():
            work(key_block, True)

        @pl.when(jnp.logical_not(edge))
        def _():
            work(key_block, False)

        return carry

    lax.fori_loop(0, query_block + 1, one, 0)


def forward_kernel(
    place, begin, kv0, kv1, kv2, kv3, q2, out2, out_t, total, kvs, kvt, queries, most, acc
):
    group = place[0]
    front = lane_of((BLOCK, 128)) < HDIM
    for rel, kv in enumerate((kv0, kv1, kv2, kv3)):
        for j in range(4):
            block = 4 * j + (group ^ rel)
            kvs[block] = kv[j]
            kvt[block] = jnp.where(front, 1.0, kv[j].astype(WIDE)).T.astype(LOW)

    def one_query_block(j, carry):
        query_block = 4 * j + group
        queries[:HALF, :], queries[HALF:, :] = padded_queries(q2[j])
        most[...] = jnp.full((1, BLOCK), -1e30, WIDE)
        acc[...] = jnp.zeros((128, BLOCK), WIDE)

        def work(key_block, masked):
            for half in range(2):
                at = slice(half * HALF, half * HALF + HALF)
                scores = nt(kvs[key_block], queries[at, :])
                if masked:
                    ok = allowed_keys(key_block, query_block, half, begin[j][:, at])
                    scores = jnp.where(ok, scores, -1e30)
                old = most[:, at]
                new = jnp.maximum(old, jnp.max(scores, axis=0, keepdims=True))
                weights = jnp.exp(scores - new).astype(LOW)
                acc[:, at] = acc[:, at] * jnp.exp(old - new) + nn(kvt[key_block], weights)
                most[:, at] = new

        for_key_blocks(query_block, 16, work)
        weight_sum = acc[:1, :]
        done = acc[...] / weight_sum
        out_t[j] = done
        total[j] = most[...] + jnp.log(weight_sum)
        rows = done.T
        x, y = rows[:HALF], rows[HALF:]
        out2[j] = jnp.where(lane_of(x.shape) < HDIM, pltpu.roll(x, HDIM, 1), y).astype(LOW)
        return carry

    lax.fori_loop(0, 4, one_query_block, 0)


def backward_kernel(
    place, begin, kv0, kv1, kv2, kv3, q2, d2, out_t, total,
    dq2, keep, send, kvs, kvt, queries, grads, dot_rows, acc, dkv,
):
    group = place[0]
    for rel, kv in enumerate((kv0, kv1, kv2, kv3)):
        for j in range(4):
            block = 4 * j + (group ^ rel)
            kvs[block] = kv[j]
            kvt[block] = kv[j].astype(WIDE).T.astype(LOW)
    dkv[...] = jnp.zeros(dkv.shape, WIDE)

    def one_query_block(j, carry):
        query_block = 4 * j + group
        queries[:HALF, :], queries[HALF:, :] = padded_queries(q2[j])
        grads[:HALF, :], grads[HALF:, :] = padded_behind(d2[j])
        dot_rows[...] = jnp.sum(grads[...].astype(WIDE).T * out_t[j], axis=0, keepdims=True)
        acc[...] = jnp.zeros((128, BLOCK), WIDE)

        def work(key_block, masked):
            terms = []
            for half in range(2):
                at = slice(half * HALF, half * HALF + HALF)
                scores = nt(kvs[key_block], queries[at, :])
                probs = jnp.exp(scores - total[j][:, at])
                if masked:
                    ok = allowed_keys(key_block, query_block, half, begin[j][:, at])
                    probs = jnp.where(ok, probs, 0.0)
                grad_probs = nt(kvs[key_block], grads[at, :])
                grad_scores = (probs * (grad_probs - dot_rows[:, at])).astype(LOW)
                terms.append(
                    nn(grad_scores, queries[at, :]) + nn(probs.astype(LOW), grads[at, :])
                )
                acc[:, at] += nn(kvt[key_block], grad_scores)
            dkv[key_block] += terms[0] + terms[1]

        for_key_blocks(query_block, 16, work)
        rows = acc[...].T
        x, y = rows[:HALF], rows[HALF:]
        dq2[j] = jnp.where(lane_of(x.shape) < HDIM, x, pltpu.roll(y, HDIM, 1)).astype(LOW)
        return carry

    lax.fori_loop(0, 4, one_query_block, 0)
    for j in range(4):
        for k in range(2):
            keep[k, j] = dkv[4 * j + (group ^ (2 * k))].astype(LOW)
            send[k, j] = dkv[4 * j + (group ^ (2 * k + 1))].astype(LOW)


def branch_kernel(heads2, w, attended, partial):
    for pair in range(2):
        lanes = slice(pair * 128, pair * 128 + 128)
        x, y = exchange_halves(heads2[2 * pair].astype(WIDE), heads2[2 * pair + 1].astype(WIDE))
        attended[:HALF, lanes] = x.astype(LOW)
        attended[HALF:, lanes] = y.astype(LOW)
    for n in range(4):
        at = slice(n * 512, n * 512 + 512)
        partial[:, at] = nn(attended[...], w[:, at]).astype(LOW)


def grad_attended_kernel(grad, w, packed):
    g = nt(grad[...], w[...])
    for pair in range(2):
        lanes = slice(pair * 128, pair * 128 + 128)
        both = exchange_halves(g[:HALF, lanes], g[HALF:, lanes])
        for one in range(2):
            packed[2 * pair + one] = both[one].astype(LOW)


def grad_project_kernel(
    parts, w, cosine, sine, tok, mean, scale, grad_mixed, partial, gain_sum, shift_sum, bias_sum
):
    for pair in range(2):
        lanes = slice(pair * 128, pair * 128 + 128)
        even, odd = parts[2 * pair].astype(WIDE), parts[2 * pair + 1].astype(WIDE)
        k, v = exchange_halves(even[:BLOCK], odd[:BLOCK])
        q = jnp.concatenate(exchange_halves(even[BLOCK:], odd[BLOCK:]), axis=0)
        q = turn(q, cosine[...], sine[...], -1.0) * 0.125
        k = turn(k, cosine[...], sine[...], -1.0)
        for c, part in enumerate((q, k, v)):
            start = c * 256 + pair * 128
            low = part.astype(LOW)
            grad_mixed[:, start : start + 128] = low
            bias_sum[c : c + 1, lanes] = jnp.sum(low.astype(WIDE), axis=0, keepdims=True)
    for n in range(4):
        at = slice(n * 512, n * 512 + 512)
        total = nt(grad_mixed[:, :256], w[0, at, :])
        total += nt(grad_mixed[:, 256:512], w[1, at, :])
        total += nt(grad_mixed[:, 512:], w[2, at, :])
        partial[:, at] = total.astype(LOW)
        normal = (tok[:, at].astype(WIDE) - mean[...]) * scale[...]
        gain_sum[:, at] = jnp.sum(total * normal, axis=0, keepdims=True)
        shift_sum[:, at] = jnp.sum(total, axis=0, keepdims=True)


def weight_kernel(place, left, right, mine, theirs, turned):
    core = place[0]
    turned[...] = left[...].astype(WIDE).T.astype(LOW)

    def one(n, carry):
        both = nn(turned[...], right[:, pl.ds(pl.multiple_of(n * 256, 256), 256)])
        first, second = both[:, :128], both[:, 128:]
        mine[n] = jnp.where(core == 0, first, second).astype(LOW)
        theirs[n] = jnp.where(core == 0, second, first).astype(LOW)
        return carry

    lax.fori_loop(0, 8, one, 0)


def weight_grads(left, right, core):
    width = left.shape[1]
    out = jax.ShapeDtypeStruct((8, width, 128), LOW)
    return kernel_call(
        weight_kernel,
        (out, out),
        (left, right),
        scalars=(core,),
        scratch=(pltpu.VMEM((width, left.shape[0]), LOW),),
        flops=2 * left.size * right.shape[1],
    )


def swapped(x, axis):
    return lax.ppermute(x, axis, [(0, 1), (1, 0)])


def summed_over_ctx(mine, theirs):
    here = (mine.astype(WIDE) + swapped(theirs, "core").astype(WIDE)).astype(LOW)
    rows = here.shape[1]
    here = here.reshape(2, 4, rows, 128)
    z = lax.axis_index(Z)
    total = lax.dynamic_index_in_dim(here, z, 1, False).astype(WIDE)
    for k in range(1, 4):
        part = lax.dynamic_index_in_dim(here, lax.rem(z + k, 4), 1, False)
        total += lax.ppermute(part, Z, [(i, (i + k) % 4) for i in range(4)]).astype(WIDE)
    xh = lax.axis_index("xh")
    other = lax.dynamic_index_in_dim(total, 1 - xh, 0, False).astype(LOW)
    return lax.dynamic_index_in_dim(total, xh, 0, False) + swapped(other, "xh").astype(WIDE)


def everywhere(part, axis):
    copies = jnp.broadcast_to(part, (lax.axis_size(axis), *part.shape))
    return lax.all_to_all(copies, axis, split_axis=0, concat_axis=0, tiled=True)


def tp_share(partial):
    parts = partial.reshape(8, -1, partial.shape[1])
    parts = lax.all_to_all(parts, TP, split_axis=0, concat_axis=0, tiled=True)
    return jnp.sum(parts.astype(WIDE), axis=0)


def tp_gather(share):
    parts = everywhere(share, TP)
    return parts.reshape(-1, share.shape[1])


def norm_forward(values, gain, shift):
    center = values - jnp.mean(values, axis=-1, keepdims=True)
    scaling = lax.rsqrt(jnp.mean(center * center, axis=-1, keepdims=True) + 1e-05)
    normal_rows = center * scaling
    return (normal_rows * gain + shift, normal_rows, scaling)


def norm_backward(grad_out, normal_rows, scaling, gain):
    scaled = grad_out * gain
    return scaling * (
        scaled
        - jnp.mean(scaled, axis=-1, keepdims=True)
        - normal_rows * jnp.mean(scaled * normal_rows, axis=-1, keepdims=True)
    )


def shape_of(*dims, kind=LOW):
    return jax.ShapeDtypeStruct(dims, kind)


def body(
    tokens, cotangent, segment_ids, first_gain, first_shift, second_gain, second_shift,
    w_qkv, qkv_bias, w_out, w_gate_up, w_down,
):
    ctx = lax.axis_index(CTX)
    tp = lax.axis_index(TP)
    group = lax.axis_index(("zl", "core"))
    core = lax.axis_index("core").reshape(1)
    group_here = group.reshape(1)

    def my_share(array):
        return lax.dynamic_slice_in_dim(array, tp * 64, 64)

    labels = jnp.arange(DOCS, dtype=jnp.int32)
    starts = jnp.sum((segment_ids[None, :] < labels[:, None]).astype(jnp.int32), axis=1)
    begins = jnp.sum(
        jnp.where(segment_ids[None, :] == labels[:, None], starts[:, None], 0), axis=0
    )
    begin = lax.dynamic_index_in_dim(begins.reshape(4, 4, 1, BLOCK), group, 1, False)
    own = lax.dynamic_slice_in_dim(begins, ctx * BLOCK, BLOCK)
    places = ctx * BLOCK + jnp.arange(BLOCK, dtype=jnp.int32) - own
    frequency = 10000.0 ** (-jnp.arange(8, dtype=WIDE) / 8.0)
    angles = frequency[:, None] * places.astype(WIDE)[None, :]
    cosine = jnp.cos(angles).T
    sine = jnp.sin(angles).T
    one, zero = jnp.ones((BLOCK, 48), WIDE), jnp.zeros((BLOCK, 48), WIDE)
    cosine = jnp.concatenate([cosine, cosine, one] * 2, axis=1)
    sine = jnp.concatenate([sine, sine, zero] * 2, axis=1)

    w3 = jnp.transpose(w_qkv, (1, 0, 2))
    gain_row, shift_row = first_gain[None], first_shift[None]
    normed_low, mean1, scale1, packed = kernel_call(
        project_kernel,
        (
            shape_of(BLOCK, 2048),
            shape_of(BLOCK, 1, kind=WIDE),
            shape_of(BLOCK, 1, kind=WIDE),
            shape_of(4, 768, 128),
        ),
        (tokens, gain_row, shift_row, w3, qkv_bias, cosine, sine),
        flops=2 * 512 * 2048 * 768,
    )
    spread = lax.all_to_all(packed, SPREAD, split_axis=0, concat_axis=0, tiled=True)
    kv = spread[:, :BLOCK]
    q2 = spread[:, BLOCK:]
    kv_z = swapped(kv, "zl")
    kv_c = swapped(jnp.stack([kv, kv_z]), "core")
    kv_parts = (kv, kv_c[0], kv_z, kv_c[1])
    heads2, out_t, total = kernel_call(
        forward_kernel,
        (shape_of(4, HALF, 128), shape_of(4, 128, BLOCK, kind=WIDE), shape_of(4, 1, BLOCK, kind=WIDE)),
        (begin, *kv_parts, q2),
        scalars=(group_here,),
        scratch=(
            pltpu.VMEM((16, BLOCK, 128), LOW),
            pltpu.VMEM((16, 128, BLOCK), LOW),
            pltpu.VMEM((BLOCK, 128), LOW),
            pltpu.VMEM((1, BLOCK), WIDE),
            pltpu.VMEM((128, BLOCK), WIDE),
        ),
        flops=34 * 4 * BLOCK * BLOCK * 128,
        exps=34 * BLOCK * BLOCK,
    )
    heads2 = lax.all_to_all(heads2, SPREAD, split_axis=0, concat_axis=0, tiled=True)
    attended_low, partial_branch = kernel_call(
        branch_kernel,
        (shape_of(BLOCK, 256), shape_of(BLOCK, 2048)),
        (heads2, w_out),
        flops=2 * 512 * 256 * 2048,
    )
    middle = my_share(tokens).astype(WIDE) + tp_share(partial_branch)
    second, second_rows, second_scale = norm_forward(middle, second_gain, second_shift)
    second_low = tp_gather(second.astype(LOW))

    gate_up = jnp.einsum("td,dcf->tcf", second_low, w_gate_up, preferred_element_type=WIDE)
    gate, up = gate_up[:, 0], gate_up[:, 1]
    sigmoid_gate = jax.nn.sigmoid(gate)
    activated = gate * sigmoid_gate
    hidden_low = (activated * up).astype(LOW)
    grad_hidden = jnp.einsum("td,fd->tf", cotangent, w_down, preferred_element_type=WIDE)
    grad_gate = grad_hidden * up * sigmoid_gate * (1.0 + gate * (1.0 - sigmoid_gate))
    grad_gate = grad_gate.astype(LOW)
    grad_up = (grad_hidden * activated).astype(LOW)
    partial_second = jnp.einsum(
        "tcf,dcf->td", jnp.stack([grad_gate, grad_up], axis=1), w_gate_up, preferred_element_type=WIDE
    ).astype(LOW)
    grad_second = tp_share(partial_second)
    grad_middle = my_share(cotangent).astype(WIDE) + norm_backward(
        grad_second, second_rows, second_scale, second_gain
    )
    grad_branch = tp_gather(grad_middle.astype(LOW))

    partial_feed = jnp.dot(hidden_low, w_down, preferred_element_type=WIDE).astype(LOW)
    layer_out = tp_gather((middle + tp_share(partial_feed)).astype(LOW))

    gate_mine, gate_theirs = weight_grads(grad_gate, second_low, core)
    up_mine, up_theirs = weight_grads(grad_up, second_low, core)
    down_mine, down_theirs = weight_grads(hidden_low, cotangent, core)

    grad2 = kernel_call(
        grad_attended_kernel,
        shape_of(4, HALF, 128),
        (grad_branch, w_out),
        flops=2 * 512 * 256 * 2048,
    )
    grad2 = lax.all_to_all(grad2, SPREAD, split_axis=0, concat_axis=0, tiled=True)
    dq2, keep, send = kernel_call(
        backward_kernel,
        (shape_of(4, HALF, 128), shape_of(2, 4, BLOCK, 128), shape_of(2, 4, BLOCK, 128)),
        (begin, *kv_parts, q2, grad2, out_t, total),
        scalars=(group_here,),
        scratch=(
            pltpu.VMEM((16, BLOCK, 128), LOW),
            pltpu.VMEM((16, 128, BLOCK), LOW),
            pltpu.VMEM((BLOCK, 128), LOW),
            pltpu.VMEM((BLOCK, 128), LOW),
            pltpu.VMEM((1, BLOCK), WIDE),
            pltpu.VMEM((128, BLOCK), WIDE),
            pltpu.VMEM((16, BLOCK, 128), WIDE),
        ),
        flops=34 * 10 * BLOCK * BLOCK * 128,
        exps=34 * BLOCK * BLOCK,
    )
    dkv = keep.astype(WIDE) + swapped(send, "core").astype(WIDE)
    dkv = dkv[0] + swapped(dkv[1].astype(LOW), "zl").astype(WIDE)
    grads = jnp.concatenate([dkv.astype(LOW), dq2], axis=1)
    grads = lax.all_to_all(grads, SPREAD, split_axis=0, concat_axis=0, tiled=True)
    grad_mixed, partial_normed, gain_sum, shift_sum, bias_sum = kernel_call(
        grad_project_kernel,
        (
            shape_of(BLOCK, 768),
            shape_of(BLOCK, 2048),
            shape_of(1, 2048, kind=WIDE),
            shape_of(1, 2048, kind=WIDE),
            shape_of(3, 256, kind=WIDE),
        ),
        (grads, w3, cosine, sine, tokens, mean1, scale1),
        flops=2 * 512 * 2048 * 768,
    )
    grad_normed = tp_share(partial_normed)
    first_rows = (my_share(tokens).astype(WIDE) - my_share(mean1)) * my_share(scale1)
    grad_tokens = grad_middle + norm_backward(grad_normed, first_rows, my_share(scale1), first_gain)
    grad_tokens = tp_gather(grad_tokens.astype(LOW))

    vectors = jnp.concatenate(
        [
            gain_sum,
            shift_sum,
            jnp.sum(grad_second * second_rows, axis=0, keepdims=True),
            jnp.sum(grad_second, axis=0, keepdims=True),
        ],
        axis=0,
    )
    vectors = jnp.sum(everywhere(vectors, TP), axis=0)
    vectors = jnp.concatenate([vectors.reshape(32, 256), bias_sum], axis=0)
    vectors = jnp.sum(everywhere(vectors, CTX), axis=0)
    bias_grad = vectors[32:]
    vectors = vectors[:32].reshape(4, 2048)

    out_mine, out_theirs = weight_grads(attended_low, grad_branch, core)
    qkv_mine, qkv_theirs = weight_grads(grad_mixed, normed_low, core)
    grad_gate_w = summed_over_ctx(gate_mine, gate_theirs)
    grad_up_w = summed_over_ctx(up_mine, up_theirs)
    grad_down_w = summed_over_ctx(down_mine, down_theirs)
    grad_out_w = summed_over_ctx(out_mine, out_theirs)
    grad_qkv_w = summed_over_ctx(qkv_mine, qkv_theirs)
    return (
        layer_out,
        grad_tokens,
        vectors[0],
        vectors[1],
        vectors[2],
        vectors[3],
        jnp.transpose(grad_qkv_w.reshape(3, 256, 128), (2, 0, 1)),
        bias_grad,
        grad_out_w,
        jnp.transpose(jnp.stack([grad_gate_w, grad_up_w]), (2, 0, 1)),
        grad_down_w,
    )


def solution(mesh):
    fine = Mesh(
        mesh.devices.reshape(2, 2, 2, 2, 4, 2), ("xh", "zh", "zl", "core", "y", "xl")
    )
    rows = P(CTX, None)
    return jax.shard_map(
        body,
        mesh=fine,
        in_specs=(
            rows, rows, P(), P(), P(), P(), P(),
            P(None, None, TP), P(None, TP), P(TP, None), P(None, None, TP), P(TP, None),
        ),
        out_specs=(
            rows, rows, P(), P(), P(), P(),
            P(CTX, None, TP), P(None, TP), P(TP, CTX), P(CTX, None, TP), P(TP, CTX),
        ),
        check_vma=False,
    )
```

```python
import functools

import jax
import jax.numpy as jnp
from jax import lax
from jax.experimental import pallas as pl
from jax.experimental.pallas import tpu as pltpu
from jax.sharding import Mesh
from jax.sharding import PartitionSpec as P

HDIM = 64
DOCS = 3
BLOCK = 512
HALF = 256
LOW = jnp.bfloat16
WIDE = jnp.float32
CTX = ("xh", "zh", "zl", "core")
TP = ("y", "xl")
SPREAD = ("xh", "zh")
Z = ("zh", "zl")


def kernel_call(body, out_shape, inputs, scalars=(), scratch=(), flops=0, exps=0, mib=16, far=()):
    operands = (*inputs, *far)
    moved = sum(a.size * a.dtype.itemsize for a in (*operands, *jax.tree.leaves(out_shape)))
    in_specs = [pl.BlockSpec(memory_space=pltpu.SMEM)] * len(scalars)
    in_specs += [pl.BlockSpec(memory_space=pltpu.VMEM)] * len(inputs)
    in_specs += [pl.BlockSpec(memory_space=pl.ANY)] * len(far)
    return pl.pallas_call(
        body,
        out_shape=out_shape,
        in_specs=in_specs,
        out_specs=jax.tree.map(lambda _: pl.BlockSpec(memory_space=pltpu.VMEM), out_shape),
        scratch_shapes=list(scratch),
        compiler_params=pltpu.CompilerParams(vmem_limit_bytes=mib * 1024 * 1024),
        cost_estimate=pl.CostEstimate(flops=flops, bytes_accessed=moved, transcendentals=exps),
    )(*scalars, *operands)


def lane_of(shape):
    return lax.broadcasted_iota(jnp.int32, shape, len(shape) - 1)


def exchange_halves(a, b):
    front = lane_of(a.shape) < HDIM
    return (
        jnp.where(front, a, pltpu.roll(b, HDIM, 1)),
        jnp.where(front, pltpu.roll(a, HDIM, 1), b),
    )


def nt(a, b):
    return lax.dot_general(a, b, (((1,), (1,)), ((), ())), preferred_element_type=WIDE)


def nn(a, b):
    return lax.dot_general(a, b, (((1,), (0,)), ((), ())), preferred_element_type=WIDE)


def turn(x, cosine, sine, sign):
    lane = lax.rem(lane_of(x.shape), HDIM)
    ahead = pltpu.roll(x, x.shape[1] - 8, 1)
    behind = pltpu.roll(x, 8, 1)
    swapped = jnp.where(lane < 8, -ahead, behind) * sign
    return x * cosine + swapped * sine


def rotation_table(angles_table):
    tokens = angles_table.shape[1]
    rest = jnp.zeros((112, tokens), WIDE)
    x = jnp.concatenate([angles_table, rest], axis=0).T
    lane = lane_of(x.shape)
    c = jnp.where(lane < 8, x, 0.0)
    c = c + pltpu.roll(c, 8, 1)
    c = c + pltpu.roll(c, HDIM, 1) + jnp.where(lax.rem(lane, HDIM) < 16, 0.0, 1.0)
    s = jnp.where((lane >= 8) & (lane < 16), x, 0.0)
    s = s + pltpu.roll(s, 120, 1)
    s = s + pltpu.roll(s, HDIM, 1)
    return c, s


def project_kernel(
    place, tok, gain, shift, w, bias, table,
    normed, mean_out, scale_out, kv_out, q0, q1, q2, q3, cosine_out, sine_out, kept,
):
    rows = 64

    def norm_rows(i, carry):
        at = pl.ds(pl.multiple_of(i * rows, rows), rows)
        x = tok[at, :].astype(WIDE)
        mean = jnp.mean(x, axis=-1, keepdims=True)
        center = x - mean
        scale = lax.rsqrt(jnp.mean(center * center, axis=-1, keepdims=True) + 1e-05)
        normed[at, :] = (center * scale * gain[...] + shift[...]).astype(LOW)
        mean_out[at, :] = mean
        scale_out[at, :] = scale
        return carry

    lax.fori_loop(0, BLOCK // rows, norm_rows, 0)
    cosine, sine = rotation_table(table[...])
    cosine_out[...] = cosine
    sine_out[...] = sine
    mixed = [nn(normed[...], w[c]) + bias[c : c + 1, :] for c in range(3)]
    for pair in range(2):
        lanes = slice(pair * 128, pair * 128 + 128)
        q = turn(mixed[0][:, lanes], cosine, sine, 1.0) * 0.125
        k = turn(mixed[1][:, lanes], cosine, sine, 1.0)
        kv = exchange_halves(k, mixed[2][:, lanes])
        qq = exchange_halves(q[:HALF], q[HALF:])
        for one in range(2):
            kv_out[2 * pair + one] = kv[one].astype(LOW)
            kept[2 * pair + one] = qq[one].astype(LOW)
    for k, out in enumerate((q0, q1, q2, q3)):
        out[...] = kept[place[1] ^ k]


def padded_queries(q2):
    x = q2.astype(WIDE)
    front = lane_of(x.shape) < HDIM
    return (
        jnp.where(front, x, 0.0).astype(LOW),
        jnp.where(front, pltpu.roll(x, HDIM, 1), 0.0).astype(LOW),
    )


def padded_behind(d2):
    x = d2.astype(WIDE)
    front = lane_of(x.shape) < HDIM
    return (
        jnp.where(front, 0.0, pltpu.roll(x, HDIM, 1)).astype(LOW),
        jnp.where(front, 0.0, x).astype(LOW),
    )


def allowed_keys(key_block, first_query, begin):
    shape = (BLOCK, begin.shape[1])
    key_at = key_block * BLOCK + lax.broadcasted_iota(jnp.int32, shape, 0)
    query_at = first_query + lax.broadcasted_iota(jnp.int32, shape, 1)
    return (key_at <= query_at) & (key_at >= begin)


def forward_kernel(
    place, begin, kv0, kv1, kv2, kv3, q0, q1, q2, q3,
    o0, o1, o2, o3, out_t, total, kvs, kvt, queries, peak, acc, kept_q, kept_o,
):
    group, me = place[0], place[1]
    front = lane_of((BLOCK, 128)) < HDIM
    for k, q in enumerate((q0, q1, q2, q3)):
        kept_q[me ^ k] = q[...]
    for rel, kv in enumerate((kv0, kv1, kv2, kv3)):
        for j in range(4):
            block = 4 * j + (group ^ rel)
            kvs[block] = kv[j]
            kvt[block] = jnp.where(front, 1.0, kv[j].astype(WIDE)).T.astype(LOW)

    def one_query_block(j, carry):
        query_block = 4 * j + group
        queries[:HALF, :], queries[HALF:, :] = padded_queries(kept_q[j])
        peak[...] = jnp.full((1, BLOCK), -1e30, WIDE)
        acc[...] = jnp.zeros((128, BLOCK), WIDE)

        def four_blocks(t, carry):
            scores = []
            for key_block in [4 * t + k for k in range(4)]:
                ok = allowed_keys(key_block, query_block * BLOCK, begin[j])
                scores.append(jnp.where(ok, nt(kvs[key_block], queries[...]), -1e30))
            old = peak[...]
            new = old
            for one in scores:
                new = jnp.maximum(new, jnp.max(one, axis=0, keepdims=True))
            total_now = acc[...] * jnp.exp(old - new)
            for k in range(4):
                weights = jnp.exp(scores[k] - new).astype(LOW)
                total_now += nn(kvt[4 * t + k], weights)
            acc[...] = total_now
            peak[...] = new
            return carry

        lax.fori_loop(0, j + 1, four_blocks, 0)
        weight_sum = acc[:1, :]
        done = acc[...] / weight_sum
        out_t[j] = done
        total[j] = peak[...] + jnp.log(weight_sum)
        rows = done.T
        x, y = rows[:HALF], rows[HALF:]
        kept_o[j] = jnp.where(lane_of(x.shape) < HDIM, pltpu.roll(x, HDIM, 1), y).astype(LOW)
        return carry

    lax.fori_loop(0, 4, one_query_block, 0)
    for k, out in enumerate((o0, o1, o2, o3)):
        out[...] = kept_o[me ^ k]


def backward_kernel(
    place, begin, kv0, kv1, kv2, kv3, q0, q1, q2, q3, d0, d1, d2, d3, out_t, total,
    g0, g1, g2, g3, keep0, keep1, send0, send1,
    kvs, kvt, queries, grads, dot_rows, acc, dkv, kept_q, kept_d, kept_g,
):
    group, me = place[0], place[1]
    for k in range(4):
        kept_q[me ^ k] = (q0, q1, q2, q3)[k][...]
        kept_d[me ^ k] = (d0, d1, d2, d3)[k][...]
    for rel, kv in enumerate((kv0, kv1, kv2, kv3)):
        for j in range(4):
            block = 4 * j + (group ^ rel)
            kvs[block] = kv[j]
            kvt[block] = kv[j].astype(WIDE).T.astype(LOW)
    dkv[...] = jnp.zeros(dkv.shape, WIDE)

    def one_query_block(j, carry):
        query_block = 4 * j + group
        queries[:HALF, :], queries[HALF:, :] = padded_queries(kept_q[j])
        grads[:HALF, :], grads[HALF:, :] = padded_behind(kept_d[j])
        dot_rows[...] = jnp.sum(grads[...].astype(WIDE).T * out_t[j], axis=0, keepdims=True)
        acc[...] = jnp.zeros((128, BLOCK), WIDE)

        def four_blocks(t, carry):
            for key_block in [4 * t + k for k in range(4)]:
                term = 0.0
                for half in range(2):
                    at = slice(half * HALF, half * HALF + HALF)
                    ok = allowed_keys(key_block, query_block * BLOCK + half * HALF, begin[j][:, at])
                    scores = nt(kvs[key_block], queries[at, :])
                    probs = jnp.where(ok, jnp.exp(scores - total[j][:, at]), 0.0)
                    grad_probs = nt(kvs[key_block], grads[at, :])
                    grad_scores = (probs * (grad_probs - dot_rows[:, at])).astype(LOW)
                    term += nn(grad_scores, queries[at, :]) + nn(probs.astype(LOW), grads[at, :])
                    acc[:, at] += nn(kvt[key_block], grad_scores)
                dkv[key_block] += term
            return carry

        lax.fori_loop(0, j + 1, four_blocks, 0)
        rows = acc[...].T
        x, y = rows[:HALF], rows[HALF:]
        kept_g[j] = jnp.where(lane_of(x.shape) < HDIM, x, pltpu.roll(y, HDIM, 1)).astype(LOW)
        return carry

    lax.fori_loop(0, 4, one_query_block, 0)
    for k, out in enumerate((g0, g1, g2, g3)):
        out[...] = kept_g[me ^ k]
    for rel, out in enumerate((keep0, send0, keep1, send1)):
        for k in range(4):
            out[k] = dkv[4 * (me ^ k) + (group ^ rel)].astype(LOW)


def branch_kernel(place, h0, h1, h2, h3, w, attended, partial, kept):
    for k, h in enumerate((h0, h1, h2, h3)):
        kept[place[1] ^ k] = h[...]
    for pair in range(2):
        lanes = slice(pair * 128, pair * 128 + 128)
        x, y = exchange_halves(kept[2 * pair].astype(WIDE), kept[2 * pair + 1].astype(WIDE))
        attended[:HALF, lanes] = x.astype(LOW)
        attended[HALF:, lanes] = y.astype(LOW)
    for n in range(4):
        at = slice(n * 512, n * 512 + 512)
        partial[:, at] = nn(attended[...], w[:, at]).astype(LOW)


def grad_attended_kernel(place, grad, w, d0, d1, d2, d3, kept):
    g = nt(grad[...], w[...])
    for pair in range(2):
        lanes = slice(pair * 128, pair * 128 + 128)
        both = exchange_halves(g[:HALF, lanes], g[HALF:, lanes])
        for one in range(2):
            kept[2 * pair + one] = both[one].astype(LOW)
    for k, out in enumerate((d0, d1, d2, d3)):
        out[...] = kept[place[1] ^ k]


def grad_project_kernel(
    place, w, cosine, sine, tok, mean, scale, p0, p1, p2, p3, g0, g1, g2, g3,
    grad_mixed, partial, gain_sum, shift_sum, bias_sum, parts, kept, sems,
):
    moves = []
    for k in range(4):
        at = place[1] ^ k
        moves.append(pltpu.make_async_copy((p0, p1, p2, p3)[k], parts.at[at], sems.at[k]))
        moves.append(pltpu.make_async_copy((g0, g1, g2, g3)[k], kept.at[at], sems.at[4 + k]))
    for move in moves:
        move.start()
    for move in moves:
        move.wait()
    for pair in range(2):
        lanes = slice(pair * 128, pair * 128 + 128)
        k, v = exchange_halves(parts[2 * pair].astype(WIDE), parts[2 * pair + 1].astype(WIDE))
        q = exchange_halves(kept[2 * pair].astype(WIDE), kept[2 * pair + 1].astype(WIDE))
        q = jnp.concatenate(q, axis=0)
        q = turn(q, cosine[...], sine[...], -1.0) * 0.125
        k = turn(k, cosine[...], sine[...], -1.0)
        for c, part in enumerate((q, k, v)):
            start = c * 256 + pair * 128
            low = part.astype(LOW)
            grad_mixed[:, start : start + 128] = low
            bias_sum[c : c + 1, lanes] = jnp.sum(low.astype(WIDE), axis=0, keepdims=True)
    for n in range(4):
        at = slice(n * 512, n * 512 + 512)
        total = nt(grad_mixed[:, :256], w[0, at, :])
        total += nt(grad_mixed[:, 256:512], w[1, at, :])
        total += nt(grad_mixed[:, 512:], w[2, at, :])
        partial[:, at] = total.astype(LOW)
        normal = (tok[:, at].astype(WIDE) - mean[...]) * scale[...]
        gain_sum[:, at] = jnp.sum(total * normal, axis=0, keepdims=True)
        shift_sum[:, at] = jnp.sum(total, axis=0, keepdims=True)


def for_rows(work):
    rows = 16

    def one(i, carry):
        work(pl.ds(pl.multiple_of(i * rows, rows), rows))
        return carry

    lax.fori_loop(0, 64 // rows, one, 0)


def summed(parts, at):
    total = parts[0, at, :].astype(WIDE)
    for k in range(1, 8):
        total += parts[k, at, :].astype(WIDE)
    return total


def copy_out(copies, at, value):
    low = value.astype(LOW)
    for k in range(8):
        copies[k, at, :] = low


def second_norm_kernel(parts, tok, gain, shift, copies, middle, normal, scale_out):
    def work(at):
        x = tok[at, :].astype(WIDE) + summed(parts, at)
        center = x - jnp.mean(x, axis=-1, keepdims=True)
        scale = lax.rsqrt(jnp.mean(center * center, axis=-1, keepdims=True) + 1e-05)
        rows = center * scale
        copy_out(copies, at, rows * gain[...] + shift[...])
        middle[at, :] = x
        normal[at, :] = rows
        scale_out[at, :] = scale

    for_rows(work)


def norm_gradient(grad, rows, scale, gain):
    scaled = grad * gain
    return scale * (
        scaled
        - jnp.mean(scaled, axis=-1, keepdims=True)
        - rows * jnp.mean(scaled * rows, axis=-1, keepdims=True)
    )


def second_gradient_kernel(parts, cot, normal, scale, gain, copies, grad_middle, sums):
    sums[...] = jnp.zeros(sums.shape, WIDE)

    def work(at):
        grad, rows = summed(parts, at), normal[at, :]
        done = cot[at, :].astype(WIDE) + norm_gradient(grad, rows, scale[at, :], gain[...])
        copy_out(copies, at, done)
        grad_middle[at, :] = done
        sums[0:1, :] += jnp.sum(grad * rows, axis=0, keepdims=True)
        sums[1:2, :] += jnp.sum(grad, axis=0, keepdims=True)

    for_rows(work)


def layer_out_kernel(parts, middle, copies):
    for_rows(lambda at: copy_out(copies, at, middle[at, :] + summed(parts, at)))


def first_gradient_kernel(parts, grad_middle, tok, mean, scale, gain, copies):
    def work(at):
        rows = (tok[at, :].astype(WIDE) - mean[at, :]) * scale[at, :]
        done = norm_gradient(summed(parts, at), rows, scale[at, :], gain[...])
        copy_out(copies, at, grad_middle[at, :] + done)

    for_rows(work)


def weight_kernel(widths, place, *refs):
    count = len(widths)
    lefts, rights = refs[:count], refs[count : 2 * count]
    mine, theirs, turned = refs[2 * count :]
    first_core = place[2] == 0
    start = 0
    for left, right, width in zip(lefts, rights, widths):
        turned[:width, :] = left[...].astype(WIDE).T.astype(LOW)

        def one(n, carry, start=start, right=right, width=width):
            columns = right[:, pl.ds(pl.multiple_of(n * 256, 256), 256)]
            both = nn(turned[:width, :], columns)
            first, second = both[:, :128], both[:, 128:]
            at = pl.ds(start, width)
            mine[n, at, :] = jnp.where(first_core, first, second).astype(LOW)
            theirs[n, at, :] = jnp.where(first_core, second, first).astype(LOW)
            return carry

        lax.fori_loop(0, 8, one, 0, unroll=4)
        start += width


def weight_grads(pairs, place):
    lefts, rights = [a for a, _ in pairs], [b for _, b in pairs]
    widths = tuple(a.shape[1] for a in lefts)
    out = jax.ShapeDtypeStruct((8, sum(widths), 128), LOW)
    return kernel_call(
        functools.partial(weight_kernel, widths),
        (out, out),
        (*lefts, *rights),
        scalars=(place,),
        scratch=(pltpu.VMEM((max(widths), BLOCK), LOW),),
        flops=2 * sum(widths) * BLOCK * 2048,
    )


def swapped(x, axis):
    return lax.ppermute(x, axis, [(0, 1), (1, 0)])


def across(pieces):
    moved = [
        lax.ppermute(pieces[k], SPREAD, [(i, i ^ k) for i in range(4)]) for k in range(1, 4)
    ]
    return (pieces[0], *moved)


def z_parts(mine, received):
    rows = mine.shape[1]
    mine, received = mine.reshape(2, 4, rows, 128), received.reshape(2, 4, rows, 128)
    z = lax.axis_index(Z)
    done = []
    for k in range(4):
        at = lax.rem(z + k, 4)
        a, b = (lax.dynamic_index_in_dim(x, at, 1, False).astype(WIDE) for x in (mine, received))
        done.append((a + b).astype(LOW))
    return done


def z_permute(part, distance):
    return lax.ppermute(part, Z, [(i, (i + distance) % 4) for i in range(4)])


def xh_halves(moved):
    xh = lax.axis_index("xh")

    def added(at):
        return sum(lax.dynamic_index_in_dim(x, at, 0, False).astype(WIDE) for x in moved)

    return added(xh), added(1 - xh).astype(LOW)


def settled_kernel(x, out, sem):
    move = pltpu.make_async_copy(x, out, sem)
    move.start()
    move.wait()


def settled(x):
    return pl.pallas_call(
        settled_kernel,
        out_shape=jax.ShapeDtypeStruct(x.shape, x.dtype),
        in_specs=[pl.BlockSpec(memory_space=pl.ANY)],
        out_specs=pl.BlockSpec(memory_space=pl.ANY),
        scratch_shapes=[pltpu.SemaphoreType.DMA],
        cost_estimate=pl.CostEstimate(flops=0, bytes_accessed=2 * x.size * 2, transcendentals=0),
    )(x)


def tp_parts(partial):
    parts = partial.reshape(8, -1, partial.shape[1])
    return lax.all_to_all(parts, TP, split_axis=0, concat_axis=0, tiled=True)


def tp_rows(copies):
    rows = lax.all_to_all(copies, TP, split_axis=0, concat_axis=0, tiled=True)
    return rows.reshape(-1, copies.shape[2])


def summed_by_pairs(x, pairs):
    for axis, size, distance in pairs:
        x = x + lax.ppermute(x, axis, [(i, i ^ distance) for i in range(size)])
    return x


def shape_of(*dims, kind=LOW):
    return jax.ShapeDtypeStruct(dims, kind)


def body(
    tokens, cotangent, segment_ids, first_gain, first_shift, second_gain, second_shift,
    w_qkv, qkv_bias, w_out, w_gate_up, w_down,
):
    ctx = lax.axis_index(CTX)
    tp = lax.axis_index(TP)
    group = lax.axis_index(("zl", "core"))
    place = jnp.stack([group, lax.axis_index(SPREAD), lax.axis_index("core")])

    def my_share(array):
        return lax.dynamic_slice_in_dim(array, tp * 64, 64)

    labels = jnp.arange(DOCS, dtype=jnp.int32)
    starts = jnp.sum((segment_ids[None, :] < labels[:, None]).astype(jnp.int32), axis=1)
    begins = jnp.sum(
        jnp.where(segment_ids[None, :] == labels[:, None], starts[:, None], 0), axis=0
    )
    begin = lax.dynamic_index_in_dim(begins.reshape(4, 4, 1, BLOCK), group, 1, False)
    own = lax.dynamic_slice_in_dim(begins, ctx * BLOCK, BLOCK)
    places = ctx * BLOCK + jnp.arange(BLOCK, dtype=jnp.int32) - own
    frequency = 10000.0 ** (-jnp.arange(8, dtype=WIDE) / 8.0)
    angles = frequency[:, None] * places.astype(WIDE)[None, :]
    table = jnp.concatenate([jnp.cos(angles), jnp.sin(angles)], axis=0)

    w3 = jnp.transpose(w_qkv, (1, 0, 2))
    quarter = shape_of(HALF, 128)
    normed_low, mean1, scale1, kv, *queries, cosine, sine = kernel_call(
        project_kernel,
        (
            shape_of(BLOCK, 2048),
            shape_of(BLOCK, 1, kind=WIDE),
            shape_of(BLOCK, 1, kind=WIDE),
            shape_of(4, BLOCK, 128),
            *[quarter] * 4,
            shape_of(BLOCK, 128, kind=WIDE),
            shape_of(BLOCK, 128, kind=WIDE),
        ),
        (tokens, first_gain[None], first_shift[None], w3, qkv_bias, table),
        scalars=(place,),
        scratch=(pltpu.VMEM((4, HALF, 128), LOW),),
        flops=2 * 512 * 2048 * 768,
    )
    kv = lax.all_to_all(kv, SPREAD, split_axis=0, concat_axis=0, tiled=True)
    queries = across(queries)
    kv_z, *queries = lax.optimization_barrier((swapped(kv, "zl"), *queries))
    kv_parts = (kv, swapped(kv, "core"), kv_z, swapped(kv_z, "core"))
    *heads, out_t, total = kernel_call(
        forward_kernel,
        (*[quarter] * 4, shape_of(4, 128, BLOCK, kind=WIDE), shape_of(4, 1, BLOCK, kind=WIDE)),
        (begin, *kv_parts, *queries),
        scalars=(place,),
        scratch=(
            pltpu.VMEM((16, BLOCK, 128), LOW),
            pltpu.VMEM((16, 128, BLOCK), LOW),
            pltpu.VMEM((BLOCK, 128), LOW),
            pltpu.VMEM((1, BLOCK), WIDE),
            pltpu.VMEM((128, BLOCK), WIDE),
            pltpu.VMEM((4, HALF, 128), LOW),
            pltpu.VMEM((4, HALF, 128), LOW),
        ),
        flops=40 * 4 * BLOCK * BLOCK * 128,
        mib=32,
        exps=40 * BLOCK * BLOCK,
    )
    heads = across(heads)
    attended_low, partial_branch = kernel_call(
        branch_kernel,
        (shape_of(BLOCK, 256), shape_of(BLOCK, 2048)),
        (*heads, w_out),
        scalars=(place,),
        scratch=(pltpu.VMEM((4, HALF, 128), LOW),),
        flops=2 * 512 * 256 * 2048,
    )
    share = shape_of(64, 2048, kind=WIDE)
    copies = shape_of(8, 64, 2048)
    copies2, middle, second_rows, second_scale = kernel_call(
        second_norm_kernel,
        (copies, share, share, shape_of(64, 1, kind=WIDE)),
        (tp_parts(partial_branch), my_share(tokens), second_gain[None], second_shift[None]),
    )
    second_low, cot_share = lax.optimization_barrier((tp_rows(copies2), my_share(cotangent)))

    gate_up = jnp.einsum("td,dcf->tcf", second_low, w_gate_up, preferred_element_type=WIDE)
    gate, up = gate_up[:, 0], gate_up[:, 1]
    sigmoid_gate = jax.nn.sigmoid(gate)
    activated = gate * sigmoid_gate
    hidden_low = (activated * up).astype(LOW)
    grad_hidden = jnp.einsum("td,fd->tf", cotangent, w_down, preferred_element_type=WIDE)
    grad_gate = grad_hidden * up * sigmoid_gate * (1.0 + gate * (1.0 - sigmoid_gate))
    grad_gate = grad_gate.astype(LOW)
    grad_up = (grad_hidden * activated).astype(LOW)
    partial_second = jnp.einsum(
        "tcf,dcf->td", jnp.stack([grad_gate, grad_up], axis=1), w_gate_up, preferred_element_type=WIDE
    ).astype(LOW)
    grad_gate, partial_second = lax.optimization_barrier((grad_gate, partial_second))
    second_parts = tp_parts(partial_second)

    feed_mine, feed_theirs = weight_grads(
        ((grad_gate, second_low), (grad_up, second_low), (hidden_low, cotangent)), place
    )
    second_parts, feed_mine, feed_theirs = lax.optimization_barrier(
        (second_parts, feed_mine, feed_theirs)
    )
    copies3, grad_middle, second_sums = kernel_call(
        second_gradient_kernel,
        (copies, share, shape_of(2, 2048, kind=WIDE)),
        (second_parts, cot_share, second_rows, second_scale, second_gain[None]),
    )
    grad_branch = tp_rows(copies3)
    feed_received = swapped(feed_theirs, "core")
    feed_z = z_parts(feed_mine, feed_received)
    feed_1, feed_3 = z_permute(feed_z[1], 1), z_permute(feed_z[3], 3)

    grads = kernel_call(
        grad_attended_kernel,
        (*[quarter] * 4,),
        (grad_branch, w_out),
        scalars=(place,),
        scratch=(pltpu.VMEM((4, HALF, 128), LOW),),
        flops=2 * 512 * 256 * 2048,
    )
    hidden_low, feed_1, feed_3, *grads = lax.optimization_barrier(
        (hidden_low, feed_1, feed_3, *grads)
    )
    partial_feed = jnp.dot(hidden_low, w_down, preferred_element_type=WIDE).astype(LOW)
    *grads, partial_feed, feed_2 = lax.optimization_barrier(
        (*across(grads), partial_feed, feed_z[2])
    )
    feed_parts = tp_parts(partial_feed)
    feed_2 = z_permute(feed_2, 2)
    backward = kernel_call(
        backward_kernel,
        (*[quarter] * 4, *[shape_of(4, BLOCK, 128)] * 4),
        (begin, *kv_parts, *queries, *grads, out_t, total),
        scalars=(place,),
        scratch=(
            pltpu.VMEM((16, BLOCK, 128), LOW),
            pltpu.VMEM((16, 128, BLOCK), LOW),
            pltpu.VMEM((BLOCK, 128), LOW),
            pltpu.VMEM((BLOCK, 128), LOW),
            pltpu.VMEM((1, BLOCK), WIDE),
            pltpu.VMEM((128, BLOCK), WIDE),
            pltpu.VMEM((16, BLOCK, 128), WIDE),
            *[pltpu.VMEM((4, HALF, 128), LOW)] * 3,
        ),
        flops=40 * 10 * BLOCK * BLOCK * 128,
        mib=32,
        exps=40 * BLOCK * BLOCK,
    )
    *backward, feed_parts, feed_2 = lax.optimization_barrier((*backward, feed_parts, feed_2))
    *grad_queries, keep0, keep1, send0, send1 = backward
    feed_keep, feed_send = xh_halves([feed_z[0], feed_1, feed_2, feed_3])
    far, feed_send = lax.optimization_barrier((swapped(send1, "core"), feed_send))
    feed_received = swapped(feed_send, "xh")
    far = (keep1.astype(WIDE) + far.astype(WIDE)).astype(LOW)
    far, send0 = lax.optimization_barrier((far, send0))
    near = keep0.astype(WIDE) + swapped(send0, "core").astype(WIDE)
    near, feed_parts = lax.optimization_barrier((near, feed_parts))
    copies4 = kernel_call(layer_out_kernel, copies, (feed_parts, middle))
    layer_out = tp_rows(copies4)
    far, *grad_queries = lax.optimization_barrier((swapped(far, "zl"), *across(grad_queries)))
    grad_kv = across([(near[k] + far[k].astype(WIDE)).astype(LOW) for k in range(4)])
    layer_out, feed_received, *grad_kv = lax.optimization_barrier(
        (layer_out, feed_received, *grad_kv)
    )
    layer_out = settled(layer_out)
    grad_mixed, partial_normed, gain_sum, shift_sum, bias_sum = kernel_call(
        grad_project_kernel,
        (
            shape_of(BLOCK, 768),
            shape_of(BLOCK, 2048),
            shape_of(1, 2048, kind=WIDE),
            shape_of(1, 2048, kind=WIDE),
            shape_of(3, 256, kind=WIDE),
        ),
        (w3, cosine, sine, tokens, mean1, scale1),
        far=(*grad_kv, *grad_queries),
        scalars=(place,),
        scratch=(
            pltpu.VMEM((4, BLOCK, 128), LOW),
            pltpu.VMEM((4, HALF, 128), LOW),
            pltpu.SemaphoreType.DMA((8,)),
        ),
        flops=2 * 512 * 2048 * 768,
    )
    grad_mixed, partial_normed = lax.optimization_barrier((grad_mixed, partial_normed))
    normed_parts = tp_parts(partial_normed)

    rest_mine, rest_theirs = weight_grads(
        ((grad_mixed, normed_low), (attended_low, grad_branch)), place
    )
    vectors = jnp.concatenate([gain_sum, shift_sum, second_sums], axis=0).reshape(32, 256)
    vectors = jnp.concatenate([vectors, bias_sum], axis=0)
    normed_parts, rest_mine, vectors = lax.optimization_barrier((normed_parts, rest_mine, vectors))
    rest_received = swapped(rest_theirs, "core")
    vectors = summed_by_pairs(
        vectors, (("core", 2, 1), ("zl", 2, 1), ("zh", 2, 1), ("xh", 2, 1))
    )
    bias_grad = vectors[32:]
    rest_z = z_parts(rest_mine, rest_received)

    copies5 = kernel_call(
        first_gradient_kernel,
        copies,
        (
            normed_parts,
            grad_middle,
            my_share(tokens),
            my_share(mean1),
            my_share(scale1),
            first_gain[None],
        ),
    )
    grad_tokens = settled(tp_rows(copies5))

    vectors = vectors[:32].reshape(4, 2048)
    vectors = summed_by_pairs(vectors, (("y", 4, 1), ("y", 4, 2), ("xl", 2, 1)))
    rest_keep, rest_send = xh_halves(
        [rest_z[0], *[z_permute(rest_z[k], k) for k in range(1, 4)]]
    )
    rest_w = rest_keep + swapped(rest_send, "xh").astype(WIDE)
    feed_w = feed_keep + feed_received.astype(WIDE)
    return (
        layer_out,
        grad_tokens,
        vectors[0],
        vectors[1],
        vectors[2],
        vectors[3],
        jnp.transpose(rest_w[:768].reshape(3, 256, 128), (2, 0, 1)),
        bias_grad,
        rest_w[768:],
        jnp.transpose(feed_w[:1408].reshape(2, 704, 128), (2, 0, 1)),
        feed_w[1408:],
    )


def solution(mesh):
    fine = Mesh(
        mesh.devices.reshape(2, 2, 2, 2, 4, 2), ("xh", "zh", "zl", "core", "y", "xl")
    )
    rows = P(CTX, None)
    return jax.shard_map(
        body,
        mesh=fine,
        in_specs=(
            rows, rows, P(), P(), P(), P(), P(),
            P(None, None, TP), P(None, TP), P(TP, None), P(None, None, TP), P(TP, None),
        ),
        out_specs=(
            rows, rows, P(), P(), P(), P(),
            P(CTX, None, TP), P(None, TP), P(TP, CTX), P(CTX, None, TP), P(TP, CTX),
        ),
        check_vma=False,
    )
```

```python
import functools

import jax
import jax.numpy as jnp
from jax import lax
from jax.experimental import pallas as pl
from jax.experimental.pallas import tpu as pltpu
from jax.sharding import Mesh
from jax.sharding import PartitionSpec as P

HDIM = 64
DOCS = 3
BLOCK = 512
HALF = 256
LOW = jnp.bfloat16
WIDE = jnp.float32
CTX = ("xh", "zh", "zl", "core")
TP = ("y", "xl")
SPREAD = ("xh", "zh")
Z = ("zh", "zl")


def size_of(a):
    return a.size * jnp.dtype(a.dtype).itemsize


def kernel_call(
    body, outs, inputs, *, small=(), small_outs=(), scalars=(), scratch=(), late=0, flops=0, exps=0, mib=12
):
    counts = [len(x) for x in (scalars, inputs, small, outs, small_outs, inputs, outs)]

    def run(*refs):
        groups, at = [], 0
        for n in counts:
            groups.append(refs[at : at + n])
            at += n
        scalar_refs, far_in, near_in, far_out, near_out, held_in, held_out = groups
        arrived, left, *rest = refs[at:]
        moves = [
            pltpu.make_async_copy(a, b, arrived.at[k]) for k, (a, b) in enumerate(zip(far_in, held_in))
        ]
        for move in moves:
            move.start()
        early = len(moves) - late
        for move in moves[:early]:
            move.wait()

        def arrive():
            for move in moves[early:]:
                move.wait()

        body(
            *([arrive] if late else []),
            *scalar_refs, *held_in, *near_in, *held_out, *near_out, *rest,
        )
        moves = [
            pltpu.make_async_copy(a, b, left.at[k]) for k, (a, b) in enumerate(zip(held_out, far_out))
        ]
        for move in moves:
            move.start()
        for move in moves:
            move.wait()

    vmem, hbm = pl.BlockSpec(memory_space=pltpu.VMEM), pl.BlockSpec(memory_space=pltpu.HBM)
    held = [pltpu.VMEM(a.shape, a.dtype) for a in (*inputs, *outs)]
    limit = sum(size_of(a) for a in (*inputs, *outs, *small, *small_outs)) + mib * 1024 * 1024
    return pl.pallas_call(
        run,
        out_shape=(*outs, *small_outs),
        in_specs=[pl.BlockSpec(memory_space=pltpu.SMEM)] * len(scalars)
        + [hbm] * len(inputs)
        + [vmem] * len(small),
        out_specs=(*[hbm] * len(outs), *[vmem] * len(small_outs)),
        scratch_shapes=[
            *held,
            pltpu.SemaphoreType.DMA((len(inputs),)),
            pltpu.SemaphoreType.DMA((max(1, len(outs)),)),
            *scratch,
        ],
        compiler_params=pltpu.CompilerParams(vmem_limit_bytes=limit),
        cost_estimate=pl.CostEstimate(
            flops=flops,
            bytes_accessed=sum(size_of(a) for a in (*inputs, *outs)),
            transcendentals=exps,
        ),
    )(*scalars, *inputs, *small)


def lane_of(shape):
    return lax.broadcasted_iota(jnp.int32, shape, len(shape) - 1)


def exchange_halves(a, b):
    front = lane_of(a.shape) < HDIM
    return (
        jnp.where(front, a, pltpu.roll(b, HDIM, 1)),
        jnp.where(front, pltpu.roll(a, HDIM, 1), b),
    )


def nt(a, b):
    return lax.dot_general(a, b, (((1,), (1,)), ((), ())), preferred_element_type=WIDE)


def nn(a, b):
    return lax.dot_general(a, b, (((1,), (0,)), ((), ())), preferred_element_type=WIDE)


def turn(x, cosine, sine, sign):
    lane = lax.rem(lane_of(x.shape), HDIM)
    ahead = pltpu.roll(x, x.shape[1] - 8, 1)
    behind = pltpu.roll(x, 8, 1)
    swapped = jnp.where(lane < 8, -ahead, behind) * sign
    return x * cosine + swapped * sine


def rotation_table(angles_table):
    tokens = angles_table.shape[1]
    rest = jnp.zeros((112, tokens), WIDE)
    x = jnp.concatenate([angles_table, rest], axis=0).T
    lane = lane_of(x.shape)
    c = jnp.where(lane < 8, x, 0.0)
    c = c + pltpu.roll(c, 8, 1)
    c = c + pltpu.roll(c, HDIM, 1) + jnp.where(lax.rem(lane, HDIM) < 16, 0.0, 1.0)
    s = jnp.where((lane >= 8) & (lane < 16), x, 0.0)
    s = s + pltpu.roll(s, 120, 1)
    s = s + pltpu.roll(s, HDIM, 1)
    return c, s


def project_kernel(
    arrive, place, tok, table, w, gain, shift, bias,
    normed, stats, kv0, kv1, kv2, kv3, q0, q1, q2, q3, cosine_out, sine_out, kept_kv, kept_q,
):
    rows = 64

    def norm_rows(i, carry):
        at = pl.ds(pl.multiple_of(i * rows, rows), rows)
        x = tok[at, :].astype(WIDE)
        mean = jnp.mean(x, axis=-1, keepdims=True)
        center = x - mean
        scale = lax.rsqrt(jnp.mean(center * center, axis=-1, keepdims=True) + 1e-05)
        normed[at, :] = (center * scale * gain[...] + shift[...]).astype(LOW)
        stats[at, :] = jnp.where(lane_of((rows, 128)) < HDIM, mean, scale)
        return carry

    lax.fori_loop(0, BLOCK // rows, norm_rows, 0)
    cosine, sine = rotation_table(table[...])
    cosine_out[...] = cosine
    sine_out[...] = sine
    arrive()
    mixed = [nn(normed[...], w[c]) + bias[c : c + 1, :] for c in range(3)]
    for pair in range(2):
        lanes = slice(pair * 128, pair * 128 + 128)
        q = turn(mixed[0][:, lanes], cosine, sine, 1.0) * 0.125
        k = turn(mixed[1][:, lanes], cosine, sine, 1.0)
        kv = exchange_halves(k, mixed[2][:, lanes])
        qq = exchange_halves(q[:HALF], q[HALF:])
        for one in range(2):
            kept_kv[2 * pair + one] = kv[one].astype(LOW)
            kept_q[2 * pair + one] = qq[one].astype(LOW)
    for k in range(4):
        (kv0, kv1, kv2, kv3)[k][...] = kept_kv[place[1] ^ k]
        (q0, q1, q2, q3)[k][...] = kept_q[place[1] ^ k]


def padded_queries(q2):
    x = q2.astype(WIDE)
    front = lane_of(x.shape) < HDIM
    return (
        jnp.where(front, x, 0.0).astype(LOW),
        jnp.where(front, pltpu.roll(x, HDIM, 1), 0.0).astype(LOW),
    )


def padded_behind(d2):
    x = d2.astype(WIDE)
    front = lane_of(x.shape) < HDIM
    return (
        jnp.where(front, 0.0, pltpu.roll(x, HDIM, 1)).astype(LOW),
        jnp.where(front, 0.0, x).astype(LOW),
    )


def allowed_keys(key_block, first_query, begin):
    shape = (BLOCK, begin.shape[1])
    key_at = key_block * BLOCK + lax.broadcasted_iota(jnp.int32, shape, 0)
    query_at = first_query + lax.broadcasted_iota(jnp.int32, shape, 1)
    return (key_at <= query_at) & (key_at >= begin)


def key_blocks(place, rels, t):
    return [4 * t + (place[0] ^ rel) for rel in rels], place[1] ^ t


def forward_kernel(rels, first, last, *refs):
    place, kv0, kv1, q0, q1, q2, q3, begin = refs[:8]
    if first:
        acc_out, peak_out, kvt, queries, kept_q = refs[8:]
    else:
        acc_in, peak_in, o0, o1, o2, o3, out_t, total, kvt, queries, kept_q, kept_o = refs[8:]
        acc_out, peak_out = out_t, total
    me = place[1]
    front = lane_of((BLOCK, 128)) < HDIM
    for k, q in enumerate((q0, q1, q2, q3)):
        kept_q[me ^ k] = q[...]
    for i, kv in enumerate((kv0, kv1)):
        for t in range(4):
            kvt[i, t] = jnp.where(front, 1.0, kv[t].astype(WIDE)).T.astype(LOW)

    def one_query_block(j, carry):
        first_query = (4 * j + place[0]) * BLOCK
        queries[:HALF, :], queries[HALF:, :] = padded_queries(kept_q[j])
        if first:
            peak_out[j] = jnp.full((8, BLOCK), -1e30, WIDE)
            acc_out[j] = jnp.zeros((128, BLOCK), WIDE)
        else:
            peak_out[j] = peak_in[j]
            acc_out[j] = acc_in[j]

        def two_blocks(t, carry):
            blocks, at = key_blocks(place, rels, t)
            scores = []
            for i, kv in enumerate((kv0, kv1)):
                ok = allowed_keys(blocks[i], first_query, begin[j, :1])
                scores.append(jnp.where(ok, nt(kv[at], queries[...]), -1e30))
            old = peak_out[j, :1]
            new = old
            for one in scores:
                new = jnp.maximum(new, jnp.max(one, axis=0, keepdims=True))
            done = acc_out[j] * jnp.exp(old - new)
            for i in range(2):
                done += nn(kvt[i, at], jnp.exp(scores[i] - new).astype(LOW))
            acc_out[j] = done
            peak_out[j, :1] = new
            return carry

        lax.fori_loop(0, j + 1, two_blocks, 0)
        if last:
            weight_sum = acc_out[j, :1]
            done = acc_out[j] / weight_sum
            out_t[j] = done
            total[j, :1] = peak_out[j, :1] + jnp.log(weight_sum)
            rows = done.T
            x, y = rows[:HALF], rows[HALF:]
            kept_o[j] = jnp.where(lane_of(x.shape) < HDIM, pltpu.roll(x, HDIM, 1), y).astype(LOW)
        return carry

    lax.fori_loop(0, 4, one_query_block, 0)
    if last:
        for k, out in enumerate((o0, o1, o2, o3)):
            out[...] = kept_o[me ^ k]


def backward_kernel(rels, first, *refs):
    place, kv0, kv1, q0, q1, q2, q3, d0, d1, d2, d3, out_t, total, begin = refs[:14]
    if first:
        acc, keep, send, kvt, queries, grads, dot_rows, dkv, kept_q, kept_d = refs[14:]
    else:
        (
            acc_in, g0, g1, g2, g3, keep, send,
            kvt, queries, grads, dot_rows, dkv, kept_q, kept_d, acc, kept_g,
        ) = refs[14:]
    me = place[1]
    for k in range(4):
        kept_q[me ^ k] = (q0, q1, q2, q3)[k][...]
        kept_d[me ^ k] = (d0, d1, d2, d3)[k][...]
    for i, kv in enumerate((kv0, kv1)):
        for t in range(4):
            kvt[i, t] = kv[t].astype(WIDE).T.astype(LOW)
    dkv[...] = jnp.zeros(dkv.shape, WIDE)

    def one_query_block(j, carry):
        first_query = (4 * j + place[0]) * BLOCK
        queries[:HALF, :], queries[HALF:, :] = padded_queries(kept_q[j])
        grads[:HALF, :], grads[HALF:, :] = padded_behind(kept_d[j])
        dot_rows[...] = jnp.sum(grads[...].astype(WIDE).T * out_t[j], axis=0, keepdims=True)
        acc[j] = jnp.zeros((128, BLOCK), WIDE) if first else acc_in[j]

        def two_blocks(t, carry):
            blocks, at = key_blocks(place, rels, t)
            for i, kv in enumerate((kv0, kv1)):
                term = 0.0
                for half in range(2):
                    some = slice(half * HALF, half * HALF + HALF)
                    ok = allowed_keys(blocks[i], first_query + half * HALF, begin[j, :1, some])
                    scores = nt(kv[at], queries[some, :])
                    probs = jnp.where(ok, jnp.exp(scores - total[j, :1, some]), 0.0)
                    grad_probs = nt(kv[at], grads[some, :])
                    grad_scores = (probs * (grad_probs - dot_rows[:, some])).astype(LOW)
                    term += nn(grad_scores, queries[some, :]) + nn(probs.astype(LOW), grads[some, :])
                    acc[j, :, some] += nn(kvt[i, at], grad_scores)
                dkv[i, at] += term
            return carry

        lax.fori_loop(0, j + 1, two_blocks, 0)
        if not first:
            rows = acc[j].T
            x, y = rows[:HALF], rows[HALF:]
            kept_g[j] = jnp.where(lane_of(x.shape) < HDIM, x, pltpu.roll(y, HDIM, 1)).astype(LOW)
        return carry

    lax.fori_loop(0, 4, one_query_block, 0)
    if not first:
        for k, out in enumerate((g0, g1, g2, g3)):
            out[...] = kept_g[me ^ k]
    for t in range(4):
        keep[t] = dkv[0, t].astype(LOW)
        send[t] = dkv[1, t].astype(LOW)


def branch_kernel(arrive, place, h0, h1, h2, h3, w, attended, partial, kept):
    for k, h in enumerate((h0, h1, h2, h3)):
        kept[place[1] ^ k] = h[...]
    for pair in range(2):
        lanes = slice(pair * 128, pair * 128 + 128)
        x, y = exchange_halves(kept[2 * pair].astype(WIDE), kept[2 * pair + 1].astype(WIDE))
        attended[:HALF, lanes] = x.astype(LOW)
        attended[HALF:, lanes] = y.astype(LOW)
    arrive()
    for n in range(4):
        at = slice(n * 512, n * 512 + 512)
        partial[:, at] = nn(attended[...], w[:, at]).astype(LOW)


def grad_attended_kernel(place, grad, w, d0, d1, d2, d3, kept):
    g = nt(grad[...], w[...])
    for pair in range(2):
        lanes = slice(pair * 128, pair * 128 + 128)
        both = exchange_halves(g[:HALF, lanes], g[HALF:, lanes])
        for one in range(2):
            kept[2 * pair + one] = both[one].astype(LOW)
    for k, out in enumerate((d0, d1, d2, d3)):
        out[...] = kept[place[1] ^ k]


def grad_project_kernel(
    arrive, place, p0, p1, p2, p3, g0, g1, g2, g3, cosine, sine, tok, stats, w,
    grad_mixed, partial, gain_sum, shift_sum, bias_sum, parts, kept,
):
    for k in range(4):
        parts[place[1] ^ k] = (p0, p1, p2, p3)[k][...]
        kept[place[1] ^ k] = (g0, g1, g2, g3)[k][...]
    for pair in range(2):
        lanes = slice(pair * 128, pair * 128 + 128)
        k, v = exchange_halves(parts[2 * pair].astype(WIDE), parts[2 * pair + 1].astype(WIDE))
        q = exchange_halves(kept[2 * pair].astype(WIDE), kept[2 * pair + 1].astype(WIDE))
        q = jnp.concatenate(q, axis=0)
        q = turn(q, cosine[...], sine[...], -1.0) * 0.125
        k = turn(k, cosine[...], sine[...], -1.0)
        for c, part in enumerate((q, k, v)):
            start = c * 256 + pair * 128
            low = part.astype(LOW)
            grad_mixed[:, start : start + 128] = low
            bias_sum[c : c + 1, lanes] = jnp.sum(low.astype(WIDE), axis=0, keepdims=True)
    arrive()
    mean, scale = stats[:, 0:1], stats[:, 64:65]
    for n in range(4):
        at = slice(n * 512, n * 512 + 512)
        total = nt(grad_mixed[:, :256], w[0, at, :])
        total += nt(grad_mixed[:, 256:512], w[1, at, :])
        total += nt(grad_mixed[:, 512:], w[2, at, :])
        partial[:, at] = total.astype(LOW)
        normal = (tok[:, at].astype(WIDE) - mean) * scale
        gain_sum[:, at] = jnp.sum(total * normal, axis=0, keepdims=True)
        shift_sum[:, at] = jnp.sum(total, axis=0, keepdims=True)


def hidden_gradient_kernel(cot, w, grad_hidden):
    grad_hidden[...] = nt(cot[...], w[...])


def feed_kernel(arrive, second, w_gate, w_up, grad_hidden, hidden, grad_gate, grad_up, partial):
    gate = nt(second[...], w_gate[0])
    arrive()
    up = nt(second[...], w_up[0])
    sigmoid = 1.0 / (1.0 + jnp.exp(-gate))
    activated = gate * sigmoid
    hidden[...] = (activated * up).astype(LOW)
    grad = grad_hidden[...]
    grad_up[...] = (grad * activated).astype(LOW)
    grad_gate[...] = (grad * up * sigmoid * (1.0 + gate * (1.0 - sigmoid))).astype(LOW)
    for n in range(4):
        at = slice(n * 512, n * 512 + 512)
        partial[:, at] = (nn(grad_gate[...], w_gate[0, :, at]) + nn(grad_up[...], w_up[0, :, at])).astype(LOW)


def for_rows(work):
    rows = 16

    def one(i, carry):
        work(pl.ds(pl.multiple_of(i * rows, rows), rows))
        return carry

    lax.fori_loop(0, 64 // rows, one, 0)


def summed(parts, at):
    total = parts[0, at, :].astype(WIDE)
    for k in range(1, 8):
        total += parts[k, at, :].astype(WIDE)
    return total


def copy_out(copies, at, value):
    low = value.astype(LOW)
    for k in range(8):
        copies[k, at, :] = low


def second_norm_kernel(parts, tok, gain, shift, copies, middle, normal, stats):
    def work(at):
        x = tok[at, :].astype(WIDE) + summed(parts, at)
        center = x - jnp.mean(x, axis=-1, keepdims=True)
        scale = lax.rsqrt(jnp.mean(center * center, axis=-1, keepdims=True) + 1e-05)
        rows = center * scale
        copy_out(copies, at, rows * gain[...] + shift[...])
        middle[at, :] = x
        normal[at, :] = rows
        stats[at, :] = jnp.broadcast_to(scale, (scale.shape[0], 128))

    for_rows(work)


def norm_gradient(grad, rows, scale, gain):
    scaled = grad * gain
    return scale * (
        scaled
        - jnp.mean(scaled, axis=-1, keepdims=True)
        - rows * jnp.mean(scaled * rows, axis=-1, keepdims=True)
    )


def second_gradient_kernel(parts, cot, normal, stats, gain, copies, grad_middle, sums):
    sums[...] = jnp.zeros(sums.shape, WIDE)

    def work(at):
        grad, rows = summed(parts, at), normal[at, :]
        done = cot[at, :].astype(WIDE) + norm_gradient(grad, rows, stats[at, 0:1], gain[...])
        copy_out(copies, at, done)
        grad_middle[at, :] = done
        sums[0:1, :] += jnp.sum(grad * rows, axis=0, keepdims=True)
        sums[1:2, :] += jnp.sum(grad, axis=0, keepdims=True)

    for_rows(work)


def feed_sum_kernel(place, parts, middle, out):
    rows = 16
    mine = place[3]

    def one(i, carry):
        at = pl.ds(pl.multiple_of(i * rows, rows), rows)
        total = parts[0, at, :].astype(WIDE)
        for k in range(1, 4):
            total += parts[k, at, :].astype(WIDE)
        here = i * rows - mine * 64
        own = pl.ds(pl.multiple_of(jnp.clip(here, 0, 64 - rows), rows), rows)
        inside = (here >= 0) & (here < 64)
        out[at, :] = (total + jnp.where(inside, middle[own, :], 0.0)).astype(LOW)
        return carry

    lax.fori_loop(0, 128 // rows, one, 0)


def layer_out_kernel(a, b, copies):
    rows = 16

    def one(i, carry):
        at = pl.ds(pl.multiple_of(i * rows, rows), rows)
        low = (a[at, :].astype(WIDE) + b[at, :].astype(WIDE)).astype(LOW)
        for k in range(4):
            copies[k, at, :] = low
        return carry

    lax.fori_loop(0, 128 // rows, one, 0)


def first_gradient_kernel(parts, grad_middle, tok, stats, gain, copies):
    def work(at):
        mean, scale = stats[at, 0:1], stats[at, 64:65]
        rows = (tok[at, :].astype(WIDE) - mean) * scale
        done = norm_gradient(summed(parts, at), rows, scale, gain[...])
        copy_out(copies, at, grad_middle[at, :] + done)

    for_rows(work)


def weight_kernel(widths, place, *refs):
    count = len(widths)
    lefts, rights = refs[:count], refs[count : 2 * count]
    mine, theirs, turned = refs[2 * count :]
    first_core = place[2] == 0
    start = 0
    for left, right, width in zip(lefts, rights, widths):
        turned[:width, :] = left[...].astype(WIDE).T.astype(LOW)

        def one(n, carry, start=start, right=right, width=width):
            columns = right[:, pl.ds(pl.multiple_of(n * 256, 256), 256)]
            both = nn(turned[:width, :], columns)
            first, second = both[:, :128], both[:, 128:]
            at = pl.ds(start, width)
            mine[n, at, :] = jnp.where(first_core, first, second).astype(LOW)
            theirs[n, at, :] = jnp.where(first_core, second, first).astype(LOW)
            return carry

        lax.fori_loop(0, 8, one, 0, unroll=4)
        start += width


def weight_grads(pairs, place):
    lefts, rights = [a for a, _ in pairs], [b for _, b in pairs]
    widths = tuple(a.shape[1] for a in lefts)
    out = jax.ShapeDtypeStruct((8, sum(widths), 128), LOW)
    return kernel_call(
        functools.partial(weight_kernel, widths),
        (out, out),
        (*lefts, *rights),
        scalars=(place,),
        scratch=(pltpu.VMEM((max(widths), BLOCK), LOW),),
        flops=2 * sum(widths) * BLOCK * 2048,
    )


def swapped(x, axis):
    return lax.ppermute(x, axis, [(0, 1), (1, 0)])


def across(pieces):
    moved = [
        lax.ppermute(pieces[k], SPREAD, [(i, i ^ k) for i in range(4)]) for k in range(1, 4)
    ]
    return (pieces[0], *moved)


def z_parts(mine, received):
    rows = mine.shape[1]
    mine, received = mine.reshape(2, 4, rows, 128), received.reshape(2, 4, rows, 128)
    z = lax.axis_index(Z)
    done = []
    for k in range(4):
        at = lax.rem(z + k, 4)
        a, b = (lax.dynamic_index_in_dim(x, at, 1, False).astype(WIDE) for x in (mine, received))
        done.append((a + b).astype(LOW))
    return done


def z_permute(part, distance):
    return lax.ppermute(part, Z, [(i, (i + distance) % 4) for i in range(4)])


def xh_halves(moved):
    xh = lax.axis_index("xh")

    def added(at):
        return sum(lax.dynamic_index_in_dim(x, at, 0, False).astype(WIDE) for x in moved)

    return added(xh), added(1 - xh).astype(LOW)


def dealt(x, axis):
    return lax.all_to_all(x, axis, split_axis=0, concat_axis=0, tiled=True)


def tp_parts(partial):
    return dealt(partial.reshape(8, -1, partial.shape[1]), TP)


def tp_rows(copies):
    return dealt(copies, TP).reshape(-1, copies.shape[2])


def summed_by_pairs(x, pairs):
    for axis, size, distance in pairs:
        x = x + lax.ppermute(x, axis, [(i, i ^ distance) for i in range(size)])
    return x


def shape_of(*dims, kind=LOW):
    return jax.ShapeDtypeStruct(dims, kind)


def body(
    tokens, cotangent, segment_ids, first_gain, first_shift, second_gain, second_shift,
    w_qkv, qkv_bias, w_out, w_gate_up, w_down,
):
    ctx = lax.axis_index(CTX)
    tp = lax.axis_index(TP)
    group = lax.axis_index(("zl", "core"))
    place = jnp.stack(
        [group, lax.axis_index(SPREAD), lax.axis_index("core"), lax.axis_index("xl")]
    )
    tied = lax.optimization_barrier

    def my_share(array):
        return lax.dynamic_slice_in_dim(array, tp * 64, 64)

    labels = jnp.arange(DOCS, dtype=jnp.int32)
    starts = jnp.sum((segment_ids[None, :] < labels[:, None]).astype(jnp.int32), axis=1)
    begins = jnp.sum(
        jnp.where(segment_ids[None, :] == labels[:, None], starts[:, None], 0), axis=0
    )
    begin = lax.dynamic_index_in_dim(begins.reshape(4, 4, 1, BLOCK), group, 1, False)
    begin = jnp.broadcast_to(begin, (4, 8, BLOCK))
    own = lax.dynamic_slice_in_dim(begins, ctx * BLOCK, BLOCK)
    places = ctx * BLOCK + jnp.arange(BLOCK, dtype=jnp.int32) - own
    frequency = 10000.0 ** (-jnp.arange(8, dtype=WIDE) / 8.0)
    angles = frequency[:, None] * places.astype(WIDE)[None, :]
    table = jnp.concatenate([jnp.cos(angles), jnp.sin(angles)], axis=0)

    w3 = jnp.transpose(w_qkv, (1, 0, 2))
    w2 = jnp.transpose(w_gate_up, (1, 2, 0))
    quarter, block = shape_of(HALF, 128), shape_of(BLOCK, 128)
    wide_block = shape_of(BLOCK, 128, kind=WIDE)
    four = pltpu.VMEM((4, HALF, 128), LOW)
    normed_low, stats1, *packed, cosine, sine = kernel_call(
        project_kernel,
        (shape_of(BLOCK, 2048), wide_block, *[block] * 4, *[quarter] * 4, wide_block, wide_block),
        (tokens, table, w3),
        small=(first_gain[None], first_shift[None], qkv_bias),
        scalars=(place,),
        scratch=(pltpu.VMEM((4, BLOCK, 128), LOW), four),
        late=1,
        flops=2 * 512 * 2048 * 768,
    )
    kv = jnp.stack(across(packed[:4]))
    queries = across(packed[4:])
    kv_c = swapped(kv, "core")
    state = (shape_of(4, 128, BLOCK, kind=WIDE), shape_of(4, 8, BLOCK, kind=WIDE))
    acc, peak = kernel_call(
        functools.partial(forward_kernel, (0, 1), True, False),
        state,
        (kv, kv_c, *queries, begin),
        scalars=(place,),
        scratch=(pltpu.VMEM((2, 4, 128, BLOCK), LOW), pltpu.VMEM((BLOCK, 128), LOW), four),
        flops=20 * 4 * BLOCK * BLOCK * 128,
        exps=20 * BLOCK * BLOCK,
        mib=24,
    )
    acc, peak, kv_z = tied((acc, peak, swapped(kv, "zl")))
    kv_zc = swapped(kv_z, "core")
    *heads, out_t, total = kernel_call(
        functools.partial(forward_kernel, (2, 3), False, True),
        (*[quarter] * 4, *state),
        (kv_z, kv_zc, *queries, begin, acc, peak),
        scalars=(place,),
        scratch=(pltpu.VMEM((2, 4, 128, BLOCK), LOW), pltpu.VMEM((BLOCK, 128), LOW), four, four),
        flops=20 * 4 * BLOCK * BLOCK * 128,
        exps=20 * BLOCK * BLOCK,
        mib=24,
    )
    heads = across(heads)
    attended_low, partial_branch = kernel_call(
        branch_kernel,
        (shape_of(BLOCK, 256), shape_of(BLOCK, 2048)),
        (*heads, w_out),
        scalars=(place,),
        scratch=(four,),
        late=1,
        flops=2 * 512 * 256 * 2048,
    )
    share = shape_of(64, 2048, kind=WIDE)
    copies = shape_of(8, 64, 2048)
    branch_parts, tok_share, cot_share = tied(
        (tp_parts(partial_branch), my_share(tokens), my_share(cotangent))
    )
    copies2, middle, second_rows, stats2 = kernel_call(
        second_norm_kernel,
        (copies, share, share, shape_of(64, 128, kind=WIDE)),
        (branch_parts, tok_share),
        small=(second_gain[None], second_shift[None]),
    )
    (grad_hidden,) = kernel_call(
        hidden_gradient_kernel,
        (shape_of(BLOCK, 704, kind=WIDE),),
        (tied((cotangent, copies2))[0], w_down),
        flops=2 * 512 * 2048 * 704,
    )
    second_low, grad_hidden = tied((tp_rows(copies2), grad_hidden))
    strip = shape_of(BLOCK, 704)
    hidden_low, grad_gate, grad_up, partial_second = kernel_call(
        feed_kernel,
        (strip, strip, strip, shape_of(BLOCK, 2048)),
        (second_low, w2[:1], w2[1:], grad_hidden),
        late=2,
        flops=8 * 512 * 2048 * 704,
        mib=24,
    )
    second_parts = tp_parts(partial_second)

    feed_mine, feed_theirs = weight_grads(
        ((grad_gate, second_low), (grad_up, second_low), (hidden_low, cotangent)), place
    )
    second_parts, feed_mine, feed_theirs = tied((second_parts, feed_mine, feed_theirs))
    copies3, grad_middle, second_sums = kernel_call(
        second_gradient_kernel,
        (copies, share),
        (second_parts, cot_share, second_rows, stats2),
        small=(second_gain[None],),
        small_outs=(shape_of(2, 2048, kind=WIDE),),
    )
    grad_branch = tp_rows(copies3)
    partial_feed = jnp.dot(hidden_low, w_down, preferred_element_type=WIDE).astype(LOW)
    grad_branch, partial_feed = tied((grad_branch, partial_feed))
    feed_received = swapped(feed_theirs, "core")
    feed_z = z_parts(feed_mine, feed_received)
    feed_1, feed_3 = z_permute(feed_z[1], 1), z_permute(feed_z[3], 3)
    feed_parts = dealt(partial_feed.reshape(4, 128, 2048), "y")

    grads = kernel_call(
        grad_attended_kernel,
        (*[quarter] * 4,),
        (grad_branch, w_out),
        scalars=(place,),
        scratch=(four,),
        flops=2 * 512 * 256 * 2048,
    )
    feed_1, feed_3, *grads = tied((feed_1, feed_3, *grads))
    *grads, feed_2 = tied((*across(grads), feed_z[2]))
    feed_2 = z_permute(feed_2, 2)
    scratch = (
        pltpu.VMEM((2, 4, 128, BLOCK), LOW),
        pltpu.VMEM((BLOCK, 128), LOW),
        pltpu.VMEM((BLOCK, 128), LOW),
        pltpu.VMEM((1, BLOCK), WIDE),
        pltpu.VMEM((2, 4, BLOCK, 128), WIDE),
        four,
        four,
    )
    blocks = shape_of(4, BLOCK, 128)
    acc, keep1, send1 = kernel_call(
        functools.partial(backward_kernel, (2, 3), True),
        (state[0], blocks, blocks),
        (kv_z, kv_zc, *queries, *grads, out_t, total, begin),
        scalars=(place,),
        scratch=scratch,
        flops=20 * 10 * BLOCK * BLOCK * 128,
        exps=20 * BLOCK * BLOCK,
        mib=28,
    )
    acc, send1, feed_parts = tied((acc, send1, feed_parts))
    (feed_half,) = kernel_call(
        feed_sum_kernel, (shape_of(128, 2048),), (feed_parts, middle), scalars=(place,)
    )
    far = (keep1.astype(WIDE) + swapped(send1, "core").astype(WIDE)).astype(LOW)
    acc, far, feed_half = tied((acc, far, feed_half))
    near = kernel_call(
        functools.partial(backward_kernel, (0, 1), False),
        (*[quarter] * 4, blocks, blocks),
        (kv, kv_c, *queries, *grads, out_t, total, begin, acc),
        scalars=(place,),
        scratch=(*scratch, pltpu.VMEM((4, 128, BLOCK), WIDE), four),
        flops=20 * 10 * BLOCK * BLOCK * 128,
        exps=20 * BLOCK * BLOCK,
        mib=28,
    )
    *near, far, feed_other, feed_2 = tied(
        (*near, swapped(far, "zl"), swapped(feed_half, "xl"), feed_2)
    )
    *grad_queries, keep0, send0 = near
    near = keep0.astype(WIDE) + swapped(send0, "core").astype(WIDE)
    grad_queries = across(grad_queries)
    grad_kv = across([(near[k] + far[k].astype(WIDE)).astype(LOW) for k in range(4)])
    (copies4,) = kernel_call(layer_out_kernel, (shape_of(4, 128, 2048),), (feed_half, feed_other))
    layer_out = dealt(copies4, "y").reshape(BLOCK, 2048)
    feed_keep, feed_send = xh_halves([feed_z[0], feed_1, feed_2, feed_3])
    feed_other = swapped(feed_send, "xh")
    grad_mixed, partial_normed, gain_sum, shift_sum, bias_sum = kernel_call(
        grad_project_kernel,
        (shape_of(BLOCK, 768), shape_of(BLOCK, 2048)),
        (*grad_kv, *grad_queries, cosine, sine, tokens, stats1, w3),
        small_outs=(
            shape_of(1, 2048, kind=WIDE),
            shape_of(1, 2048, kind=WIDE),
            shape_of(3, 256, kind=WIDE),
        ),
        scalars=(place,),
        scratch=(pltpu.VMEM((4, BLOCK, 128), LOW), four),
        late=3,
        flops=2 * 512 * 2048 * 768,
    )
    partial_normed, layer_out, feed_other = tied((partial_normed, layer_out, feed_other))
    normed_parts = tp_parts(partial_normed)

    rest_mine, rest_theirs = weight_grads(
        ((grad_mixed, normed_low), (attended_low, grad_branch)), place
    )
    vectors = jnp.concatenate([gain_sum, shift_sum, second_sums], axis=0).reshape(32, 256)
    vectors = jnp.concatenate([vectors, bias_sum], axis=0)
    normed_parts, rest_mine, vectors = tied((normed_parts, rest_mine, vectors))
    rest_received = swapped(rest_theirs, "core")
    (copies5,) = kernel_call(
        first_gradient_kernel,
        (copies,),
        (normed_parts, grad_middle, tok_share, my_share(stats1)),
        small=(first_gain[None],),
    )
    grad_tokens = tp_rows(copies5)

    rest_z = z_parts(rest_mine, rest_received)
    vectors, *rest_z = tied((vectors, *rest_z))
    vectors = summed_by_pairs(vectors, (("core", 2, 1), ("zl", 2, 1), ("zh", 2, 1)))
    vectors, *rest_z = tied(
        (vectors, rest_z[0], *[z_permute(rest_z[k], k) for k in range(1, 4)])
    )
    rest_keep, rest_send = xh_halves(rest_z)
    vectors, rest_send = tied((vectors, rest_send))
    rest_w = rest_keep + swapped(rest_send, "xh").astype(WIDE)
    feed_w = feed_keep + feed_other.astype(WIDE)
    vectors = summed_by_pairs(vectors, (("xh", 2, 1),))
    bias_grad = vectors[32:]
    vectors = vectors[:32].reshape(4, 2048)
    vectors = summed_by_pairs(vectors, (("y", 4, 1), ("y", 4, 2), ("xl", 2, 1)))
    return (
        layer_out,
        grad_tokens,
        vectors[0],
        vectors[1],
        vectors[2],
        vectors[3],
        jnp.transpose(rest_w[:768].reshape(3, 256, 128), (2, 0, 1)),
        bias_grad,
        rest_w[768:],
        jnp.transpose(feed_w[:1408].reshape(2, 704, 128), (2, 0, 1)),
        feed_w[1408:],
    )


def solution(mesh):
    fine = Mesh(
        mesh.devices.reshape(2, 2, 2, 2, 4, 2), ("xh", "zh", "zl", "core", "y", "xl")
    )
    rows = P(CTX, None)
    return jax.shard_map(
        body,
        mesh=fine,
        in_specs=(
            rows, rows, P(), P(), P(), P(), P(),
            P(None, None, TP), P(None, TP), P(TP, None), P(None, None, TP), P(TP, None),
        ),
        out_specs=(
            rows, rows, P(), P(), P(), P(),
            P(CTX, None, TP), P(None, TP), P(TP, CTX), P(CTX, None, TP), P(TP, CTX),
        ),
        check_vma=False,
    )
```

```python
import functools

import jax
import jax.numpy as jnp
from jax import lax
from jax.experimental import pallas as pl
from jax.experimental.pallas import tpu as pltpu
from jax.sharding import Mesh
from jax.sharding import PartitionSpec as P

HDIM = 64
DOCS = 3
BLOCK = 512
HALF = 256
LOW = jnp.bfloat16
WIDE = jnp.float32
CTX = ("xh", "zh", "zl", "core")
TP = ("y", "xl")
SPREAD = ("xh", "zh")
Z = ("zh", "zl")


def size_of(a):
    return a.size * jnp.dtype(a.dtype).itemsize


def kernel_call(
    body, outs, inputs, *, small=(), small_outs=(), scalars=(), scratch=(), late=0, flops=0, exps=0, mib=12, quick=False, moved=0
):
    counts = [len(x) for x in (scalars, inputs, small, outs, small_outs, inputs, outs)]

    def run(*refs):
        groups, at = [], 0
        for n in counts:
            groups.append(refs[at : at + n])
            at += n
        scalar_refs, far_in, near_in, far_out, near_out, held_in, held_out = groups
        arrived, left, *rest = refs[at:]
        moves = [
            pltpu.make_async_copy(a, b, arrived.at[k]) for k, (a, b) in enumerate(zip(far_in, held_in))
        ]
        for move in moves:
            move.start()
        early = len(moves) - late
        for move in moves[:early]:
            move.wait()

        def arrive():
            for move in moves[early:]:
                move.wait()

        body(
            *([arrive] if late else []),
            *scalar_refs, *held_in, *near_in, *held_out, *near_out, *rest,
        )
        moves = [
            pltpu.make_async_copy(a, b, left.at[k]) for k, (a, b) in enumerate(zip(held_out, far_out))
        ]
        for move in moves:
            move.start()
        for move in moves:
            move.wait()

    vmem, hbm = pl.BlockSpec(memory_space=pltpu.VMEM), pl.BlockSpec(memory_space=pltpu.HBM)
    held = [pltpu.VMEM(a.shape, a.dtype) for a in (*inputs, *outs)]
    limit = sum(size_of(a) for a in (*inputs, *outs, *small, *small_outs)) + mib * 1024 * 1024
    return pl.pallas_call(
        run,
        out_shape=(*[pltpu.HBM(a.shape, a.dtype) for a in outs], *small_outs),
        in_specs=[pl.BlockSpec(memory_space=pltpu.SMEM)] * len(scalars)
        + [pl.BlockSpec(memory_space=pl.ANY)] * moved
        + [hbm] * (len(inputs) - moved)
        + [vmem] * len(small),
        out_specs=(*[hbm] * len(outs), *[vmem] * len(small_outs)),
        scratch_shapes=[
            *held,
            pltpu.SemaphoreType.DMA((len(inputs),)),
            pltpu.SemaphoreType.DMA((max(1, len(outs)),)),
            *scratch,
        ],
        compiler_params=pltpu.CompilerParams(vmem_limit_bytes=limit),
        cost_estimate=pl.CostEstimate(
            flops=flops,
            bytes_accessed=0 if quick else sum(size_of(a) for a in (*inputs, *outs)),
            transcendentals=exps,
        ),
    )(
        *scalars,
        *inputs[:moved],
        *[pltpu.with_memory_space_constraint(a, pltpu.HBM) for a in inputs[moved:]],
        *small,
    )


def lane_of(shape):
    return lax.broadcasted_iota(jnp.int32, shape, len(shape) - 1)


def exchange_halves(a, b):
    front = lane_of(a.shape) < HDIM
    return (
        jnp.where(front, a, pltpu.roll(b, HDIM, 1)),
        jnp.where(front, pltpu.roll(a, HDIM, 1), b),
    )


def nt(a, b):
    return lax.dot_general(a, b, (((1,), (1,)), ((), ())), preferred_element_type=WIDE)


def nn(a, b):
    return lax.dot_general(a, b, (((1,), (0,)), ((), ())), preferred_element_type=WIDE)


def turn(x, cosine, sine, sign):
    lane = lax.rem(lane_of(x.shape), HDIM)
    ahead = pltpu.roll(x, x.shape[1] - 8, 1)
    behind = pltpu.roll(x, 8, 1)
    swapped = jnp.where(lane < 8, -ahead, behind) * sign
    return x * cosine + swapped * sine


def rotation_table(angles_table):
    tokens = angles_table.shape[1]
    rest = jnp.zeros((112, tokens), WIDE)
    x = jnp.concatenate([angles_table, rest], axis=0).T
    lane = lane_of(x.shape)
    c = jnp.where(lane < 8, x, 0.0)
    c = c + pltpu.roll(c, 8, 1)
    c = c + pltpu.roll(c, HDIM, 1) + jnp.where(lax.rem(lane, HDIM) < 16, 0.0, 1.0)
    s = jnp.where((lane >= 8) & (lane < 16), x, 0.0)
    s = s + pltpu.roll(s, 120, 1)
    s = s + pltpu.roll(s, HDIM, 1)
    return c, s


def project_kernel(
    arrive, place, tok, table, w, gain, shift, bias,
    normed, stats, kv0, kv1, kv2, kv3, q0, q1, q2, q3, cosine_out, sine_out, kept_kv, kept_q,
):
    rows = 64

    def norm_rows(i, carry):
        at = pl.ds(pl.multiple_of(i * rows, rows), rows)
        x = tok[at, :].astype(WIDE)
        mean = jnp.mean(x, axis=-1, keepdims=True)
        center = x - mean
        scale = lax.rsqrt(jnp.mean(center * center, axis=-1, keepdims=True) + 1e-05)
        normed[at, :] = (center * scale * gain[...] + shift[...]).astype(LOW)
        stats[at, :] = jnp.where(lane_of((rows, 128)) < HDIM, mean, scale)
        return carry

    lax.fori_loop(0, BLOCK // rows, norm_rows, 0)
    cosine, sine = rotation_table(table[...])
    cosine_out[...] = cosine
    sine_out[...] = sine
    arrive()
    mixed = [nn(normed[...], w[c]) + bias[c : c + 1, :] for c in range(3)]
    for pair in range(2):
        lanes = slice(pair * 128, pair * 128 + 128)
        q = turn(mixed[0][:, lanes], cosine, sine, 1.0) * 0.125
        k = turn(mixed[1][:, lanes], cosine, sine, 1.0)
        kv = exchange_halves(k, mixed[2][:, lanes])
        qq = exchange_halves(q[:HALF], q[HALF:])
        for one in range(2):
            kept_kv[2 * pair + one] = kv[one].astype(LOW)
            kept_q[2 * pair + one] = qq[one].astype(LOW)
    for k in range(4):
        (kv0, kv1, kv2, kv3)[k][...] = kept_kv[place[1] ^ k]
        (q0, q1, q2, q3)[k][...] = kept_q[place[1] ^ k]


def padded_queries(q2):
    x = q2.astype(WIDE)
    front = lane_of(x.shape) < HDIM
    return (
        jnp.where(front, x, 0.0).astype(LOW),
        jnp.where(front, pltpu.roll(x, HDIM, 1), 0.0).astype(LOW),
    )


def padded_behind(d2):
    x = d2.astype(WIDE)
    front = lane_of(x.shape) < HDIM
    return (
        jnp.where(front, 0.0, pltpu.roll(x, HDIM, 1)).astype(LOW),
        jnp.where(front, 0.0, x).astype(LOW),
    )


def allowed_keys(key_block, first_query, begin):
    shape = (BLOCK, begin.shape[1])
    key_at = key_block * BLOCK + lax.broadcasted_iota(jnp.int32, shape, 0)
    query_at = first_query + lax.broadcasted_iota(jnp.int32, shape, 1)
    return (key_at <= query_at) & (key_at >= begin)


def key_blocks(place, rels, t):
    return [4 * t + (place[0] ^ rel) for rel in rels], place[1] ^ t


def forward_kernel(rels, first, last, *refs):
    place, kv0, kv1, q0, q1, q2, q3, begin = refs[:8]
    if first:
        acc_out, peak_out, kvt, queries, kept_q = refs[8:]
    else:
        acc_in, peak_in, o0, o1, o2, o3, out_t, total, kvt, queries, kept_q, kept_o = refs[8:]
        acc_out, peak_out = out_t, total
    me = place[1]
    front = lane_of((BLOCK, 128)) < HDIM
    for k, q in enumerate((q0, q1, q2, q3)):
        kept_q[me ^ k] = q[...]
    for i, kv in enumerate((kv0, kv1)):
        for t in range(4):
            kvt[i, t] = jnp.where(front, 1.0, kv[t].astype(WIDE)).T.astype(LOW)

    def one_query_block(j, carry):
        first_query = (4 * j + place[0]) * BLOCK
        queries[:HALF, :], queries[HALF:, :] = padded_queries(kept_q[j])
        if first:
            peak_out[j] = jnp.full((8, BLOCK), -1e30, WIDE)
            acc_out[j] = jnp.zeros((128, BLOCK), WIDE)
        else:
            peak_out[j] = peak_in[j]
            acc_out[j] = acc_in[j]

        def two_blocks(t, carry):
            blocks, at = key_blocks(place, rels, t)
            scores = []
            for i, kv in enumerate((kv0, kv1)):
                ok = allowed_keys(blocks[i], first_query, begin[j, :1])
                scores.append(jnp.where(ok, nt(kv[at], queries[...]), -1e30))
            old = peak_out[j, :1]
            new = old
            for one in scores:
                new = jnp.maximum(new, jnp.max(one, axis=0, keepdims=True))
            done = acc_out[j] * jnp.exp(old - new)
            for i in range(2):
                done += nn(kvt[i, at], jnp.exp(scores[i] - new).astype(LOW))
            acc_out[j] = done
            peak_out[j, :1] = new
            return carry

        lax.fori_loop(0, j + 1, two_blocks, 0)
        if last:
            weight_sum = acc_out[j, :1]
            done = acc_out[j] / weight_sum
            out_t[j] = done
            total[j, :1] = peak_out[j, :1] + jnp.log(weight_sum)
            rows = done.T
            x, y = rows[:HALF], rows[HALF:]
            kept_o[j] = jnp.where(lane_of(x.shape) < HDIM, pltpu.roll(x, HDIM, 1), y).astype(LOW)
        return carry

    lax.fori_loop(0, 4, one_query_block, 0)
    if last:
        for k, out in enumerate((o0, o1, o2, o3)):
            out[...] = kept_o[me ^ k]


def backward_kernel(rels, first, *refs):
    place, kv0, kv1, q0, q1, q2, q3, d0, d1, d2, d3, out_t, total, begin = refs[:14]
    if first:
        acc, keep, send, kvt, queries, grads, dot_rows, dkv, kept_q, kept_d = refs[14:]
    else:
        (
            acc_in, g0, g1, g2, g3, keep, send,
            kvt, queries, grads, dot_rows, dkv, kept_q, kept_d, acc, kept_g,
        ) = refs[14:]
    me = place[1]
    for k in range(4):
        kept_q[me ^ k] = (q0, q1, q2, q3)[k][...]
        kept_d[me ^ k] = (d0, d1, d2, d3)[k][...]
    for i, kv in enumerate((kv0, kv1)):
        for t in range(4):
            kvt[i, t] = kv[t].astype(WIDE).T.astype(LOW)
    dkv[...] = jnp.zeros(dkv.shape, WIDE)

    def one_query_block(j, carry):
        first_query = (4 * j + place[0]) * BLOCK
        queries[:HALF, :], queries[HALF:, :] = padded_queries(kept_q[j])
        grads[:HALF, :], grads[HALF:, :] = padded_behind(kept_d[j])
        dot_rows[...] = jnp.sum(grads[...].astype(WIDE).T * out_t[j], axis=0, keepdims=True)
        acc[j] = jnp.zeros((128, BLOCK), WIDE) if first else acc_in[j]

        def two_blocks(t, carry):
            blocks, at = key_blocks(place, rels, t)
            for i, kv in enumerate((kv0, kv1)):
                term = 0.0
                for half in range(2):
                    some = slice(half * HALF, half * HALF + HALF)
                    ok = allowed_keys(blocks[i], first_query + half * HALF, begin[j, :1, some])
                    scores = nt(kv[at], queries[some, :])
                    probs = jnp.where(ok, jnp.exp(scores - total[j, :1, some]), 0.0)
                    grad_probs = nt(kv[at], grads[some, :])
                    grad_scores = (probs * (grad_probs - dot_rows[:, some])).astype(LOW)
                    term += nn(grad_scores, queries[some, :]) + nn(probs.astype(LOW), grads[some, :])
                    acc[j, :, some] += nn(kvt[i, at], grad_scores)
                dkv[i, at] += term
            return carry

        lax.fori_loop(0, j + 1, two_blocks, 0)
        if not first:
            rows = acc[j].T
            x, y = rows[:HALF], rows[HALF:]
            kept_g[j] = jnp.where(lane_of(x.shape) < HDIM, x, pltpu.roll(y, HDIM, 1)).astype(LOW)
        return carry

    lax.fori_loop(0, 4, one_query_block, 0)
    if not first:
        for k, out in enumerate((g0, g1, g2, g3)):
            out[...] = kept_g[me ^ k]
    for t in range(4):
        keep[t] = dkv[0, t].astype(LOW)
        send[t] = dkv[1, t].astype(LOW)


def branch_kernel(arrive, place, h0, h1, h2, h3, w, attended, partial, kept):
    for k, h in enumerate((h0, h1, h2, h3)):
        kept[place[1] ^ k] = h[...]
    for pair in range(2):
        lanes = slice(pair * 128, pair * 128 + 128)
        x, y = exchange_halves(kept[2 * pair].astype(WIDE), kept[2 * pair + 1].astype(WIDE))
        attended[:HALF, lanes] = x.astype(LOW)
        attended[HALF:, lanes] = y.astype(LOW)
    arrive()
    for n in range(4):
        at = slice(n * 512, n * 512 + 512)
        partial[:, at] = nn(attended[...], w[:, at]).astype(LOW)


def grad_attended_kernel(place, grad, w, d0, d1, d2, d3, kept):
    g = nt(grad[...], w[...])
    for pair in range(2):
        lanes = slice(pair * 128, pair * 128 + 128)
        both = exchange_halves(g[:HALF, lanes], g[HALF:, lanes])
        for one in range(2):
            kept[2 * pair + one] = both[one].astype(LOW)
    for k, out in enumerate((d0, d1, d2, d3)):
        out[...] = kept[place[1] ^ k]


def grad_project_kernel(
    arrive, place, p0, p1, p2, p3, g0, g1, g2, g3, cosine, sine, tok, stats, w,
    grad_mixed, partial, gain_sum, shift_sum, bias_sum, parts, kept,
):
    for k in range(4):
        parts[place[1] ^ k] = (p0, p1, p2, p3)[k][...]
        kept[place[1] ^ k] = (g0, g1, g2, g3)[k][...]
    for pair in range(2):
        lanes = slice(pair * 128, pair * 128 + 128)
        k, v = exchange_halves(parts[2 * pair].astype(WIDE), parts[2 * pair + 1].astype(WIDE))
        q = exchange_halves(kept[2 * pair].astype(WIDE), kept[2 * pair + 1].astype(WIDE))
        q = jnp.concatenate(q, axis=0)
        q = turn(q, cosine[...], sine[...], -1.0) * 0.125
        k = turn(k, cosine[...], sine[...], -1.0)
        for c, part in enumerate((q, k, v)):
            start = c * 256 + pair * 128
            low = part.astype(LOW)
            grad_mixed[:, start : start + 128] = low
            bias_sum[c : c + 1, lanes] = jnp.sum(low.astype(WIDE), axis=0, keepdims=True)
    arrive()
    mean, scale = stats[:, 0:1], stats[:, 64:65]
    for n in range(4):
        at = slice(n * 512, n * 512 + 512)
        total = nt(grad_mixed[:, :256], w[0, at, :])
        total += nt(grad_mixed[:, 256:512], w[1, at, :])
        total += nt(grad_mixed[:, 512:], w[2, at, :])
        partial[:, at] = total.astype(LOW)
        normal = (tok[:, at].astype(WIDE) - mean) * scale
        gain_sum[:, at] = jnp.sum(total * normal, axis=0, keepdims=True)
        shift_sum[:, at] = jnp.sum(total, axis=0, keepdims=True)


def hidden_gradient_kernel(cot, w, grad_hidden):
    grad_hidden[...] = nt(cot[...], w[...])


def feed_kernel(arrive, second, w_gate, w_up, grad_hidden, hidden, grad_gate, grad_up, partial):
    gate = nt(second[...], w_gate[0])
    arrive()
    up = nt(second[...], w_up[0])
    sigmoid = 1.0 / (1.0 + jnp.exp(-gate))
    activated = gate * sigmoid
    hidden[...] = (activated * up).astype(LOW)
    grad = grad_hidden[...]
    grad_up[...] = (grad * activated).astype(LOW)
    grad_gate[...] = (grad * up * sigmoid * (1.0 + gate * (1.0 - sigmoid))).astype(LOW)
    for n in range(4):
        at = slice(n * 512, n * 512 + 512)
        partial[:, at] = (nn(grad_gate[...], w_gate[0, :, at]) + nn(grad_up[...], w_up[0, :, at])).astype(LOW)


def for_rows(work):
    rows = 16

    def one(i, carry):
        work(pl.ds(pl.multiple_of(i * rows, rows), rows))
        return carry

    lax.fori_loop(0, 64 // rows, one, 0)


def summed(parts, at):
    total = parts[0, at, :].astype(WIDE)
    for k in range(1, 8):
        total += parts[k, at, :].astype(WIDE)
    return total


def copy_out(copies, at, value):
    low = value.astype(LOW)
    for k in range(8):
        copies[k, at, :] = low


def second_norm_kernel(parts, tok, gain, shift, copies, middle, normal, stats):
    def work(at):
        x = tok[at, :].astype(WIDE) + summed(parts, at)
        center = x - jnp.mean(x, axis=-1, keepdims=True)
        scale = lax.rsqrt(jnp.mean(center * center, axis=-1, keepdims=True) + 1e-05)
        rows = center * scale
        copy_out(copies, at, rows * gain[...] + shift[...])
        middle[at, :] = x
        normal[at, :] = rows
        stats[at, :] = jnp.broadcast_to(scale, (scale.shape[0], 128))

    for_rows(work)


def norm_gradient(grad, rows, scale, gain):
    scaled = grad * gain
    return scale * (
        scaled
        - jnp.mean(scaled, axis=-1, keepdims=True)
        - rows * jnp.mean(scaled * rows, axis=-1, keepdims=True)
    )


def second_gradient_kernel(parts, cot, normal, stats, gain, copies, grad_middle, sums):
    sums[...] = jnp.zeros(sums.shape, WIDE)

    def work(at):
        grad, rows = summed(parts, at), normal[at, :]
        done = cot[at, :].astype(WIDE) + norm_gradient(grad, rows, stats[at, 0:1], gain[...])
        copy_out(copies, at, done)
        grad_middle[at, :] = done
        sums[0:1, :] += jnp.sum(grad * rows, axis=0, keepdims=True)
        sums[1:2, :] += jnp.sum(grad, axis=0, keepdims=True)

    for_rows(work)


def feed_sum_kernel(place, parts, middle, out):
    rows = 16
    mine = place[3]

    def one(i, carry):
        at = pl.ds(pl.multiple_of(i * rows, rows), rows)
        total = parts[0, at, :].astype(WIDE)
        for k in range(1, 4):
            total += parts[k, at, :].astype(WIDE)
        here = i * rows - mine * 64
        own = pl.ds(pl.multiple_of(jnp.clip(here, 0, 64 - rows), rows), rows)
        inside = (here >= 0) & (here < 64)
        out[at, :] = (total + jnp.where(inside, middle[own, :], 0.0)).astype(LOW)
        return carry

    lax.fori_loop(0, 128 // rows, one, 0)


def layer_out_kernel(a, b, copies):
    rows = 16

    def one(i, carry):
        at = pl.ds(pl.multiple_of(i * rows, rows), rows)
        low = (a[at, :].astype(WIDE) + b[at, :].astype(WIDE)).astype(LOW)
        for k in range(4):
            copies[k, at, :] = low
        return carry

    lax.fori_loop(0, 128 // rows, one, 0)


def first_gradient_kernel(parts, grad_middle, tok, stats, gain, copies):
    def work(at):
        mean, scale = stats[at, 0:1], stats[at, 64:65]
        rows = (tok[at, :].astype(WIDE) - mean) * scale
        done = norm_gradient(summed(parts, at), rows, scale, gain[...])
        copy_out(copies, at, grad_middle[at, :] + done)

    for_rows(work)


def weight_kernel(widths, place, *refs):
    count = len(widths)
    lefts, rights = refs[:count], refs[count : 2 * count]
    mine, theirs, turned = refs[2 * count :]
    first_core = place[2] == 0
    start = 0
    for left, right, width in zip(lefts, rights, widths):
        turned[:width, :] = left[...].astype(WIDE).T.astype(LOW)

        def one(n, carry, start=start, right=right, width=width):
            columns = right[:, pl.ds(pl.multiple_of(n * 256, 256), 256)]
            both = nn(turned[:width, :], columns)
            first, second = both[:, :128], both[:, 128:]
            at = pl.ds(start, width)
            mine[n, at, :] = jnp.where(first_core, first, second).astype(LOW)
            theirs[n, at, :] = jnp.where(first_core, second, first).astype(LOW)
            return carry

        lax.fori_loop(0, 8, one, 0, unroll=4)
        start += width


def weight_grads(pairs, place):
    lefts, rights = [a for a, _ in pairs], [b for _, b in pairs]
    widths = tuple(a.shape[1] for a in lefts)
    out = jax.ShapeDtypeStruct((8, sum(widths), 128), LOW)
    return kernel_call(
        functools.partial(weight_kernel, widths),
        (out, out),
        (*lefts, *rights),
        scalars=(place,),
        scratch=(pltpu.VMEM((max(widths), BLOCK), LOW),),
        quick=True,
    )


def swapped(x, axis):
    return lax.ppermute(x, axis, [(0, 1), (1, 0)])


def across(pieces):
    moved = [
        lax.ppermute(pieces[k], SPREAD, [(i, i ^ k) for i in range(4)]) for k in range(1, 4)
    ]
    return (pieces[0], *moved)


def z_parts_kernel(z, mine, received, *outs):
    total = (mine[...].astype(WIDE) + received[...].astype(WIDE)).astype(LOW)
    for k, out in enumerate(outs):

        @pl.when(pl.program_id(0) == k)
        def _(out=out):
            out[...] = total


def z_parts(mine, received):
    rows = mine.shape[1]

    def taken(k, xh, z):
        return (xh * 4 + lax.rem(z[0] + k, 4), 0, 0)

    def given(part):
        def at(k, xh, z):
            return (jnp.where(k < part, 0, jnp.where(k == part, xh, 1)), 0, 0)

        return pl.BlockSpec((1, rows, 128), at)

    return pl.pallas_call(
        z_parts_kernel,
        grid_spec=pltpu.PrefetchScalarGridSpec(
            num_scalar_prefetch=1,
            grid=(4, 2),
            in_specs=[pl.BlockSpec((1, rows, 128), taken)] * 2,
            out_specs=[given(part) for part in range(4)],
        ),
        out_shape=[pltpu.HBM((2, rows, 128), LOW)] * 4,
        compiler_params=pltpu.CompilerParams(vmem_limit_bytes=24 * 1024 * 1024),
        cost_estimate=pl.CostEstimate(flops=0, bytes_accessed=0, transcendentals=0),
    )(
        lax.axis_index(Z).reshape(1),
        *[pltpu.with_memory_space_constraint(a, pltpu.HBM) for a in (mine, received)],
    )


def settled_kernel(x, out, held, came, went):
    rows = held.shape[0] // 4
    parts = [pl.ds(k * rows, rows) for k in range(4)]
    inward = [pltpu.make_async_copy(x.at[p], held.at[p], came.at[k]) for k, p in enumerate(parts)]
    outward = [pltpu.make_async_copy(held.at[p], out.at[p], went.at[k]) for k, p in enumerate(parts)]
    for move in inward:
        move.start()
    for come, go in zip(inward, outward):
        come.wait()
        go.start()
    for move in outward:
        move.wait()


def settled(x):
    hbm = pl.BlockSpec(memory_space=pltpu.HBM)
    return pl.pallas_call(
        settled_kernel,
        out_shape=pltpu.HBM(x.shape, x.dtype),
        in_specs=[hbm],
        out_specs=hbm,
        scratch_shapes=[
            pltpu.VMEM(x.shape, x.dtype),
            pltpu.SemaphoreType.DMA((4,)),
            pltpu.SemaphoreType.DMA((4,)),
        ],
        compiler_params=pltpu.CompilerParams(vmem_limit_bytes=8 * 1024 * 1024),
        cost_estimate=pl.CostEstimate(flops=0, bytes_accessed=0, transcendentals=0),
    )(pltpu.with_memory_space_constraint(x, pltpu.HBM))


def z_permute(part, distance):
    return lax.ppermute(part, Z, [(i, (i + distance) % 4) for i in range(4)])


def xh_halves(moved):
    xh = lax.axis_index("xh")

    def added(at):
        return sum(lax.dynamic_index_in_dim(x, at, 0, False).astype(WIDE) for x in moved)

    return added(xh), added(1 - xh).astype(LOW)


def dealt(x, axis):
    return lax.all_to_all(x, axis, split_axis=0, concat_axis=0, tiled=True)


def tp_parts(partial):
    return dealt(partial.reshape(8, -1, partial.shape[1]), TP)


def tp_rows(copies):
    return dealt(copies, TP).reshape(-1, copies.shape[2])


def summed_by_pairs(x, pairs):
    for axis, size, distance in pairs:
        x = x + lax.ppermute(x, axis, [(i, i ^ distance) for i in range(size)])
    return x


def shape_of(*dims, kind=LOW):
    return jax.ShapeDtypeStruct(dims, kind)


def body(
    tokens, cotangent, segment_ids, first_gain, first_shift, second_gain, second_shift,
    w_qkv, qkv_bias, w_out, w_gate_up, w_down,
):
    ctx = lax.axis_index(CTX)
    tp = lax.axis_index(TP)
    group = lax.axis_index(("zl", "core"))
    place = jnp.stack(
        [group, lax.axis_index(SPREAD), lax.axis_index("core"), lax.axis_index("xl")]
    )
    tied = lax.optimization_barrier

    def my_share(array):
        return lax.dynamic_slice_in_dim(array, tp * 64, 64)

    labels = jnp.arange(DOCS, dtype=jnp.int32)
    starts = jnp.sum((segment_ids[None, :] < labels[:, None]).astype(jnp.int32), axis=1)
    begins = jnp.sum(
        jnp.where(segment_ids[None, :] == labels[:, None], starts[:, None], 0), axis=0
    )
    begin = lax.dynamic_index_in_dim(begins.reshape(4, 4, 1, BLOCK), group, 1, False)
    begin = jnp.broadcast_to(begin, (4, 8, BLOCK))
    own = lax.dynamic_slice_in_dim(begins, ctx * BLOCK, BLOCK)
    places = ctx * BLOCK + jnp.arange(BLOCK, dtype=jnp.int32) - own
    frequency = 10000.0 ** (-jnp.arange(8, dtype=WIDE) / 8.0)
    angles = frequency[:, None] * places.astype(WIDE)[None, :]
    table = jnp.concatenate([jnp.cos(angles), jnp.sin(angles)], axis=0)

    w3 = jnp.transpose(w_qkv, (1, 0, 2))
    w2 = jnp.transpose(w_gate_up, (1, 2, 0))
    quarter, block = shape_of(HALF, 128), shape_of(BLOCK, 128)
    wide_block = shape_of(BLOCK, 128, kind=WIDE)
    four = pltpu.VMEM((4, HALF, 128), LOW)
    normed_low, stats1, *packed, cosine, sine = kernel_call(
        project_kernel,
        (shape_of(BLOCK, 2048), wide_block, *[block] * 4, *[quarter] * 4, wide_block, wide_block),
        (tokens, table, w3),
        small=(first_gain[None], first_shift[None], qkv_bias),
        scalars=(place,),
        scratch=(pltpu.VMEM((4, BLOCK, 128), LOW), four),
        late=1,
        flops=2 * 512 * 2048 * 768,
    )
    kv, *queries = tied((jnp.stack(across(packed[:4])), *across(packed[4:])))
    kv_c = swapped(kv, "core")
    state = (shape_of(4, 128, BLOCK, kind=WIDE), shape_of(4, 8, BLOCK, kind=WIDE))
    acc, peak = kernel_call(
        functools.partial(forward_kernel, (0, 1), True, False),
        state,
        (kv, kv_c, *queries, begin),
        scalars=(place,),
        scratch=(pltpu.VMEM((2, 4, 128, BLOCK), LOW), pltpu.VMEM((BLOCK, 128), LOW), four),
        flops=20 * 4 * BLOCK * BLOCK * 128,
        exps=20 * BLOCK * BLOCK,
        mib=24,
    )
    acc, peak, kv_z = tied((acc, peak, swapped(kv, "zl")))
    kv_zc = swapped(kv_z, "core")
    *heads, out_t, total = kernel_call(
        functools.partial(forward_kernel, (2, 3), False, True),
        (*[quarter] * 4, *state),
        (kv_z, kv_zc, *queries, begin, acc, peak),
        scalars=(place,),
        scratch=(pltpu.VMEM((2, 4, 128, BLOCK), LOW), pltpu.VMEM((BLOCK, 128), LOW), four, four),
        flops=20 * 4 * BLOCK * BLOCK * 128,
        exps=20 * BLOCK * BLOCK,
        mib=24,
    )
    heads = across(heads)
    attended_low, partial_branch = kernel_call(
        branch_kernel,
        (shape_of(BLOCK, 256), shape_of(BLOCK, 2048)),
        (*heads, w_out),
        scalars=(place,),
        scratch=(four,),
        late=1,
        flops=2 * 512 * 256 * 2048,
    )
    share = shape_of(64, 2048, kind=WIDE)
    copies = shape_of(8, 64, 2048)
    branch_parts, tok_share, cot_share = tied(
        (tp_parts(partial_branch), my_share(tokens), my_share(cotangent))
    )
    copies2, middle, second_rows, stats2 = kernel_call(
        second_norm_kernel,
        (copies, share, share, shape_of(64, 128, kind=WIDE)),
        (branch_parts, tok_share),
        moved=1,
        small=(second_gain[None], second_shift[None]),
    )
    (grad_hidden,) = kernel_call(
        hidden_gradient_kernel,
        (shape_of(BLOCK, 704, kind=WIDE),),
        (tied((cotangent, copies2))[0], w_down),
        flops=2 * 512 * 2048 * 704,
    )
    second_low, grad_hidden = tied((tp_rows(copies2), grad_hidden))
    strip = shape_of(BLOCK, 704)
    hidden_low, grad_gate, grad_up, partial_second = kernel_call(
        feed_kernel,
        (strip, strip, strip, shape_of(BLOCK, 2048)),
        (second_low, w2[:1], w2[1:], grad_hidden),
        moved=1,
        late=2,
        flops=8 * 512 * 2048 * 704,
        mib=24,
    )
    second_parts = tp_parts(partial_second)

    feed_mine, feed_theirs = weight_grads(
        ((grad_gate, second_low), (grad_up, second_low), (hidden_low, cotangent)), place
    )
    second_parts, feed_mine, feed_theirs = tied((second_parts, feed_mine, feed_theirs))
    copies3, grad_middle, second_sums = kernel_call(
        second_gradient_kernel,
        (copies, share),
        (second_parts, cot_share, second_rows, stats2),
        moved=1,
        small=(second_gain[None],),
        small_outs=(shape_of(2, 2048, kind=WIDE),),
    )
    grad_branch = tp_rows(copies3)
    partial_feed = jnp.dot(hidden_low, w_down, preferred_element_type=WIDE).astype(LOW)
    grad_branch, partial_feed = tied((grad_branch, partial_feed))
    feed_z = z_parts(feed_mine, swapped(feed_theirs, "core"))
    feed_1, feed_3 = z_permute(feed_z[1], 1), z_permute(feed_z[3], 3)

    grads = kernel_call(
        grad_attended_kernel,
        (*[quarter] * 4,),
        (grad_branch, w_out),
        moved=1,
        scalars=(place,),
        scratch=(four,),
        flops=2 * 512 * 256 * 2048,
    )
    feed_1, feed_3, partial_feed, *grads = tied((feed_1, feed_3, partial_feed, *grads))
    feed_parts = dealt(partial_feed.reshape(4, 128, 2048), "y")
    *grads, feed_2 = tied((*across(grads), feed_z[2]))
    feed_2 = z_permute(feed_2, 2)
    scratch = (
        pltpu.VMEM((2, 4, 128, BLOCK), LOW),
        pltpu.VMEM((BLOCK, 128), LOW),
        pltpu.VMEM((BLOCK, 128), LOW),
        pltpu.VMEM((1, BLOCK), WIDE),
        pltpu.VMEM((2, 4, BLOCK, 128), WIDE),
        four,
        four,
    )
    blocks = shape_of(4, BLOCK, 128)
    acc, keep1, send1 = kernel_call(
        functools.partial(backward_kernel, (2, 3), True),
        (state[0], blocks, blocks),
        (kv_z, kv_zc, *queries, *grads, out_t, total, begin),
        scalars=(place,),
        scratch=scratch,
        flops=20 * 10 * BLOCK * BLOCK * 128,
        exps=20 * BLOCK * BLOCK,
        mib=28,
    )
    acc, send1, feed_parts, feed_2 = tied((acc, send1, feed_parts, feed_2))
    (feed_half,) = kernel_call(
        feed_sum_kernel,
        (shape_of(128, 2048),),
        (feed_parts, middle),
        scalars=(place,),
        moved=1,
    )
    far = (keep1.astype(WIDE) + swapped(send1, "core").astype(WIDE)).astype(LOW)
    feed_keep, feed_send = xh_halves([feed_z[0], feed_1, feed_2, feed_3])
    acc, far, feed_half, feed_send = tied((acc, far, feed_half, feed_send))
    near = kernel_call(
        functools.partial(backward_kernel, (0, 1), False),
        (*[quarter] * 4, blocks, blocks),
        (kv, kv_c, *queries, *grads, out_t, total, begin, acc),
        scalars=(place,),
        scratch=(*scratch, pltpu.VMEM((4, 128, BLOCK), WIDE), four),
        flops=20 * 10 * BLOCK * BLOCK * 128,
        exps=20 * BLOCK * BLOCK,
        mib=28,
    )
    *near, far, feed_other, feed_received = tied(
        (*near, swapped(far, "zl"), swapped(feed_half, "xl"), swapped(feed_send, "xh"))
    )
    *grad_queries, keep0, send0 = near
    near = keep0.astype(WIDE) + swapped(send0, "core").astype(WIDE)
    grad_queries = across(grad_queries)
    grad_kv = across([(near[k] + far[k].astype(WIDE)).astype(LOW) for k in range(4)])
    (copies4,) = kernel_call(layer_out_kernel, (shape_of(4, 128, 2048),), (feed_half, feed_other))
    layer_out = dealt(copies4, "y").reshape(BLOCK, 2048)
    grad_mixed, partial_normed, gain_sum, shift_sum, bias_sum = kernel_call(
        grad_project_kernel,
        (shape_of(BLOCK, 768), shape_of(BLOCK, 2048)),
        (*grad_kv, *grad_queries, cosine, sine, tokens, stats1, w3),
        small_outs=(
            shape_of(1, 2048, kind=WIDE),
            shape_of(1, 2048, kind=WIDE),
            shape_of(3, 256, kind=WIDE),
        ),
        scalars=(place,),
        scratch=(pltpu.VMEM((4, BLOCK, 128), LOW), four),
        late=3,
        flops=2 * 512 * 2048 * 768,
    )
    partial_normed, layer_out = tied((partial_normed, layer_out))
    layer_out = settled(layer_out)
    normed_parts = tp_parts(partial_normed)

    rest_mine, rest_theirs = weight_grads(
        ((grad_mixed, normed_low), (attended_low, grad_branch)), place
    )
    rest_z = z_parts(rest_mine, swapped(rest_theirs, "core"))
    vectors = jnp.concatenate([gain_sum, shift_sum, second_sums], axis=0).reshape(32, 256)
    vectors = jnp.concatenate([vectors, bias_sum], axis=0)
    vectors = summed_by_pairs(vectors, (("core", 2, 1), ("zl", 2, 1), ("zh", 2, 1)))
    vectors, *rest_z = tied((vectors, *rest_z))
    vectors = summed_by_pairs(vectors, (("xh", 2, 1),))
    normed_parts, vectors = tied((normed_parts, vectors))
    (copies5,) = kernel_call(
        first_gradient_kernel,
        (copies,),
        (normed_parts, grad_middle, tok_share, my_share(stats1)),
        moved=1,
        small=(first_gain[None],),
    )
    copies5, vectors = tied((copies5, vectors))
    grad_tokens = settled(tp_rows(copies5))

    rest_z = (rest_z[0], *[z_permute(rest_z[k], k) for k in range(1, 4)])
    rest_keep, rest_send = xh_halves(rest_z)
    rest_w = rest_keep + swapped(rest_send, "xh").astype(WIDE)
    feed_w = feed_keep + feed_received.astype(WIDE)
    bias_grad = vectors[32:]
    vectors = vectors[:32].reshape(4, 2048)
    vectors += sum(
        lax.ppermute(vectors, "y", [(i, i ^ k) for i in range(4)]) for k in range(1, 4)
    )
    vectors = summed_by_pairs(vectors, (("xl", 2, 1),))
    return (
        layer_out,
        grad_tokens,
        vectors[0],
        vectors[1],
        vectors[2],
        vectors[3],
        jnp.transpose(rest_w[:768].reshape(3, 256, 128), (2, 0, 1)),
        bias_grad,
        rest_w[768:],
        jnp.transpose(feed_w[:1408].reshape(2, 704, 128), (2, 0, 1)),
        feed_w[1408:],
    )


def solution(mesh):
    fine = Mesh(
        mesh.devices.reshape(2, 2, 2, 2, 4, 2), ("xh", "zh", "zl", "core", "y", "xl")
    )
    rows = P(CTX, None)
    return jax.shard_map(
        body,
        mesh=fine,
        in_specs=(
            rows, rows, P(), P(), P(), P(), P(),
            P(None, None, TP), P(None, TP), P(TP, None), P(None, None, TP), P(TP, None),
        ),
        out_specs=(
            rows, rows, P(), P(), P(), P(),
            P(CTX, None, TP), P(None, TP), P(TP, CTX), P(CTX, None, TP), P(TP, CTX),
        ),
        check_vma=False,
    )
```

```python
import functools

import jax
import jax.numpy as jnp
from jax import lax
from jax.experimental import pallas as pl
from jax.experimental.pallas import tpu as pltpu
from jax.sharding import Mesh
from jax.sharding import PartitionSpec as P

HDIM = 64
DOCS = 3
BLOCK = 512
HALF = 256
LOW = jnp.bfloat16
WIDE = jnp.float32
CTX = ("xh", "zh", "zl", "core")
TP = ("y", "xl")
SPREAD = ("xh", "zh")
Z = ("zh", "zl")


def size_of(a):
    return a.size * jnp.dtype(a.dtype).itemsize


def kernel_call(
    body, outs, inputs, *, small=(), small_outs=(), scalars=(), scratch=(), late=0, flops=0, exps=0, mib=12, quick=False, moved=0
):
    inputs = [a if isinstance(a, tuple) else (a, 0, a.shape[0]) for a in inputs]
    counts = [len(x) for x in (scalars, inputs, small, outs, small_outs, inputs, outs)]

    def run(*refs):
        groups, at = [], 0
        for n in counts:
            groups.append(refs[at : at + n])
            at += n
        scalar_refs, far_in, near_in, far_out, near_out, held_in, held_out = groups
        arrived, left, *rest = refs[at:]
        moves = [
            pltpu.make_async_copy(a.at[pl.ds(start, rows)], b, arrived.at[k])
            for k, (a, b, (_, start, rows)) in enumerate(zip(far_in, held_in, inputs))
        ]
        for move in moves:
            move.start()
        early = len(moves) - late
        for move in moves[:early]:
            move.wait()

        def arrive():
            for move in moves[early:]:
                move.wait()

        body(
            *([arrive] if late else []),
            *scalar_refs, *held_in, *near_in, *held_out, *near_out, *rest,
        )
        moves = [
            pltpu.make_async_copy(a, b, left.at[k]) for k, (a, b) in enumerate(zip(held_out, far_out))
        ]
        for move in moves:
            move.start()
        for move in moves:
            move.wait()

    vmem, hbm = pl.BlockSpec(memory_space=pltpu.VMEM), pl.BlockSpec(memory_space=pltpu.HBM)
    taken = [shape_of(rows, *a.shape[1:], kind=a.dtype) for a, _, rows in inputs]
    held = [pltpu.VMEM(a.shape, a.dtype) for a in (*taken, *outs)]
    limit = sum(size_of(a) for a in (*taken, *outs, *small, *small_outs)) + mib * 1024 * 1024
    return pl.pallas_call(
        run,
        out_shape=(*[pltpu.HBM(a.shape, a.dtype) for a in outs], *small_outs),
        in_specs=[pl.BlockSpec(memory_space=pltpu.SMEM)] * len(scalars)
        + [pl.BlockSpec(memory_space=pl.ANY)] * moved
        + [hbm] * (len(inputs) - moved)
        + [vmem] * len(small),
        out_specs=(*[hbm] * len(outs), *[vmem] * len(small_outs)),
        scratch_shapes=[
            *held,
            pltpu.SemaphoreType.DMA((len(inputs),)),
            pltpu.SemaphoreType.DMA((max(1, len(outs)),)),
            *scratch,
        ],
        compiler_params=pltpu.CompilerParams(vmem_limit_bytes=limit),
        cost_estimate=pl.CostEstimate(
            flops=flops,
            bytes_accessed=0 if quick else sum(size_of(a) for a in (*taken, *outs)),
            transcendentals=exps,
        ),
    )(
        *scalars,
        *[a for a, _, _ in inputs[:moved]],
        *[pltpu.with_memory_space_constraint(a, pltpu.HBM) for a, _, _ in inputs[moved:]],
        *small,
    )


def lane_of(shape):
    return lax.broadcasted_iota(jnp.int32, shape, len(shape) - 1)


def exchange_halves(a, b):
    front = lane_of(a.shape) < HDIM
    return (
        jnp.where(front, a, pltpu.roll(b, HDIM, 1)),
        jnp.where(front, pltpu.roll(a, HDIM, 1), b),
    )


def nt(a, b):
    return lax.dot_general(a, b, (((1,), (1,)), ((), ())), preferred_element_type=WIDE)


def nn(a, b):
    return lax.dot_general(a, b, (((1,), (0,)), ((), ())), preferred_element_type=WIDE)


def turn(x, cosine, sine, sign):
    lane = lax.rem(lane_of(x.shape), HDIM)
    ahead = pltpu.roll(x, x.shape[1] - 8, 1)
    behind = pltpu.roll(x, 8, 1)
    swapped = jnp.where(lane < 8, -ahead, behind) * sign
    return x * cosine + swapped * sine


def rotation_table(angles_table):
    tokens = angles_table.shape[1]
    rest = jnp.zeros((112, tokens), WIDE)
    x = jnp.concatenate([angles_table, rest], axis=0).T
    lane = lane_of(x.shape)
    c = jnp.where(lane < 8, x, 0.0)
    c = c + pltpu.roll(c, 8, 1)
    c = c + pltpu.roll(c, HDIM, 1) + jnp.where(lax.rem(lane, HDIM) < 16, 0.0, 1.0)
    s = jnp.where((lane >= 8) & (lane < 16), x, 0.0)
    s = s + pltpu.roll(s, 120, 1)
    s = s + pltpu.roll(s, HDIM, 1)
    return c, s


def project_kernel(
    arrive, place, tok, table, w, gain, shift, bias,
    normed, stats, x0, x1, x2, x3, cosine_out, sine_out, kept,
):
    rows = 64

    def norm_rows(i, carry):
        at = pl.ds(pl.multiple_of(i * rows, rows), rows)
        x = tok[at, :].astype(WIDE)
        mean = jnp.mean(x, axis=-1, keepdims=True)
        center = x - mean
        scale = lax.rsqrt(jnp.mean(center * center, axis=-1, keepdims=True) + 1e-05)
        normed[at, :] = (center * scale * gain[...] + shift[...]).astype(LOW)
        stats[at, :] = jnp.where(lane_of((rows, 128)) < HDIM, mean, scale)
        return carry

    lax.fori_loop(0, BLOCK // rows, norm_rows, 0)
    cosine, sine = rotation_table(table[...])
    cosine_out[...] = cosine
    sine_out[...] = sine
    arrive()
    mixed = [nn(normed[...], w[c]) + bias[c : c + 1, :] for c in range(3)]
    for pair in range(2):
        lanes = slice(pair * 128, pair * 128 + 128)
        q = turn(mixed[0][:, lanes], cosine, sine, 1.0) * 0.125
        k = turn(mixed[1][:, lanes], cosine, sine, 1.0)
        kv = exchange_halves(k, mixed[2][:, lanes])
        qq = exchange_halves(q[:HALF], q[HALF:])
        for one in range(2):
            kept[2 * pair + one, :BLOCK, :] = kv[one].astype(LOW)
            kept[2 * pair + one, BLOCK:, :] = qq[one].astype(LOW)
    for k, out in enumerate((x0, x1, x2, x3)):
        out[...] = kept[place[1] ^ k]


def padded_queries(q2):
    x = q2.astype(WIDE)
    front = lane_of(x.shape) < HDIM
    return (
        jnp.where(front, x, 0.0).astype(LOW),
        jnp.where(front, pltpu.roll(x, HDIM, 1), 0.0).astype(LOW),
    )


def padded_behind(d2):
    x = d2.astype(WIDE)
    front = lane_of(x.shape) < HDIM
    return (
        jnp.where(front, 0.0, pltpu.roll(x, HDIM, 1)).astype(LOW),
        jnp.where(front, 0.0, x).astype(LOW),
    )


def allowed_keys(key_block, first_query, begin):
    shape = (BLOCK, begin.shape[1])
    key_at = key_block * BLOCK + lax.broadcasted_iota(jnp.int32, shape, 0)
    query_at = first_query + lax.broadcasted_iota(jnp.int32, shape, 1)
    return (key_at <= query_at) & (key_at >= begin)


def key_blocks(place, rels, t):
    return [4 * t + (place[0] ^ rel) for rel in rels], place[1] ^ t


def forward_kernel(rels, first, last, *refs):
    place, kv0, kv1, q0, q1, q2, q3, begin = refs[:8]
    if first:
        acc_out, peak_out, kvt, queries, kept_q = refs[8:]
    else:
        acc_in, peak_in, o0, o1, o2, o3, out_t, total, kvt, queries, kept_q, kept_o = refs[8:]
        acc_out, peak_out = out_t, total
    me = place[1]
    front = lane_of((BLOCK, 128)) < HDIM
    for k, q in enumerate((q0, q1, q2, q3)):
        kept_q[me ^ k] = q[...]
    for i, kv in enumerate((kv0, kv1)):
        for t in range(4):
            kvt[i, t] = jnp.where(front, 1.0, kv[t].astype(WIDE)).T.astype(LOW)

    def one_query_block(j, carry):
        first_query = (4 * j + place[0]) * BLOCK
        queries[:HALF, :], queries[HALF:, :] = padded_queries(kept_q[j])
        if first:
            peak_out[j] = jnp.full((8, BLOCK), -1e30, WIDE)
            acc_out[j] = jnp.zeros((128, BLOCK), WIDE)
        else:
            peak_out[j] = peak_in[j]
            acc_out[j] = acc_in[j]

        def two_blocks(t, carry):
            blocks, at = key_blocks(place, rels, t)
            scores = []
            for i, kv in enumerate((kv0, kv1)):
                ok = allowed_keys(blocks[i], first_query, begin[j, :1])
                scores.append(jnp.where(ok, nt(kv[at], queries[...]), -1e30))
            old = peak_out[j, :1]
            new = old
            for one in scores:
                new = jnp.maximum(new, jnp.max(one, axis=0, keepdims=True))
            done = acc_out[j] * jnp.exp(old - new)
            for i in range(2):
                done += nn(kvt[i, at], jnp.exp(scores[i] - new).astype(LOW))
            acc_out[j] = done
            peak_out[j, :1] = new
            return carry

        lax.fori_loop(0, j + 1, two_blocks, 0)
        if last:
            weight_sum = acc_out[j, :1]
            done = acc_out[j] / weight_sum
            out_t[j] = done
            total[j, :1] = peak_out[j, :1] + jnp.log(weight_sum)
            rows = done.T
            x, y = rows[:HALF], rows[HALF:]
            kept_o[j] = jnp.where(lane_of(x.shape) < HDIM, pltpu.roll(x, HDIM, 1), y).astype(LOW)
        return carry

    lax.fori_loop(0, 4, one_query_block, 0)
    if last:
        for k, out in enumerate((o0, o1, o2, o3)):
            out[...] = kept_o[me ^ k]


def backward_kernel(rels, first, *refs):
    place, kv0, kv1, q0, q1, q2, q3, d0, d1, d2, d3, out_t, total, begin = refs[:14]
    if first:
        acc, keep, send, kvt, queries, grads, dot_rows, dkv, kept_q, kept_d = refs[14:]
    else:
        (
            acc_in, g0, g1, g2, g3, keep, send,
            kvt, queries, grads, dot_rows, dkv, kept_q, kept_d, acc, kept_g,
        ) = refs[14:]
    me = place[1]
    for k in range(4):
        kept_q[me ^ k] = (q0, q1, q2, q3)[k][...]
        kept_d[me ^ k] = (d0, d1, d2, d3)[k][...]
    for i, kv in enumerate((kv0, kv1)):
        for t in range(4):
            kvt[i, t] = kv[t].astype(WIDE).T.astype(LOW)
    dkv[...] = jnp.zeros(dkv.shape, WIDE)

    def one_query_block(j, carry):
        first_query = (4 * j + place[0]) * BLOCK
        queries[:HALF, :], queries[HALF:, :] = padded_queries(kept_q[j])
        grads[:HALF, :], grads[HALF:, :] = padded_behind(kept_d[j])
        dot_rows[...] = jnp.sum(grads[...].astype(WIDE).T * out_t[j], axis=0, keepdims=True)
        acc[j] = jnp.zeros((128, BLOCK), WIDE) if first else acc_in[j]

        def two_blocks(t, carry):
            blocks, at = key_blocks(place, rels, t)
            for i, kv in enumerate((kv0, kv1)):
                term = 0.0
                for half in range(2):
                    some = slice(half * HALF, half * HALF + HALF)
                    ok = allowed_keys(blocks[i], first_query + half * HALF, begin[j, :1, some])
                    scores = nt(kv[at], queries[some, :])
                    probs = jnp.where(ok, jnp.exp(scores - total[j, :1, some]), 0.0)
                    grad_probs = nt(kv[at], grads[some, :])
                    grad_scores = (probs * (grad_probs - dot_rows[:, some])).astype(LOW)
                    term += nn(grad_scores, queries[some, :]) + nn(probs.astype(LOW), grads[some, :])
                    acc[j, :, some] += nn(kvt[i, at], grad_scores)
                dkv[i, at] += term
            return carry

        lax.fori_loop(0, j + 1, two_blocks, 0)
        if not first:
            rows = acc[j].T
            x, y = rows[:HALF], rows[HALF:]
            kept_g[j] = jnp.where(lane_of(x.shape) < HDIM, x, pltpu.roll(y, HDIM, 1)).astype(LOW)
        return carry

    lax.fori_loop(0, 4, one_query_block, 0)
    if not first:
        for k, out in enumerate((g0, g1, g2, g3)):
            out[...] = kept_g[me ^ k]
    for t in range(4):
        keep[t] = dkv[0, t].astype(LOW)
        send[t] = dkv[1, t].astype(LOW)


def branch_kernel(arrive, place, h0, h1, h2, h3, w, attended, partial, kept):
    for k, h in enumerate((h0, h1, h2, h3)):
        kept[place[1] ^ k] = h[...]
    for pair in range(2):
        lanes = slice(pair * 128, pair * 128 + 128)
        x, y = exchange_halves(kept[2 * pair].astype(WIDE), kept[2 * pair + 1].astype(WIDE))
        attended[:HALF, lanes] = x.astype(LOW)
        attended[HALF:, lanes] = y.astype(LOW)
    arrive()
    for n in range(4):
        at = slice(n * 512, n * 512 + 512)
        partial[:, at] = nn(attended[...], w[:, at]).astype(LOW)


def grad_attended_kernel(place, grad, w, d0, d1, d2, d3, kept):
    g = nt(grad[...], w[...])
    for pair in range(2):
        lanes = slice(pair * 128, pair * 128 + 128)
        both = exchange_halves(g[:HALF, lanes], g[HALF:, lanes])
        for one in range(2):
            kept[2 * pair + one] = both[one].astype(LOW)
    for k, out in enumerate((d0, d1, d2, d3)):
        out[...] = kept[place[1] ^ k]


def join_kernel(keep, received, far, g0, g1, g2, g3, x0, x1, x2, x3):
    for k in range(4):
        total = keep[k].astype(WIDE) + received[k].astype(WIDE) + far[k].astype(WIDE)
        out = (x0, x1, x2, x3)[k]
        out[:BLOCK, :] = total.astype(LOW)
        out[BLOCK:, :] = (g0, g1, g2, g3)[k][...]


def grad_project_kernel(
    arrive, place, x0, x1, x2, x3, cosine, sine, tok, stats, w,
    grad_mixed, partial, gain_sum, shift_sum, bias_sum, parts, kept,
):
    for k, x in enumerate((x0, x1, x2, x3)):
        parts[place[1] ^ k] = x[:BLOCK, :]
        kept[place[1] ^ k] = x[BLOCK:, :]
    for pair in range(2):
        lanes = slice(pair * 128, pair * 128 + 128)
        k, v = exchange_halves(parts[2 * pair].astype(WIDE), parts[2 * pair + 1].astype(WIDE))
        q = exchange_halves(kept[2 * pair].astype(WIDE), kept[2 * pair + 1].astype(WIDE))
        q = jnp.concatenate(q, axis=0)
        q = turn(q, cosine[...], sine[...], -1.0) * 0.125
        k = turn(k, cosine[...], sine[...], -1.0)
        for c, part in enumerate((q, k, v)):
            start = c * 256 + pair * 128
            low = part.astype(LOW)
            grad_mixed[:, start : start + 128] = low
            bias_sum[c : c + 1, lanes] = jnp.sum(low.astype(WIDE), axis=0, keepdims=True)
    arrive()
    mean, scale = stats[:, 0:1], stats[:, 64:65]
    for n in range(4):
        at = slice(n * 512, n * 512 + 512)
        total = nt(grad_mixed[:, :256], w[0, at, :])
        total += nt(grad_mixed[:, 256:512], w[1, at, :])
        total += nt(grad_mixed[:, 512:], w[2, at, :])
        partial[:, at] = total.astype(LOW)
        normal = (tok[:, at].astype(WIDE) - mean) * scale
        gain_sum[:, at] = jnp.sum(total * normal, axis=0, keepdims=True)
        shift_sum[:, at] = jnp.sum(total, axis=0, keepdims=True)


def hidden_gradient_kernel(cot, w, grad_hidden):
    grad_hidden[...] = nt(cot[...], w[...])


def feed_kernel(arrive, second, w_gate, w_up, grad_hidden, hidden, grad_gate, grad_up, partial):
    gate = nt(second[...], w_gate[0])
    arrive()
    up = nt(second[...], w_up[0])
    sigmoid = 1.0 / (1.0 + jnp.exp(-gate))
    activated = gate * sigmoid
    hidden[...] = (activated * up).astype(LOW)
    grad = grad_hidden[...]
    grad_up[...] = (grad * activated).astype(LOW)
    grad_gate[...] = (grad * up * sigmoid * (1.0 + gate * (1.0 - sigmoid))).astype(LOW)
    for n in range(4):
        at = slice(n * 512, n * 512 + 512)
        partial[:, at] = (nn(grad_gate[...], w_gate[0, :, at]) + nn(grad_up[...], w_up[0, :, at])).astype(LOW)


def for_rows(work):
    rows = 16

    def one(i, carry):
        work(pl.ds(pl.multiple_of(i * rows, rows), rows))
        return carry

    lax.fori_loop(0, 64 // rows, one, 0)


def summed(parts, at):
    total = parts[0, at, :].astype(WIDE)
    for k in range(1, 8):
        total += parts[k, at, :].astype(WIDE)
    return total


def copy_out(copies, at, value):
    low = value.astype(LOW)
    for k in range(8):
        copies[k, at, :] = low


def second_norm_kernel(parts, tok, gain, shift, copies, middle, normal, stats):
    def work(at):
        x = tok[at, :].astype(WIDE) + summed(parts, at)
        center = x - jnp.mean(x, axis=-1, keepdims=True)
        scale = lax.rsqrt(jnp.mean(center * center, axis=-1, keepdims=True) + 1e-05)
        rows = center * scale
        copy_out(copies, at, rows * gain[...] + shift[...])
        middle[at, :] = x
        normal[at, :] = rows
        stats[at, :] = jnp.broadcast_to(scale, (scale.shape[0], 128))

    for_rows(work)


def norm_gradient(grad, rows, scale, gain):
    scaled = grad * gain
    return scale * (
        scaled
        - jnp.mean(scaled, axis=-1, keepdims=True)
        - rows * jnp.mean(scaled * rows, axis=-1, keepdims=True)
    )


def second_gradient_kernel(parts, cot, normal, stats, gain, copies, grad_middle, sums):
    sums[...] = jnp.zeros(sums.shape, WIDE)

    def work(at):
        grad, rows = summed(parts, at), normal[at, :]
        done = cot[at, :].astype(WIDE) + norm_gradient(grad, rows, stats[at, 0:1], gain[...])
        copy_out(copies, at, done)
        grad_middle[at, :] = done
        sums[0:1, :] += jnp.sum(grad * rows, axis=0, keepdims=True)
        sums[1:2, :] += jnp.sum(grad, axis=0, keepdims=True)

    for_rows(work)


def feed_sum_kernel(place, parts, middle, out):
    rows = 16
    mine = place[3]

    def one(i, carry):
        at = pl.ds(pl.multiple_of(i * rows, rows), rows)
        total = parts[0, at, :].astype(WIDE)
        for k in range(1, 4):
            total += parts[k, at, :].astype(WIDE)
        here = i * rows - mine * 64
        own = pl.ds(pl.multiple_of(jnp.clip(here, 0, 64 - rows), rows), rows)
        inside = (here >= 0) & (here < 64)
        out[at, :] = (total + jnp.where(inside, middle[own, :], 0.0)).astype(LOW)
        return carry

    lax.fori_loop(0, 128 // rows, one, 0)


def layer_out_kernel(a, b, copies):
    rows = 16

    def one(i, carry):
        at = pl.ds(pl.multiple_of(i * rows, rows), rows)
        low = (a[at, :].astype(WIDE) + b[at, :].astype(WIDE)).astype(LOW)
        for k in range(4):
            copies[k, at, :] = low
        return carry

    lax.fori_loop(0, 128 // rows, one, 0)


def first_gradient_kernel(parts, grad_middle, tok, stats, vectors, gain, copies):
    def work(at):
        mean, scale = stats[at, 0:1], stats[at, 64:65]
        rows = (tok[at, :].astype(WIDE) - mean) * scale
        done = norm_gradient(summed(parts, at), rows, scale, gain[...])
        low = (grad_middle[at, :] + done).astype(LOW)
        extra = vectors[at, :].astype(LOW)
        for k in range(8):
            copies[k, at, :2048] = low
            copies[k, at, 2048:] = extra

    for_rows(work)


def weight_kernel(widths, sources, arrive, place, *refs):
    count = max(max(pair) for pair in sources) + 1
    inputs = refs[:count]
    mine, theirs, turned = refs[count:]
    first_core = place[2] == 0
    start = 0
    for n, ((left, right), width) in enumerate(zip(sources, widths)):
        if n == 1:
            arrive()
        left, right = inputs[left], inputs[right]
        turned[:width, :] = left[...].astype(WIDE).T.astype(LOW)

        def one(n, carry, start=start, right=right, width=width):
            columns = right[:, pl.ds(pl.multiple_of(n * 256, 256), 256)]
            both = nn(turned[:width, :], columns)
            first, second = both[:, :128], both[:, 128:]
            at = pl.ds(start, width)
            mine[n, at, :] = jnp.where(first_core, first, second).astype(LOW)
            theirs[n, at, :] = jnp.where(first_core, second, first).astype(LOW)
            return carry

        lax.fori_loop(0, 8, one, 0, unroll=4)
        start += width


def weight_grads(pairs, place):
    inputs, sources = [], []
    for pair in pairs:
        for a in pair:
            if not any(a is b for b in inputs):
                inputs.append(a)
        sources.append(tuple(next(k for k, b in enumerate(inputs) if b is a) for a in pair))
    widths = tuple(a.shape[1] for a, _ in pairs)
    out = jax.ShapeDtypeStruct((8, sum(widths), 128), LOW)
    return kernel_call(
        functools.partial(weight_kernel, widths, sources),
        (out, out),
        inputs,
        scalars=(place,),
        scratch=(pltpu.VMEM((max(widths), BLOCK), LOW),),
        late=len(inputs) - 2,
        quick=True,
    )


def swapped(x, axis):
    return lax.ppermute(x, axis, [(0, 1), (1, 0)])


def across(pieces):
    moved = [
        lax.ppermute(pieces[k], SPREAD, [(i, i ^ k) for i in range(4)]) for k in range(1, 4)
    ]
    return (pieces[0], *moved)


def z_parts_kernel(place, mine, received, *refs):
    outs, (held_a, held_b, done, came, went) = refs[:4], refs[4:]
    z = place[0]
    order = [(k, xh) for k in (1, 3, 2, 0) for xh in range(2)]
    moves = []
    for n, (k, xh) in enumerate(order):
        at = xh * 4 + lax.rem(z + k, 4)
        moves.append(
            (
                pltpu.make_async_copy(mine.at[at], held_a.at[n], came.at[2 * n]),
                pltpu.make_async_copy(received.at[at], held_b.at[n], came.at[2 * n + 1]),
                pltpu.make_async_copy(done.at[n], outs[k].at[xh], went.at[n]),
            )
        )
    for a, b, _ in moves:
        a.start()
        b.start()
    for n, (a, b, out) in enumerate(moves):
        a.wait()
        b.wait()
        done[n] = (held_a[n].astype(WIDE) + held_b[n].astype(WIDE)).astype(LOW)
        out.start()
    for _, _, out in moves:
        out.wait()


def z_parts(mine, received):
    rows = mine.shape[1]
    hbm = pl.BlockSpec(memory_space=pltpu.HBM)
    held = pltpu.VMEM((8, rows, 128), LOW)
    return pl.pallas_call(
        z_parts_kernel,
        in_specs=[pl.BlockSpec(memory_space=pltpu.SMEM), hbm, hbm],
        out_specs=[hbm] * 4,
        out_shape=[pltpu.HBM((2, rows, 128), LOW)] * 4,
        scratch_shapes=[
            held,
            held,
            held,
            pltpu.SemaphoreType.DMA((16,)),
            pltpu.SemaphoreType.DMA((8,)),
        ],
        compiler_params=pltpu.CompilerParams(vmem_limit_bytes=24 * 1024 * 1024),
        cost_estimate=pl.CostEstimate(flops=0, bytes_accessed=0, transcendentals=0),
    )(
        lax.axis_index(Z).reshape(1),
        *[pltpu.with_memory_space_constraint(a, pltpu.HBM) for a in (mine, received)],
    )


def settled_kernel(x, out, held, came, went):
    rows = x.shape[1]
    moves = []
    for k in range(x.shape[0]):
        at = pl.ds(k * rows, rows)
        moves.append(
            (
                pltpu.make_async_copy(x.at[k], held.at[k], came.at[k]),
                pltpu.make_async_copy(held.at[k, :, pl.ds(0, 2048)], out.at[at], went.at[k]),
            )
        )
    for come, _ in moves:
        come.start()
    for come, go in moves:
        come.wait()
        go.start()
    for _, go in moves:
        go.wait()


def settled_and_summed_kernel(x, out, total, held, came, went):
    settled_kernel(x, out, held, came, went)
    done = held[0, :, 2048:].astype(WIDE)
    for k in range(1, 8):
        done += held[k, :, 2048:].astype(WIDE)
    total[...] = done


def settled(x, summed_too=False):
    hbm = pl.BlockSpec(memory_space=pltpu.HBM)
    parts, rows = x.shape[:2]
    out = [pltpu.HBM((parts * rows, 2048), x.dtype)]
    specs = [hbm]
    if summed_too:
        out.append(shape_of(rows, 128, kind=WIDE))
        specs.append(pl.BlockSpec(memory_space=pltpu.VMEM))
    return pl.pallas_call(
        settled_and_summed_kernel if summed_too else settled_kernel,
        out_shape=out,
        in_specs=[pl.BlockSpec(memory_space=pl.ANY)],
        out_specs=specs,
        scratch_shapes=[
            pltpu.VMEM(x.shape, x.dtype),
            pltpu.SemaphoreType.DMA((parts,)),
            pltpu.SemaphoreType.DMA((parts,)),
        ],
        compiler_params=pltpu.CompilerParams(vmem_limit_bytes=8 * 1024 * 1024),
        cost_estimate=pl.CostEstimate(flops=0, bytes_accessed=0, transcendentals=0),
    )(x)


def z_permute(part, distance):
    return lax.ppermute(part, Z, [(i, (i + distance) % 4) for i in range(4)])


def xh_halves(moved):
    xh = lax.axis_index("xh")

    def added(at):
        return sum(lax.dynamic_index_in_dim(x, at, 0, False).astype(WIDE) for x in moved)

    return added(xh), added(1 - xh).astype(LOW)


def dealt(x, axis):
    return lax.all_to_all(x, axis, split_axis=0, concat_axis=0, tiled=True)


def tp_parts(partial):
    return dealt(partial.reshape(8, -1, partial.shape[1]), TP)


def tp_rows(copies):
    return dealt(copies, TP).reshape(-1, copies.shape[2])


def summed_by_pairs(x, pairs):
    for axis, size, distance in pairs:
        x = x + lax.ppermute(x, axis, [(i, i ^ distance) for i in range(size)])
    return x


def shape_of(*dims, kind=LOW):
    return jax.ShapeDtypeStruct(dims, kind)


def body(
    tokens, cotangent, segment_ids, first_gain, first_shift, second_gain, second_shift,
    w_qkv, qkv_bias, w_out, w_gate_up, w_down,
):
    ctx = lax.axis_index(CTX)
    tp = lax.axis_index(TP)
    group = lax.axis_index(("zl", "core"))
    place = jnp.stack(
        [group, lax.axis_index(SPREAD), lax.axis_index("core"), lax.axis_index("xl")]
    )
    tied = lax.optimization_barrier

    def my_share(array):
        return lax.dynamic_slice_in_dim(array, tp * 64, 64)

    labels = jnp.arange(DOCS, dtype=jnp.int32)
    starts = jnp.sum((segment_ids[None, :] < labels[:, None]).astype(jnp.int32), axis=1)
    begins = jnp.sum(
        jnp.where(segment_ids[None, :] == labels[:, None], starts[:, None], 0), axis=0
    )
    begin = lax.dynamic_index_in_dim(begins.reshape(4, 4, 1, BLOCK), group, 1, False)
    begin = jnp.broadcast_to(begin, (4, 8, BLOCK))
    own = lax.dynamic_slice_in_dim(begins, ctx * BLOCK, BLOCK)
    places = ctx * BLOCK + jnp.arange(BLOCK, dtype=jnp.int32) - own
    frequency = 10000.0 ** (-jnp.arange(8, dtype=WIDE) / 8.0)
    angles = frequency[:, None] * places.astype(WIDE)[None, :]
    table = jnp.concatenate([jnp.cos(angles), jnp.sin(angles)], axis=0)

    w3 = jnp.transpose(w_qkv, (1, 0, 2))
    w2 = jnp.transpose(w_gate_up, (1, 2, 0))
    quarter, piece = shape_of(HALF, 128), shape_of(BLOCK + HALF, 128)
    wide_block = shape_of(BLOCK, 128, kind=WIDE)
    four = pltpu.VMEM((4, HALF, 128), LOW)
    normed_low, stats1, *packed, cosine, sine = kernel_call(
        project_kernel,
        (shape_of(BLOCK, 2048), wide_block, *[piece] * 4, wide_block, wide_block),
        (tokens, table, w3),
        small=(first_gain[None], first_shift[None], qkv_bias),
        scalars=(place,),
        scratch=(pltpu.VMEM((4, BLOCK + HALF, 128), LOW),),
        late=1,
        flops=2 * 512 * 2048 * 768,
    )
    packed = across(packed)
    kv = jnp.stack([x[:BLOCK] for x in packed])
    queries = [(x, BLOCK, HALF) for x in packed]
    kv_c = swapped(kv, "core")
    state = (shape_of(4, 128, BLOCK, kind=WIDE), shape_of(4, 8, BLOCK, kind=WIDE))
    acc, peak = kernel_call(
        functools.partial(forward_kernel, (0, 1), True, False),
        state,
        (kv, kv_c, *queries, begin),
        scalars=(place,),
        scratch=(pltpu.VMEM((2, 4, 128, BLOCK), LOW), pltpu.VMEM((BLOCK, 128), LOW), four),
        flops=20 * 4 * BLOCK * BLOCK * 128,
        exps=20 * BLOCK * BLOCK,
        mib=24,
    )
    acc, peak, kv_z = tied((acc, peak, swapped(kv, "zl")))
    kv_zc = swapped(kv_z, "core")
    *heads, out_t, total = kernel_call(
        functools.partial(forward_kernel, (2, 3), False, True),
        (*[quarter] * 4, *state),
        (kv_z, kv_zc, *queries, begin, acc, peak),
        scalars=(place,),
        scratch=(pltpu.VMEM((2, 4, 128, BLOCK), LOW), pltpu.VMEM((BLOCK, 128), LOW), four, four),
        flops=20 * 4 * BLOCK * BLOCK * 128,
        exps=20 * BLOCK * BLOCK,
        mib=24,
    )
    heads = across(heads)
    attended_low, partial_branch = kernel_call(
        branch_kernel,
        (shape_of(BLOCK, 256), shape_of(BLOCK, 2048)),
        (*heads, w_out),
        scalars=(place,),
        scratch=(four,),
        late=1,
        flops=2 * 512 * 256 * 2048,
    )
    share = shape_of(64, 2048, kind=WIDE)
    copies = shape_of(8, 64, 2048)
    branch_parts, tok_share, cot_share = tied(
        (tp_parts(partial_branch), my_share(tokens), my_share(cotangent))
    )
    copies2, middle, second_rows, stats2 = kernel_call(
        second_norm_kernel,
        (copies, share, share, shape_of(64, 128, kind=WIDE)),
        (branch_parts, tok_share),
        moved=1,
        small=(second_gain[None], second_shift[None]),
    )
    (grad_hidden,) = kernel_call(
        hidden_gradient_kernel,
        (shape_of(BLOCK, 704, kind=WIDE),),
        (tied((cotangent, copies2))[0], w_down),
        flops=2 * 512 * 2048 * 704,
    )
    second_low, grad_hidden = tied((tp_rows(copies2), grad_hidden))
    strip = shape_of(BLOCK, 704)
    hidden_low, grad_gate, grad_up, partial_second = kernel_call(
        feed_kernel,
        (strip, strip, strip, shape_of(BLOCK, 2048)),
        (second_low, w2[:1], w2[1:], grad_hidden),
        moved=1,
        late=2,
        flops=8 * 512 * 2048 * 704,
        mib=24,
    )
    second_parts = tp_parts(partial_second)

    feed_mine, feed_theirs = weight_grads(
        ((grad_gate, second_low), (grad_up, second_low), (hidden_low, cotangent)), place
    )
    second_parts, feed_mine, feed_theirs = tied((second_parts, feed_mine, feed_theirs))
    copies3, grad_middle, second_sums = kernel_call(
        second_gradient_kernel,
        (copies, share),
        (second_parts, cot_share, second_rows, stats2),
        moved=1,
        small=(second_gain[None],),
        small_outs=(shape_of(2, 2048, kind=WIDE),),
    )
    grad_branch = tp_rows(copies3)
    partial_feed = jnp.dot(hidden_low, w_down, preferred_element_type=WIDE).astype(LOW)
    grad_branch, partial_feed = tied((grad_branch, partial_feed))
    feed_z = z_parts(feed_mine, swapped(feed_theirs, "core"))
    feed_1, feed_3 = z_permute(feed_z[1], 1), z_permute(feed_z[3], 3)

    grads = kernel_call(
        grad_attended_kernel,
        (*[quarter] * 4,),
        (grad_branch, w_out),
        moved=1,
        scalars=(place,),
        scratch=(four,),
        flops=2 * 512 * 256 * 2048,
    )
    feed_1, feed_3, partial_feed, *grads = tied((feed_1, feed_3, partial_feed, *grads))
    feed_parts = dealt(partial_feed.reshape(4, 128, 2048), "y")
    *grads, feed_2 = tied((*across(grads), feed_z[2]))
    feed_2 = z_permute(feed_2, 2)
    scratch = (
        pltpu.VMEM((2, 4, 128, BLOCK), LOW),
        pltpu.VMEM((BLOCK, 128), LOW),
        pltpu.VMEM((BLOCK, 128), LOW),
        pltpu.VMEM((1, BLOCK), WIDE),
        pltpu.VMEM((2, 4, BLOCK, 128), WIDE),
        four,
        four,
    )
    blocks = shape_of(4, BLOCK, 128)
    acc, keep1, send1 = kernel_call(
        functools.partial(backward_kernel, (2, 3), True),
        (state[0], blocks, blocks),
        (kv_z, kv_zc, *queries, *grads, out_t, total, begin),
        scalars=(place,),
        scratch=scratch,
        flops=20 * 10 * BLOCK * BLOCK * 128,
        exps=20 * BLOCK * BLOCK,
        mib=28,
    )
    acc, send1, feed_parts, feed_2 = tied((acc, send1, feed_parts, feed_2))
    (feed_half,) = kernel_call(
        feed_sum_kernel,
        (shape_of(128, 2048),),
        (feed_parts, middle),
        scalars=(place,),
        moved=1,
    )
    far = (keep1.astype(WIDE) + swapped(send1, "core").astype(WIDE)).astype(LOW)
    feed_keep, feed_send = xh_halves([feed_z[0], feed_1, feed_2, feed_3])
    acc, far, feed_half, feed_send = tied((acc, far, feed_half, feed_send))
    near = kernel_call(
        functools.partial(backward_kernel, (0, 1), False),
        (*[quarter] * 4, blocks, blocks),
        (kv, kv_c, *queries, *grads, out_t, total, begin, acc),
        scalars=(place,),
        scratch=(*scratch, pltpu.VMEM((4, 128, BLOCK), WIDE), four),
        flops=20 * 10 * BLOCK * BLOCK * 128,
        exps=20 * BLOCK * BLOCK,
        mib=28,
    )
    *near, far, feed_other, feed_received = tied(
        (*near, swapped(far, "zl"), swapped(feed_half, "xl"), swapped(feed_send, "xh"))
    )
    *grad_queries, keep0, send0 = near
    pieces = kernel_call(
        join_kernel,
        (*[piece] * 4,),
        (keep0, swapped(send0, "core"), far, *grad_queries),
    )
    (copies4,) = kernel_call(layer_out_kernel, (shape_of(4, 128, 2048),), (feed_half, feed_other))
    *pieces, copies4 = tied((*pieces, copies4))
    pieces = across(pieces)
    layer_out = dealt(copies4, "y")
    grad_mixed, partial_normed, gain_sum, shift_sum, bias_sum = kernel_call(
        grad_project_kernel,
        (shape_of(BLOCK, 768), shape_of(BLOCK, 2048)),
        (*pieces, cosine, sine, tokens, stats1, w3),
        small_outs=(
            shape_of(1, 2048, kind=WIDE),
            shape_of(1, 2048, kind=WIDE),
            shape_of(3, 256, kind=WIDE),
        ),
        scalars=(place,),
        scratch=(pltpu.VMEM((4, BLOCK, 128), LOW), four),
        late=3,
        flops=2 * 512 * 2048 * 768,
    )
    partial_normed, layer_out = tied((partial_normed, layer_out))
    (layer_out,) = settled(layer_out)
    normed_parts = tp_parts(partial_normed)

    rest_mine, rest_theirs = weight_grads(
        ((grad_mixed, normed_low), (attended_low, grad_branch)), place
    )
    rest_z = z_parts(rest_mine, swapped(rest_theirs, "core"))
    vectors = jnp.concatenate([gain_sum, shift_sum, second_sums], axis=0).reshape(32, 256)
    vectors = jnp.concatenate([vectors, bias_sum], axis=0)
    vectors = summed_by_pairs(vectors, (("core", 2, 1), ("zl", 2, 1), ("zh", 2, 1)))
    vectors, *rest_z = tied((vectors, *rest_z))
    vectors = summed_by_pairs(vectors, (("xh", 2, 1),))
    rest_1, rest_3 = z_permute(rest_z[1], 1), z_permute(rest_z[3], 3)
    normed_parts, vectors, rest_1, rest_3 = tied((normed_parts, vectors, rest_1, rest_3))
    bias_grad = vectors[32:]
    (copies5,) = kernel_call(
        first_gradient_kernel,
        (shape_of(8, 64, 2048 + 128),),
        (normed_parts, grad_middle, tok_share, my_share(stats1), vectors[:32].reshape(64, 128)),
        moved=1,
        small=(first_gain[None],),
    )
    grad_tokens, vectors = settled(dealt(copies5, TP), summed_too=True)
    vectors = vectors.reshape(4, 2048)

    rest_z = (rest_z[0], rest_1, z_permute(rest_z[2], 2), rest_3)
    rest_keep, rest_send = xh_halves(rest_z)
    rest_w = rest_keep + swapped(rest_send, "xh").astype(WIDE)
    feed_w = feed_keep + feed_received.astype(WIDE)
    return (
        layer_out,
        grad_tokens,
        vectors[0],
        vectors[1],
        vectors[2],
        vectors[3],
        jnp.transpose(rest_w[:768].reshape(3, 256, 128), (2, 0, 1)),
        bias_grad,
        rest_w[768:],
        jnp.transpose(feed_w[:1408].reshape(2, 704, 128), (2, 0, 1)),
        feed_w[1408:],
    )


def solution(mesh):
    fine = Mesh(
        mesh.devices.reshape(2, 2, 2, 2, 4, 2), ("xh", "zh", "zl", "core", "y", "xl")
    )
    rows = P(CTX, None)
    return jax.shard_map(
        body,
        mesh=fine,
        in_specs=(
            rows, rows, P(), P(), P(), P(), P(),
            P(None, None, TP), P(None, TP), P(TP, None), P(None, None, TP), P(TP, None),
        ),
        out_specs=(
            rows, rows, P(), P(), P(), P(),
            P(CTX, None, TP), P(None, TP), P(TP, CTX), P(CTX, None, TP), P(TP, CTX),
        ),
        check_vma=False,
    )
```

```python
import functools

import jax
import jax.numpy as jnp
from jax import lax
from jax.experimental import pallas as pl
from jax.experimental.pallas import tpu as pltpu
from jax.sharding import Mesh
from jax.sharding import PartitionSpec as P

HDIM = 64
DOCS = 3
BLOCK = 512
HALF = 256
LOW = jnp.bfloat16
WIDE = jnp.float32
CTX = ("xh", "zh", "zl", "core")
TP = ("y", "xl")
SPREAD = ("xh", "zh")
Z = ("zh", "zl")


def size_of(a):
    return a.size * jnp.dtype(a.dtype).itemsize


def gathered_order(place):
    x, y = place[3], place[4]
    row = [lax.rem(y + k, 4) * 2 for k in range(4)]
    other = 1 - x
    return [
        row[0] + x, row[0] + other,
        row[3] + x, row[1] + x, row[2] + x,
        row[3] + other, row[1] + other, row[2] + other,
    ]


def deal_rows(place, rows, outs):
    tp = place[4] * 2 + place[3]
    for k, out in enumerate(outs):
        out[...] = rows[pl.ds(pl.multiple_of((tp ^ k) * 64, 64), 64), :]


def kernel_call(
    body, outs, inputs, *, small=(), small_outs=(), scalars=(), scratch=(), late=0, flops=0, exps=0, mib=12, quick=False, moved=0
):
    inputs = [a if isinstance(a, (tuple, list)) else (a, 0, a.shape[0]) for a in inputs]
    flat = [x for a in inputs for x in (a if isinstance(a, list) else a[:1])]
    counts = [len(x) for x in (scalars, flat, small, outs, small_outs, inputs, outs)]

    def run(*refs):
        groups, at = [], 0
        for n in counts:
            groups.append(refs[at : at + n])
            at += n
        scalar_refs, far_in, near_in, far_out, near_out, held_in, held_out = groups
        arrived, left, *rest = refs[at:]
        pairs, ends = [], []
        for a, held in zip(inputs, held_in):
            if isinstance(a, list):
                rows = a[0].shape[0]
                for index in gathered_order(scalar_refs[0]):
                    pairs.append((None, held.at[pl.ds(pl.multiple_of(index * rows, rows), rows)]))
            else:
                pairs.append((pl.ds(a[1], a[2]), held))
            ends.append(len(pairs))
        moves = [
            pltpu.make_async_copy(x if part is None else x.at[part], held, arrived.at[k])
            for k, (x, (part, held)) in enumerate(zip(far_in, pairs))
        ]
        for move in moves:
            move.start()
        early = ends[len(inputs) - late - 1]
        for move in moves[:early]:
            move.wait()

        def arrive():
            for move in moves[early:]:
                move.wait()

        body(
            *([arrive] if late else []),
            *scalar_refs, *held_in, *near_in, *held_out, *near_out, *rest,
        )
        moves = [
            pltpu.make_async_copy(a, b, left.at[k]) for k, (a, b) in enumerate(zip(held_out, far_out))
        ]
        for move in moves:
            move.start()
        for move in moves:
            move.wait()

    vmem, hbm = pl.BlockSpec(memory_space=pltpu.VMEM), pl.BlockSpec(memory_space=pltpu.HBM)
    taken = [
        shape_of(8 * a[0].shape[0], a[0].shape[1], kind=a[0].dtype)
        if isinstance(a, list)
        else shape_of(a[2], *a[0].shape[1:], kind=a[0].dtype)
        for a in inputs
    ]
    held = [pltpu.VMEM(a.shape, a.dtype) for a in (*taken, *outs)]
    limit = sum(size_of(a) for a in (*taken, *outs, *small, *small_outs)) + mib * 1024 * 1024
    return pl.pallas_call(
        run,
        out_shape=(*[pltpu.HBM(a.shape, a.dtype) for a in outs], *small_outs),
        in_specs=[pl.BlockSpec(memory_space=pltpu.SMEM)] * len(scalars)
        + [pl.BlockSpec(memory_space=pl.ANY)] * moved
        + [hbm] * (len(flat) - moved)
        + [vmem] * len(small),
        out_specs=(*[hbm] * len(outs), *[vmem] * len(small_outs)),
        scratch_shapes=[
            *held,
            pltpu.SemaphoreType.DMA((len(flat),)),
            pltpu.SemaphoreType.DMA((max(1, len(outs)),)),
            *scratch,
        ],
        compiler_params=pltpu.CompilerParams(vmem_limit_bytes=limit),
        cost_estimate=pl.CostEstimate(
            flops=flops,
            bytes_accessed=0 if quick else sum(size_of(a) for a in (*taken, *outs)),
            transcendentals=exps,
        ),
    )(
        *scalars,
        *flat[:moved],
        *[pltpu.with_memory_space_constraint(a, pltpu.HBM) for a in flat[moved:]],
        *small,
    )


def lane_of(shape):
    return lax.broadcasted_iota(jnp.int32, shape, len(shape) - 1)


def exchange_halves(a, b):
    front = lane_of(a.shape) < HDIM
    return (
        jnp.where(front, a, pltpu.roll(b, HDIM, 1)),
        jnp.where(front, pltpu.roll(a, HDIM, 1), b),
    )


def nt(a, b):
    return lax.dot_general(a, b, (((1,), (1,)), ((), ())), preferred_element_type=WIDE)


def nn(a, b):
    return lax.dot_general(a, b, (((1,), (0,)), ((), ())), preferred_element_type=WIDE)


def turn(x, cosine, sine, sign):
    lane = lax.rem(lane_of(x.shape), HDIM)
    ahead = pltpu.roll(x, x.shape[1] - 8, 1)
    behind = pltpu.roll(x, 8, 1)
    swapped = jnp.where(lane < 8, -ahead, behind) * sign
    return x * cosine + swapped * sine


def rotation_table(angles_table):
    tokens = angles_table.shape[1]
    rest = jnp.zeros((112, tokens), WIDE)
    x = jnp.concatenate([angles_table, rest], axis=0).T
    lane = lane_of(x.shape)
    c = jnp.where(lane < 8, x, 0.0)
    c = c + pltpu.roll(c, 8, 1)
    c = c + pltpu.roll(c, HDIM, 1) + jnp.where(lax.rem(lane, HDIM) < 16, 0.0, 1.0)
    s = jnp.where((lane >= 8) & (lane < 16), x, 0.0)
    s = s + pltpu.roll(s, 120, 1)
    s = s + pltpu.roll(s, HDIM, 1)
    return c, s


def project_kernel(
    arrive, place, tok, table, w, gain, shift, bias,
    normed, stats, x0, x1, x2, x3, cosine_out, sine_out, kept,
):
    rows = 64

    def norm_rows(i, carry):
        at = pl.ds(pl.multiple_of(i * rows, rows), rows)
        x = tok[at, :].astype(WIDE)
        mean = jnp.mean(x, axis=-1, keepdims=True)
        center = x - mean
        scale = lax.rsqrt(jnp.mean(center * center, axis=-1, keepdims=True) + 1e-05)
        normed[at, :] = (center * scale * gain[...] + shift[...]).astype(LOW)
        stats[at, :] = jnp.where(lane_of((rows, 128)) < HDIM, mean, scale)
        return carry

    lax.fori_loop(0, BLOCK // rows, norm_rows, 0)
    cosine, sine = rotation_table(table[...])
    cosine_out[...] = cosine
    sine_out[...] = sine
    arrive()
    mixed = [nn(normed[...], w[c]) + bias[c : c + 1, :] for c in range(3)]
    for pair in range(2):
        lanes = slice(pair * 128, pair * 128 + 128)
        q = turn(mixed[0][:, lanes], cosine, sine, 1.0) * 0.125
        k = turn(mixed[1][:, lanes], cosine, sine, 1.0)
        kv = exchange_halves(k, mixed[2][:, lanes])
        qq = exchange_halves(q[:HALF], q[HALF:])
        for one in range(2):
            kept[2 * pair + one, :BLOCK, :] = kv[one].astype(LOW)
            kept[2 * pair + one, BLOCK:, :] = qq[one].astype(LOW)
    for k, out in enumerate((x0, x1, x2, x3)):
        out[...] = kept[place[1] ^ k]


def padded_queries(q2):
    x = q2.astype(WIDE)
    front = lane_of(x.shape) < HDIM
    return (
        jnp.where(front, x, 0.0).astype(LOW),
        jnp.where(front, pltpu.roll(x, HDIM, 1), 0.0).astype(LOW),
    )


def padded_behind(d2):
    x = d2.astype(WIDE)
    front = lane_of(x.shape) < HDIM
    return (
        jnp.where(front, 0.0, pltpu.roll(x, HDIM, 1)).astype(LOW),
        jnp.where(front, 0.0, x).astype(LOW),
    )


def allowed_keys(key_block, first_query, begin):
    shape = (BLOCK, begin.shape[1])
    key_at = key_block * BLOCK + lax.broadcasted_iota(jnp.int32, shape, 0)
    query_at = first_query + lax.broadcasted_iota(jnp.int32, shape, 1)
    return (key_at <= query_at) & (key_at >= begin)


def key_blocks(place, rels, t):
    return [4 * t + (place[0] ^ rel) for rel in rels], place[1] ^ t


def forward_kernel(rels, first, last, *refs):
    place, kv0, kv1, q0, q1, q2, q3, begin = refs[:8]
    if first:
        acc_out, peak_out, kvt, queries, kept_q = refs[8:]
    else:
        acc_in, peak_in, o0, o1, o2, o3, out_t, total, kvt, queries, kept_q, kept_o = refs[8:]
        acc_out, peak_out = out_t, total
    me = place[1]
    front = lane_of((BLOCK, 128)) < HDIM
    for k, q in enumerate((q0, q1, q2, q3)):
        kept_q[me ^ k] = q[...]
    for i, kv in enumerate((kv0, kv1)):
        for t in range(4):
            kvt[i, t] = jnp.where(front, 1.0, kv[t].astype(WIDE)).T.astype(LOW)

    def one_query_block(j, carry):
        first_query = (4 * j + place[0]) * BLOCK
        queries[:HALF, :], queries[HALF:, :] = padded_queries(kept_q[j])
        if first:
            peak_out[j] = jnp.full((8, BLOCK), -1e30, WIDE)
            acc_out[j] = jnp.zeros((128, BLOCK), WIDE)
        else:
            peak_out[j] = peak_in[j]
            acc_out[j] = acc_in[j]

        def two_blocks(t, carry):
            blocks, at = key_blocks(place, rels, t)
            scores = []
            for i, kv in enumerate((kv0, kv1)):
                ok = allowed_keys(blocks[i], first_query, begin[j, :1])
                scores.append(jnp.where(ok, nt(kv[at], queries[...]), -1e30))
            old = peak_out[j, :1]
            new = old
            for one in scores:
                new = jnp.maximum(new, jnp.max(one, axis=0, keepdims=True))
            done = acc_out[j] * jnp.exp(old - new)
            for i in range(2):
                done += nn(kvt[i, at], jnp.exp(scores[i] - new).astype(LOW))
            acc_out[j] = done
            peak_out[j, :1] = new
            return carry

        lax.fori_loop(0, j + 1, two_blocks, 0)
        if last:
            weight_sum = acc_out[j, :1]
            done = acc_out[j] / weight_sum
            out_t[j] = done
            total[j, :1] = peak_out[j, :1] + jnp.log(weight_sum)
            rows = done.T
            x, y = rows[:HALF], rows[HALF:]
            kept_o[j] = jnp.where(lane_of(x.shape) < HDIM, pltpu.roll(x, HDIM, 1), y).astype(LOW)
        return carry

    lax.fori_loop(0, 4, one_query_block, 0)
    if last:
        for k, out in enumerate((o0, o1, o2, o3)):
            out[...] = kept_o[me ^ k]


def backward_kernel(rels, first, *refs):
    place, kv0, kv1, q0, q1, q2, q3, d0, d1, d2, d3, out_t, total, begin = refs[:14]
    if first:
        acc, keep, send, kvt, queries, grads, dot_rows, dkv, kept_q, kept_d = refs[14:]
    else:
        (
            acc_in, g0, g1, g2, g3, keep, send,
            kvt, queries, grads, dot_rows, dkv, kept_q, kept_d, acc, kept_g,
        ) = refs[14:]
    me = place[1]
    for k in range(4):
        kept_q[me ^ k] = (q0, q1, q2, q3)[k][...]
        kept_d[me ^ k] = (d0, d1, d2, d3)[k][...]
    for i, kv in enumerate((kv0, kv1)):
        for t in range(4):
            kvt[i, t] = kv[t].astype(WIDE).T.astype(LOW)
    dkv[...] = jnp.zeros(dkv.shape, WIDE)

    def one_query_block(j, carry):
        first_query = (4 * j + place[0]) * BLOCK
        queries[:HALF, :], queries[HALF:, :] = padded_queries(kept_q[j])
        grads[:HALF, :], grads[HALF:, :] = padded_behind(kept_d[j])
        dot_rows[...] = jnp.sum(grads[...].astype(WIDE).T * out_t[j], axis=0, keepdims=True)
        acc[j] = jnp.zeros((128, BLOCK), WIDE) if first else acc_in[j]

        def two_blocks(t, carry):
            blocks, at = key_blocks(place, rels, t)
            for i, kv in enumerate((kv0, kv1)):
                term = 0.0
                for half in range(2):
                    some = slice(half * HALF, half * HALF + HALF)
                    ok = allowed_keys(blocks[i], first_query + half * HALF, begin[j, :1, some])
                    scores = nt(kv[at], queries[some, :])
                    probs = jnp.where(ok, jnp.exp(scores - total[j, :1, some]), 0.0)
                    grad_probs = nt(kv[at], grads[some, :])
                    grad_scores = (probs * (grad_probs - dot_rows[:, some])).astype(LOW)
                    term += nn(grad_scores, queries[some, :]) + nn(probs.astype(LOW), grads[some, :])
                    acc[j, :, some] += nn(kvt[i, at], grad_scores)
                dkv[i, at] += term
            return carry

        lax.fori_loop(0, j + 1, two_blocks, 0)
        if not first:
            rows = acc[j].T
            x, y = rows[:HALF], rows[HALF:]
            kept_g[j] = jnp.where(lane_of(x.shape) < HDIM, x, pltpu.roll(y, HDIM, 1)).astype(LOW)
        return carry

    lax.fori_loop(0, 4, one_query_block, 0)
    if not first:
        for k, out in enumerate((g0, g1, g2, g3)):
            out[...] = kept_g[me ^ k]
    for t in range(4):
        keep[t] = dkv[0, t].astype(LOW)
        send[t] = dkv[1, t].astype(LOW)


def branch_kernel(arrive, place, h0, h1, h2, h3, w, attended, *refs):
    outs, (partial, kept) = refs[:8], refs[8:]
    for k, h in enumerate((h0, h1, h2, h3)):
        kept[place[1] ^ k] = h[...]
    for pair in range(2):
        lanes = slice(pair * 128, pair * 128 + 128)
        x, y = exchange_halves(kept[2 * pair].astype(WIDE), kept[2 * pair + 1].astype(WIDE))
        attended[:HALF, lanes] = x.astype(LOW)
        attended[HALF:, lanes] = y.astype(LOW)
    arrive()
    for n in range(4):
        at = slice(n * 512, n * 512 + 512)
        partial[:, at] = nn(attended[...], w[:, at]).astype(LOW)
    deal_rows(place, partial, outs)


def grad_attended_kernel(place, grad, w, d0, d1, d2, d3, kept):
    g = nt(grad[...], w[...])
    for pair in range(2):
        lanes = slice(pair * 128, pair * 128 + 128)
        both = exchange_halves(g[:HALF, lanes], g[HALF:, lanes])
        for one in range(2):
            kept[2 * pair + one] = both[one].astype(LOW)
    for k, out in enumerate((d0, d1, d2, d3)):
        out[...] = kept[place[1] ^ k]


def join_kernel(keep, received, far, g0, g1, g2, g3, x0, x1, x2, x3):
    for k in range(4):
        total = keep[k].astype(WIDE) + received[k].astype(WIDE) + far[k].astype(WIDE)
        out = (x0, x1, x2, x3)[k]
        out[:BLOCK, :] = total.astype(LOW)
        out[BLOCK:, :] = (g0, g1, g2, g3)[k][...]


def grad_project_kernel(
    arrive, place, x0, x1, x2, x3, cosine, sine, tok, stats, w,
    grad_mixed, partial, gain_sum, shift_sum, bias_sum, parts, kept,
):
    for k, x in enumerate((x0, x1, x2, x3)):
        parts[place[1] ^ k] = x[:BLOCK, :]
        kept[place[1] ^ k] = x[BLOCK:, :]
    for pair in range(2):
        lanes = slice(pair * 128, pair * 128 + 128)
        k, v = exchange_halves(parts[2 * pair].astype(WIDE), parts[2 * pair + 1].astype(WIDE))
        q = exchange_halves(kept[2 * pair].astype(WIDE), kept[2 * pair + 1].astype(WIDE))
        q = jnp.concatenate(q, axis=0)
        q = turn(q, cosine[...], sine[...], -1.0) * 0.125
        k = turn(k, cosine[...], sine[...], -1.0)
        for c, part in enumerate((q, k, v)):
            start = c * 256 + pair * 128
            low = part.astype(LOW)
            grad_mixed[:, start : start + 128] = low
            bias_sum[c : c + 1, lanes] = jnp.sum(low.astype(WIDE), axis=0, keepdims=True)
    arrive()
    mean, scale = stats[:, 0:1], stats[:, 64:65]
    for n in range(4):
        at = slice(n * 512, n * 512 + 512)
        total = nt(grad_mixed[:, :256], w[0, at, :])
        total += nt(grad_mixed[:, 256:512], w[1, at, :])
        total += nt(grad_mixed[:, 512:], w[2, at, :])
        partial[:, at] = total.astype(LOW)
        normal = (tok[:, at].astype(WIDE) - mean) * scale
        gain_sum[:, at] = jnp.sum(total * normal, axis=0, keepdims=True)
        shift_sum[:, at] = jnp.sum(total, axis=0, keepdims=True)


def hidden_gradient_kernel(cot, w, grad_hidden):
    grad_hidden[...] = nt(cot[...], w[...])


def feed_kernel(arrive, place, second, w_gate, w_up, grad_hidden, hidden, grad_gate, grad_up, partial):
    gate = nt(second[...], w_gate[0])
    arrive()
    up = nt(second[...], w_up[0])
    sigmoid = 1.0 / (1.0 + jnp.exp(-gate))
    activated = gate * sigmoid
    hidden[...] = (activated * up).astype(LOW)
    grad = grad_hidden[...]
    grad_up[...] = (grad * activated).astype(LOW)
    grad_gate[...] = (grad * up * sigmoid * (1.0 + gate * (1.0 - sigmoid))).astype(LOW)
    for n in range(4):
        at = slice(n * 512, n * 512 + 512)
        partial[:, at] = (nn(grad_gate[...], w_gate[0, :, at]) + nn(grad_up[...], w_up[0, :, at])).astype(LOW)


def for_rows(work):
    rows = 16

    def one(i, carry):
        work(pl.ds(pl.multiple_of(i * rows, rows), rows))
        return carry

    lax.fori_loop(0, 64 // rows, one, 0)


def summed(parts, at):
    one = [parts[k][at, :] for k in range(8)] if isinstance(parts, tuple) else [parts[k, at, :] for k in range(8)]
    total = one[0].astype(WIDE)
    for x in one[1:]:
        total += x.astype(WIDE)
    return total


def second_norm_kernel(*refs):
    parts, (tok, gain, shift, low, middle, normal, stats) = refs[:8], refs[8:]

    def work(at):
        x = tok[at, :].astype(WIDE) + summed(parts, at)
        center = x - jnp.mean(x, axis=-1, keepdims=True)
        scale = lax.rsqrt(jnp.mean(center * center, axis=-1, keepdims=True) + 1e-05)
        rows = center * scale
        low[at, :] = (rows * gain[...] + shift[...]).astype(LOW)
        middle[at, :] = x
        normal[at, :] = rows
        stats[at, :] = jnp.broadcast_to(scale, (scale.shape[0], 128))

    for_rows(work)


def norm_gradient(grad, rows, scale, gain):
    scaled = grad * gain
    return scale * (
        scaled
        - jnp.mean(scaled, axis=-1, keepdims=True)
        - rows * jnp.mean(scaled * rows, axis=-1, keepdims=True)
    )


def second_gradient_kernel(parts, cot, normal, stats, gain, copies, grad_middle, sums):
    sums[...] = jnp.zeros(sums.shape, WIDE)

    def work(at):
        grad, rows = summed(parts, at), normal[at, :]
        done = cot[at, :].astype(WIDE) + norm_gradient(grad, rows, stats[at, 0:1], gain[...])
        low = done.astype(LOW)
        for k in range(8):
            copies[k, at, :] = low
        grad_middle[at, :] = done
        sums[0:1, :] += jnp.sum(grad * rows, axis=0, keepdims=True)
        sums[1:2, :] += jnp.sum(grad, axis=0, keepdims=True)

    for_rows(work)


def feed_sum_kernel(place, parts, middle, out):
    rows = 16
    mine = place[3]

    def one(i, carry):
        at = pl.ds(pl.multiple_of(i * rows, rows), rows)
        total = parts[0, at, :].astype(WIDE)
        for k in range(1, 4):
            total += parts[k, at, :].astype(WIDE)
        here = i * rows - mine * 64
        own = pl.ds(pl.multiple_of(jnp.clip(here, 0, 64 - rows), rows), rows)
        inside = (here >= 0) & (here < 64)
        out[at, :] = (total + jnp.where(inside, middle[own, :], 0.0)).astype(LOW)
        return carry

    lax.fori_loop(0, 128 // rows, one, 0)


def layer_out_kernel(a, b, copies):
    rows = 16

    def one(i, carry):
        at = pl.ds(pl.multiple_of(i * rows, rows), rows)
        low = (a[at, :].astype(WIDE) + b[at, :].astype(WIDE)).astype(LOW)
        for k in range(4):
            copies[k, at, :] = low
        return carry

    lax.fori_loop(0, 128 // rows, one, 0)


def first_gradient_kernel(parts, grad_middle, tok, stats, vectors, gain, low):
    def work(at):
        mean, scale = stats[at, 0:1], stats[at, 64:65]
        rows = (tok[at, :].astype(WIDE) - mean) * scale
        done = norm_gradient(summed(parts, at), rows, scale, gain[...])
        low[at, :2048] = (grad_middle[at, :] + done).astype(LOW)
        low[at, 2048:] = vectors[at, :].astype(LOW)

    for_rows(work)


def last_kernel(place, gathered, out, total):
    out[...] = gathered[:, :2048]
    done = gathered[:64, 2048:].astype(WIDE)
    for k in range(1, 8):
        done += gathered[k * 64 : k * 64 + 64, 2048:].astype(WIDE)
    total[...] = done


def weight_kernel(widths, sources, arrive, place, *refs):
    count = max(max(pair) for pair in sources) + 1
    inputs = refs[:count]
    mine, theirs, turned = refs[count:]
    first_core = place[2] == 0
    start = 0
    for n, ((left, right), width) in enumerate(zip(sources, widths)):
        if n == 1:
            arrive()
        left, right = inputs[left], inputs[right]
        turned[:width, :] = left[...].astype(WIDE).T.astype(LOW)

        def one(n, carry, start=start, right=right, width=width):
            columns = right[:, pl.ds(pl.multiple_of(n * 256, 256), 256)]
            both = nn(turned[:width, :], columns)
            first, second = both[:, :128], both[:, 128:]
            at = pl.ds(start, width)
            mine[n, at, :] = jnp.where(first_core, first, second).astype(LOW)
            theirs[n, at, :] = jnp.where(first_core, second, first).astype(LOW)
            return carry

        lax.fori_loop(0, 8, one, 0, unroll=4)
        start += width


def weight_grads(pairs, place):
    inputs, sources = [], []
    for pair in pairs:
        for a in pair:
            if not any(a is b for b in inputs):
                inputs.append(a)
        sources.append(tuple(next(k for k, b in enumerate(inputs) if b is a) for a in pair))
    widths = tuple(a.shape[1] for a, _ in pairs)
    out = jax.ShapeDtypeStruct((8, sum(widths), 128), LOW)
    return kernel_call(
        functools.partial(weight_kernel, widths, sources),
        (out, out),
        inputs,
        scalars=(place,),
        scratch=(pltpu.VMEM((max(widths), BLOCK), LOW),),
        late=len(inputs) - 2,
        quick=True,
    )


def swapped(x, axis):
    return lax.ppermute(x, axis, [(0, 1), (1, 0)])


def across(pieces):
    moved = [
        lax.ppermute(pieces[k], SPREAD, [(i, i ^ k) for i in range(4)]) for k in range(1, 4)
    ]
    return (pieces[0], *moved)


def z_parts_kernel(place, mine, received, *refs):
    outs, (held_a, held_b, done, came, went) = refs[:4], refs[4:]
    z = place[0]
    order = [(k, xh) for k in (1, 3, 2, 0) for xh in range(2)]
    moves = []
    for n, (k, xh) in enumerate(order):
        at = xh * 4 + lax.rem(z + k, 4)
        moves.append(
            (
                pltpu.make_async_copy(mine.at[at], held_a.at[n], came.at[2 * n]),
                pltpu.make_async_copy(received.at[at], held_b.at[n], came.at[2 * n + 1]),
                pltpu.make_async_copy(done.at[n], outs[k].at[xh], went.at[n]),
            )
        )
    for a, b, _ in moves:
        a.start()
        b.start()
    for n, (a, b, out) in enumerate(moves):
        a.wait()
        b.wait()
        done[n] = (held_a[n].astype(WIDE) + held_b[n].astype(WIDE)).astype(LOW)
        out.start()
    for _, _, out in moves:
        out.wait()


def z_parts(mine, received):
    rows = mine.shape[1]
    hbm = pl.BlockSpec(memory_space=pltpu.HBM)
    held = pltpu.VMEM((8, rows, 128), LOW)
    return pl.pallas_call(
        z_parts_kernel,
        in_specs=[pl.BlockSpec(memory_space=pltpu.SMEM), hbm, hbm],
        out_specs=[hbm] * 4,
        out_shape=[pltpu.HBM((2, rows, 128), LOW)] * 4,
        scratch_shapes=[
            held,
            held,
            held,
            pltpu.SemaphoreType.DMA((16,)),
            pltpu.SemaphoreType.DMA((8,)),
        ],
        compiler_params=pltpu.CompilerParams(vmem_limit_bytes=24 * 1024 * 1024),
        cost_estimate=pl.CostEstimate(flops=0, bytes_accessed=0, transcendentals=0),
    )(
        lax.axis_index(Z).reshape(1),
        *[pltpu.with_memory_space_constraint(a, pltpu.HBM) for a in (mine, received)],
    )


def settled_kernel(x, out, held, came, went):
    rows = x.shape[1]
    moves = []
    for k in range(x.shape[0]):
        at = pl.ds(k * rows, rows)
        moves.append(
            (
                pltpu.make_async_copy(x.at[k], held.at[k], came.at[k]),
                pltpu.make_async_copy(held.at[k, :, pl.ds(0, 2048)], out.at[at], went.at[k]),
            )
        )
    for come, _ in moves:
        come.start()
    for come, go in moves:
        come.wait()
        go.start()
    for _, go in moves:
        go.wait()


def settled(x):
    hbm = pl.BlockSpec(memory_space=pltpu.HBM)
    parts, rows = x.shape[:2]
    return pl.pallas_call(
        settled_kernel,
        out_shape=pltpu.HBM((parts * rows, 2048), x.dtype),
        in_specs=[pl.BlockSpec(memory_space=pl.ANY)],
        out_specs=hbm,
        scratch_shapes=[
            pltpu.VMEM(x.shape, x.dtype),
            pltpu.SemaphoreType.DMA((parts,)),
            pltpu.SemaphoreType.DMA((parts,)),
        ],
        compiler_params=pltpu.CompilerParams(vmem_limit_bytes=8 * 1024 * 1024),
        cost_estimate=pl.CostEstimate(flops=0, bytes_accessed=0, transcendentals=0),
    )(x)


def z_permute(part, distance):
    return lax.ppermute(part, Z, [(i, (i + distance) % 4) for i in range(4)])


def xh_halves(moved):
    xh = lax.axis_index("xh")

    def added(at):
        return sum(lax.dynamic_index_in_dim(x, at, 0, False).astype(WIDE) for x in moved)

    return added(xh), added(1 - xh).astype(LOW)


def dealt(x, axis):
    return lax.all_to_all(x, axis, split_axis=0, concat_axis=0, tiled=True)


def tp_parts(partial):
    return dealt(partial.reshape(8, -1, partial.shape[1]), TP)


def y_moved(x, distance):
    return lax.ppermute(x, "y", [(i, (i + distance) % 4) for i in range(4)])


def scattered(pieces):
    moved = {
        k: lax.ppermute(pieces[k], TP, [(i, i ^ k) for i in range(8)]) for k in (5, 4, 7, 3, 6, 2, 1)
    }
    return [pieces[0], *[moved[k] for k in range(1, 8)]]


def gathered(share):
    across_x = swapped(share, "xl")
    back, ahead, far = (y_moved(share, k) for k in (1, 3, 2))
    return [
        share, across_x, back, ahead, far,
        y_moved(across_x, 1), y_moved(across_x, 3), swapped(far, "xl"),
    ]


def summed_by_pairs(x, pairs):
    for axis, size, distance in pairs:
        x = x + lax.ppermute(x, axis, [(i, i ^ distance) for i in range(size)])
    return x


def shape_of(*dims, kind=LOW):
    return jax.ShapeDtypeStruct(dims, kind)


def body(
    tokens, cotangent, segment_ids, first_gain, first_shift, second_gain, second_shift,
    w_qkv, qkv_bias, w_out, w_gate_up, w_down,
):
    ctx = lax.axis_index(CTX)
    tp = lax.axis_index(TP)
    group = lax.axis_index(("zl", "core"))
    place = jnp.stack(
        [group, lax.axis_index(SPREAD), lax.axis_index("core"), lax.axis_index("xl"), lax.axis_index("y")]
    )
    tied = lax.optimization_barrier

    def my_share(array):
        return lax.dynamic_slice_in_dim(array, tp * 64, 64)

    labels = jnp.arange(DOCS, dtype=jnp.int32)
    starts = jnp.sum((segment_ids[None, :] < labels[:, None]).astype(jnp.int32), axis=1)
    begins = jnp.sum(
        jnp.where(segment_ids[None, :] == labels[:, None], starts[:, None], 0), axis=0
    )
    begin = lax.dynamic_index_in_dim(begins.reshape(4, 4, 1, BLOCK), group, 1, False)
    begin = jnp.broadcast_to(begin, (4, 8, BLOCK))
    own = lax.dynamic_slice_in_dim(begins, ctx * BLOCK, BLOCK)
    places = ctx * BLOCK + jnp.arange(BLOCK, dtype=jnp.int32) - own
    frequency = 10000.0 ** (-jnp.arange(8, dtype=WIDE) / 8.0)
    angles = frequency[:, None] * places.astype(WIDE)[None, :]
    table = jnp.concatenate([jnp.cos(angles), jnp.sin(angles)], axis=0)

    w3 = jnp.transpose(w_qkv, (1, 0, 2))
    w2 = jnp.transpose(w_gate_up, (1, 2, 0))
    quarter, piece = shape_of(HALF, 128), shape_of(BLOCK + HALF, 128)
    wide_block = shape_of(BLOCK, 128, kind=WIDE)
    four = pltpu.VMEM((4, HALF, 128), LOW)
    normed_low, stats1, *packed, cosine, sine = kernel_call(
        project_kernel,
        (shape_of(BLOCK, 2048), wide_block, *[piece] * 4, wide_block, wide_block),
        (tokens, table, w3),
        small=(first_gain[None], first_shift[None], qkv_bias),
        scalars=(place,),
        scratch=(pltpu.VMEM((4, BLOCK + HALF, 128), LOW),),
        late=1,
        flops=2 * 512 * 2048 * 768,
    )
    (grad_hidden,) = kernel_call(
        hidden_gradient_kernel,
        (shape_of(BLOCK, 704, kind=WIDE),),
        (cotangent, w_down),
        flops=2 * 512 * 2048 * 704,
    )
    *packed, grad_hidden, tok_share, cot_share = tied(
        (*across(packed), grad_hidden, my_share(tokens), my_share(cotangent))
    )
    kv = jnp.stack([x[:BLOCK] for x in packed])
    queries = [(x, BLOCK, HALF) for x in packed]
    kv_c = swapped(kv, "core")
    state = (shape_of(4, 128, BLOCK, kind=WIDE), shape_of(4, 8, BLOCK, kind=WIDE))
    acc, peak = kernel_call(
        functools.partial(forward_kernel, (0, 1), True, False),
        state,
        (kv, kv_c, *queries, begin),
        scalars=(place,),
        scratch=(pltpu.VMEM((2, 4, 128, BLOCK), LOW), pltpu.VMEM((BLOCK, 128), LOW), four),
        flops=20 * 4 * BLOCK * BLOCK * 128,
        exps=20 * BLOCK * BLOCK,
        mib=24,
    )
    acc, peak, kv_z = tied((acc, peak, swapped(kv, "zl")))
    kv_zc = swapped(kv_z, "core")
    *heads, out_t, total = kernel_call(
        functools.partial(forward_kernel, (2, 3), False, True),
        (*[quarter] * 4, *state),
        (kv_z, kv_zc, *queries, begin, acc, peak),
        scalars=(place,),
        scratch=(pltpu.VMEM((2, 4, 128, BLOCK), LOW), pltpu.VMEM((BLOCK, 128), LOW), four, four),
        flops=20 * 4 * BLOCK * BLOCK * 128,
        exps=20 * BLOCK * BLOCK,
        mib=24,
    )
    heads = across(heads)
    share, low_share = shape_of(64, 2048, kind=WIDE), shape_of(64, 2048)
    attended_low, *partial_branch = kernel_call(
        branch_kernel,
        (shape_of(BLOCK, 256), *[low_share] * 8),
        (*heads, w_out),
        scalars=(place,),
        scratch=(pltpu.VMEM((BLOCK, 2048), LOW), four),
        late=1,
        flops=2 * 512 * 256 * 2048,
    )
    branch_parts = scattered(partial_branch)
    second_share, middle, second_rows, stats2 = kernel_call(
        second_norm_kernel,
        (low_share, share, share, shape_of(64, 128, kind=WIDE)),
        (*branch_parts, tok_share),
        small=(second_gain[None], second_shift[None]),
    )
    second_low = gathered(second_share)
    strip = shape_of(BLOCK, 704)
    hidden_low, grad_gate, grad_up, partial_second = kernel_call(
        feed_kernel,
        (strip, strip, strip, shape_of(BLOCK, 2048)),
        (second_low, (w2, 0, 1), (w2, 1, 1), grad_hidden),
        scalars=(place,),
        late=2,
        flops=8 * 512 * 2048 * 704,
        mib=24,
    )
    second_parts = tp_parts(partial_second)

    feed_mine, feed_theirs = weight_grads(
        ((grad_gate, second_low), (grad_up, second_low), (hidden_low, cotangent)), place
    )
    second_parts, feed_mine, feed_theirs = tied((second_parts, feed_mine, feed_theirs))
    copies, grad_middle, second_sums = kernel_call(
        second_gradient_kernel,
        (shape_of(8, 64, 2048), share),
        (second_parts, cot_share, second_rows, stats2),
        moved=1,
        small=(second_gain[None],),
        small_outs=(shape_of(2, 2048, kind=WIDE),),
    )
    grad_branch = dealt(copies, TP).reshape(BLOCK, 2048)
    partial_feed = jnp.dot(hidden_low, w_down, preferred_element_type=WIDE).astype(LOW)
    grad_branch, partial_feed = tied((grad_branch, partial_feed))
    feed_z = z_parts(feed_mine, swapped(feed_theirs, "core"))
    feed_1, feed_3 = z_permute(feed_z[1], 1), z_permute(feed_z[3], 3)
    grads = kernel_call(
        grad_attended_kernel,
        (*[quarter] * 4,),
        (grad_branch, w_out),
        moved=1,
        scalars=(place,),
        scratch=(four,),
        flops=2 * 512 * 256 * 2048,
    )
    feed_1, feed_3, partial_feed, *grads = tied((feed_1, feed_3, partial_feed, *grads))
    feed_parts = dealt(partial_feed.reshape(4, 128, 2048), "y")
    *grads, feed_2 = tied((*across(grads), feed_z[2]))
    feed_2 = z_permute(feed_2, 2)
    scratch = (
        pltpu.VMEM((2, 4, 128, BLOCK), LOW),
        pltpu.VMEM((BLOCK, 128), LOW),
        pltpu.VMEM((BLOCK, 128), LOW),
        pltpu.VMEM((1, BLOCK), WIDE),
        pltpu.VMEM((2, 4, BLOCK, 128), WIDE),
        four,
        four,
    )
    blocks = shape_of(4, BLOCK, 128)
    acc, keep1, send1 = kernel_call(
        functools.partial(backward_kernel, (2, 3), True),
        (state[0], blocks, blocks),
        (kv_z, kv_zc, *queries, *grads, out_t, total, begin),
        scalars=(place,),
        scratch=scratch,
        flops=20 * 10 * BLOCK * BLOCK * 128,
        exps=20 * BLOCK * BLOCK,
        mib=28,
    )
    acc, send1, feed_parts, feed_2 = tied((acc, send1, feed_parts, feed_2))
    (feed_half,) = kernel_call(
        feed_sum_kernel,
        (shape_of(128, 2048),),
        (feed_parts, middle),
        scalars=(place,),
        moved=1,
    )
    far = (keep1.astype(WIDE) + swapped(send1, "core").astype(WIDE)).astype(LOW)
    feed_keep, feed_send = xh_halves([feed_z[0], feed_1, feed_2, feed_3])
    acc, far, feed_half, feed_send = tied((acc, far, feed_half, feed_send))
    near = kernel_call(
        functools.partial(backward_kernel, (0, 1), False),
        (*[quarter] * 4, blocks, blocks),
        (kv, kv_c, *queries, *grads, out_t, total, begin, acc),
        scalars=(place,),
        scratch=(*scratch, pltpu.VMEM((4, 128, BLOCK), WIDE), four),
        flops=20 * 10 * BLOCK * BLOCK * 128,
        exps=20 * BLOCK * BLOCK,
        mib=28,
    )
    *near, far, feed_other, feed_received = tied(
        (*near, swapped(far, "zl"), swapped(feed_half, "xl"), swapped(feed_send, "xh"))
    )
    *grad_queries, keep0, send0 = near
    pieces = kernel_call(
        join_kernel,
        (*[piece] * 4,),
        (keep0, swapped(send0, "core"), far, *grad_queries),
    )
    (copies4,) = kernel_call(layer_out_kernel, (shape_of(4, 128, 2048),), (feed_half, feed_other))
    *pieces, copies4 = tied((*pieces, copies4))
    pieces = across(pieces)
    layer_out = dealt(copies4, "y")
    grad_mixed, partial_normed, gain_sum, shift_sum, bias_sum = kernel_call(
        grad_project_kernel,
        (shape_of(BLOCK, 768), shape_of(BLOCK, 2048)),
        (*pieces, cosine, sine, tokens, stats1, w3),
        small_outs=(
            shape_of(1, 2048, kind=WIDE),
            shape_of(1, 2048, kind=WIDE),
            shape_of(3, 256, kind=WIDE),
        ),
        scalars=(place,),
        scratch=(pltpu.VMEM((4, BLOCK, 128), LOW), four),
        late=3,
        flops=2 * 512 * 2048 * 768,
    )
    partial_normed, layer_out = tied((partial_normed, layer_out))
    layer_out = settled(layer_out)
    normed_parts = tp_parts(partial_normed)

    rest_mine, rest_theirs = weight_grads(
        ((grad_mixed, normed_low), (attended_low, grad_branch)), place
    )
    rest_z = z_parts(rest_mine, swapped(rest_theirs, "core"))
    vectors = jnp.concatenate([gain_sum, shift_sum, second_sums], axis=0).reshape(32, 256)
    vectors = jnp.concatenate([vectors, bias_sum], axis=0)
    vectors = summed_by_pairs(vectors, (("core", 2, 1), ("zl", 2, 1), ("zh", 2, 1)))
    vectors, *rest_z = tied((vectors, *rest_z))
    vectors = summed_by_pairs(vectors, (("xh", 2, 1),))
    rest_1, rest_3 = z_permute(rest_z[1], 1), z_permute(rest_z[3], 3)
    normed_parts, vectors = tied((normed_parts, vectors))
    bias_grad = vectors[32:]
    (last_share,) = kernel_call(
        first_gradient_kernel,
        (shape_of(64, 2048 + 128),),
        (normed_parts, grad_middle, tok_share, my_share(stats1), vectors[:32].reshape(64, 128)),
        moved=1,
        small=(first_gain[None],),
    )
    last_share, rest_1, rest_3, rest_2 = tied((last_share, rest_1, rest_3, rest_z[2]))
    grad_tokens, vectors = kernel_call(
        last_kernel,
        (shape_of(BLOCK, 2048),),
        (gathered(last_share),),
        scalars=(place,),
        small_outs=(shape_of(64, 128, kind=WIDE),),
        quick=True,
    )
    vectors = vectors.reshape(4, 2048)
    rest_z = (rest_z[0], rest_1, z_permute(rest_2, 2), rest_3)
    rest_keep, rest_send = xh_halves(rest_z)
    rest_received, grad_tokens, vectors = tied((swapped(rest_send, "xh"), grad_tokens, vectors))
    rest_w = rest_keep + rest_received.astype(WIDE)
    feed_w = feed_keep + feed_received.astype(WIDE)
    return (
        layer_out,
        grad_tokens,
        vectors[0],
        vectors[1],
        vectors[2],
        vectors[3],
        jnp.transpose(rest_w[:768].reshape(3, 256, 128), (2, 0, 1)),
        bias_grad,
        rest_w[768:],
        jnp.transpose(feed_w[:1408].reshape(2, 704, 128), (2, 0, 1)),
        feed_w[1408:],
    )


def solution(mesh):
    fine = Mesh(
        mesh.devices.reshape(2, 2, 2, 2, 4, 2), ("xh", "zh", "zl", "core", "y", "xl")
    )
    rows = P(CTX, None)
    return jax.shard_map(
        body,
        mesh=fine,
        in_specs=(
            rows, rows, P(), P(), P(), P(), P(),
            P(None, None, TP), P(None, TP), P(TP, None), P(None, None, TP), P(TP, None),
        ),
        out_specs=(
            rows, rows, P(), P(), P(), P(),
            P(CTX, None, TP), P(None, TP), P(TP, CTX), P(CTX, None, TP), P(TP, CTX),
        ),
        check_vma=False,
    )
```

```python
import functools

import jax
import jax.numpy as jnp
from jax import lax
from jax.experimental import pallas as pl
from jax.experimental.pallas import tpu as pltpu
from jax.sharding import Mesh
from jax.sharding import PartitionSpec as P

HDIM = 64
DOCS = 3
BLOCK = 512
HALF = 256
LOW = jnp.bfloat16
WIDE = jnp.float32
CTX = ("xh", "zh", "zl", "core")
TP = ("y", "xl")
SPREAD = ("xh", "zh")
Z = ("zh", "zl")


def size_of(a):
    return a.size * jnp.dtype(a.dtype).itemsize


def gathered_order(place):
    x, y = place[3], place[4]
    row = [lax.rem(y + k, 4) * 2 for k in range(4)]
    other = 1 - x
    return [
        row[0] + x, row[0] + other,
        row[3] + x, row[1] + x, row[2] + x,
        row[3] + other, row[1] + other, row[2] + other,
    ]


def deal_rows(place, rows, outs):
    tp = place[4] * 2 + place[3]
    for k, out in enumerate(outs):
        out[...] = rows[pl.ds(pl.multiple_of((tp ^ k) * 64, 64), 64), :]


def kernel_call(
    body, outs, inputs, *, small=(), small_outs=(), scalars=(), scratch=(), late=0, flops=0, exps=0, mib=12, quick=False, moved=0
):
    inputs = [a if isinstance(a, (tuple, list)) else (a, 0, a.shape[0]) for a in inputs]
    flat = [x for a in inputs for x in (a if isinstance(a, list) else a[:1])]
    counts = [len(x) for x in (scalars, flat, small, outs, small_outs, inputs, outs)]

    def run(*refs):
        groups, at = [], 0
        for n in counts:
            groups.append(refs[at : at + n])
            at += n
        scalar_refs, far_in, near_in, far_out, near_out, held_in, held_out = groups
        arrived, left, *rest = refs[at:]
        pairs, ends = [], []
        for a, held in zip(inputs, held_in):
            if isinstance(a, list):
                rows = a[0].shape[0]
                for index in gathered_order(scalar_refs[0]):
                    pairs.append((None, held.at[pl.ds(pl.multiple_of(index * rows, rows), rows)]))
            else:
                pairs.append((pl.ds(a[1], a[2]), held))
            ends.append(len(pairs))
        moves = [
            pltpu.make_async_copy(x if part is None else x.at[part], held, arrived.at[k])
            for k, (x, (part, held)) in enumerate(zip(far_in, pairs))
        ]
        for move in moves:
            move.start()
        early = ends[len(inputs) - late - 1]
        for move in moves[:early]:
            move.wait()

        def arrive():
            for move in moves[early:]:
                move.wait()

        body(
            *([arrive] if late else []),
            *scalar_refs, *held_in, *near_in, *held_out, *near_out, *rest,
        )
        moves = [
            pltpu.make_async_copy(a, b, left.at[k]) for k, (a, b) in enumerate(zip(held_out, far_out))
        ]
        for move in moves:
            move.start()
        for move in moves:
            move.wait()

    vmem, hbm = pl.BlockSpec(memory_space=pltpu.VMEM), pl.BlockSpec(memory_space=pltpu.HBM)
    taken = [
        shape_of(8 * a[0].shape[0], a[0].shape[1], kind=a[0].dtype)
        if isinstance(a, list)
        else shape_of(a[2], *a[0].shape[1:], kind=a[0].dtype)
        for a in inputs
    ]
    held = [pltpu.VMEM(a.shape, a.dtype) for a in (*taken, *outs)]
    limit = sum(size_of(a) for a in (*taken, *outs, *small, *small_outs)) + mib * 1024 * 1024
    return pl.pallas_call(
        run,
        out_shape=(*[pltpu.HBM(a.shape, a.dtype) for a in outs], *small_outs),
        in_specs=[pl.BlockSpec(memory_space=pltpu.SMEM)] * len(scalars)
        + [pl.BlockSpec(memory_space=pl.ANY)] * moved
        + [hbm] * (len(flat) - moved)
        + [vmem] * len(small),
        out_specs=(*[hbm] * len(outs), *[vmem] * len(small_outs)),
        scratch_shapes=[
            *held,
            pltpu.SemaphoreType.DMA((len(flat),)),
            pltpu.SemaphoreType.DMA((max(1, len(outs)),)),
            *scratch,
        ],
        compiler_params=pltpu.CompilerParams(vmem_limit_bytes=limit),
        cost_estimate=pl.CostEstimate(
            flops=flops,
            bytes_accessed=0 if quick else sum(size_of(a) for a in (*taken, *outs)),
            transcendentals=exps,
        ),
    )(
        *scalars,
        *flat[:moved],
        *[pltpu.with_memory_space_constraint(a, pltpu.HBM) for a in flat[moved:]],
        *small,
    )


def lane_of(shape):
    return lax.broadcasted_iota(jnp.int32, shape, len(shape) - 1)


def exchange_halves(a, b):
    front = lane_of(a.shape) < HDIM
    return (
        jnp.where(front, a, pltpu.roll(b, HDIM, 1)),
        jnp.where(front, pltpu.roll(a, HDIM, 1), b),
    )


def nt(a, b):
    return lax.dot_general(a, b, (((1,), (1,)), ((), ())), preferred_element_type=WIDE)


def nn(a, b):
    return lax.dot_general(a, b, (((1,), (0,)), ((), ())), preferred_element_type=WIDE)


def turn(x, cosine, sine, sign):
    lane = lax.rem(lane_of(x.shape), HDIM)
    ahead = pltpu.roll(x, x.shape[1] - 8, 1)
    behind = pltpu.roll(x, 8, 1)
    swapped = jnp.where(lane < 8, -ahead, behind) * sign
    return x * cosine + swapped * sine


def rotation_table(angles_table):
    tokens = angles_table.shape[1]
    rest = jnp.zeros((112, tokens), WIDE)
    x = jnp.concatenate([angles_table, rest], axis=0).T
    lane = lane_of(x.shape)
    c = jnp.where(lane < 8, x, 0.0)
    c = c + pltpu.roll(c, 8, 1)
    c = c + pltpu.roll(c, HDIM, 1) + jnp.where(lax.rem(lane, HDIM) < 16, 0.0, 1.0)
    s = jnp.where((lane >= 8) & (lane < 16), x, 0.0)
    s = s + pltpu.roll(s, 120, 1)
    s = s + pltpu.roll(s, HDIM, 1)
    return c, s


def project_kernel(
    arrive, place, tok, table, w, gain, shift, bias,
    normed, stats, x0, x1, x2, x3, cosine_out, sine_out, kept,
):
    rows = 64

    def norm_rows(i, carry):
        at = pl.ds(pl.multiple_of(i * rows, rows), rows)
        x = tok[at, :].astype(WIDE)
        mean = jnp.mean(x, axis=-1, keepdims=True)
        center = x - mean
        scale = lax.rsqrt(jnp.mean(center * center, axis=-1, keepdims=True) + 1e-05)
        normed[at, :] = (center * scale * gain[...] + shift[...]).astype(LOW)
        stats[at, :] = jnp.where(lane_of((rows, 128)) < HDIM, mean, scale)
        return carry

    lax.fori_loop(0, BLOCK // rows, norm_rows, 0)
    cosine, sine = rotation_table(table[...])
    cosine_out[...] = cosine
    sine_out[...] = sine
    arrive()
    mixed = [nn(normed[...], w[c]) + bias[c : c + 1, :] for c in range(3)]
    for pair in range(2):
        lanes = slice(pair * 128, pair * 128 + 128)
        q = turn(mixed[0][:, lanes], cosine, sine, 1.0) * 0.125
        k = turn(mixed[1][:, lanes], cosine, sine, 1.0)
        kv = exchange_halves(k, mixed[2][:, lanes])
        qq = exchange_halves(q[:HALF], q[HALF:])
        for one in range(2):
            kept[2 * pair + one, :BLOCK, :] = kv[one].astype(LOW)
            kept[2 * pair + one, BLOCK:, :] = qq[one].astype(LOW)
    for k, out in enumerate((x0, x1, x2, x3)):
        out[...] = kept[place[1] ^ k]


def padded_queries(q2):
    x = q2.astype(WIDE)
    front = lane_of(x.shape) < HDIM
    return (
        jnp.where(front, x, 0.0).astype(LOW),
        jnp.where(front, pltpu.roll(x, HDIM, 1), 0.0).astype(LOW),
    )


def padded_behind(d2):
    x = d2.astype(WIDE)
    front = lane_of(x.shape) < HDIM
    return (
        jnp.where(front, 0.0, pltpu.roll(x, HDIM, 1)).astype(LOW),
        jnp.where(front, 0.0, x).astype(LOW),
    )


def allowed_keys(key_block, first_query, begin):
    shape = (BLOCK, begin.shape[1])
    key_at = key_block * BLOCK + lax.broadcasted_iota(jnp.int32, shape, 0)
    query_at = first_query + lax.broadcasted_iota(jnp.int32, shape, 1)
    return (key_at <= query_at) & (key_at >= begin)


def for_steps(count, work):
    def pair(i, carry):
        work([2 * i, 2 * i + 1])
        return carry

    lax.fori_loop(0, count // 2, pair, 0)

    @pl.when(lax.rem(count, 2) == 1)
    def _():
        work([count - 1])


def key_blocks(place, rels, t):
    return [4 * t + (place[0] ^ rel) for rel in rels], place[1] ^ t


def forward_kernel(rels, first, last, *refs):
    place, kv0, kv1, q0, q1, q2, q3, begin = refs[:8]
    if first:
        acc_out, peak_out, kvt, queries, kept_q = refs[8:]
    else:
        acc_in, peak_in, o0, o1, o2, o3, out_t, total, kvt, queries, kept_q, kept_o = refs[8:]
        acc_out, peak_out = out_t, total
    me = place[1]
    front = lane_of((BLOCK, 128)) < HDIM
    for k, q in enumerate((q0, q1, q2, q3)):
        kept_q[me ^ k] = q[...]
    for i, kv in enumerate((kv0, kv1)):
        for t in range(4):
            kvt[i, t] = jnp.where(front, 1.0, kv[t].astype(WIDE)).T.astype(LOW)

    def one_query_block(j, carry):
        first_query = (4 * j + place[0]) * BLOCK
        queries[:HALF, :], queries[HALF:, :] = padded_queries(kept_q[j])
        if first:
            peak_out[j] = jnp.full((8, BLOCK), -1e30, WIDE)
            acc_out[j] = jnp.zeros((128, BLOCK), WIDE)
        else:
            peak_out[j] = peak_in[j]
            acc_out[j] = acc_in[j]

        def some_blocks(steps):
            scores, sources = [], []
            for t in steps:
                blocks, at = key_blocks(place, rels, t)
                for i, kv in enumerate((kv0, kv1)):
                    ok = allowed_keys(blocks[i], first_query, begin[j, :1])
                    scores.append(jnp.where(ok, nt(kv[at], queries[...]), -1e30))
                    sources.append((i, at))
            old = peak_out[j, :1]
            new = old
            for one in scores:
                new = jnp.maximum(new, jnp.max(one, axis=0, keepdims=True))
            done = acc_out[j] * jnp.exp(old - new)
            for one, (i, at) in zip(scores, sources):
                done += nn(kvt[i, at], jnp.exp(one - new).astype(LOW))
            acc_out[j] = done
            peak_out[j, :1] = new

        for_steps(j + 1, some_blocks)
        if last:
            weight_sum = acc_out[j, :1]
            done = acc_out[j] / weight_sum
            out_t[j] = done
            total[j, :1] = peak_out[j, :1] + jnp.log(weight_sum)
            rows = done.T
            x, y = rows[:HALF], rows[HALF:]
            kept_o[j] = jnp.where(lane_of(x.shape) < HDIM, pltpu.roll(x, HDIM, 1), y).astype(LOW)
        return carry

    lax.fori_loop(0, 4, one_query_block, 0)
    if last:
        for k, out in enumerate((o0, o1, o2, o3)):
            out[...] = kept_o[me ^ k]


def backward_kernel(rels, first, *refs):
    place, kv0, kv1, q0, q1, q2, q3, d0, d1, d2, d3, out_t, total, begin = refs[:14]
    if first:
        acc, keep, send, kvt, queries, grads, dot_rows, dkv, kept_q, kept_d = refs[14:]
    else:
        (
            acc_in, g0, g1, g2, g3, keep, send,
            kvt, queries, grads, dot_rows, dkv, kept_q, kept_d, acc, kept_g,
        ) = refs[14:]
    me = place[1]
    for k in range(4):
        kept_q[me ^ k] = (q0, q1, q2, q3)[k][...]
        kept_d[me ^ k] = (d0, d1, d2, d3)[k][...]
    for i, kv in enumerate((kv0, kv1)):
        for t in range(4):
            kvt[i, t] = kv[t].astype(WIDE).T.astype(LOW)
    dkv[...] = jnp.zeros(dkv.shape, WIDE)

    def one_query_block(j, carry):
        first_query = (4 * j + place[0]) * BLOCK
        queries[:HALF, :], queries[HALF:, :] = padded_queries(kept_q[j])
        grads[:HALF, :], grads[HALF:, :] = padded_behind(kept_d[j])
        dot_rows[...] = jnp.sum(grads[...].astype(WIDE).T * out_t[j], axis=0, keepdims=True)
        acc[j] = jnp.zeros((128, BLOCK), WIDE) if first else acc_in[j]

        def some_blocks(steps):
            for t in steps:
                blocks, at = key_blocks(place, rels, t)
                for i, kv in enumerate((kv0, kv1)):
                    term = 0.0
                    for half in range(2):
                        some = slice(half * HALF, half * HALF + HALF)
                        ok = allowed_keys(blocks[i], first_query + half * HALF, begin[j, :1, some])
                        scores = nt(kv[at], queries[some, :])
                        probs = jnp.where(ok, jnp.exp(scores - total[j, :1, some]), 0.0)
                        grad_probs = nt(kv[at], grads[some, :])
                        grad_scores = (probs * (grad_probs - dot_rows[:, some])).astype(LOW)
                        term += nn(grad_scores, queries[some, :])
                        term += nn(probs.astype(LOW), grads[some, :])
                        acc[j, :, some] += nn(kvt[i, at], grad_scores)
                    dkv[i, at] += term

        for_steps(j + 1, some_blocks)
        if not first:
            rows = acc[j].T
            x, y = rows[:HALF], rows[HALF:]
            kept_g[j] = jnp.where(lane_of(x.shape) < HDIM, x, pltpu.roll(y, HDIM, 1)).astype(LOW)
        return carry

    lax.fori_loop(0, 4, one_query_block, 0)
    if not first:
        for k, out in enumerate((g0, g1, g2, g3)):
            out[...] = kept_g[me ^ k]
    for t in range(4):
        keep[t] = dkv[0, t].astype(LOW)
        send[t] = dkv[1, t].astype(LOW)


def branch_kernel(arrive, place, h0, h1, h2, h3, w, attended, *refs):
    outs, (partial, kept) = refs[:8], refs[8:]
    for k, h in enumerate((h0, h1, h2, h3)):
        kept[place[1] ^ k] = h[...]
    for pair in range(2):
        lanes = slice(pair * 128, pair * 128 + 128)
        x, y = exchange_halves(kept[2 * pair].astype(WIDE), kept[2 * pair + 1].astype(WIDE))
        attended[:HALF, lanes] = x.astype(LOW)
        attended[HALF:, lanes] = y.astype(LOW)
    arrive()
    for n in range(4):
        at = slice(n * 512, n * 512 + 512)
        partial[:, at] = nn(attended[...], w[:, at]).astype(LOW)
    deal_rows(place, partial, outs)


def grad_attended_kernel(place, grad, w, d0, d1, d2, d3, kept):
    g = nt(grad[...], w[...])
    for pair in range(2):
        lanes = slice(pair * 128, pair * 128 + 128)
        both = exchange_halves(g[:HALF, lanes], g[HALF:, lanes])
        for one in range(2):
            kept[2 * pair + one] = both[one].astype(LOW)
    for k, out in enumerate((d0, d1, d2, d3)):
        out[...] = kept[place[1] ^ k]


def join_kernel(keep, received, far, g0, g1, g2, g3, x0, x1, x2, x3):
    for k in range(4):
        total = keep[k].astype(WIDE) + received[k].astype(WIDE) + far[k].astype(WIDE)
        out = (x0, x1, x2, x3)[k]
        out[:BLOCK, :] = total.astype(LOW)
        out[BLOCK:, :] = (g0, g1, g2, g3)[k][...]


def grad_project_kernel(
    arrive, place, x0, x1, x2, x3, cosine, sine, tok, stats, w,
    grad_mixed, partial, gain_sum, shift_sum, bias_sum, parts, kept,
):
    for k, x in enumerate((x0, x1, x2, x3)):
        parts[place[1] ^ k] = x[:BLOCK, :]
        kept[place[1] ^ k] = x[BLOCK:, :]
    for pair in range(2):
        lanes = slice(pair * 128, pair * 128 + 128)
        k, v = exchange_halves(parts[2 * pair].astype(WIDE), parts[2 * pair + 1].astype(WIDE))
        q = exchange_halves(kept[2 * pair].astype(WIDE), kept[2 * pair + 1].astype(WIDE))
        q = jnp.concatenate(q, axis=0)
        q = turn(q, cosine[...], sine[...], -1.0) * 0.125
        k = turn(k, cosine[...], sine[...], -1.0)
        for c, part in enumerate((q, k, v)):
            start = c * 256 + pair * 128
            low = part.astype(LOW)
            grad_mixed[:, start : start + 128] = low
            bias_sum[c : c + 1, lanes] = jnp.sum(low.astype(WIDE), axis=0, keepdims=True)
    arrive()
    mean, scale = stats[:, 0:1], stats[:, 64:65]
    for n in range(4):
        at = slice(n * 512, n * 512 + 512)
        total = nt(grad_mixed[:, :256], w[0, at, :])
        total += nt(grad_mixed[:, 256:512], w[1, at, :])
        total += nt(grad_mixed[:, 512:], w[2, at, :])
        partial[:, at] = total.astype(LOW)
        normal = (tok[:, at].astype(WIDE) - mean) * scale
        gain_sum[:, at] = jnp.sum(total * normal, axis=0, keepdims=True)
        shift_sum[:, at] = jnp.sum(total, axis=0, keepdims=True)


def hidden_gradient_kernel(cot, w, grad_hidden):
    grad_hidden[...] = nt(cot[...], w[...])


def feed_kernel(arrive, place, second, w_gate, w_up, grad_hidden, hidden, grad_gate, grad_up, partial):
    gate = nt(second[...], w_gate[0])
    arrive()
    up = nt(second[...], w_up[0])
    sigmoid = 1.0 / (1.0 + jnp.exp(-gate))
    activated = gate * sigmoid
    hidden[...] = (activated * up).astype(LOW)
    grad = grad_hidden[...]
    grad_up[...] = (grad * activated).astype(LOW)
    grad_gate[...] = (grad * up * sigmoid * (1.0 + gate * (1.0 - sigmoid))).astype(LOW)
    for n in range(4):
        at = slice(n * 512, n * 512 + 512)
        partial[:, at] = (nn(grad_gate[...], w_gate[0, :, at]) + nn(grad_up[...], w_up[0, :, at])).astype(LOW)


def for_rows(work):
    rows = 16

    def one(i, carry):
        work(pl.ds(pl.multiple_of(i * rows, rows), rows))
        return carry

    lax.fori_loop(0, 64 // rows, one, 0)


def summed(parts, at):
    one = [parts[k][at, :] for k in range(8)] if isinstance(parts, tuple) else [parts[k, at, :] for k in range(8)]
    total = one[0].astype(WIDE)
    for x in one[1:]:
        total += x.astype(WIDE)
    return total


def second_norm_kernel(*refs):
    parts, (tok, gain, shift, low, middle, normal, stats) = refs[:8], refs[8:]

    def work(at):
        x = tok[at, :].astype(WIDE) + summed(parts, at)
        center = x - jnp.mean(x, axis=-1, keepdims=True)
        scale = lax.rsqrt(jnp.mean(center * center, axis=-1, keepdims=True) + 1e-05)
        rows = center * scale
        low[at, :] = (rows * gain[...] + shift[...]).astype(LOW)
        middle[at, :] = x
        normal[at, :] = rows
        stats[at, :] = jnp.broadcast_to(scale, (scale.shape[0], 128))

    for_rows(work)


def norm_gradient(grad, rows, scale, gain):
    scaled = grad * gain
    return scale * (
        scaled
        - jnp.mean(scaled, axis=-1, keepdims=True)
        - rows * jnp.mean(scaled * rows, axis=-1, keepdims=True)
    )


def second_gradient_kernel(parts, cot, normal, stats, gain, copies, grad_middle, sums):
    sums[...] = jnp.zeros(sums.shape, WIDE)

    def work(at):
        grad, rows = summed(parts, at), normal[at, :]
        done = cot[at, :].astype(WIDE) + norm_gradient(grad, rows, stats[at, 0:1], gain[...])
        low = done.astype(LOW)
        for k in range(8):
            copies[k, at, :] = low
        grad_middle[at, :] = done
        sums[0:1, :] += jnp.sum(grad * rows, axis=0, keepdims=True)
        sums[1:2, :] += jnp.sum(grad, axis=0, keepdims=True)

    for_rows(work)


def feed_sum_kernel(place, parts, middle, out):
    rows = 16
    mine = place[3]

    def one(i, carry):
        at = pl.ds(pl.multiple_of(i * rows, rows), rows)
        total = parts[0, at, :].astype(WIDE)
        for k in range(1, 4):
            total += parts[k, at, :].astype(WIDE)
        here = i * rows - mine * 64
        own = pl.ds(pl.multiple_of(jnp.clip(here, 0, 64 - rows), rows), rows)
        inside = (here >= 0) & (here < 64)
        out[at, :] = (total + jnp.where(inside, middle[own, :], 0.0)).astype(LOW)
        return carry

    lax.fori_loop(0, 128 // rows, one, 0)


def layer_out_kernel(a, b, copies):
    rows = 16

    def one(i, carry):
        at = pl.ds(pl.multiple_of(i * rows, rows), rows)
        low = (a[at, :].astype(WIDE) + b[at, :].astype(WIDE)).astype(LOW)
        for k in range(4):
            copies[k, at, :] = low
        return carry

    lax.fori_loop(0, 128 // rows, one, 0)


def first_gradient_kernel(parts, grad_middle, tok, stats, vectors, gain, low):
    def work(at):
        mean, scale = stats[at, 0:1], stats[at, 64:65]
        rows = (tok[at, :].astype(WIDE) - mean) * scale
        done = norm_gradient(summed(parts, at), rows, scale, gain[...])
        low[at, :2048] = (grad_middle[at, :] + done).astype(LOW)
        low[at, 2048:] = vectors[at, :].astype(LOW)

    for_rows(work)


def last_kernel(place, gathered, out, total):
    out[...] = gathered[:, :2048]
    done = gathered[:64, 2048:].astype(WIDE)
    for k in range(1, 8):
        done += gathered[k * 64 : k * 64 + 64, 2048:].astype(WIDE)
    total[...] = done


def weight_kernel(widths, sources, arrive, place, *refs):
    count = max(max(pair) for pair in sources) + 1
    inputs = refs[:count]
    mine, theirs, turned = refs[count:]
    first_core = place[2] == 0
    start = 0
    for n, ((left, right), width) in enumerate(zip(sources, widths)):
        if n == 1:
            arrive()
        left, right = inputs[left], inputs[right]
        turned[:width, :] = left[...].astype(WIDE).T.astype(LOW)

        def one(n, carry, start=start, right=right, width=width):
            columns = right[:, pl.ds(pl.multiple_of(n * 256, 256), 256)]
            both = nn(turned[:width, :], columns)
            first, second = both[:, :128], both[:, 128:]
            at = pl.ds(start, width)
            mine[n, at, :] = jnp.where(first_core, first, second).astype(LOW)
            theirs[n, at, :] = jnp.where(first_core, second, first).astype(LOW)
            return carry

        lax.fori_loop(0, 8, one, 0, unroll=4)
        start += width


def weight_grads(pairs, place):
    inputs, sources = [], []
    for pair in pairs:
        for a in pair:
            if not any(a is b for b in inputs):
                inputs.append(a)
        sources.append(tuple(next(k for k, b in enumerate(inputs) if b is a) for a in pair))
    widths = tuple(a.shape[1] for a, _ in pairs)
    out = jax.ShapeDtypeStruct((8, sum(widths), 128), LOW)
    return kernel_call(
        functools.partial(weight_kernel, widths, sources),
        (out, out),
        inputs,
        scalars=(place,),
        scratch=(pltpu.VMEM((max(widths), BLOCK), LOW),),
        late=len(inputs) - 2,
        quick=True,
    )


def swapped(x, axis):
    return lax.ppermute(x, axis, [(0, 1), (1, 0)])


def across(pieces):
    moved = [
        lax.ppermute(pieces[k], SPREAD, [(i, i ^ k) for i in range(4)]) for k in range(1, 4)
    ]
    return (pieces[0], *moved)


def z_parts_kernel(place, mine, received, *refs):
    outs, (held_a, held_b, done, came, went) = refs[:4], refs[4:]
    z = place[0]
    order = [(k, xh) for k in (1, 3, 2, 0) for xh in range(2)]
    moves = []
    for n, (k, xh) in enumerate(order):
        at = xh * 4 + lax.rem(z + k, 4)
        moves.append(
            (
                pltpu.make_async_copy(mine.at[at], held_a.at[n], came.at[2 * n]),
                pltpu.make_async_copy(received.at[at], held_b.at[n], came.at[2 * n + 1]),
                pltpu.make_async_copy(done.at[n], outs[k].at[xh], went.at[n]),
            )
        )
    for a, b, _ in moves:
        a.start()
        b.start()
    for n, (a, b, out) in enumerate(moves):
        a.wait()
        b.wait()
        done[n] = (held_a[n].astype(WIDE) + held_b[n].astype(WIDE)).astype(LOW)
        out.start()
    for _, _, out in moves:
        out.wait()


def z_parts(mine, received):
    rows = mine.shape[1]
    hbm = pl.BlockSpec(memory_space=pltpu.HBM)
    held = pltpu.VMEM((8, rows, 128), LOW)
    return pl.pallas_call(
        z_parts_kernel,
        in_specs=[pl.BlockSpec(memory_space=pltpu.SMEM), hbm, hbm],
        out_specs=[hbm] * 4,
        out_shape=[pltpu.HBM((2, rows, 128), LOW)] * 4,
        scratch_shapes=[
            held,
            held,
            held,
            pltpu.SemaphoreType.DMA((16,)),
            pltpu.SemaphoreType.DMA((8,)),
        ],
        compiler_params=pltpu.CompilerParams(vmem_limit_bytes=24 * 1024 * 1024),
        cost_estimate=pl.CostEstimate(flops=0, bytes_accessed=0, transcendentals=0),
    )(
        lax.axis_index(Z).reshape(1),
        *[pltpu.with_memory_space_constraint(a, pltpu.HBM) for a in (mine, received)],
    )


def settled_kernel(x, out, held, came, went):
    rows = x.shape[1]
    moves = []
    for k in range(x.shape[0]):
        at = pl.ds(k * rows, rows)
        moves.append(
            (
                pltpu.make_async_copy(x.at[k], held.at[k], came.at[k]),
                pltpu.make_async_copy(held.at[k, :, pl.ds(0, 2048)], out.at[at], went.at[k]),
            )
        )
    for come, _ in moves:
        come.start()
    for come, go in moves:
        come.wait()
        go.start()
    for _, go in moves:
        go.wait()


def settled(x):
    hbm = pl.BlockSpec(memory_space=pltpu.HBM)
    parts, rows = x.shape[:2]
    return pl.pallas_call(
        settled_kernel,
        out_shape=pltpu.HBM((parts * rows, 2048), x.dtype),
        in_specs=[pl.BlockSpec(memory_space=pl.ANY)],
        out_specs=hbm,
        scratch_shapes=[
            pltpu.VMEM(x.shape, x.dtype),
            pltpu.SemaphoreType.DMA((parts,)),
            pltpu.SemaphoreType.DMA((parts,)),
        ],
        compiler_params=pltpu.CompilerParams(vmem_limit_bytes=8 * 1024 * 1024),
        cost_estimate=pl.CostEstimate(flops=0, bytes_accessed=0, transcendentals=0),
    )(x)


def z_permute(part, distance):
    return lax.ppermute(part, Z, [(i, (i + distance) % 4) for i in range(4)])


def xh_halves(moved):
    xh = lax.axis_index("xh")

    def added(at):
        return sum(lax.dynamic_index_in_dim(x, at, 0, False).astype(WIDE) for x in moved)

    return added(xh), added(1 - xh).astype(LOW)


def dealt(x, axis):
    return lax.all_to_all(x, axis, split_axis=0, concat_axis=0, tiled=True)


def tp_parts(partial):
    return dealt(partial.reshape(8, -1, partial.shape[1]), TP)


def y_moved(x, distance):
    return lax.ppermute(x, "y", [(i, (i + distance) % 4) for i in range(4)])


def scattered(pieces):
    moved = {
        k: lax.ppermute(pieces[k], TP, [(i, i ^ k) for i in range(8)]) for k in (5, 4, 7, 3, 6, 2, 1)
    }
    return [pieces[0], *[moved[k] for k in range(1, 8)]]


def gathered(share, *beside):
    across_x, *beside = lax.optimization_barrier((swapped(share, "xl"), *beside))
    back, ahead, far = (y_moved(share, k) for k in (1, 3, 2))
    shares = [
        share, across_x, back, ahead, far,
        y_moved(across_x, 1), y_moved(across_x, 3), swapped(far, "xl"),
    ]
    return (shares, *beside) if beside else shares


def summed_by_pairs(x, pairs):
    for axis, size, distance in pairs:
        x = x + lax.ppermute(x, axis, [(i, i ^ distance) for i in range(size)])
    return x


def shape_of(*dims, kind=LOW):
    return jax.ShapeDtypeStruct(dims, kind)


def body(
    tokens, cotangent, segment_ids, first_gain, first_shift, second_gain, second_shift,
    w_qkv, qkv_bias, w_out, w_gate_up, w_down,
):
    ctx = lax.axis_index(CTX)
    tp = lax.axis_index(TP)
    group = lax.axis_index(("zl", "core"))
    place = jnp.stack(
        [group, lax.axis_index(SPREAD), lax.axis_index("core"), lax.axis_index("xl"), lax.axis_index("y")]
    )
    tied = lax.optimization_barrier

    def my_share(array):
        return lax.dynamic_slice_in_dim(array, tp * 64, 64)

    labels = jnp.arange(DOCS, dtype=jnp.int32)
    starts = jnp.sum((segment_ids[None, :] < labels[:, None]).astype(jnp.int32), axis=1)
    begins = jnp.sum(
        jnp.where(segment_ids[None, :] == labels[:, None], starts[:, None], 0), axis=0
    )
    begin = lax.dynamic_index_in_dim(begins.reshape(4, 4, 1, BLOCK), group, 1, False)
    begin = jnp.broadcast_to(begin, (4, 8, BLOCK))
    own = lax.dynamic_slice_in_dim(begins, ctx * BLOCK, BLOCK)
    places = ctx * BLOCK + jnp.arange(BLOCK, dtype=jnp.int32) - own
    frequency = 10000.0 ** (-jnp.arange(8, dtype=WIDE) / 8.0)
    angles = frequency[:, None] * places.astype(WIDE)[None, :]
    table = jnp.concatenate([jnp.cos(angles), jnp.sin(angles)], axis=0)

    w3 = jnp.transpose(w_qkv, (1, 0, 2))
    w2 = jnp.transpose(w_gate_up, (1, 2, 0))
    quarter, piece = shape_of(HALF, 128), shape_of(BLOCK + HALF, 128)
    wide_block = shape_of(BLOCK, 128, kind=WIDE)
    four = pltpu.VMEM((4, HALF, 128), LOW)
    normed_low, stats1, *packed, cosine, sine = kernel_call(
        project_kernel,
        (shape_of(BLOCK, 2048), wide_block, *[piece] * 4, wide_block, wide_block),
        (tokens, table, w3),
        small=(first_gain[None], first_shift[None], qkv_bias),
        scalars=(place,),
        scratch=(pltpu.VMEM((4, BLOCK + HALF, 128), LOW),),
        late=1,
        flops=2 * 512 * 2048 * 768,
    )
    (grad_hidden,) = kernel_call(
        hidden_gradient_kernel,
        (shape_of(BLOCK, 704, kind=WIDE),),
        (cotangent, w_down),
        flops=2 * 512 * 2048 * 704,
    )
    *packed, grad_hidden, tok_share, cot_share = tied(
        (*across(packed), grad_hidden, my_share(tokens), my_share(cotangent))
    )
    kv = jnp.stack([x[:BLOCK] for x in packed])
    queries = [(x, BLOCK, HALF) for x in packed]
    kv_c = swapped(kv, "core")
    state = (shape_of(4, 128, BLOCK, kind=WIDE), shape_of(4, 8, BLOCK, kind=WIDE))
    acc, peak = kernel_call(
        functools.partial(forward_kernel, (0, 1), True, False),
        state,
        (kv, kv_c, *queries, begin),
        scalars=(place,),
        scratch=(pltpu.VMEM((2, 4, 128, BLOCK), LOW), pltpu.VMEM((BLOCK, 128), LOW), four),
        flops=20 * 4 * BLOCK * BLOCK * 128,
        exps=20 * BLOCK * BLOCK,
        mib=24,
    )
    acc, peak, kv_z = tied((acc, peak, swapped(kv, "zl")))
    kv_zc = swapped(kv_z, "core")
    *heads, out_t, total = kernel_call(
        functools.partial(forward_kernel, (2, 3), False, True),
        (*[quarter] * 4, *state),
        (kv_z, kv_zc, *queries, begin, acc, peak),
        scalars=(place,),
        scratch=(pltpu.VMEM((2, 4, 128, BLOCK), LOW), pltpu.VMEM((BLOCK, 128), LOW), four, four),
        flops=20 * 4 * BLOCK * BLOCK * 128,
        exps=20 * BLOCK * BLOCK,
        mib=24,
    )
    heads = across(heads)
    share, low_share = shape_of(64, 2048, kind=WIDE), shape_of(64, 2048)
    attended_low, *partial_branch = kernel_call(
        branch_kernel,
        (shape_of(BLOCK, 256), *[low_share] * 8),
        (*heads, w_out),
        scalars=(place,),
        scratch=(pltpu.VMEM((BLOCK, 2048), LOW), four),
        late=1,
        flops=2 * 512 * 256 * 2048,
    )
    branch_parts = scattered(partial_branch)
    second_share, middle, second_rows, stats2 = kernel_call(
        second_norm_kernel,
        (low_share, share, share, shape_of(64, 128, kind=WIDE)),
        (*branch_parts, tok_share),
        small=(second_gain[None], second_shift[None]),
    )
    second_low = gathered(second_share)
    strip = shape_of(BLOCK, 704)
    hidden_low, grad_gate, grad_up, partial_second = kernel_call(
        feed_kernel,
        (strip, strip, strip, shape_of(BLOCK, 2048)),
        (second_low, (w2, 0, 1), (w2, 1, 1), grad_hidden),
        scalars=(place,),
        late=2,
        flops=8 * 512 * 2048 * 704,
        mib=24,
    )
    second_parts = tp_parts(partial_second)

    feed_mine, feed_theirs = weight_grads(
        ((grad_gate, second_low), (grad_up, second_low), (hidden_low, cotangent)), place
    )
    second_parts, feed_mine, feed_theirs = tied((second_parts, feed_mine, feed_theirs))
    copies, grad_middle, second_sums = kernel_call(
        second_gradient_kernel,
        (shape_of(8, 64, 2048), share),
        (second_parts, cot_share, second_rows, stats2),
        moved=1,
        small=(second_gain[None],),
        small_outs=(shape_of(2, 2048, kind=WIDE),),
    )
    grad_branch = dealt(copies, TP).reshape(BLOCK, 2048)
    partial_feed = jnp.dot(hidden_low, w_down, preferred_element_type=WIDE).astype(LOW)
    grad_branch, partial_feed = tied((grad_branch, partial_feed))
    feed_z = z_parts(feed_mine, swapped(feed_theirs, "core"))
    feed_1, feed_3 = z_permute(feed_z[1], 1), z_permute(feed_z[3], 3)
    grads = kernel_call(
        grad_attended_kernel,
        (*[quarter] * 4,),
        (grad_branch, w_out),
        moved=1,
        scalars=(place,),
        scratch=(four,),
        flops=2 * 512 * 256 * 2048,
    )
    feed_1, feed_3, partial_feed, *grads = tied((feed_1, feed_3, partial_feed, *grads))
    feed_parts = dealt(partial_feed.reshape(4, 128, 2048), "y")
    *grads, feed_2 = tied((*across(grads), feed_z[2]))
    feed_2 = z_permute(feed_2, 2)
    scratch = (
        pltpu.VMEM((2, 4, 128, BLOCK), LOW),
        pltpu.VMEM((BLOCK, 128), LOW),
        pltpu.VMEM((BLOCK, 128), LOW),
        pltpu.VMEM((1, BLOCK), WIDE),
        pltpu.VMEM((2, 4, BLOCK, 128), WIDE),
        four,
        four,
    )
    blocks = shape_of(4, BLOCK, 128)
    acc, keep1, send1 = kernel_call(
        functools.partial(backward_kernel, (2, 3), True),
        (state[0], blocks, blocks),
        (kv_z, kv_zc, *queries, *grads, out_t, total, begin),
        scalars=(place,),
        scratch=scratch,
        flops=20 * 10 * BLOCK * BLOCK * 128,
        exps=20 * BLOCK * BLOCK,
        mib=28,
    )
    acc, send1, feed_parts, feed_2 = tied((acc, send1, feed_parts, feed_2))
    (feed_half,) = kernel_call(
        feed_sum_kernel,
        (shape_of(128, 2048),),
        (feed_parts, middle),
        scalars=(place,),
        moved=1,
    )
    far = (keep1.astype(WIDE) + swapped(send1, "core").astype(WIDE)).astype(LOW)
    acc, far, feed_half = tied((acc, far, feed_half))
    near = kernel_call(
        functools.partial(backward_kernel, (0, 1), False),
        (*[quarter] * 4, blocks, blocks),
        (kv, kv_c, *queries, *grads, out_t, total, begin, acc),
        scalars=(place,),
        scratch=(*scratch, pltpu.VMEM((4, 128, BLOCK), WIDE), four),
        flops=20 * 10 * BLOCK * BLOCK * 128,
        exps=20 * BLOCK * BLOCK,
        mib=28,
    )
    *near, far, feed_other = tied((*near, swapped(far, "zl"), swapped(feed_half, "xl")))
    *grad_queries, keep0, send0 = near
    pieces = kernel_call(
        join_kernel,
        (*[piece] * 4,),
        (keep0, swapped(send0, "core"), far, *grad_queries),
    )
    (copies4,) = kernel_call(layer_out_kernel, (shape_of(4, 128, 2048),), (feed_half, feed_other))
    feed_keep, feed_send = xh_halves([feed_z[0], feed_1, feed_2, feed_3])
    *pieces, copies4, feed_send = tied((*pieces, copies4, feed_send))
    *pieces, feed_send = tied((*across(pieces), feed_send))
    feed_received = swapped(feed_send, "xh")
    layer_out = dealt(copies4, "y")
    grad_mixed, partial_normed, gain_sum, shift_sum, bias_sum = kernel_call(
        grad_project_kernel,
        (shape_of(BLOCK, 768), shape_of(BLOCK, 2048)),
        (*pieces, cosine, sine, tokens, stats1, w3),
        small_outs=(
            shape_of(1, 2048, kind=WIDE),
            shape_of(1, 2048, kind=WIDE),
            shape_of(3, 256, kind=WIDE),
        ),
        scalars=(place,),
        scratch=(pltpu.VMEM((4, BLOCK, 128), LOW), four),
        late=3,
        flops=2 * 512 * 2048 * 768,
    )
    partial_normed, layer_out = tied((partial_normed, layer_out))
    layer_out = settled(layer_out)
    normed_parts = tp_parts(partial_normed)

    rest_mine, rest_theirs = weight_grads(
        ((grad_mixed, normed_low), (attended_low, grad_branch)), place
    )
    rest_mine, rest_theirs, feed_received = tied((rest_mine, rest_theirs, feed_received))
    rest_z = z_parts(rest_mine, swapped(rest_theirs, "core"))
    vectors = jnp.concatenate([gain_sum, shift_sum, second_sums], axis=0).reshape(32, 256)
    vectors = jnp.concatenate([vectors, bias_sum], axis=0)
    vectors = summed_by_pairs(vectors, (("core", 2, 1), ("zl", 2, 1), ("zh", 2, 1)))
    vectors, *rest_z = tied((vectors, *rest_z))
    vectors = summed_by_pairs(vectors, (("xh", 2, 1),))
    rest_1, rest_3 = z_permute(rest_z[1], 1), z_permute(rest_z[3], 3)
    normed_parts, vectors = tied((normed_parts, vectors))
    bias_grad = vectors[32:]
    (last_share,) = kernel_call(
        first_gradient_kernel,
        (shape_of(64, 2048 + 128),),
        (normed_parts, grad_middle, tok_share, my_share(stats1), vectors[:32].reshape(64, 128)),
        moved=1,
        small=(first_gain[None],),
    )
    last_shares, rest_1, rest_3 = gathered(last_share, rest_1, rest_3)
    grad_tokens, vectors = kernel_call(
        last_kernel,
        (shape_of(BLOCK, 2048),),
        (last_shares,),
        scalars=(place,),
        small_outs=(shape_of(64, 128, kind=WIDE),),
        quick=True,
    )
    vectors = vectors.reshape(4, 2048)
    rest_z = (rest_z[0], rest_1, z_permute(rest_z[2], 2), rest_3)
    rest_keep, rest_send = xh_halves(rest_z)
    rest_w = rest_keep + swapped(rest_send, "xh").astype(WIDE)
    feed_w = feed_keep + feed_received.astype(WIDE)
    return (
        layer_out,
        grad_tokens,
        vectors[0],
        vectors[1],
        vectors[2],
        vectors[3],
        jnp.transpose(rest_w[:768].reshape(3, 256, 128), (2, 0, 1)),
        bias_grad,
        rest_w[768:],
        jnp.transpose(feed_w[:1408].reshape(2, 704, 128), (2, 0, 1)),
        feed_w[1408:],
    )


def solution(mesh):
    fine = Mesh(
        mesh.devices.reshape(2, 2, 2, 2, 4, 2), ("xh", "zh", "zl", "core", "y", "xl")
    )
    rows = P(CTX, None)
    return jax.shard_map(
        body,
        mesh=fine,
        in_specs=(
            rows, rows, P(), P(), P(), P(), P(),
            P(None, None, TP), P(None, TP), P(TP, None), P(None, None, TP), P(TP, None),
        ),
        out_specs=(
            rows, rows, P(), P(), P(), P(),
            P(CTX, None, TP), P(None, TP), P(TP, CTX), P(CTX, None, TP), P(TP, CTX),
        ),
        check_vma=False,
    )
```

```python
import functools

import jax
import jax.numpy as jnp
from jax import lax
from jax.experimental import pallas as pl
from jax.experimental.pallas import tpu as pltpu
from jax.sharding import Mesh
from jax.sharding import PartitionSpec as P

HDIM = 64
DOCS = 3
BLOCK = 512
HALF = 256
LOW = jnp.bfloat16
WIDE = jnp.float32
CTX = ("xh", "zh", "zl", "core")
TP = ("y", "xl")
SPREAD = ("xh", "zh")
Z = ("zh", "zl")


def size_of(a):
    return a.size * jnp.dtype(a.dtype).itemsize


def gathered_order(place):
    x, y = place[3], place[4]
    row = [lax.rem(y + k, 4) * 2 for k in range(4)]
    other = 1 - x
    return [
        row[0] + x, row[0] + other,
        row[3] + x, row[1] + x, row[2] + x,
        row[3] + other, row[1] + other, row[2] + other,
    ]


def deal_rows(place, rows, outs):
    x, y = place[3], place[4]
    far = lax.rem(y + 2, 4)
    firsts = [
        lax.rem(y + 1, 4) * 2, lax.rem(y + 3, 4) * 2,
        far * 2 + 1 - x, y * 2 + x, y * 2 + 1 - x, far * 2 + x,
    ]
    for first, out in zip(firsts, outs):
        out[...] = rows[pl.ds(pl.multiple_of(first * 64, 64), out.shape[0]), :]


def meet_kernel(place, below, above, crossed, other, far, out_other, out_far):
    column = pl.multiple_of((1 - place[3]) * 64, 64)

    def work(at):
        there = pl.ds(pl.multiple_of(column + at.start, 16), at.size)
        total = other[at, :].astype(WIDE) + below[there, :].astype(WIDE) + above[there, :].astype(WIDE)
        out_other[at, :] = total.astype(LOW)
        out_far[at, :] = (far[at, :].astype(WIDE) + crossed[at, :].astype(WIDE)).astype(LOW)

    for_rows(work)


def kernel_call(
    body, outs, inputs, *, small=(), small_outs=(), scalars=(), scratch=(), late=0, flops=0, exps=0, mib=12, quick=False, moved=0
):
    inputs = [a if isinstance(a, (tuple, list)) else (a, 0, a.shape[0]) for a in inputs]
    flat = [x for a in inputs for x in (a if isinstance(a, list) else a[:1])]
    counts = [len(x) for x in (scalars, flat, small, outs, small_outs, inputs, outs)]

    def run(*refs):
        groups, at = [], 0
        for n in counts:
            groups.append(refs[at : at + n])
            at += n
        scalar_refs, far_in, near_in, far_out, near_out, held_in, held_out = groups
        arrived, left, *rest = refs[at:]
        pairs, ends = [], []
        for a, held in zip(inputs, held_in):
            if isinstance(a, list):
                rows = a[0].shape[0]
                for index in gathered_order(scalar_refs[0]):
                    pairs.append((None, held.at[pl.ds(pl.multiple_of(index * rows, rows), rows)]))
            else:
                pairs.append((pl.ds(a[1], a[2]), held))
            ends.append(len(pairs))
        moves = [
            pltpu.make_async_copy(x if part is None else x.at[part], held, arrived.at[k])
            for k, (x, (part, held)) in enumerate(zip(far_in, pairs))
        ]
        for move in moves:
            move.start()
        early = ends[len(inputs) - late - 1]
        for move in moves[:early]:
            move.wait()

        def arrive():
            for move in moves[early:]:
                move.wait()

        body(
            *([arrive] if late else []),
            *scalar_refs, *held_in, *near_in, *held_out, *near_out, *rest,
        )
        moves = [
            pltpu.make_async_copy(a, b, left.at[k]) for k, (a, b) in enumerate(zip(held_out, far_out))
        ]
        for move in moves:
            move.start()
        for move in moves:
            move.wait()

    vmem, hbm = pl.BlockSpec(memory_space=pltpu.VMEM), pl.BlockSpec(memory_space=pltpu.HBM)
    taken = [
        shape_of(8 * a[0].shape[0], a[0].shape[1], kind=a[0].dtype)
        if isinstance(a, list)
        else shape_of(a[2], *a[0].shape[1:], kind=a[0].dtype)
        for a in inputs
    ]
    held = [pltpu.VMEM(a.shape, a.dtype) for a in (*taken, *outs)]
    limit = sum(size_of(a) for a in (*taken, *outs, *small, *small_outs)) + mib * 1024 * 1024
    return pl.pallas_call(
        run,
        out_shape=(*[pltpu.HBM(a.shape, a.dtype) for a in outs], *small_outs),
        in_specs=[pl.BlockSpec(memory_space=pltpu.SMEM)] * len(scalars)
        + [pl.BlockSpec(memory_space=pl.ANY)] * moved
        + [hbm] * (len(flat) - moved)
        + [vmem] * len(small),
        out_specs=(*[hbm] * len(outs), *[vmem] * len(small_outs)),
        scratch_shapes=[
            *held,
            pltpu.SemaphoreType.DMA((len(flat),)),
            pltpu.SemaphoreType.DMA((max(1, len(outs)),)),
            *scratch,
        ],
        compiler_params=pltpu.CompilerParams(vmem_limit_bytes=limit),
        cost_estimate=pl.CostEstimate(
            flops=flops,
            bytes_accessed=0 if quick else sum(size_of(a) for a in (*taken, *outs)),
            transcendentals=exps,
        ),
    )(
        *scalars,
        *flat[:moved],
        *[pltpu.with_memory_space_constraint(a, pltpu.HBM) for a in flat[moved:]],
        *small,
    )


def lane_of(shape):
    return lax.broadcasted_iota(jnp.int32, shape, len(shape) - 1)


def exchange_halves(a, b):
    front = lane_of(a.shape) < HDIM
    return (
        jnp.where(front, a, pltpu.roll(b, HDIM, 1)),
        jnp.where(front, pltpu.roll(a, HDIM, 1), b),
    )


def nt(a, b):
    return lax.dot_general(a, b, (((1,), (1,)), ((), ())), preferred_element_type=WIDE)


def nn(a, b):
    return lax.dot_general(a, b, (((1,), (0,)), ((), ())), preferred_element_type=WIDE)


def turn(x, cosine, sine, sign):
    lane = lax.rem(lane_of(x.shape), HDIM)
    ahead = pltpu.roll(x, x.shape[1] - 8, 1)
    behind = pltpu.roll(x, 8, 1)
    swapped = jnp.where(lane < 8, -ahead, behind) * sign
    return x * cosine + swapped * sine


def rotation_table(angles_table):
    tokens = angles_table.shape[1]
    rest = jnp.zeros((112, tokens), WIDE)
    x = jnp.concatenate([angles_table, rest], axis=0).T
    lane = lane_of(x.shape)
    c = jnp.where(lane < 8, x, 0.0)
    c = c + pltpu.roll(c, 8, 1)
    c = c + pltpu.roll(c, HDIM, 1) + jnp.where(lax.rem(lane, HDIM) < 16, 0.0, 1.0)
    s = jnp.where((lane >= 8) & (lane < 16), x, 0.0)
    s = s + pltpu.roll(s, 120, 1)
    s = s + pltpu.roll(s, HDIM, 1)
    return c, s


def project_kernel(
    arrive, place, tok, table, w, gain, shift, bias,
    normed, stats, x0, x1, x2, x3, cosine_out, sine_out, kept,
):
    rows = 64

    def norm_rows(i, carry):
        at = pl.ds(pl.multiple_of(i * rows, rows), rows)
        x = tok[at, :].astype(WIDE)
        mean = jnp.mean(x, axis=-1, keepdims=True)
        center = x - mean
        scale = lax.rsqrt(jnp.mean(center * center, axis=-1, keepdims=True) + 1e-05)
        normed[at, :] = (center * scale * gain[...] + shift[...]).astype(LOW)
        stats[at, :] = jnp.where(lane_of((rows, 128)) < HDIM, mean, scale)
        return carry

    lax.fori_loop(0, BLOCK // rows, norm_rows, 0)
    cosine, sine = rotation_table(table[...])
    cosine_out[...] = cosine
    sine_out[...] = sine
    arrive()
    mixed = [nn(normed[...], w[c]) + bias[c : c + 1, :] for c in range(3)]
    for pair in range(2):
        lanes = slice(pair * 128, pair * 128 + 128)
        q = turn(mixed[0][:, lanes], cosine, sine, 1.0) * 0.125
        k = turn(mixed[1][:, lanes], cosine, sine, 1.0)
        kv = exchange_halves(k, mixed[2][:, lanes])
        qq = exchange_halves(q[:HALF], q[HALF:])
        for one in range(2):
            kept[2 * pair + one, :BLOCK, :] = kv[one].astype(LOW)
            kept[2 * pair + one, BLOCK:, :] = qq[one].astype(LOW)
    for k, out in enumerate((x0, x1, x2, x3)):
        out[...] = kept[place[1] ^ k]


def padded_queries(q2):
    x = q2.astype(WIDE)
    front = lane_of(x.shape) < HDIM
    return (
        jnp.where(front, x, 0.0).astype(LOW),
        jnp.where(front, pltpu.roll(x, HDIM, 1), 0.0).astype(LOW),
    )


def padded_behind(d2):
    x = d2.astype(WIDE)
    front = lane_of(x.shape) < HDIM
    return (
        jnp.where(front, 0.0, pltpu.roll(x, HDIM, 1)).astype(LOW),
        jnp.where(front, 0.0, x).astype(LOW),
    )


def allowed_keys(key_block, first_query, begin):
    shape = (BLOCK, begin.shape[1])
    key_at = key_block * BLOCK + lax.broadcasted_iota(jnp.int32, shape, 0)
    query_at = first_query + lax.broadcasted_iota(jnp.int32, shape, 1)
    return (key_at <= query_at) & (key_at >= begin)


def for_steps(count, work):
    def pair(i, carry):
        work([2 * i, 2 * i + 1])
        return carry

    lax.fori_loop(0, count // 2, pair, 0)

    @pl.when(lax.rem(count, 2) == 1)
    def _():
        work([count - 1])


def key_blocks(place, rels, t):
    return [4 * t + (place[0] ^ rel) for rel in rels], place[1] ^ t


def forward_kernel(rels, first, last, *refs):
    place, kv0, kv1, q0, q1, q2, q3, begin = refs[:8]
    if first:
        acc_out, peak_out, kvt, queries, kept_q = refs[8:]
    else:
        acc_in, peak_in, o0, o1, o2, o3, out_t, total, kvt, queries, kept_q, kept_o = refs[8:]
        acc_out, peak_out = out_t, total
    me = place[1]
    front = lane_of((BLOCK, 128)) < HDIM
    for k, q in enumerate((q0, q1, q2, q3)):
        kept_q[me ^ k] = q[...]
    for i, kv in enumerate((kv0, kv1)):
        for t in range(4):
            kvt[i, t] = jnp.where(front, 1.0, kv[t].astype(WIDE)).T.astype(LOW)

    def one_query_block(j, carry):
        first_query = (4 * j + place[0]) * BLOCK
        queries[:HALF, :], queries[HALF:, :] = padded_queries(kept_q[j])
        if first:
            peak_out[j] = jnp.full((8, BLOCK), -1e30, WIDE)
            acc_out[j] = jnp.zeros((128, BLOCK), WIDE)
        else:
            peak_out[j] = peak_in[j]
            acc_out[j] = acc_in[j]

        def some_blocks(steps):
            scores, sources = [], []
            for t in steps:
                blocks, at = key_blocks(place, rels, t)
                for i, kv in enumerate((kv0, kv1)):
                    ok = allowed_keys(blocks[i], first_query, begin[j, :1])
                    scores.append(jnp.where(ok, nt(kv[at], queries[...]), -1e30))
                    sources.append((i, at))
            old = peak_out[j, :1]
            new = old
            for one in scores:
                new = jnp.maximum(new, jnp.max(one, axis=0, keepdims=True))
            done = acc_out[j] * jnp.exp(old - new)
            for one, (i, at) in zip(scores, sources):
                done += nn(kvt[i, at], jnp.exp(one - new).astype(LOW))
            acc_out[j] = done
            peak_out[j, :1] = new

        for_steps(j + 1, some_blocks)
        if last:
            weight_sum = acc_out[j, :1]
            done = acc_out[j] / weight_sum
            out_t[j] = done
            total[j, :1] = peak_out[j, :1] + jnp.log(weight_sum)
            rows = done.T
            x, y = rows[:HALF], rows[HALF:]
            kept_o[j] = jnp.where(lane_of(x.shape) < HDIM, pltpu.roll(x, HDIM, 1), y).astype(LOW)
        return carry

    lax.fori_loop(0, 4, one_query_block, 0)
    if last:
        for k, out in enumerate((o0, o1, o2, o3)):
            out[...] = kept_o[me ^ k]


def backward_kernel(rels, first, *refs):
    place, kv0, kv1, q0, q1, q2, q3, d0, d1, d2, d3, out_t, total, begin = refs[:14]
    if first:
        acc, keep, send, kvt, queries, grads, dot_rows, dkv, kept_q, kept_d = refs[14:]
    else:
        (
            acc_in, g0, g1, g2, g3, keep, send,
            kvt, queries, grads, dot_rows, dkv, kept_q, kept_d, acc, kept_g,
        ) = refs[14:]
    me = place[1]
    for k in range(4):
        kept_q[me ^ k] = (q0, q1, q2, q3)[k][...]
        kept_d[me ^ k] = (d0, d1, d2, d3)[k][...]
    for i, kv in enumerate((kv0, kv1)):
        for t in range(4):
            kvt[i, t] = kv[t].astype(WIDE).T.astype(LOW)
    dkv[...] = jnp.zeros(dkv.shape, WIDE)

    def one_query_block(j, carry):
        first_query = (4 * j + place[0]) * BLOCK
        queries[:HALF, :], queries[HALF:, :] = padded_queries(kept_q[j])
        grads[:HALF, :], grads[HALF:, :] = padded_behind(kept_d[j])
        dot_rows[...] = jnp.sum(grads[...].astype(WIDE).T * out_t[j], axis=0, keepdims=True)
        acc[j] = jnp.zeros((128, BLOCK), WIDE) if first else acc_in[j]

        def some_blocks(steps):
            for t in steps:
                blocks, at = key_blocks(place, rels, t)
                for i, kv in enumerate((kv0, kv1)):
                    term = 0.0
                    for half in range(2):
                        some = slice(half * HALF, half * HALF + HALF)
                        ok = allowed_keys(blocks[i], first_query + half * HALF, begin[j, :1, some])
                        scores = nt(kv[at], queries[some, :])
                        probs = jnp.where(ok, jnp.exp(scores - total[j, :1, some]), 0.0)
                        grad_probs = nt(kv[at], grads[some, :])
                        grad_scores = (probs * (grad_probs - dot_rows[:, some])).astype(LOW)
                        term += nn(grad_scores, queries[some, :])
                        term += nn(probs.astype(LOW), grads[some, :])
                        acc[j, :, some] += nn(kvt[i, at], grad_scores)
                    dkv[i, at] += term

        for_steps(j + 1, some_blocks)
        if not first:
            rows = acc[j].T
            x, y = rows[:HALF], rows[HALF:]
            kept_g[j] = jnp.where(lane_of(x.shape) < HDIM, x, pltpu.roll(y, HDIM, 1)).astype(LOW)
        return carry

    lax.fori_loop(0, 4, one_query_block, 0)
    if not first:
        for k, out in enumerate((g0, g1, g2, g3)):
            out[...] = kept_g[me ^ k]
    for t in range(4):
        keep[t] = dkv[0, t].astype(LOW)
        send[t] = dkv[1, t].astype(LOW)


def branch_kernel(arrive, place, h0, h1, h2, h3, w, attended, *refs):
    outs, (partial, kept) = refs[:6], refs[6:]
    for k, h in enumerate((h0, h1, h2, h3)):
        kept[place[1] ^ k] = h[...]
    for pair in range(2):
        lanes = slice(pair * 128, pair * 128 + 128)
        x, y = exchange_halves(kept[2 * pair].astype(WIDE), kept[2 * pair + 1].astype(WIDE))
        attended[:HALF, lanes] = x.astype(LOW)
        attended[HALF:, lanes] = y.astype(LOW)
    arrive()
    for n in range(4):
        at = slice(n * 512, n * 512 + 512)
        partial[:, at] = nn(attended[...], w[:, at]).astype(LOW)
    deal_rows(place, partial, outs)


def grad_attended_kernel(place, grad, w, d0, d1, d2, d3, kept):
    g = nt(grad[...], w[...])
    for pair in range(2):
        lanes = slice(pair * 128, pair * 128 + 128)
        both = exchange_halves(g[:HALF, lanes], g[HALF:, lanes])
        for one in range(2):
            kept[2 * pair + one] = both[one].astype(LOW)
    for k, out in enumerate((d0, d1, d2, d3)):
        out[...] = kept[place[1] ^ k]


def join_kernel(keep, received, far, g0, g1, g2, g3, x0, x1, x2, x3):
    for k in range(4):
        total = keep[k].astype(WIDE) + received[k].astype(WIDE) + far[k].astype(WIDE)
        out = (x0, x1, x2, x3)[k]
        out[:BLOCK, :] = total.astype(LOW)
        out[BLOCK:, :] = (g0, g1, g2, g3)[k][...]


def grad_project_kernel(
    arrive, place, x0, x1, x2, x3, cosine, sine, tok, stats, w,
    grad_mixed, partial, gain_sum, shift_sum, bias_sum, parts, kept,
):
    for k, x in enumerate((x0, x1, x2, x3)):
        parts[place[1] ^ k] = x[:BLOCK, :]
        kept[place[1] ^ k] = x[BLOCK:, :]
    for pair in range(2):
        lanes = slice(pair * 128, pair * 128 + 128)
        k, v = exchange_halves(parts[2 * pair].astype(WIDE), parts[2 * pair + 1].astype(WIDE))
        q = exchange_halves(kept[2 * pair].astype(WIDE), kept[2 * pair + 1].astype(WIDE))
        q = jnp.concatenate(q, axis=0)
        q = turn(q, cosine[...], sine[...], -1.0) * 0.125
        k = turn(k, cosine[...], sine[...], -1.0)
        for c, part in enumerate((q, k, v)):
            start = c * 256 + pair * 128
            low = part.astype(LOW)
            grad_mixed[:, start : start + 128] = low
            bias_sum[c : c + 1, lanes] = jnp.sum(low.astype(WIDE), axis=0, keepdims=True)
    arrive()
    mean, scale = stats[:, 0:1], stats[:, 64:65]
    for n in range(4):
        at = slice(n * 512, n * 512 + 512)
        total = nt(grad_mixed[:, :256], w[0, at, :])
        total += nt(grad_mixed[:, 256:512], w[1, at, :])
        total += nt(grad_mixed[:, 512:], w[2, at, :])
        partial[:, at] = total.astype(LOW)
        normal = (tok[:, at].astype(WIDE) - mean) * scale
        gain_sum[:, at] = jnp.sum(total * normal, axis=0, keepdims=True)
        shift_sum[:, at] = jnp.sum(total, axis=0, keepdims=True)


def hidden_gradient_kernel(cot, w, grad_hidden):
    grad_hidden[...] = nt(cot[...], w[...])


def feed_kernel(arrive, place, second, w_gate, w_up, grad_hidden, hidden, grad_gate, grad_up, partial):
    gate = nt(second[...], w_gate[0])
    arrive()
    up = nt(second[...], w_up[0])
    sigmoid = 1.0 / (1.0 + jnp.exp(-gate))
    activated = gate * sigmoid
    hidden[...] = (activated * up).astype(LOW)
    grad = grad_hidden[...]
    grad_up[...] = (grad * activated).astype(LOW)
    grad_gate[...] = (grad * up * sigmoid * (1.0 + gate * (1.0 - sigmoid))).astype(LOW)
    for n in range(4):
        at = slice(n * 512, n * 512 + 512)
        partial[:, at] = (nn(grad_gate[...], w_gate[0, :, at]) + nn(grad_up[...], w_up[0, :, at])).astype(LOW)


def for_rows(work):
    rows = 16

    def one(i, carry):
        work(pl.ds(pl.multiple_of(i * rows, rows), rows))
        return carry

    lax.fori_loop(0, 64 // rows, one, 0)


def summed(parts, at):
    total = parts[0, at, :].astype(WIDE)
    for k in range(1, 8):
        total += parts[k, at, :].astype(WIDE)
    return total


def second_norm_kernel(
    place, below, above, own, other, far, tok, gain, shift, low, middle, normal, stats
):
    column = pl.multiple_of(place[3] * 64, 64)

    def work(at):
        there = pl.ds(pl.multiple_of(column + at.start, 16), at.size)
        x = tok[at, :].astype(WIDE) + own[at, :].astype(WIDE)
        x += below[there, :].astype(WIDE) + above[there, :].astype(WIDE)
        x += other[at, :].astype(WIDE) + far[at, :].astype(WIDE)
        center = x - jnp.mean(x, axis=-1, keepdims=True)
        scale = lax.rsqrt(jnp.mean(center * center, axis=-1, keepdims=True) + 1e-05)
        rows = center * scale
        low[at, :] = (rows * gain[...] + shift[...]).astype(LOW)
        middle[at, :] = x
        normal[at, :] = rows
        stats[at, :] = jnp.broadcast_to(scale, (scale.shape[0], 128))

    for_rows(work)


def norm_gradient(grad, rows, scale, gain):
    scaled = grad * gain
    return scale * (
        scaled
        - jnp.mean(scaled, axis=-1, keepdims=True)
        - rows * jnp.mean(scaled * rows, axis=-1, keepdims=True)
    )


def second_gradient_kernel(parts, cot, normal, stats, gain, copies, grad_middle, sums):
    sums[...] = jnp.zeros(sums.shape, WIDE)

    def work(at):
        grad, rows = summed(parts, at), normal[at, :]
        done = cot[at, :].astype(WIDE) + norm_gradient(grad, rows, stats[at, 0:1], gain[...])
        low = done.astype(LOW)
        for k in range(8):
            copies[k, at, :] = low
        grad_middle[at, :] = done
        sums[0:1, :] += jnp.sum(grad * rows, axis=0, keepdims=True)
        sums[1:2, :] += jnp.sum(grad, axis=0, keepdims=True)

    for_rows(work)


def feed_sum_kernel(place, parts, middle, out):
    rows = 16
    mine = place[3]

    def one(i, carry):
        at = pl.ds(pl.multiple_of(i * rows, rows), rows)
        total = parts[0, at, :].astype(WIDE)
        for k in range(1, 4):
            total += parts[k, at, :].astype(WIDE)
        here = i * rows - mine * 64
        own = pl.ds(pl.multiple_of(jnp.clip(here, 0, 64 - rows), rows), rows)
        inside = (here >= 0) & (here < 64)
        out[at, :] = (total + jnp.where(inside, middle[own, :], 0.0)).astype(LOW)
        return carry

    lax.fori_loop(0, 128 // rows, one, 0)


def layer_out_kernel(a, b, copies):
    rows = 16

    def one(i, carry):
        at = pl.ds(pl.multiple_of(i * rows, rows), rows)
        low = (a[at, :].astype(WIDE) + b[at, :].astype(WIDE)).astype(LOW)
        for k in range(4):
            copies[k, at, :] = low
        return carry

    lax.fori_loop(0, 128 // rows, one, 0)


def first_gradient_kernel(parts, grad_middle, tok, stats, vectors, gain, low):
    def work(at):
        mean, scale = stats[at, 0:1], stats[at, 64:65]
        rows = (tok[at, :].astype(WIDE) - mean) * scale
        done = norm_gradient(summed(parts, at), rows, scale, gain[...])
        low[at, :2048] = (grad_middle[at, :] + done).astype(LOW)
        low[at, 2048:] = vectors[at, :].astype(LOW)

    for_rows(work)


def last_kernel(place, *refs):
    shares, (out, total, held, came, went) = refs[:8], refs[8:]
    moves = []
    for k, (x, index) in enumerate(zip(shares, gathered_order(place))):
        at = pl.ds(pl.multiple_of(index * 64, 64), 64)
        moves.append(
            (
                pltpu.make_async_copy(x, held.at[k], came.at[k]),
                pltpu.make_async_copy(held.at[k, :, pl.ds(0, 2048)], out.at[at], went.at[k]),
            )
        )
    for come, _ in moves:
        come.start()
    for come, go in moves:
        come.wait()
        go.start()
    done = held[0, :, 2048:].astype(WIDE)
    for k in range(1, 8):
        done += held[k, :, 2048:].astype(WIDE)
    total[...] = done
    for _, go in moves:
        go.wait()


def last_call(shares, place):
    hbm = pl.BlockSpec(memory_space=pltpu.HBM)
    return pl.pallas_call(
        last_kernel,
        out_shape=(pltpu.HBM((BLOCK, 2048), LOW), shape_of(64, 128, kind=WIDE)),
        in_specs=[pl.BlockSpec(memory_space=pltpu.SMEM), *[hbm] * 8],
        out_specs=(hbm, pl.BlockSpec(memory_space=pltpu.VMEM)),
        scratch_shapes=[
            pltpu.VMEM((8, 64, 2048 + 128), LOW),
            pltpu.SemaphoreType.DMA((8,)),
            pltpu.SemaphoreType.DMA((8,)),
        ],
        compiler_params=pltpu.CompilerParams(vmem_limit_bytes=8 * 1024 * 1024),
        cost_estimate=pl.CostEstimate(flops=0, bytes_accessed=0, transcendentals=0),
    )(place, *[pltpu.with_memory_space_constraint(a, pltpu.HBM) for a in shares])


def weight_kernel(widths, sources, arrive, place, *refs):
    count = max(max(pair) for pair in sources) + 1
    inputs = refs[:count]
    mine, theirs, turned = refs[count:]
    first_core = place[2] == 0
    start = 0
    for n, ((left, right), width) in enumerate(zip(sources, widths)):
        if n == 1:
            arrive()
        left, right = inputs[left], inputs[right]
        turned[:width, :] = left[...].astype(WIDE).T.astype(LOW)

        def one(n, carry, start=start, right=right, width=width):
            columns = right[:, pl.ds(pl.multiple_of(n * 256, 256), 256)]
            both = nn(turned[:width, :], columns)
            first, second = both[:, :128], both[:, 128:]
            at = pl.ds(start, width)
            mine[n, at, :] = jnp.where(first_core, first, second).astype(LOW)
            theirs[n, at, :] = jnp.where(first_core, second, first).astype(LOW)
            return carry

        lax.fori_loop(0, 8, one, 0, unroll=4)
        start += width


def weight_grads(pairs, place):
    inputs, sources = [], []
    for pair in pairs:
        for a in pair:
            if not any(a is b for b in inputs):
                inputs.append(a)
        sources.append(tuple(next(k for k, b in enumerate(inputs) if b is a) for a in pair))
    widths = tuple(a.shape[1] for a, _ in pairs)
    out = jax.ShapeDtypeStruct((8, sum(widths), 128), LOW)
    return kernel_call(
        functools.partial(weight_kernel, widths, sources),
        (out, out),
        inputs,
        scalars=(place,),
        scratch=(pltpu.VMEM((max(widths), BLOCK), LOW),),
        late=len(inputs) - 2,
        quick=True,
    )


def swapped(x, axis):
    return lax.ppermute(x, axis, [(0, 1), (1, 0)])


def across(pieces):
    moved = [
        lax.ppermute(pieces[k], SPREAD, [(i, i ^ k) for i in range(4)]) for k in range(1, 4)
    ]
    return (pieces[0], *moved)


def z_parts_kernel(place, mine, received, *refs):
    outs, (held_a, held_b, done, came, went) = refs[:4], refs[4:]
    z = place[0]
    order = [(k, xh) for k in (1, 3, 2, 0) for xh in range(2)]
    moves = []
    for n, (k, xh) in enumerate(order):
        at = xh * 4 + lax.rem(z + k, 4)
        moves.append(
            (
                pltpu.make_async_copy(mine.at[at], held_a.at[n], came.at[2 * n]),
                pltpu.make_async_copy(received.at[at], held_b.at[n], came.at[2 * n + 1]),
                pltpu.make_async_copy(done.at[n], outs[k].at[xh], went.at[n]),
            )
        )
    for a, b, _ in moves:
        a.start()
        b.start()
    for n, (a, b, out) in enumerate(moves):
        a.wait()
        b.wait()
        done[n] = (held_a[n].astype(WIDE) + held_b[n].astype(WIDE)).astype(LOW)
        out.start()
    for _, _, out in moves:
        out.wait()


def z_parts(mine, received):
    rows = mine.shape[1]
    hbm = pl.BlockSpec(memory_space=pltpu.HBM)
    held = pltpu.VMEM((8, rows, 128), LOW)
    return pl.pallas_call(
        z_parts_kernel,
        in_specs=[pl.BlockSpec(memory_space=pltpu.SMEM), hbm, hbm],
        out_specs=[hbm] * 4,
        out_shape=[pltpu.HBM((2, rows, 128), LOW)] * 4,
        scratch_shapes=[
            held,
            held,
            held,
            pltpu.SemaphoreType.DMA((16,)),
            pltpu.SemaphoreType.DMA((8,)),
        ],
        compiler_params=pltpu.CompilerParams(vmem_limit_bytes=24 * 1024 * 1024),
        cost_estimate=pl.CostEstimate(flops=0, bytes_accessed=0, transcendentals=0),
    )(
        lax.axis_index(Z).reshape(1),
        *[pltpu.with_memory_space_constraint(a, pltpu.HBM) for a in (mine, received)],
    )


def settled_kernel(x, out, held, came, went):
    rows = x.shape[1]
    moves = []
    for k in range(x.shape[0]):
        at = pl.ds(k * rows, rows)
        moves.append(
            (
                pltpu.make_async_copy(x.at[k], held.at[k], came.at[k]),
                pltpu.make_async_copy(held.at[k, :, pl.ds(0, 2048)], out.at[at], went.at[k]),
            )
        )
    for come, _ in moves:
        come.start()
    for come, go in moves:
        come.wait()
        go.start()
    for _, go in moves:
        go.wait()


def settled(x):
    hbm = pl.BlockSpec(memory_space=pltpu.HBM)
    parts, rows = x.shape[:2]
    return pl.pallas_call(
        settled_kernel,
        out_shape=pltpu.HBM((parts * rows, 2048), x.dtype),
        in_specs=[pl.BlockSpec(memory_space=pl.ANY)],
        out_specs=hbm,
        scratch_shapes=[
            pltpu.VMEM(x.shape, x.dtype),
            pltpu.SemaphoreType.DMA((parts,)),
            pltpu.SemaphoreType.DMA((parts,)),
        ],
        compiler_params=pltpu.CompilerParams(vmem_limit_bytes=8 * 1024 * 1024),
        cost_estimate=pl.CostEstimate(flops=0, bytes_accessed=0, transcendentals=0),
    )(x)


def z_permute(part, distance):
    return lax.ppermute(part, Z, [(i, (i + distance) % 4) for i in range(4)])


def xh_halves(moved):
    xh = lax.axis_index("xh")

    def added(at):
        return sum(lax.dynamic_index_in_dim(x, at, 0, False).astype(WIDE) for x in moved)

    return added(xh), added(1 - xh).astype(LOW)


def dealt(x, axis):
    return lax.all_to_all(x, axis, split_axis=0, concat_axis=0, tiled=True)


def tp_parts(partial):
    return dealt(partial.reshape(8, -1, partial.shape[1]), TP)


def y_moved(x, distance):
    return lax.ppermute(x, "y", [(i, (i + distance) % 4) for i in range(4)])


def gathered(share, *beside):
    across_x, *beside = lax.optimization_barrier((swapped(share, "xl"), *beside))
    back, ahead, far = (y_moved(share, k) for k in (1, 3, 2))
    shares = [
        share, across_x, back, ahead, far,
        y_moved(across_x, 1), y_moved(across_x, 3), swapped(far, "xl"),
    ]
    return (shares, *beside) if beside else shares


def summed_by_pairs(x, pairs):
    for axis, size, distance in pairs:
        x = x + lax.ppermute(x, axis, [(i, i ^ distance) for i in range(size)])
    return x


def shape_of(*dims, kind=LOW):
    return jax.ShapeDtypeStruct(dims, kind)


def body(
    tokens, cotangent, segment_ids, first_gain, first_shift, second_gain, second_shift,
    w_qkv, qkv_bias, w_out, w_gate_up, w_down,
):
    ctx = lax.axis_index(CTX)
    tp = lax.axis_index(TP)
    group = lax.axis_index(("zl", "core"))
    place = jnp.stack(
        [group, lax.axis_index(SPREAD), lax.axis_index("core"), lax.axis_index("xl"), lax.axis_index("y")]
    )
    tied = lax.optimization_barrier

    def my_share(array):
        return lax.dynamic_slice_in_dim(array, tp * 64, 64)

    labels = jnp.arange(DOCS, dtype=jnp.int32)
    starts = jnp.sum((segment_ids[None, :] < labels[:, None]).astype(jnp.int32), axis=1)
    begins = jnp.sum(
        jnp.where(segment_ids[None, :] == labels[:, None], starts[:, None], 0), axis=0
    )
    begin = lax.dynamic_index_in_dim(begins.reshape(4, 4, 1, BLOCK), group, 1, False)
    begin = jnp.broadcast_to(begin, (4, 8, BLOCK))
    own = lax.dynamic_slice_in_dim(begins, ctx * BLOCK, BLOCK)
    places = ctx * BLOCK + jnp.arange(BLOCK, dtype=jnp.int32) - own
    frequency = 10000.0 ** (-jnp.arange(8, dtype=WIDE) / 8.0)
    angles = frequency[:, None] * places.astype(WIDE)[None, :]
    table = jnp.concatenate([jnp.cos(angles), jnp.sin(angles)], axis=0)

    w3 = jnp.transpose(w_qkv, (1, 0, 2))
    w2 = jnp.transpose(w_gate_up, (1, 2, 0))
    quarter, piece = shape_of(HALF, 128), shape_of(BLOCK + HALF, 128)
    wide_block = shape_of(BLOCK, 128, kind=WIDE)
    four = pltpu.VMEM((4, HALF, 128), LOW)
    normed_low, stats1, *packed, cosine, sine = kernel_call(
        project_kernel,
        (shape_of(BLOCK, 2048), wide_block, *[piece] * 4, wide_block, wide_block),
        (tokens, table, w3),
        small=(first_gain[None], first_shift[None], qkv_bias),
        scalars=(place,),
        scratch=(pltpu.VMEM((4, BLOCK + HALF, 128), LOW),),
        late=1,
        flops=2 * 512 * 2048 * 768,
    )
    (grad_hidden,) = kernel_call(
        hidden_gradient_kernel,
        (shape_of(BLOCK, 704, kind=WIDE),),
        (cotangent, w_down),
        flops=2 * 512 * 2048 * 704,
    )
    *packed, grad_hidden, tok_share, cot_share = tied(
        (*across(packed), grad_hidden, my_share(tokens), my_share(cotangent))
    )
    kv = jnp.stack([x[:BLOCK] for x in packed])
    queries = [(x, BLOCK, HALF) for x in packed]
    kv_c = swapped(kv, "core")
    state = (shape_of(4, 128, BLOCK, kind=WIDE), shape_of(4, 8, BLOCK, kind=WIDE))
    acc, peak = kernel_call(
        functools.partial(forward_kernel, (0, 1), True, False),
        state,
        (kv, kv_c, *queries, begin),
        scalars=(place,),
        scratch=(pltpu.VMEM((2, 4, 128, BLOCK), LOW), pltpu.VMEM((BLOCK, 128), LOW), four),
        flops=20 * 4 * BLOCK * BLOCK * 128,
        exps=20 * BLOCK * BLOCK,
        mib=24,
    )
    acc, peak, kv_z = tied((acc, peak, swapped(kv, "zl")))
    kv_zc = swapped(kv_z, "core")
    *heads, out_t, total = kernel_call(
        functools.partial(forward_kernel, (2, 3), False, True),
        (*[quarter] * 4, *state),
        (kv_z, kv_zc, *queries, begin, acc, peak),
        scalars=(place,),
        scratch=(pltpu.VMEM((2, 4, 128, BLOCK), LOW), pltpu.VMEM((BLOCK, 128), LOW), four, four),
        flops=20 * 4 * BLOCK * BLOCK * 128,
        exps=20 * BLOCK * BLOCK,
        mib=24,
    )
    heads = across(heads)
    share, low_share = shape_of(64, 2048, kind=WIDE), shape_of(64, 2048)
    attended_low, *partial_branch = kernel_call(
        branch_kernel,
        (shape_of(BLOCK, 256), *[shape_of(128, 2048)] * 2, *[low_share] * 4),
        (*heads, w_out),
        scalars=(place,),
        scratch=(pltpu.VMEM((BLOCK, 2048), LOW), four),
        late=1,
        flops=2 * 512 * 256 * 2048,
    )
    to_above, to_below, to_other, own_part, other_part, far_part = partial_branch
    from_below, from_above = y_moved(to_above, 1), y_moved(to_below, 3)
    other_part, far_part = kernel_call(
        meet_kernel,
        (low_share, low_share),
        (from_below, from_above, swapped(to_other, "xl"), other_part, far_part),
        scalars=(place,),
        quick=True,
    )
    other_part, far_part = swapped(other_part, "xl"), y_moved(far_part, 2)
    second_share, middle, second_rows, stats2 = kernel_call(
        second_norm_kernel,
        (low_share, share, share, shape_of(64, 128, kind=WIDE)),
        (from_below, from_above, own_part, other_part, far_part, tok_share),
        scalars=(place,),
        small=(second_gain[None], second_shift[None]),
    )
    second_low = gathered(second_share)
    strip = shape_of(BLOCK, 704)
    hidden_low, grad_gate, grad_up, partial_second = kernel_call(
        feed_kernel,
        (strip, strip, strip, shape_of(BLOCK, 2048)),
        (second_low, (w2, 0, 1), (w2, 1, 1), grad_hidden),
        scalars=(place,),
        late=2,
        flops=8 * 512 * 2048 * 704,
        mib=24,
    )
    second_parts = tp_parts(partial_second)

    feed_mine, feed_theirs = weight_grads(
        ((grad_gate, second_low), (grad_up, second_low), (hidden_low, cotangent)), place
    )
    second_parts, feed_mine, feed_theirs = tied((second_parts, feed_mine, feed_theirs))
    copies, grad_middle, second_sums = kernel_call(
        second_gradient_kernel,
        (shape_of(8, 64, 2048), share),
        (second_parts, cot_share, second_rows, stats2),
        moved=1,
        small=(second_gain[None],),
        small_outs=(shape_of(2, 2048, kind=WIDE),),
    )
    grad_branch = dealt(copies, TP).reshape(BLOCK, 2048)
    partial_feed = jnp.dot(hidden_low, w_down, preferred_element_type=WIDE).astype(LOW)
    grad_branch, partial_feed = tied((grad_branch, partial_feed))
    feed_z = z_parts(feed_mine, swapped(feed_theirs, "core"))
    feed_1, feed_3 = z_permute(feed_z[1], 1), z_permute(feed_z[3], 3)
    grads = kernel_call(
        grad_attended_kernel,
        (*[quarter] * 4,),
        (grad_branch, w_out),
        moved=1,
        scalars=(place,),
        scratch=(four,),
        flops=2 * 512 * 256 * 2048,
    )
    feed_1, feed_3, partial_feed, *grads = tied((feed_1, feed_3, partial_feed, *grads))
    feed_parts = dealt(partial_feed.reshape(4, 128, 2048), "y")
    *grads, feed_2 = tied((*across(grads), feed_z[2]))
    feed_2 = z_permute(feed_2, 2)
    scratch = (
        pltpu.VMEM((2, 4, 128, BLOCK), LOW),
        pltpu.VMEM((BLOCK, 128), LOW),
        pltpu.VMEM((BLOCK, 128), LOW),
        pltpu.VMEM((1, BLOCK), WIDE),
        pltpu.VMEM((2, 4, BLOCK, 128), WIDE),
        four,
        four,
    )
    blocks = shape_of(4, BLOCK, 128)
    acc, keep1, send1 = kernel_call(
        functools.partial(backward_kernel, (2, 3), True),
        (state[0], blocks, blocks),
        (kv_z, kv_zc, *queries, *grads, out_t, total, begin),
        scalars=(place,),
        scratch=scratch,
        flops=20 * 10 * BLOCK * BLOCK * 128,
        exps=20 * BLOCK * BLOCK,
        mib=28,
    )
    acc, send1, feed_parts, feed_2 = tied((acc, send1, feed_parts, feed_2))
    (feed_half,) = kernel_call(
        feed_sum_kernel,
        (shape_of(128, 2048),),
        (feed_parts, middle),
        scalars=(place,),
        moved=1,
    )
    far = (keep1.astype(WIDE) + swapped(send1, "core").astype(WIDE)).astype(LOW)
    acc, far, feed_half = tied((acc, far, feed_half))
    near = kernel_call(
        functools.partial(backward_kernel, (0, 1), False),
        (*[quarter] * 4, blocks, blocks),
        (kv, kv_c, *queries, *grads, out_t, total, begin, acc),
        scalars=(place,),
        scratch=(*scratch, pltpu.VMEM((4, 128, BLOCK), WIDE), four),
        flops=20 * 10 * BLOCK * BLOCK * 128,
        exps=20 * BLOCK * BLOCK,
        mib=28,
    )
    *near, far, feed_other = tied((*near, swapped(far, "zl"), swapped(feed_half, "xl")))
    *grad_queries, keep0, send0 = near
    pieces = kernel_call(
        join_kernel,
        (*[piece] * 4,),
        (keep0, swapped(send0, "core"), far, *grad_queries),
    )
    (copies4,) = kernel_call(layer_out_kernel, (shape_of(4, 128, 2048),), (feed_half, feed_other))
    *pieces, copies4, feed_0, feed_1, feed_2, feed_3 = tied(
        (*pieces, copies4, feed_z[0], feed_1, feed_2, feed_3)
    )
    feed_keep, feed_send = xh_halves([feed_0, feed_1, feed_2, feed_3])
    *pieces, feed_send = tied((*across(pieces), feed_send))
    feed_received = swapped(feed_send, "xh")
    layer_out = dealt(copies4, "y")
    grad_mixed, partial_normed, gain_sum, shift_sum, bias_sum = kernel_call(
        grad_project_kernel,
        (shape_of(BLOCK, 768), shape_of(BLOCK, 2048)),
        (*pieces, cosine, sine, tokens, stats1, w3),
        small_outs=(
            shape_of(1, 2048, kind=WIDE),
            shape_of(1, 2048, kind=WIDE),
            shape_of(3, 256, kind=WIDE),
        ),
        scalars=(place,),
        scratch=(pltpu.VMEM((4, BLOCK, 128), LOW), four),
        late=3,
        flops=2 * 512 * 2048 * 768,
    )
    partial_normed, layer_out = tied((partial_normed, layer_out))
    layer_out = settled(layer_out)
    normed_parts = tp_parts(partial_normed)

    rest_mine, rest_theirs = weight_grads(
        ((grad_mixed, normed_low), (attended_low, grad_branch)), place
    )
    rest_mine, rest_theirs, feed_received = tied((rest_mine, rest_theirs, feed_received))
    rest_z = z_parts(rest_mine, swapped(rest_theirs, "core"))
    vectors = jnp.concatenate([gain_sum, shift_sum, second_sums], axis=0).reshape(32, 256)
    vectors = jnp.concatenate([vectors, bias_sum], axis=0)
    vectors = summed_by_pairs(vectors, (("core", 2, 1), ("zl", 2, 1), ("zh", 2, 1)))
    vectors, *rest_z = tied((vectors, *rest_z))
    vectors = summed_by_pairs(vectors, (("xh", 2, 1),))
    rest_1, rest_3 = z_permute(rest_z[1], 1), z_permute(rest_z[3], 3)
    normed_parts, vectors = tied((normed_parts, vectors))
    bias_grad = vectors[32:]
    (last_share,) = kernel_call(
        first_gradient_kernel,
        (shape_of(64, 2048 + 128),),
        (normed_parts, grad_middle, tok_share, my_share(stats1), vectors[:32].reshape(64, 128)),
        moved=1,
        small=(first_gain[None],),
    )
    last_shares, rest_1, rest_3 = gathered(last_share, rest_1, rest_3)
    grad_tokens, vectors = last_call(last_shares, place)
    vectors = vectors.reshape(4, 2048)
    rest_z = (rest_z[0], rest_1, z_permute(rest_z[2], 2), rest_3)
    rest_keep, rest_send = xh_halves(rest_z)
    rest_w = rest_keep + swapped(rest_send, "xh").astype(WIDE)
    feed_w = feed_keep + feed_received.astype(WIDE)
    return (
        layer_out,
        grad_tokens,
        vectors[0],
        vectors[1],
        vectors[2],
        vectors[3],
        jnp.transpose(rest_w[:768].reshape(3, 256, 128), (2, 0, 1)),
        bias_grad,
        rest_w[768:],
        jnp.transpose(feed_w[:1408].reshape(2, 704, 128), (2, 0, 1)),
        feed_w[1408:],
    )


def solution(mesh):
    fine = Mesh(
        mesh.devices.reshape(2, 2, 2, 2, 4, 2), ("xh", "zh", "zl", "core", "y", "xl")
    )
    rows = P(CTX, None)
    return jax.shard_map(
        body,
        mesh=fine,
        in_specs=(
            rows, rows, P(), P(), P(), P(), P(),
            P(None, None, TP), P(None, TP), P(TP, None), P(None, None, TP), P(TP, None),
        ),
        out_specs=(
            rows, rows, P(), P(), P(), P(),
            P(CTX, None, TP), P(None, TP), P(TP, CTX), P(CTX, None, TP), P(TP, CTX),
        ),
        check_vma=False,
    )
```

```python
import functools

import jax
import jax.numpy as jnp
from jax import lax
from jax.experimental import pallas as pl
from jax.experimental.pallas import tpu as pltpu
from jax.sharding import Mesh
from jax.sharding import PartitionSpec as P

HDIM = 64
DOCS = 3
BLOCK = 512
HALF = 256
LOW = jnp.bfloat16
WIDE = jnp.float32
CTX = ("xh", "zh", "zl", "core")
TP = ("y", "xl")
SPREAD = ("xh", "zh")
Z = ("zh", "zl")


def size_of(a):
    return a.size * jnp.dtype(a.dtype).itemsize


def gathered_order(place):
    x, y = place[3], place[4]
    row = [lax.rem(y + k, 4) * 2 for k in range(4)]
    other = 1 - x
    return [
        row[0] + x, row[0] + other,
        row[3] + x, row[1] + x, row[2] + x,
        row[3] + other, row[1] + other, row[2] + other,
    ]


def deal_rows(place, rows, outs):
    x, y = place[3], place[4]
    far = lax.rem(y + 2, 4)
    firsts = [
        lax.rem(y + 1, 4) * 2, lax.rem(y + 3, 4) * 2,
        far * 2 + 1 - x, y * 2 + x, y * 2 + 1 - x, far * 2 + x,
    ]
    for first, out in zip(firsts, outs):
        out[...] = rows[pl.ds(pl.multiple_of(first * 64, 64), out.shape[0]), :]


def meet_kernel(place, below, above, crossed, other, far, out_other, out_far):
    column = pl.multiple_of((1 - place[3]) * 64, 64)

    def work(at):
        there = pl.ds(pl.multiple_of(column + at.start, 16), at.size)
        total = other[at, :].astype(WIDE) + below[there, :].astype(WIDE) + above[there, :].astype(WIDE)
        out_other[at, :] = total.astype(LOW)
        out_far[at, :] = (far[at, :].astype(WIDE) + crossed[at, :].astype(WIDE)).astype(LOW)

    for_rows(work)


def kernel_call(
    body, outs, inputs, *, small=(), small_outs=(), scalars=(), scratch=(), late=0, flops=0, exps=0, mib=12, quick=False, moved=0,
    leaving=False,
):
    inputs = [a if isinstance(a, (tuple, list)) else (a, 0, a.shape[0]) for a in inputs]
    flat = [x for a in inputs for x in (a if isinstance(a, list) else a[:1])]
    counts = [len(x) for x in (scalars, flat, small, outs, small_outs, inputs, outs)]

    def run(*refs):
        groups, at = [], 0
        for n in counts:
            groups.append(refs[at : at + n])
            at += n
        scalar_refs, far_in, near_in, far_out, near_out, held_in, held_out = groups
        arrived, left, *rest = refs[at:]
        pairs, ends = [], []
        for a, held in zip(inputs, held_in):
            if isinstance(a, list):
                rows = a[0].shape[0]
                for index in gathered_order(scalar_refs[0]):
                    pairs.append((None, held.at[pl.ds(pl.multiple_of(index * rows, rows), rows)]))
            else:
                pairs.append((pl.ds(a[1], a[2]), held))
            ends.append(len(pairs))
        moves = [
            pltpu.make_async_copy(x if part is None else x.at[part], held, arrived.at[k])
            for k, (x, (part, held)) in enumerate(zip(far_in, pairs))
        ]
        for move in moves:
            move.start()
        early = ends[len(inputs) - late - 1]
        for move in moves[:early]:
            move.wait()

        def arrive():
            for move in moves[early:]:
                move.wait()

        outward = [
            pltpu.make_async_copy(a, b, left.at[k]) for k, (a, b) in enumerate(zip(held_out, far_out))
        ]
        gone = []

        def leave(*which):
            for k in which:
                outward[k].start()
                gone.append(k)

        body(
            *([arrive] if late else []),
            *([leave] if leaving else []),
            *scalar_refs, *held_in, *near_in, *held_out, *near_out, *rest,
        )
        leave(*[k for k in range(len(outward)) if k not in gone])
        for move in outward:
            move.wait()

    vmem, hbm = pl.BlockSpec(memory_space=pltpu.VMEM), pl.BlockSpec(memory_space=pltpu.HBM)
    taken = [
        shape_of(8 * a[0].shape[0], a[0].shape[1], kind=a[0].dtype)
        if isinstance(a, list)
        else shape_of(a[2], *a[0].shape[1:], kind=a[0].dtype)
        for a in inputs
    ]
    held = [pltpu.VMEM(a.shape, a.dtype) for a in (*taken, *outs)]
    limit = sum(size_of(a) for a in (*taken, *outs, *small, *small_outs)) + mib * 1024 * 1024
    return pl.pallas_call(
        run,
        out_shape=(*[pltpu.HBM(a.shape, a.dtype) for a in outs], *small_outs),
        in_specs=[pl.BlockSpec(memory_space=pltpu.SMEM)] * len(scalars)
        + [pl.BlockSpec(memory_space=pl.ANY)] * moved
        + [hbm] * (len(flat) - moved)
        + [vmem] * len(small),
        out_specs=(*[hbm] * len(outs), *[vmem] * len(small_outs)),
        scratch_shapes=[
            *held,
            pltpu.SemaphoreType.DMA((len(flat),)),
            pltpu.SemaphoreType.DMA((max(1, len(outs)),)),
            *scratch,
        ],
        compiler_params=pltpu.CompilerParams(vmem_limit_bytes=limit),
        cost_estimate=pl.CostEstimate(
            flops=flops,
            bytes_accessed=0 if quick else sum(size_of(a) for a in (*taken, *outs)),
            transcendentals=exps,
        ),
    )(
        *scalars,
        *flat[:moved],
        *[pltpu.with_memory_space_constraint(a, pltpu.HBM) for a in flat[moved:]],
        *small,
    )


def lane_of(shape):
    return lax.broadcasted_iota(jnp.int32, shape, len(shape) - 1)


def exchange_halves(a, b):
    front = lane_of(a.shape) < HDIM
    return (
        jnp.where(front, a, pltpu.roll(b, HDIM, 1)),
        jnp.where(front, pltpu.roll(a, HDIM, 1), b),
    )


def nt(a, b):
    return lax.dot_general(a, b, (((1,), (1,)), ((), ())), preferred_element_type=WIDE)


def nn(a, b):
    return lax.dot_general(a, b, (((1,), (0,)), ((), ())), preferred_element_type=WIDE)


def turn(x, cosine, sine, sign):
    lane = lax.rem(lane_of(x.shape), HDIM)
    ahead = pltpu.roll(x, x.shape[1] - 8, 1)
    behind = pltpu.roll(x, 8, 1)
    swapped = jnp.where(lane < 8, -ahead, behind) * sign
    return x * cosine + swapped * sine


def rotation_table(angles_table):
    tokens = angles_table.shape[1]
    rest = jnp.zeros((112, tokens), WIDE)
    x = jnp.concatenate([angles_table, rest], axis=0).T
    lane = lane_of(x.shape)
    c = jnp.where(lane < 8, x, 0.0)
    c = c + pltpu.roll(c, 8, 1)
    c = c + pltpu.roll(c, HDIM, 1) + jnp.where(lax.rem(lane, HDIM) < 16, 0.0, 1.0)
    s = jnp.where((lane >= 8) & (lane < 16), x, 0.0)
    s = s + pltpu.roll(s, 120, 1)
    s = s + pltpu.roll(s, HDIM, 1)
    return c, s


def project_kernel(
    arrive, leave, place, tok, table, w, gain, shift, bias,
    normed, stats, x0, x1, x2, x3, cosine_out, sine_out, kept,
):
    rows = 64

    def norm_rows(i, carry):
        at = pl.ds(pl.multiple_of(i * rows, rows), rows)
        x = tok[at, :].astype(WIDE)
        mean = jnp.mean(x, axis=-1, keepdims=True)
        center = x - mean
        scale = lax.rsqrt(jnp.mean(center * center, axis=-1, keepdims=True) + 1e-05)
        normed[at, :] = (center * scale * gain[...] + shift[...]).astype(LOW)
        stats[at, :] = jnp.where(lane_of((rows, 128)) < HDIM, mean, scale)
        return carry

    lax.fori_loop(0, BLOCK // rows, norm_rows, 0)
    cosine, sine = rotation_table(table[...])
    cosine_out[...] = cosine
    sine_out[...] = sine
    leave(0, 1, 6, 7)
    arrive()
    mixed = [nn(normed[...], w[c]) + bias[c : c + 1, :] for c in range(3)]
    for pair in range(2):
        lanes = slice(pair * 128, pair * 128 + 128)
        q = turn(mixed[0][:, lanes], cosine, sine, 1.0) * 0.125
        k = turn(mixed[1][:, lanes], cosine, sine, 1.0)
        kv = exchange_halves(k, mixed[2][:, lanes])
        qq = exchange_halves(q[:HALF], q[HALF:])
        for one in range(2):
            kept[2 * pair + one, :BLOCK, :] = kv[one].astype(LOW)
            kept[2 * pair + one, BLOCK:, :] = qq[one].astype(LOW)
    for k, out in enumerate((x0, x1, x2, x3)):
        out[...] = kept[place[1] ^ k]


def padded_queries(q2):
    x = q2.astype(WIDE)
    front = lane_of(x.shape) < HDIM
    return (
        jnp.where(front, x, 0.0).astype(LOW),
        jnp.where(front, pltpu.roll(x, HDIM, 1), 0.0).astype(LOW),
    )


def padded_behind(d2):
    x = d2.astype(WIDE)
    front = lane_of(x.shape) < HDIM
    return (
        jnp.where(front, 0.0, pltpu.roll(x, HDIM, 1)).astype(LOW),
        jnp.where(front, 0.0, x).astype(LOW),
    )


def allowed_keys(key_block, first_query, begin):
    shape = (BLOCK, begin.shape[1])
    key_at = key_block * BLOCK + lax.broadcasted_iota(jnp.int32, shape, 0)
    query_at = first_query + lax.broadcasted_iota(jnp.int32, shape, 1)
    return (key_at <= query_at) & (key_at >= begin)


def for_steps(count, work):
    def pair(i, carry):
        work([2 * i, 2 * i + 1])
        return carry

    lax.fori_loop(0, count // 2, pair, 0)

    @pl.when(lax.rem(count, 2) == 1)
    def _():
        work([count - 1])


def key_blocks(place, rels, t):
    return [4 * t + (place[0] ^ rel) for rel in rels], place[1] ^ t


def forward_kernel(rels, first, last, *refs):
    place, kv0, kv1, q0, q1, q2, q3, begin = refs[:8]
    if first:
        acc_out, peak_out, kvt, queries, kept_q = refs[8:]
    else:
        acc_in, peak_in, o0, o1, o2, o3, out_t, total, kvt, queries, kept_q, kept_o = refs[8:]
        acc_out, peak_out = out_t, total
    me = place[1]
    front = lane_of((BLOCK, 128)) < HDIM
    for k, q in enumerate((q0, q1, q2, q3)):
        kept_q[me ^ k] = q[...]
    for i, kv in enumerate((kv0, kv1)):
        for t in range(4):
            kvt[i, t] = jnp.where(front, 1.0, kv[t].astype(WIDE)).T.astype(LOW)

    def one_query_block(j, carry):
        first_query = (4 * j + place[0]) * BLOCK
        queries[:HALF, :], queries[HALF:, :] = padded_queries(kept_q[j])
        if first:
            peak_out[j] = jnp.full((8, BLOCK), -1e30, WIDE)
            acc_out[j] = jnp.zeros((128, BLOCK), WIDE)
        else:
            peak_out[j] = peak_in[j]
            acc_out[j] = acc_in[j]

        def some_blocks(steps):
            scores, sources = [], []
            for t in steps:
                blocks, at = key_blocks(place, rels, t)
                for i, kv in enumerate((kv0, kv1)):
                    ok = allowed_keys(blocks[i], first_query, begin[j, :1])
                    scores.append(jnp.where(ok, nt(kv[at], queries[...]), -1e30))
                    sources.append((i, at))
            old = peak_out[j, :1]
            new = old
            for one in scores:
                new = jnp.maximum(new, jnp.max(one, axis=0, keepdims=True))
            done = acc_out[j] * jnp.exp(old - new)
            for one, (i, at) in zip(scores, sources):
                done += nn(kvt[i, at], jnp.exp(one - new).astype(LOW))
            acc_out[j] = done
            peak_out[j, :1] = new

        for_steps(j + 1, some_blocks)
        if last:
            weight_sum = acc_out[j, :1]
            done = acc_out[j] / weight_sum
            out_t[j] = done
            total[j, :1] = peak_out[j, :1] + jnp.log(weight_sum)
            rows = done.T
            x, y = rows[:HALF], rows[HALF:]
            kept_o[j] = jnp.where(lane_of(x.shape) < HDIM, pltpu.roll(x, HDIM, 1), y).astype(LOW)
        return carry

    lax.fori_loop(0, 4, one_query_block, 0)
    if last:
        for k, out in enumerate((o0, o1, o2, o3)):
            out[...] = kept_o[me ^ k]


def backward_kernel(rels, first, *refs):
    place, kv0, kv1, q0, q1, q2, q3, d0, d1, d2, d3, out_t, total, begin = refs[:14]
    if first:
        acc, keep, send, kvt, queries, grads, dot_rows, dkv, kept_q, kept_d = refs[14:]
    else:
        (
            acc_in, g0, g1, g2, g3, keep, send,
            kvt, queries, grads, dot_rows, dkv, kept_q, kept_d, acc, kept_g,
        ) = refs[14:]
    me = place[1]
    for k in range(4):
        kept_q[me ^ k] = (q0, q1, q2, q3)[k][...]
        kept_d[me ^ k] = (d0, d1, d2, d3)[k][...]
    for i, kv in enumerate((kv0, kv1)):
        for t in range(4):
            kvt[i, t] = kv[t].astype(WIDE).T.astype(LOW)
    dkv[...] = jnp.zeros(dkv.shape, WIDE)

    def one_query_block(j, carry):
        first_query = (4 * j + place[0]) * BLOCK
        queries[:HALF, :], queries[HALF:, :] = padded_queries(kept_q[j])
        grads[:HALF, :], grads[HALF:, :] = padded_behind(kept_d[j])
        dot_rows[...] = jnp.sum(grads[...].astype(WIDE).T * out_t[j], axis=0, keepdims=True)
        acc[j] = jnp.zeros((128, BLOCK), WIDE) if first else acc_in[j]

        def some_blocks(steps):
            for t in steps:
                blocks, at = key_blocks(place, rels, t)
                for i, kv in enumerate((kv0, kv1)):
                    term = 0.0
                    for half in range(2):
                        some = slice(half * HALF, half * HALF + HALF)
                        ok = allowed_keys(blocks[i], first_query + half * HALF, begin[j, :1, some])
                        scores = nt(kv[at], queries[some, :])
                        probs = jnp.where(ok, jnp.exp(scores - total[j, :1, some]), 0.0)
                        grad_probs = nt(kv[at], grads[some, :])
                        grad_scores = (probs * (grad_probs - dot_rows[:, some])).astype(LOW)
                        term += nn(grad_scores, queries[some, :])
                        term += nn(probs.astype(LOW), grads[some, :])
                        acc[j, :, some] += nn(kvt[i, at], grad_scores)
                    dkv[i, at] += term

        for_steps(j + 1, some_blocks)
        if not first:
            rows = acc[j].T
            x, y = rows[:HALF], rows[HALF:]
            kept_g[j] = jnp.where(lane_of(x.shape) < HDIM, x, pltpu.roll(y, HDIM, 1)).astype(LOW)
        return carry

    lax.fori_loop(0, 4, one_query_block, 0)
    if not first:
        for k, out in enumerate((g0, g1, g2, g3)):
            out[...] = kept_g[me ^ k]
    for t in range(4):
        keep[t] = dkv[0, t].astype(LOW)
        send[t] = dkv[1, t].astype(LOW)


def branch_kernel(arrive, place, h0, h1, h2, h3, w, attended, *refs):
    outs, (partial, kept) = refs[:6], refs[6:]
    for k, h in enumerate((h0, h1, h2, h3)):
        kept[place[1] ^ k] = h[...]
    for pair in range(2):
        lanes = slice(pair * 128, pair * 128 + 128)
        x, y = exchange_halves(kept[2 * pair].astype(WIDE), kept[2 * pair + 1].astype(WIDE))
        attended[:HALF, lanes] = x.astype(LOW)
        attended[HALF:, lanes] = y.astype(LOW)
    arrive()
    for n in range(4):
        at = slice(n * 512, n * 512 + 512)
        partial[:, at] = nn(attended[...], w[:, at]).astype(LOW)
    deal_rows(place, partial, outs)


def grad_attended_kernel(place, grad, w, d0, d1, d2, d3, kept):
    g = nt(grad[...], w[...])
    for pair in range(2):
        lanes = slice(pair * 128, pair * 128 + 128)
        both = exchange_halves(g[:HALF, lanes], g[HALF:, lanes])
        for one in range(2):
            kept[2 * pair + one] = both[one].astype(LOW)
    for k, out in enumerate((d0, d1, d2, d3)):
        out[...] = kept[place[1] ^ k]


def join_kernel(keep, received, far, g0, g1, g2, g3, x0, x1, x2, x3):
    for k in range(4):
        total = keep[k].astype(WIDE) + received[k].astype(WIDE) + far[k].astype(WIDE)
        out = (x0, x1, x2, x3)[k]
        out[:BLOCK, :] = total.astype(LOW)
        out[BLOCK:, :] = (g0, g1, g2, g3)[k][...]


def grad_project_kernel(
    arrive, place, x0, x1, x2, x3, cosine, sine, tok, stats, w,
    grad_mixed, partial, gain_sum, shift_sum, bias_sum, parts, kept,
):
    for k, x in enumerate((x0, x1, x2, x3)):
        parts[place[1] ^ k] = x[:BLOCK, :]
        kept[place[1] ^ k] = x[BLOCK:, :]
    for pair in range(2):
        lanes = slice(pair * 128, pair * 128 + 128)
        k, v = exchange_halves(parts[2 * pair].astype(WIDE), parts[2 * pair + 1].astype(WIDE))
        q = exchange_halves(kept[2 * pair].astype(WIDE), kept[2 * pair + 1].astype(WIDE))
        q = jnp.concatenate(q, axis=0)
        q = turn(q, cosine[...], sine[...], -1.0) * 0.125
        k = turn(k, cosine[...], sine[...], -1.0)
        for c, part in enumerate((q, k, v)):
            start = c * 256 + pair * 128
            low = part.astype(LOW)
            grad_mixed[:, start : start + 128] = low
            bias_sum[c : c + 1, lanes] = jnp.sum(low.astype(WIDE), axis=0, keepdims=True)
    arrive()
    mean, scale = stats[:, 0:1], stats[:, 64:65]
    for n in range(4):
        at = slice(n * 512, n * 512 + 512)
        total = nt(grad_mixed[:, :256], w[0, at, :])
        total += nt(grad_mixed[:, 256:512], w[1, at, :])
        total += nt(grad_mixed[:, 512:], w[2, at, :])
        partial[:, at] = total.astype(LOW)
        normal = (tok[:, at].astype(WIDE) - mean) * scale
        gain_sum[:, at] = jnp.sum(total * normal, axis=0, keepdims=True)
        shift_sum[:, at] = jnp.sum(total, axis=0, keepdims=True)


def hidden_gradient_kernel(cot, w, grad_hidden):
    grad_hidden[...] = nt(cot[...], w[...])


def feed_kernel(arrive, leave, place, second, w_gate, w_up, grad_hidden, hidden, grad_gate, grad_up, partial):
    gate = nt(second[...], w_gate[0])
    arrive()
    up = nt(second[...], w_up[0])
    sigmoid = 1.0 / (1.0 + jnp.exp(-gate))
    activated = gate * sigmoid
    hidden[...] = (activated * up).astype(LOW)
    grad = grad_hidden[...]
    grad_up[...] = (grad * activated).astype(LOW)
    grad_gate[...] = (grad * up * sigmoid * (1.0 + gate * (1.0 - sigmoid))).astype(LOW)
    leave(0, 1, 2)
    for n in range(4):
        at = slice(n * 512, n * 512 + 512)
        partial[:, at] = (nn(grad_gate[...], w_gate[0, :, at]) + nn(grad_up[...], w_up[0, :, at])).astype(LOW)


def for_rows(work):
    rows = 16

    def one(i, carry):
        work(pl.ds(pl.multiple_of(i * rows, rows), rows))
        return carry

    lax.fori_loop(0, 64 // rows, one, 0)


def summed(parts, at):
    total = parts[0, at, :].astype(WIDE)
    for k in range(1, 8):
        total += parts[k, at, :].astype(WIDE)
    return total


def second_norm_kernel(
    place, below, above, own, other, far, tok, gain, shift, low, middle, normal, stats
):
    column = pl.multiple_of(place[3] * 64, 64)

    def work(at):
        there = pl.ds(pl.multiple_of(column + at.start, 16), at.size)
        x = tok[at, :].astype(WIDE) + own[at, :].astype(WIDE)
        x += below[there, :].astype(WIDE) + above[there, :].astype(WIDE)
        x += other[at, :].astype(WIDE) + far[at, :].astype(WIDE)
        center = x - jnp.mean(x, axis=-1, keepdims=True)
        scale = lax.rsqrt(jnp.mean(center * center, axis=-1, keepdims=True) + 1e-05)
        rows = center * scale
        low[at, :] = (rows * gain[...] + shift[...]).astype(LOW)
        middle[at, :] = x
        normal[at, :] = rows
        stats[at, :] = jnp.broadcast_to(scale, (scale.shape[0], 128))

    for_rows(work)


def norm_gradient(grad, rows, scale, gain):
    scaled = grad * gain
    return scale * (
        scaled
        - jnp.mean(scaled, axis=-1, keepdims=True)
        - rows * jnp.mean(scaled * rows, axis=-1, keepdims=True)
    )


def second_gradient_kernel(parts, cot, normal, stats, gain, copies, grad_middle, sums):
    sums[...] = jnp.zeros(sums.shape, WIDE)

    def work(at):
        grad, rows = summed(parts, at), normal[at, :]
        done = cot[at, :].astype(WIDE) + norm_gradient(grad, rows, stats[at, 0:1], gain[...])
        low = done.astype(LOW)
        for k in range(8):
            copies[k, at, :] = low
        grad_middle[at, :] = done
        sums[0:1, :] += jnp.sum(grad * rows, axis=0, keepdims=True)
        sums[1:2, :] += jnp.sum(grad, axis=0, keepdims=True)

    for_rows(work)


def feed_sum_kernel(place, parts, middle, out):
    rows = 16
    mine = place[3]

    def one(i, carry):
        at = pl.ds(pl.multiple_of(i * rows, rows), rows)
        total = parts[0, at, :].astype(WIDE)
        for k in range(1, 4):
            total += parts[k, at, :].astype(WIDE)
        here = i * rows - mine * 64
        own = pl.ds(pl.multiple_of(jnp.clip(here, 0, 64 - rows), rows), rows)
        inside = (here >= 0) & (here < 64)
        out[at, :] = (total + jnp.where(inside, middle[own, :], 0.0)).astype(LOW)
        return carry

    lax.fori_loop(0, 128 // rows, one, 0)


def layer_out_kernel(a, b, copies):
    rows = 16

    def one(i, carry):
        at = pl.ds(pl.multiple_of(i * rows, rows), rows)
        low = (a[at, :].astype(WIDE) + b[at, :].astype(WIDE)).astype(LOW)
        for k in range(4):
            copies[k, at, :] = low
        return carry

    lax.fori_loop(0, 128 // rows, one, 0)


def first_gradient_kernel(parts, grad_middle, tok, stats, vectors, gain, low):
    def work(at):
        mean, scale = stats[at, 0:1], stats[at, 64:65]
        rows = (tok[at, :].astype(WIDE) - mean) * scale
        done = norm_gradient(summed(parts, at), rows, scale, gain[...])
        low[at, :2048] = (grad_middle[at, :] + done).astype(LOW)
        low[at, 2048:] = vectors[at, :].astype(LOW)

    for_rows(work)


def last_kernel(place, *refs):
    shares, (out, total, held, came, went) = refs[:8], refs[8:]
    moves = []
    for k, (x, index) in enumerate(zip(shares, gathered_order(place))):
        at = pl.ds(pl.multiple_of(index * 64, 64), 64)
        moves.append(
            (
                pltpu.make_async_copy(x, held.at[k], came.at[k]),
                pltpu.make_async_copy(held.at[k, :, pl.ds(0, 2048)], out.at[at], went.at[k]),
            )
        )
    for come, _ in moves:
        come.start()
    for come, go in moves:
        come.wait()
        go.start()
    done = held[0, :, 2048:].astype(WIDE)
    for k in range(1, 8):
        done += held[k, :, 2048:].astype(WIDE)
    total[...] = done
    for _, go in moves:
        go.wait()


def last_call(shares, place):
    hbm = pl.BlockSpec(memory_space=pltpu.HBM)
    return pl.pallas_call(
        last_kernel,
        out_shape=(pltpu.HBM((BLOCK, 2048), LOW), shape_of(64, 128, kind=WIDE)),
        in_specs=[pl.BlockSpec(memory_space=pltpu.SMEM), *[hbm] * 8],
        out_specs=(hbm, pl.BlockSpec(memory_space=pltpu.VMEM)),
        scratch_shapes=[
            pltpu.VMEM((8, 64, 2048 + 128), LOW),
            pltpu.SemaphoreType.DMA((8,)),
            pltpu.SemaphoreType.DMA((8,)),
        ],
        compiler_params=pltpu.CompilerParams(vmem_limit_bytes=8 * 1024 * 1024),
        cost_estimate=pl.CostEstimate(flops=0, bytes_accessed=0, transcendentals=0),
    )(place, *[pltpu.with_memory_space_constraint(a, pltpu.HBM) for a in shares])


def weight_kernel(widths, sources, arrive, place, *refs):
    count = max(max(pair) for pair in sources) + 1
    inputs = refs[:count]
    mine, theirs, turned = refs[count:]
    first_core = place[2] == 0
    start = 0
    for n, ((left, right), width) in enumerate(zip(sources, widths)):
        if n == 1:
            arrive()
        left, right = inputs[left], inputs[right]
        turned[:width, :] = left[...].astype(WIDE).T.astype(LOW)

        def one(n, carry, start=start, right=right, width=width):
            columns = right[:, pl.ds(pl.multiple_of(n * 256, 256), 256)]
            both = nn(turned[:width, :], columns)
            first, second = both[:, :128], both[:, 128:]
            at = pl.ds(start, width)
            mine[n, at, :] = jnp.where(first_core, first, second).astype(LOW)
            theirs[n, at, :] = jnp.where(first_core, second, first).astype(LOW)
            return carry

        lax.fori_loop(0, 8, one, 0, unroll=4)
        start += width


def weight_grads(pairs, place):
    inputs, sources = [], []
    for pair in pairs:
        for a in pair:
            if not any(a is b for b in inputs):
                inputs.append(a)
        sources.append(tuple(next(k for k, b in enumerate(inputs) if b is a) for a in pair))
    widths = tuple(a.shape[1] for a, _ in pairs)
    out = jax.ShapeDtypeStruct((8, sum(widths), 128), LOW)
    return kernel_call(
        functools.partial(weight_kernel, widths, sources),
        (out, out),
        inputs,
        scalars=(place,),
        scratch=(pltpu.VMEM((max(widths), BLOCK), LOW),),
        late=len(inputs) - 2,
        quick=True,
    )


def swapped(x, axis):
    return lax.ppermute(x, axis, [(0, 1), (1, 0)])


def across(pieces):
    moved = [
        lax.ppermute(pieces[k], SPREAD, [(i, i ^ k) for i in range(4)]) for k in range(1, 4)
    ]
    return (pieces[0], *moved)


def z_parts_kernel(place, mine, received, *refs):
    outs, (held_a, held_b, done, came, went) = refs[:4], refs[4:]
    z = place[0]
    order = [(k, xh) for k in (1, 3, 2, 0) for xh in range(2)]
    moves = []
    for n, (k, xh) in enumerate(order):
        at = xh * 4 + lax.rem(z + k, 4)
        moves.append(
            (
                pltpu.make_async_copy(mine.at[at], held_a.at[n], came.at[2 * n]),
                pltpu.make_async_copy(received.at[at], held_b.at[n], came.at[2 * n + 1]),
                pltpu.make_async_copy(done.at[n], outs[k].at[xh], went.at[n]),
            )
        )
    for a, b, _ in moves:
        a.start()
        b.start()
    for n, (a, b, out) in enumerate(moves):
        a.wait()
        b.wait()
        done[n] = (held_a[n].astype(WIDE) + held_b[n].astype(WIDE)).astype(LOW)
        out.start()
    for _, _, out in moves:
        out.wait()


def z_parts(mine, received):
    rows = mine.shape[1]
    hbm = pl.BlockSpec(memory_space=pltpu.HBM)
    held = pltpu.VMEM((8, rows, 128), LOW)
    return pl.pallas_call(
        z_parts_kernel,
        in_specs=[pl.BlockSpec(memory_space=pltpu.SMEM), hbm, hbm],
        out_specs=[hbm] * 4,
        out_shape=[pltpu.HBM((2, rows, 128), LOW)] * 4,
        scratch_shapes=[
            held,
            held,
            held,
            pltpu.SemaphoreType.DMA((16,)),
            pltpu.SemaphoreType.DMA((8,)),
        ],
        compiler_params=pltpu.CompilerParams(vmem_limit_bytes=24 * 1024 * 1024),
        cost_estimate=pl.CostEstimate(flops=0, bytes_accessed=0, transcendentals=0),
    )(
        lax.axis_index(Z).reshape(1),
        *[pltpu.with_memory_space_constraint(a, pltpu.HBM) for a in (mine, received)],
    )


def settled_kernel(x, out, held, came, went):
    rows = x.shape[1]
    moves = []
    for k in range(x.shape[0]):
        at = pl.ds(k * rows, rows)
        moves.append(
            (
                pltpu.make_async_copy(x.at[k], held.at[k], came.at[k]),
                pltpu.make_async_copy(held.at[k, :, pl.ds(0, 2048)], out.at[at], went.at[k]),
            )
        )
    for come, _ in moves:
        come.start()
    for come, go in moves:
        come.wait()
        go.start()
    for _, go in moves:
        go.wait()


def settled(x):
    hbm = pl.BlockSpec(memory_space=pltpu.HBM)
    parts, rows = x.shape[:2]
    return pl.pallas_call(
        settled_kernel,
        out_shape=pltpu.HBM((parts * rows, 2048), x.dtype),
        in_specs=[pl.BlockSpec(memory_space=pl.ANY)],
        out_specs=hbm,
        scratch_shapes=[
            pltpu.VMEM(x.shape, x.dtype),
            pltpu.SemaphoreType.DMA((parts,)),
            pltpu.SemaphoreType.DMA((parts,)),
        ],
        compiler_params=pltpu.CompilerParams(vmem_limit_bytes=8 * 1024 * 1024),
        cost_estimate=pl.CostEstimate(flops=0, bytes_accessed=0, transcendentals=0),
    )(x)


def z_permute(part, distance):
    return lax.ppermute(part, Z, [(i, (i + distance) % 4) for i in range(4)])


def xh_halves(moved):
    xh = lax.axis_index("xh")

    def added(at):
        return sum(lax.dynamic_index_in_dim(x, at, 0, False).astype(WIDE) for x in moved)

    return added(xh), added(1 - xh).astype(LOW)


def dealt(x, axis):
    return lax.all_to_all(x, axis, split_axis=0, concat_axis=0, tiled=True)


def tp_parts(partial):
    return dealt(partial.reshape(8, -1, partial.shape[1]), TP)


def y_moved(x, distance):
    return lax.ppermute(x, "y", [(i, (i + distance) % 4) for i in range(4)])


def gathered(share, *beside):
    across_x, *beside = lax.optimization_barrier((swapped(share, "xl"), *beside))
    back, ahead, far = (y_moved(share, k) for k in (1, 3, 2))
    shares = [
        share, across_x, back, ahead, far,
        y_moved(across_x, 1), y_moved(across_x, 3), swapped(far, "xl"),
    ]
    return (shares, *beside) if beside else shares


def summed_by_pairs(x, pairs):
    for axis, size, distance in pairs:
        x = x + lax.ppermute(x, axis, [(i, i ^ distance) for i in range(size)])
    return x


def shape_of(*dims, kind=LOW):
    return jax.ShapeDtypeStruct(dims, kind)


def body(
    tokens, cotangent, segment_ids, first_gain, first_shift, second_gain, second_shift,
    w_qkv, qkv_bias, w_out, w_gate_up, w_down,
):
    ctx = lax.axis_index(CTX)
    tp = lax.axis_index(TP)
    group = lax.axis_index(("zl", "core"))
    place = jnp.stack(
        [group, lax.axis_index(SPREAD), lax.axis_index("core"), lax.axis_index("xl"), lax.axis_index("y")]
    )
    tied = lax.optimization_barrier

    def my_share(array):
        return lax.dynamic_slice_in_dim(array, tp * 64, 64)

    labels = jnp.arange(DOCS, dtype=jnp.int32)
    starts = jnp.sum((segment_ids[None, :] < labels[:, None]).astype(jnp.int32), axis=1)
    begins = jnp.sum(
        jnp.where(segment_ids[None, :] == labels[:, None], starts[:, None], 0), axis=0
    )
    begin = lax.dynamic_index_in_dim(begins.reshape(4, 4, 1, BLOCK), group, 1, False)
    begin = jnp.broadcast_to(begin, (4, 8, BLOCK))
    own = lax.dynamic_slice_in_dim(begins, ctx * BLOCK, BLOCK)
    places = ctx * BLOCK + jnp.arange(BLOCK, dtype=jnp.int32) - own
    frequency = 10000.0 ** (-jnp.arange(8, dtype=WIDE) / 8.0)
    angles = frequency[:, None] * places.astype(WIDE)[None, :]
    table = jnp.concatenate([jnp.cos(angles), jnp.sin(angles)], axis=0)

    w3 = jnp.transpose(w_qkv, (1, 0, 2))
    w2 = jnp.transpose(w_gate_up, (1, 2, 0))
    quarter, piece = shape_of(HALF, 128), shape_of(BLOCK + HALF, 128)
    wide_block = shape_of(BLOCK, 128, kind=WIDE)
    four = pltpu.VMEM((4, HALF, 128), LOW)
    normed_low, stats1, *packed, cosine, sine = kernel_call(
        project_kernel,
        (shape_of(BLOCK, 2048), wide_block, *[piece] * 4, wide_block, wide_block),
        (tokens, table, w3),
        small=(first_gain[None], first_shift[None], qkv_bias),
        scalars=(place,),
        scratch=(pltpu.VMEM((4, BLOCK + HALF, 128), LOW),),
        late=1,
        leaving=True,
        flops=2 * 512 * 2048 * 768,
    )
    (grad_hidden,) = kernel_call(
        hidden_gradient_kernel,
        (shape_of(BLOCK, 704, kind=WIDE),),
        (cotangent, w_down),
        flops=2 * 512 * 2048 * 704,
    )
    *packed, grad_hidden, tok_share, cot_share = tied(
        (*across(packed), grad_hidden, my_share(tokens), my_share(cotangent))
    )
    kv = jnp.stack([x[:BLOCK] for x in packed])
    queries = [(x, BLOCK, HALF) for x in packed]
    kv_c = swapped(kv, "core")
    state = (shape_of(4, 128, BLOCK, kind=WIDE), shape_of(4, 8, BLOCK, kind=WIDE))
    acc, peak = kernel_call(
        functools.partial(forward_kernel, (0, 1), True, False),
        state,
        (kv, kv_c, *queries, begin),
        scalars=(place,),
        scratch=(pltpu.VMEM((2, 4, 128, BLOCK), LOW), pltpu.VMEM((BLOCK, 128), LOW), four),
        flops=20 * 4 * BLOCK * BLOCK * 128,
        exps=20 * BLOCK * BLOCK,
        mib=24,
    )
    acc, peak, kv_z = tied((acc, peak, swapped(kv, "zl")))
    kv_zc = swapped(kv_z, "core")
    *heads, out_t, total = kernel_call(
        functools.partial(forward_kernel, (2, 3), False, True),
        (*[quarter] * 4, *state),
        (kv_z, kv_zc, *queries, begin, acc, peak),
        scalars=(place,),
        scratch=(pltpu.VMEM((2, 4, 128, BLOCK), LOW), pltpu.VMEM((BLOCK, 128), LOW), four, four),
        flops=20 * 4 * BLOCK * BLOCK * 128,
        exps=20 * BLOCK * BLOCK,
        mib=24,
    )
    heads = across(heads)
    share, low_share = shape_of(64, 2048, kind=WIDE), shape_of(64, 2048)
    attended_low, *partial_branch = kernel_call(
        branch_kernel,
        (shape_of(BLOCK, 256), *[shape_of(128, 2048)] * 2, *[low_share] * 4),
        (*heads, w_out),
        scalars=(place,),
        scratch=(pltpu.VMEM((BLOCK, 2048), LOW), four),
        late=1,
        flops=2 * 512 * 256 * 2048,
    )
    to_above, to_below, to_other, own_part, other_part, far_part = partial_branch
    from_below, from_above = y_moved(to_above, 1), y_moved(to_below, 3)
    other_part, far_part = kernel_call(
        meet_kernel,
        (low_share, low_share),
        (from_below, from_above, swapped(to_other, "xl"), other_part, far_part),
        scalars=(place,),
        quick=True,
    )
    other_part, far_part = swapped(other_part, "xl"), y_moved(far_part, 2)
    second_share, middle, second_rows, stats2 = kernel_call(
        second_norm_kernel,
        (low_share, share, share, shape_of(64, 128, kind=WIDE)),
        (from_below, from_above, own_part, other_part, far_part, tok_share),
        scalars=(place,),
        small=(second_gain[None], second_shift[None]),
    )
    second_low = gathered(second_share)
    strip = shape_of(BLOCK, 704)
    hidden_low, grad_gate, grad_up, partial_second = kernel_call(
        feed_kernel,
        (strip, strip, strip, shape_of(BLOCK, 2048)),
        (second_low, (w2, 0, 1), (w2, 1, 1), grad_hidden),
        scalars=(place,),
        late=2,
        leaving=True,
        flops=8 * 512 * 2048 * 704,
        mib=24,
    )
    second_parts = tp_parts(partial_second)

    feed_mine, feed_theirs = weight_grads(
        ((grad_gate, second_low), (grad_up, second_low), (hidden_low, cotangent)), place
    )
    second_parts, feed_mine, feed_theirs = tied((second_parts, feed_mine, feed_theirs))
    copies, grad_middle, second_sums = kernel_call(
        second_gradient_kernel,
        (shape_of(8, 64, 2048), share),
        (second_parts, cot_share, second_rows, stats2),
        moved=1,
        small=(second_gain[None],),
        small_outs=(shape_of(2, 2048, kind=WIDE),),
    )
    grad_branch = dealt(copies, TP).reshape(BLOCK, 2048)
    partial_feed = jnp.dot(hidden_low, w_down, preferred_element_type=WIDE).astype(LOW)
    grad_branch, partial_feed = tied((grad_branch, partial_feed))
    feed_z = z_parts(feed_mine, swapped(feed_theirs, "core"))
    feed_1, feed_3 = z_permute(feed_z[1], 1), z_permute(feed_z[3], 3)
    grads = kernel_call(
        grad_attended_kernel,
        (*[quarter] * 4,),
        (grad_branch, w_out),
        moved=1,
        scalars=(place,),
        scratch=(four,),
        flops=2 * 512 * 256 * 2048,
    )
    feed_1, feed_3, partial_feed, *grads = tied((feed_1, feed_3, partial_feed, *grads))
    feed_parts = dealt(partial_feed.reshape(4, 128, 2048), "y")
    *grads, feed_2 = tied((*across(grads), feed_z[2]))
    feed_2 = z_permute(feed_2, 2)
    scratch = (
        pltpu.VMEM((2, 4, 128, BLOCK), LOW),
        pltpu.VMEM((BLOCK, 128), LOW),
        pltpu.VMEM((BLOCK, 128), LOW),
        pltpu.VMEM((1, BLOCK), WIDE),
        pltpu.VMEM((2, 4, BLOCK, 128), WIDE),
        four,
        four,
    )
    blocks = shape_of(4, BLOCK, 128)
    acc, keep1, send1 = kernel_call(
        functools.partial(backward_kernel, (2, 3), True),
        (state[0], blocks, blocks),
        (kv_z, kv_zc, *queries, *grads, out_t, total, begin),
        scalars=(place,),
        scratch=scratch,
        flops=20 * 10 * BLOCK * BLOCK * 128,
        exps=20 * BLOCK * BLOCK,
        mib=28,
    )
    acc, send1, feed_parts, feed_2 = tied((acc, send1, feed_parts, feed_2))
    (feed_half,) = kernel_call(
        feed_sum_kernel,
        (shape_of(128, 2048),),
        (feed_parts, middle),
        scalars=(place,),
        moved=1,
    )
    far = (keep1.astype(WIDE) + swapped(send1, "core").astype(WIDE)).astype(LOW)
    acc, far, feed_half = tied((acc, far, feed_half))
    near = kernel_call(
        functools.partial(backward_kernel, (0, 1), False),
        (*[quarter] * 4, blocks, blocks),
        (kv, kv_c, *queries, *grads, out_t, total, begin, acc),
        scalars=(place,),
        scratch=(*scratch, pltpu.VMEM((4, 128, BLOCK), WIDE), four),
        flops=20 * 10 * BLOCK * BLOCK * 128,
        exps=20 * BLOCK * BLOCK,
        mib=28,
    )
    *near, far, feed_other = tied((*near, swapped(far, "zl"), swapped(feed_half, "xl")))
    *grad_queries, keep0, send0 = near
    pieces = kernel_call(
        join_kernel,
        (*[piece] * 4,),
        (keep0, swapped(send0, "core"), far, *grad_queries),
    )
    (copies4,) = kernel_call(layer_out_kernel, (shape_of(4, 128, 2048),), (feed_half, feed_other))
    *pieces, copies4, feed_0, feed_1, feed_2, feed_3 = tied(
        (*pieces, copies4, feed_z[0], feed_1, feed_2, feed_3)
    )
    feed_keep, feed_send = xh_halves([feed_0, feed_1, feed_2, feed_3])
    *pieces, feed_send = tied((*across(pieces), feed_send))
    feed_received = swapped(feed_send, "xh")
    layer_out = dealt(copies4, "y")
    grad_mixed, partial_normed, gain_sum, shift_sum, bias_sum = kernel_call(
        grad_project_kernel,
        (shape_of(BLOCK, 768), shape_of(BLOCK, 2048)),
        (*pieces, cosine, sine, tokens, stats1, w3),
        small_outs=(
            shape_of(1, 2048, kind=WIDE),
            shape_of(1, 2048, kind=WIDE),
            shape_of(3, 256, kind=WIDE),
        ),
        scalars=(place,),
        scratch=(pltpu.VMEM((4, BLOCK, 128), LOW), four),
        late=3,
        flops=2 * 512 * 2048 * 768,
    )
    partial_normed, layer_out = tied((partial_normed, layer_out))
    layer_out = settled(layer_out)
    normed_parts = tp_parts(partial_normed)

    rest_mine, rest_theirs = weight_grads(
        ((grad_mixed, normed_low), (attended_low, grad_branch)), place
    )
    rest_mine, rest_theirs, feed_received = tied((rest_mine, rest_theirs, feed_received))
    rest_z = z_parts(rest_mine, swapped(rest_theirs, "core"))
    vectors = jnp.concatenate([gain_sum, shift_sum, second_sums], axis=0).reshape(32, 256)
    vectors = jnp.concatenate([vectors, bias_sum], axis=0)
    vectors = summed_by_pairs(vectors, (("core", 2, 1), ("zl", 2, 1), ("zh", 2, 1)))
    vectors, *rest_z = tied((vectors, *rest_z))
    vectors = summed_by_pairs(vectors, (("xh", 2, 1),))
    rest_1, rest_3 = z_permute(rest_z[1], 1), z_permute(rest_z[3], 3)
    feed_w = feed_keep + feed_received.astype(WIDE)
    normed_parts, vectors, layer_out, feed_w = tied((normed_parts, vectors, layer_out, feed_w))
    bias_grad = vectors[32:]
    (last_share,) = kernel_call(
        first_gradient_kernel,
        (shape_of(64, 2048 + 128),),
        (normed_parts, grad_middle, tok_share, my_share(stats1), vectors[:32].reshape(64, 128)),
        moved=1,
        small=(first_gain[None],),
    )
    last_shares, rest_1, rest_3 = gathered(last_share, rest_1, rest_3)
    grad_tokens, vectors = last_call(last_shares, place)
    vectors = vectors.reshape(4, 2048)
    rest_z = (rest_z[0], rest_1, z_permute(rest_z[2], 2), rest_3)
    rest_keep, rest_send = xh_halves(rest_z)
    rest_w = rest_keep + swapped(rest_send, "xh").astype(WIDE)
    return (
        layer_out,
        grad_tokens,
        vectors[0],
        vectors[1],
        vectors[2],
        vectors[3],
        jnp.transpose(rest_w[:768].reshape(3, 256, 128), (2, 0, 1)),
        bias_grad,
        rest_w[768:],
        jnp.transpose(feed_w[:1408].reshape(2, 704, 128), (2, 0, 1)),
        feed_w[1408:],
    )


def solution(mesh):
    fine = Mesh(
        mesh.devices.reshape(2, 2, 2, 2, 4, 2), ("xh", "zh", "zl", "core", "y", "xl")
    )
    rows = P(CTX, None)
    return jax.shard_map(
        body,
        mesh=fine,
        in_specs=(
            rows, rows, P(), P(), P(), P(), P(),
            P(None, None, TP), P(None, TP), P(TP, None), P(None, None, TP), P(TP, None),
        ),
        out_specs=(
            rows, rows, P(), P(), P(), P(),
            P(CTX, None, TP), P(None, TP), P(TP, CTX), P(CTX, None, TP), P(TP, CTX),
        ),
        check_vma=False,
    )
```

```python
import functools

import jax
import jax.numpy as jnp
from jax import lax
from jax.experimental import pallas as pl
from jax.experimental.pallas import tpu as pltpu
from jax.sharding import Mesh
from jax.sharding import PartitionSpec as P

HDIM = 64
DOCS = 3
BLOCK = 512
HALF = 256
LOW = jnp.bfloat16
WIDE = jnp.float32
CTX = ("xh", "zh", "zl", "core")
TP = ("y", "xl")
SPREAD = ("xh", "zh")
Z = ("zh", "zl")


def size_of(a):
    return a.size * jnp.dtype(a.dtype).itemsize


def gathered_order(place):
    x, y = place[3], place[4]
    row = [lax.rem(y + k, 4) * 2 for k in range(4)]
    other = 1 - x
    return [
        row[0] + x, row[0] + other,
        row[3] + x, row[1] + x, row[2] + x,
        row[3] + other, row[1] + other, row[2] + other,
    ]


def deal_rows(place, rows, outs):
    x, y = place[3], place[4]
    far = lax.rem(y + 2, 4)
    firsts = [
        lax.rem(y + 1, 4) * 2, lax.rem(y + 3, 4) * 2,
        far * 2 + 1 - x, y * 2 + x, y * 2 + 1 - x, far * 2 + x,
    ]
    for first, out in zip(firsts, outs):
        out[...] = rows[pl.ds(pl.multiple_of(first * 64, 64), out.shape[0]), :]


def meet_kernel(place, below, above, crossed, other, far, out_other, out_far):
    column = pl.multiple_of((1 - place[3]) * 64, 64)

    def work(at):
        there = pl.ds(pl.multiple_of(column + at.start, 16), at.size)
        total = other[at, :].astype(WIDE) + below[there, :].astype(WIDE) + above[there, :].astype(WIDE)
        out_other[at, :] = total.astype(LOW)
        out_far[at, :] = (far[at, :].astype(WIDE) + crossed[at, :].astype(WIDE)).astype(LOW)

    for_rows(work)


def kernel_call(
    body, outs, inputs, *, small=(), small_outs=(), scalars=(), scratch=(), late=0, flops=0, exps=0, mib=12, quick=False, moved=0,
    leaving=False,
):
    inputs = [a if isinstance(a, (tuple, list)) else (a, 0, a.shape[0]) for a in inputs]
    flat = [x for a in inputs for x in (a if isinstance(a, list) else a[:1])]
    counts = [len(x) for x in (scalars, flat, small, outs, small_outs, inputs, outs)]

    def run(*refs):
        groups, at = [], 0
        for n in counts:
            groups.append(refs[at : at + n])
            at += n
        scalar_refs, far_in, near_in, far_out, near_out, held_in, held_out = groups
        arrived, left, *rest = refs[at:]
        pairs, ends = [], []
        for a, held in zip(inputs, held_in):
            if isinstance(a, list):
                rows = a[0].shape[0]
                for index in gathered_order(scalar_refs[0]):
                    pairs.append((None, held.at[pl.ds(pl.multiple_of(index * rows, rows), rows)]))
            else:
                pairs.append((pl.ds(a[1], a[2]), held))
            ends.append(len(pairs))
        moves = [
            pltpu.make_async_copy(x if part is None else x.at[part], held, arrived.at[k])
            for k, (x, (part, held)) in enumerate(zip(far_in, pairs))
        ]
        for move in moves:
            move.start()
        early = ends[len(inputs) - late - 1]
        for move in moves[:early]:
            move.wait()

        def arrive():
            for move in moves[early:]:
                move.wait()

        outward = [
            pltpu.make_async_copy(a, b, left.at[k]) for k, (a, b) in enumerate(zip(held_out, far_out))
        ]
        gone = []

        def leave(*which):
            for k in which:
                outward[k].start()
                gone.append(k)

        body(
            *([arrive] if late else []),
            *([leave] if leaving else []),
            *scalar_refs, *held_in, *near_in, *held_out, *near_out, *rest,
        )
        leave(*[k for k in range(len(outward)) if k not in gone])
        for move in outward:
            move.wait()

    vmem, hbm = pl.BlockSpec(memory_space=pltpu.VMEM), pl.BlockSpec(memory_space=pltpu.HBM)
    taken = [
        shape_of(8 * a[0].shape[0], a[0].shape[1], kind=a[0].dtype)
        if isinstance(a, list)
        else shape_of(a[2], *a[0].shape[1:], kind=a[0].dtype)
        for a in inputs
    ]
    held = [pltpu.VMEM(a.shape, a.dtype) for a in (*taken, *outs)]
    limit = sum(size_of(a) for a in (*taken, *outs, *small, *small_outs)) + mib * 1024 * 1024
    return pl.pallas_call(
        run,
        out_shape=(*[pltpu.HBM(a.shape, a.dtype) for a in outs], *small_outs),
        in_specs=[pl.BlockSpec(memory_space=pltpu.SMEM)] * len(scalars)
        + [pl.BlockSpec(memory_space=pl.ANY)] * moved
        + [hbm] * (len(flat) - moved)
        + [vmem] * len(small),
        out_specs=(*[hbm] * len(outs), *[vmem] * len(small_outs)),
        scratch_shapes=[
            *held,
            pltpu.SemaphoreType.DMA((len(flat),)),
            pltpu.SemaphoreType.DMA((max(1, len(outs)),)),
            *scratch,
        ],
        compiler_params=pltpu.CompilerParams(vmem_limit_bytes=limit),
        cost_estimate=pl.CostEstimate(
            flops=flops,
            bytes_accessed=0 if quick else sum(size_of(a) for a in (*taken, *outs)),
            transcendentals=exps,
        ),
    )(
        *scalars,
        *flat[:moved],
        *[pltpu.with_memory_space_constraint(a, pltpu.HBM) for a in flat[moved:]],
        *small,
    )


def lane_of(shape):
    return lax.broadcasted_iota(jnp.int32, shape, len(shape) - 1)


def exchange_halves(a, b):
    front = lane_of(a.shape) < HDIM
    return (
        jnp.where(front, a, pltpu.roll(b, HDIM, 1)),
        jnp.where(front, pltpu.roll(a, HDIM, 1), b),
    )


def nt(a, b):
    return lax.dot_general(a, b, (((1,), (1,)), ((), ())), preferred_element_type=WIDE)


def nn(a, b):
    return lax.dot_general(a, b, (((1,), (0,)), ((), ())), preferred_element_type=WIDE)


def turn(x, cosine, sine, sign):
    lane = lax.rem(lane_of(x.shape), HDIM)
    ahead = pltpu.roll(x, x.shape[1] - 8, 1)
    behind = pltpu.roll(x, 8, 1)
    swapped = jnp.where(lane < 8, -ahead, behind) * sign
    return x * cosine + swapped * sine


def rotation_table(angles_table):
    tokens = angles_table.shape[1]
    rest = jnp.zeros((112, tokens), WIDE)
    x = jnp.concatenate([angles_table, rest], axis=0).T
    lane = lane_of(x.shape)
    c = jnp.where(lane < 8, x, 0.0)
    c = c + pltpu.roll(c, 8, 1)
    c = c + pltpu.roll(c, HDIM, 1) + jnp.where(lax.rem(lane, HDIM) < 16, 0.0, 1.0)
    s = jnp.where((lane >= 8) & (lane < 16), x, 0.0)
    s = s + pltpu.roll(s, 120, 1)
    s = s + pltpu.roll(s, HDIM, 1)
    return c, s


def project_kernel(
    arrive, leave, place, tok, table, w, gain, shift, bias,
    normed, stats, x0, x1, x2, x3, cosine_out, sine_out, kept,
):
    rows = 64

    def norm_rows(i, carry):
        at = pl.ds(pl.multiple_of(i * rows, rows), rows)
        x = tok[at, :].astype(WIDE)
        mean = jnp.mean(x, axis=-1, keepdims=True)
        center = x - mean
        scale = lax.rsqrt(jnp.mean(center * center, axis=-1, keepdims=True) + 1e-05)
        normed[at, :] = (center * scale * gain[...] + shift[...]).astype(LOW)
        stats[at, :] = jnp.where(lane_of((rows, 128)) < HDIM, mean, scale)
        return carry

    lax.fori_loop(0, BLOCK // rows, norm_rows, 0)
    cosine, sine = rotation_table(table[...])
    cosine_out[...] = cosine
    sine_out[...] = sine
    leave(0, 1, 6, 7)
    arrive()
    mixed = [nn(normed[...], w[c]) + bias[c : c + 1, :] for c in range(3)]
    for pair in range(2):
        lanes = slice(pair * 128, pair * 128 + 128)
        q = turn(mixed[0][:, lanes], cosine, sine, 1.0) * 0.125
        k = turn(mixed[1][:, lanes], cosine, sine, 1.0)
        kv = exchange_halves(k, mixed[2][:, lanes])
        qq = exchange_halves(q[:HALF], q[HALF:])
        for one in range(2):
            kept[2 * pair + one, :BLOCK, :] = kv[one].astype(LOW)
            kept[2 * pair + one, BLOCK:, :] = qq[one].astype(LOW)
    for k, out in enumerate((x0, x1, x2, x3)):
        out[...] = kept[place[1] ^ k]


def padded_queries(q2):
    x = q2.astype(WIDE)
    front = lane_of(x.shape) < HDIM
    return (
        jnp.where(front, x, 0.0).astype(LOW),
        jnp.where(front, pltpu.roll(x, HDIM, 1), 0.0).astype(LOW),
    )


def padded_behind(d2):
    x = d2.astype(WIDE)
    front = lane_of(x.shape) < HDIM
    return (
        jnp.where(front, 0.0, pltpu.roll(x, HDIM, 1)).astype(LOW),
        jnp.where(front, 0.0, x).astype(LOW),
    )


def allowed_keys(key_block, first_query, begin):
    shape = (BLOCK, begin.shape[1])
    key_at = key_block * BLOCK + lax.broadcasted_iota(jnp.int32, shape, 0)
    query_at = first_query + lax.broadcasted_iota(jnp.int32, shape, 1)
    return (key_at <= query_at) & (key_at >= begin)


def for_steps(count, work):
    def pair(i, carry):
        work([2 * i, 2 * i + 1])
        return carry

    lax.fori_loop(0, count // 2, pair, 0)

    @pl.when(lax.rem(count, 2) == 1)
    def _():
        work([count - 1])


def key_blocks(place, rels, t):
    return [4 * t + (place[0] ^ rel) for rel in rels], place[1] ^ t


def forward_kernel(rels, first, last, *refs):
    place, kv0, kv1, q0, q1, q2, q3, begin = refs[:8]
    if first:
        acc_out, peak_out, kvt, queries, kept_q = refs[8:]
    else:
        acc_in, peak_in, o0, o1, o2, o3, out_t, total, kvt, queries, kept_q, kept_o = refs[8:]
        acc_out, peak_out = out_t, total
    me = place[1]
    front = lane_of((BLOCK, 128)) < HDIM
    for k, q in enumerate((q0, q1, q2, q3)):
        kept_q[me ^ k] = q[...]
    for i, kv in enumerate((kv0, kv1)):
        for t in range(4):
            kvt[i, t] = jnp.where(front, 1.0, kv[t].astype(WIDE)).T.astype(LOW)

    def one_query_block(j, carry):
        first_query = (4 * j + place[0]) * BLOCK
        queries[:HALF, :], queries[HALF:, :] = padded_queries(kept_q[j])
        if first:
            peak_out[j] = jnp.full((8, BLOCK), -1e30, WIDE)
            acc_out[j] = jnp.zeros((128, BLOCK), WIDE)
        else:
            peak_out[j] = peak_in[j]
            acc_out[j] = acc_in[j]

        def some_blocks(steps):
            scores, sources = [], []
            for t in steps:
                blocks, at = key_blocks(place, rels, t)
                for i, kv in enumerate((kv0, kv1)):
                    ok = allowed_keys(blocks[i], first_query, begin[j, :1])
                    scores.append(jnp.where(ok, nt(kv[at], queries[...]), -1e30))
                    sources.append((i, at))
            old = peak_out[j, :1]
            new = old
            for one in scores:
                new = jnp.maximum(new, jnp.max(one, axis=0, keepdims=True))
            done = acc_out[j] * jnp.exp(old - new)
            for one, (i, at) in zip(scores, sources):
                done += nn(kvt[i, at], jnp.exp(one - new).astype(LOW))
            acc_out[j] = done
            peak_out[j, :1] = new

        for_steps(j + 1, some_blocks)
        if last:
            weight_sum = acc_out[j, :1]
            done = acc_out[j] / weight_sum
            out_t[j] = done
            total[j, :1] = peak_out[j, :1] + jnp.log(weight_sum)
            rows = done.T
            x, y = rows[:HALF], rows[HALF:]
            kept_o[j] = jnp.where(lane_of(x.shape) < HDIM, pltpu.roll(x, HDIM, 1), y).astype(LOW)
        return carry

    lax.fori_loop(0, 4, one_query_block, 0)
    if last:
        for k, out in enumerate((o0, o1, o2, o3)):
            out[...] = kept_o[me ^ k]


def backward_kernel(rels, first, *refs):
    place, kv0, kv1, q0, q1, q2, q3, d0, d1, d2, d3, out_t, total, begin = refs[:14]
    if first:
        acc, keep, send, kvt, queries, grads, dot_rows, dkv, kept_q, kept_d = refs[14:]
    else:
        (
            acc_in, g0, g1, g2, g3, keep, send,
            kvt, queries, grads, dot_rows, dkv, kept_q, kept_d, acc, kept_g,
        ) = refs[14:]
    me = place[1]
    for k in range(4):
        kept_q[me ^ k] = (q0, q1, q2, q3)[k][...]
        kept_d[me ^ k] = (d0, d1, d2, d3)[k][...]
    for i, kv in enumerate((kv0, kv1)):
        for t in range(4):
            kvt[i, t] = kv[t].astype(WIDE).T.astype(LOW)
    dkv[...] = jnp.zeros(dkv.shape, WIDE)

    def one_query_block(j, carry):
        first_query = (4 * j + place[0]) * BLOCK
        queries[:HALF, :], queries[HALF:, :] = padded_queries(kept_q[j])
        grads[:HALF, :], grads[HALF:, :] = padded_behind(kept_d[j])
        dot_rows[...] = jnp.sum(grads[...].astype(WIDE).T * out_t[j], axis=0, keepdims=True)
        acc[j] = jnp.zeros((128, BLOCK), WIDE) if first else acc_in[j]

        def some_blocks(steps):
            for t in steps:
                blocks, at = key_blocks(place, rels, t)
                for i, kv in enumerate((kv0, kv1)):
                    term = 0.0
                    for half in range(2):
                        some = slice(half * HALF, half * HALF + HALF)
                        ok = allowed_keys(blocks[i], first_query + half * HALF, begin[j, :1, some])
                        scores = nt(kv[at], queries[some, :])
                        probs = jnp.where(ok, jnp.exp(scores - total[j, :1, some]), 0.0)
                        grad_probs = nt(kv[at], grads[some, :])
                        grad_scores = (probs * (grad_probs - dot_rows[:, some])).astype(LOW)
                        term += nn(grad_scores, queries[some, :])
                        term += nn(probs.astype(LOW), grads[some, :])
                        acc[j, :, some] += nn(kvt[i, at], grad_scores)
                    dkv[i, at] += term

        for_steps(j + 1, some_blocks)
        if not first:
            rows = acc[j].T
            x, y = rows[:HALF], rows[HALF:]
            kept_g[j] = jnp.where(lane_of(x.shape) < HDIM, x, pltpu.roll(y, HDIM, 1)).astype(LOW)
        return carry

    lax.fori_loop(0, 4, one_query_block, 0)
    if not first:
        for k, out in enumerate((g0, g1, g2, g3)):
            out[...] = kept_g[me ^ k]
    for t in range(4):
        keep[t] = dkv[0, t].astype(LOW)
        send[t] = dkv[1, t].astype(LOW)


def branch_kernel(arrive, place, h0, h1, h2, h3, w, attended, *refs):
    outs, (partial, kept) = refs[:6], refs[6:]
    for k, h in enumerate((h0, h1, h2, h3)):
        kept[place[1] ^ k] = h[...]
    for pair in range(2):
        lanes = slice(pair * 128, pair * 128 + 128)
        x, y = exchange_halves(kept[2 * pair].astype(WIDE), kept[2 * pair + 1].astype(WIDE))
        attended[:HALF, lanes] = x.astype(LOW)
        attended[HALF:, lanes] = y.astype(LOW)
    arrive()
    for n in range(4):
        at = slice(n * 512, n * 512 + 512)
        partial[:, at] = nn(attended[...], w[:, at]).astype(LOW)
    deal_rows(place, partial, outs)


def grad_attended_kernel(place, grad, w, d0, d1, d2, d3, kept):
    g = nt(grad[...], w[...])
    for pair in range(2):
        lanes = slice(pair * 128, pair * 128 + 128)
        both = exchange_halves(g[:HALF, lanes], g[HALF:, lanes])
        for one in range(2):
            kept[2 * pair + one] = both[one].astype(LOW)
    for k, out in enumerate((d0, d1, d2, d3)):
        out[...] = kept[place[1] ^ k]


def join_kernel(keep, received, far, g0, g1, g2, g3, x0, x1, x2, x3):
    for k in range(4):
        total = keep[k].astype(WIDE) + received[k].astype(WIDE) + far[k].astype(WIDE)
        out = (x0, x1, x2, x3)[k]
        out[:BLOCK, :] = total.astype(LOW)
        out[BLOCK:, :] = (g0, g1, g2, g3)[k][...]


def grad_project_kernel(
    arrive, place, x0, x1, x2, x3, cosine, sine, tok, stats, w,
    grad_mixed, partial, gain_sum, shift_sum, bias_sum, parts, kept,
):
    for k, x in enumerate((x0, x1, x2, x3)):
        parts[place[1] ^ k] = x[:BLOCK, :]
        kept[place[1] ^ k] = x[BLOCK:, :]
    for pair in range(2):
        lanes = slice(pair * 128, pair * 128 + 128)
        k, v = exchange_halves(parts[2 * pair].astype(WIDE), parts[2 * pair + 1].astype(WIDE))
        q = exchange_halves(kept[2 * pair].astype(WIDE), kept[2 * pair + 1].astype(WIDE))
        q = jnp.concatenate(q, axis=0)
        q = turn(q, cosine[...], sine[...], -1.0) * 0.125
        k = turn(k, cosine[...], sine[...], -1.0)
        for c, part in enumerate((q, k, v)):
            start = c * 256 + pair * 128
            low = part.astype(LOW)
            grad_mixed[:, start : start + 128] = low
            bias_sum[c : c + 1, lanes] = jnp.sum(low.astype(WIDE), axis=0, keepdims=True)
    arrive()
    mean, scale = stats[:, 0:1], stats[:, 64:65]
    for n in range(4):
        at = slice(n * 512, n * 512 + 512)
        total = nt(grad_mixed[:, :256], w[0, at, :])
        total += nt(grad_mixed[:, 256:512], w[1, at, :])
        total += nt(grad_mixed[:, 512:], w[2, at, :])
        partial[:, at] = total.astype(LOW)
        normal = (tok[:, at].astype(WIDE) - mean) * scale
        gain_sum[:, at] = jnp.sum(total * normal, axis=0, keepdims=True)
        shift_sum[:, at] = jnp.sum(total, axis=0, keepdims=True)


def hidden_gradient_kernel(cot, w, grad_hidden):
    grad_hidden[...] = nt(cot[...], w[...])


def feed_kernel(arrive, leave, place, second, w_gate, w_up, grad_hidden, hidden, grad_gate, grad_up, partial):
    gate = nt(second[...], w_gate[0])
    arrive()
    up = nt(second[...], w_up[0])
    sigmoid = 1.0 / (1.0 + jnp.exp(-gate))
    activated = gate * sigmoid
    hidden[...] = (activated * up).astype(LOW)
    grad = grad_hidden[...]
    grad_up[...] = (grad * activated).astype(LOW)
    grad_gate[...] = (grad * up * sigmoid * (1.0 + gate * (1.0 - sigmoid))).astype(LOW)
    leave(0, 1, 2)
    for n in range(4):
        at = slice(n * 512, n * 512 + 512)
        partial[:, at] = (nn(grad_gate[...], w_gate[0, :, at]) + nn(grad_up[...], w_up[0, :, at])).astype(LOW)


def for_rows(work):
    rows = 16

    def one(i, carry):
        work(pl.ds(pl.multiple_of(i * rows, rows), rows))
        return carry

    lax.fori_loop(0, 64 // rows, one, 0)


def summed(parts, at):
    total = parts[0, at, :].astype(WIDE)
    for k in range(1, 8):
        total += parts[k, at, :].astype(WIDE)
    return total


def second_norm_kernel(
    place, below, above, own, other, far, tok, gain, shift, low, middle, normal, stats
):
    column = pl.multiple_of(place[3] * 64, 64)

    def work(at):
        there = pl.ds(pl.multiple_of(column + at.start, 16), at.size)
        x = tok[at, :].astype(WIDE) + own[at, :].astype(WIDE)
        x += below[there, :].astype(WIDE) + above[there, :].astype(WIDE)
        x += other[at, :].astype(WIDE) + far[at, :].astype(WIDE)
        center = x - jnp.mean(x, axis=-1, keepdims=True)
        scale = lax.rsqrt(jnp.mean(center * center, axis=-1, keepdims=True) + 1e-05)
        rows = center * scale
        low[at, :] = (rows * gain[...] + shift[...]).astype(LOW)
        middle[at, :] = x
        normal[at, :] = rows
        stats[at, :] = jnp.broadcast_to(scale, (scale.shape[0], 128))

    for_rows(work)


def norm_gradient(grad, rows, scale, gain):
    scaled = grad * gain
    return scale * (
        scaled
        - jnp.mean(scaled, axis=-1, keepdims=True)
        - rows * jnp.mean(scaled * rows, axis=-1, keepdims=True)
    )


def second_gradient_kernel(parts, cot, normal, stats, gain, copies, grad_middle, sums):
    sums[...] = jnp.zeros(sums.shape, WIDE)

    def work(at):
        grad, rows = summed(parts, at), normal[at, :]
        done = cot[at, :].astype(WIDE) + norm_gradient(grad, rows, stats[at, 0:1], gain[...])
        low = done.astype(LOW)
        for k in range(8):
            copies[k, at, :] = low
        grad_middle[at, :] = done
        sums[0:1, :] += jnp.sum(grad * rows, axis=0, keepdims=True)
        sums[1:2, :] += jnp.sum(grad, axis=0, keepdims=True)

    for_rows(work)


def feed_sum_kernel(place, parts, middle, out):
    rows = 16
    mine = place[3]

    def one(i, carry):
        at = pl.ds(pl.multiple_of(i * rows, rows), rows)
        total = parts[0, at, :].astype(WIDE)
        for k in range(1, 4):
            total += parts[k, at, :].astype(WIDE)
        here = i * rows - mine * 64
        own = pl.ds(pl.multiple_of(jnp.clip(here, 0, 64 - rows), rows), rows)
        inside = (here >= 0) & (here < 64)
        out[at, :] = (total + jnp.where(inside, middle[own, :], 0.0)).astype(LOW)
        return carry

    lax.fori_loop(0, 128 // rows, one, 0)


def layer_out_kernel(a, b, copies):
    rows = 16

    def one(i, carry):
        at = pl.ds(pl.multiple_of(i * rows, rows), rows)
        low = (a[at, :].astype(WIDE) + b[at, :].astype(WIDE)).astype(LOW)
        for k in range(4):
            copies[k, at, :] = low
        return carry

    lax.fori_loop(0, 128 // rows, one, 0)


def first_gradient_kernel(parts, grad_middle, tok, stats, vectors, gain, low):
    def work(at):
        mean, scale = stats[at, 0:1], stats[at, 64:65]
        rows = (tok[at, :].astype(WIDE) - mean) * scale
        done = norm_gradient(summed(parts, at), rows, scale, gain[...])
        low[at, :2048] = (grad_middle[at, :] + done).astype(LOW)
        low[at, 2048:] = vectors[at, :].astype(LOW)

    for_rows(work)


def last_kernel(place, *refs):
    shares, (out, total, held, came, went) = refs[:8], refs[8:]
    moves = []
    for k, (x, index) in enumerate(zip(shares, gathered_order(place))):
        at = pl.ds(pl.multiple_of(index * 64, 64), 64)
        moves.append(
            (
                pltpu.make_async_copy(x, held.at[k], came.at[k]),
                pltpu.make_async_copy(held.at[k, :, pl.ds(0, 2048)], out.at[at], went.at[k]),
            )
        )
    for come, _ in moves:
        come.start()
    for come, go in moves:
        come.wait()
        go.start()
    done = held[0, :, 2048:].astype(WIDE)
    for k in range(1, 8):
        done += held[k, :, 2048:].astype(WIDE)
    total[...] = done
    for _, go in moves:
        go.wait()


def last_call(shares, place):
    hbm = pl.BlockSpec(memory_space=pltpu.HBM)
    return pl.pallas_call(
        last_kernel,
        out_shape=(pltpu.HBM((BLOCK, 2048), LOW), shape_of(64, 128, kind=WIDE)),
        in_specs=[pl.BlockSpec(memory_space=pltpu.SMEM), *[hbm] * 8],
        out_specs=(hbm, pl.BlockSpec(memory_space=pltpu.VMEM)),
        scratch_shapes=[
            pltpu.VMEM((8, 64, 2048 + 128), LOW),
            pltpu.SemaphoreType.DMA((8,)),
            pltpu.SemaphoreType.DMA((8,)),
        ],
        compiler_params=pltpu.CompilerParams(vmem_limit_bytes=8 * 1024 * 1024),
        cost_estimate=pl.CostEstimate(flops=0, bytes_accessed=0, transcendentals=0),
    )(place, *[pltpu.with_memory_space_constraint(a, pltpu.HBM) for a in shares])


def weight_kernel(widths, sources, arrive, place, *refs):
    count = max(max(pair) for pair in sources) + 1
    inputs = refs[:count]
    mine, theirs, turned = refs[count:]
    first_core = place[2] == 0
    start = 0
    for n, ((left, right), width) in enumerate(zip(sources, widths)):
        if n == 1:
            arrive()
        left, right = inputs[left], inputs[right]
        turned[:width, :] = left[...].astype(WIDE).T.astype(LOW)

        def one(n, carry, start=start, right=right, width=width):
            columns = right[:, pl.ds(pl.multiple_of(n * 256, 256), 256)]
            both = nn(turned[:width, :], columns)
            first, second = both[:, :128], both[:, 128:]
            at = pl.ds(start, width)
            mine[n, at, :] = jnp.where(first_core, first, second).astype(LOW)
            theirs[n, at, :] = jnp.where(first_core, second, first).astype(LOW)
            return carry

        lax.fori_loop(0, 8, one, 0, unroll=4)
        start += width


def weight_grads(pairs, place):
    inputs, sources = [], []
    for pair in pairs:
        for a in pair:
            if not any(a is b for b in inputs):
                inputs.append(a)
        sources.append(tuple(next(k for k, b in enumerate(inputs) if b is a) for a in pair))
    widths = tuple(a.shape[1] for a, _ in pairs)
    out = jax.ShapeDtypeStruct((8, sum(widths), 128), LOW)
    return kernel_call(
        functools.partial(weight_kernel, widths, sources),
        (out, out),
        inputs,
        scalars=(place,),
        scratch=(pltpu.VMEM((max(widths), BLOCK), LOW),),
        late=len(inputs) - 2,
        quick=True,
    )


def swapped(x, axis):
    return lax.ppermute(x, axis, [(0, 1), (1, 0)])


def across(pieces):
    moved = [
        lax.ppermute(pieces[k], SPREAD, [(i, i ^ k) for i in range(4)]) for k in range(1, 4)
    ]
    return (pieces[0], *moved)


def z_parts_kernel(place, mine, received, *refs):
    outs, (held_a, held_b, done, came, went) = refs[:4], refs[4:]
    z = place[0]
    order = [(k, xh) for k in (1, 3, 2, 0) for xh in range(2)]
    moves = []
    for n, (k, xh) in enumerate(order):
        at = xh * 4 + lax.rem(z + k, 4)
        moves.append(
            (
                pltpu.make_async_copy(mine.at[at], held_a.at[n], came.at[2 * n]),
                pltpu.make_async_copy(received.at[at], held_b.at[n], came.at[2 * n + 1]),
                pltpu.make_async_copy(done.at[n], outs[k].at[xh], went.at[n]),
            )
        )
    for a, b, _ in moves:
        a.start()
        b.start()
    for n, (a, b, out) in enumerate(moves):
        a.wait()
        b.wait()
        done[n] = (held_a[n].astype(WIDE) + held_b[n].astype(WIDE)).astype(LOW)
        out.start()
    for _, _, out in moves:
        out.wait()


def z_parts(mine, received):
    rows = mine.shape[1]
    hbm = pl.BlockSpec(memory_space=pltpu.HBM)
    held = pltpu.VMEM((8, rows, 128), LOW)
    return pl.pallas_call(
        z_parts_kernel,
        in_specs=[pl.BlockSpec(memory_space=pltpu.SMEM), hbm, hbm],
        out_specs=[hbm] * 4,
        out_shape=[pltpu.HBM((2, rows, 128), LOW)] * 4,
        scratch_shapes=[
            held,
            held,
            held,
            pltpu.SemaphoreType.DMA((16,)),
            pltpu.SemaphoreType.DMA((8,)),
        ],
        compiler_params=pltpu.CompilerParams(vmem_limit_bytes=24 * 1024 * 1024),
        cost_estimate=pl.CostEstimate(flops=0, bytes_accessed=0, transcendentals=0),
    )(
        lax.axis_index(Z).reshape(1),
        *[pltpu.with_memory_space_constraint(a, pltpu.HBM) for a in (mine, received)],
    )


def settled_kernel(x, out, held, came, went):
    rows = x.shape[1]
    moves = []
    for k in range(x.shape[0]):
        at = pl.ds(k * rows, rows)
        moves.append(
            (
                pltpu.make_async_copy(x.at[k], held.at[k], came.at[k]),
                pltpu.make_async_copy(held.at[k, :, pl.ds(0, 2048)], out.at[at], went.at[k]),
            )
        )
    for come, _ in moves:
        come.start()
    for come, go in moves:
        come.wait()
        go.start()
    for _, go in moves:
        go.wait()


def settled(x):
    hbm = pl.BlockSpec(memory_space=pltpu.HBM)
    parts, rows = x.shape[:2]
    return pl.pallas_call(
        settled_kernel,
        out_shape=pltpu.HBM((parts * rows, 2048), x.dtype),
        in_specs=[pl.BlockSpec(memory_space=pl.ANY)],
        out_specs=hbm,
        scratch_shapes=[
            pltpu.VMEM(x.shape, x.dtype),
            pltpu.SemaphoreType.DMA((parts,)),
            pltpu.SemaphoreType.DMA((parts,)),
        ],
        compiler_params=pltpu.CompilerParams(vmem_limit_bytes=8 * 1024 * 1024),
        cost_estimate=pl.CostEstimate(flops=0, bytes_accessed=0, transcendentals=0),
    )(x)


def z_permute(part, distance):
    return lax.ppermute(part, Z, [(i, (i + distance) % 4) for i in range(4)])


def xh_halves(moved):
    xh = lax.axis_index("xh")

    def added(at):
        return sum(lax.dynamic_index_in_dim(x, at, 0, False).astype(WIDE) for x in moved)

    return added(xh), added(1 - xh).astype(LOW)


def dealt(x, axis):
    return lax.all_to_all(x, axis, split_axis=0, concat_axis=0, tiled=True)


def tp_parts(partial):
    return dealt(partial.reshape(8, -1, partial.shape[1]), TP)


def y_moved(x, distance):
    return lax.ppermute(x, "y", [(i, (i + distance) % 4) for i in range(4)])


def gathered(share, *beside):
    across_x, *beside = lax.optimization_barrier((swapped(share, "xl"), *beside))
    back, ahead, far = (y_moved(share, k) for k in (1, 3, 2))
    shares = [
        share, across_x, back, ahead, far,
        y_moved(across_x, 1), y_moved(across_x, 3), swapped(far, "xl"),
    ]
    return (shares, *beside) if beside else shares


def summed_by_pairs(x, pairs):
    for axis, size, distance in pairs:
        x = x + lax.ppermute(x, axis, [(i, i ^ distance) for i in range(size)])
    return x


def shape_of(*dims, kind=LOW):
    return jax.ShapeDtypeStruct(dims, kind)


def body(
    tokens, cotangent, segment_ids, first_gain, first_shift, second_gain, second_shift,
    w_qkv, qkv_bias, w_out, w_gate_up, w_down,
):
    ctx = lax.axis_index(CTX)
    tp = lax.axis_index(TP)
    group = lax.axis_index(("zl", "core"))
    place = jnp.stack(
        [group, lax.axis_index(SPREAD), lax.axis_index("core"), lax.axis_index("xl"), lax.axis_index("y")]
    )
    tied = lax.optimization_barrier

    def my_share(array):
        return lax.dynamic_slice_in_dim(array, tp * 64, 64)

    labels = jnp.arange(DOCS, dtype=jnp.int32)
    starts = jnp.sum((segment_ids[None, :] < labels[:, None]).astype(jnp.int32), axis=1)
    begins = jnp.sum(
        jnp.where(segment_ids[None, :] == labels[:, None], starts[:, None], 0), axis=0
    )
    begin = lax.dynamic_index_in_dim(begins.reshape(4, 4, 1, BLOCK), group, 1, False)
    begin = jnp.broadcast_to(begin, (4, 8, BLOCK))
    own = lax.dynamic_slice_in_dim(begins, ctx * BLOCK, BLOCK)
    places = ctx * BLOCK + jnp.arange(BLOCK, dtype=jnp.int32) - own
    frequency = 10000.0 ** (-jnp.arange(8, dtype=WIDE) / 8.0)
    angles = frequency[:, None] * places.astype(WIDE)[None, :]
    table = jnp.concatenate([jnp.cos(angles), jnp.sin(angles)], axis=0)

    w3 = jnp.transpose(w_qkv, (1, 0, 2))
    w2 = jnp.transpose(w_gate_up, (1, 2, 0))
    quarter, piece = shape_of(HALF, 128), shape_of(BLOCK + HALF, 128)
    wide_block = shape_of(BLOCK, 128, kind=WIDE)
    four = pltpu.VMEM((4, HALF, 128), LOW)
    normed_low, stats1, *packed, cosine, sine = kernel_call(
        project_kernel,
        (shape_of(BLOCK, 2048), wide_block, *[piece] * 4, wide_block, wide_block),
        (tokens, table, w3),
        small=(first_gain[None], first_shift[None], qkv_bias),
        scalars=(place,),
        scratch=(pltpu.VMEM((4, BLOCK + HALF, 128), LOW),),
        late=1,
        leaving=True,
        flops=2 * 512 * 2048 * 768,
    )
    (grad_hidden,) = kernel_call(
        hidden_gradient_kernel,
        (shape_of(BLOCK, 704, kind=WIDE),),
        (cotangent, w_down),
        flops=2 * 512 * 2048 * 704,
    )
    *packed, grad_hidden, tok_share, cot_share = tied(
        (*across(packed), grad_hidden, my_share(tokens), my_share(cotangent))
    )
    kv = jnp.stack([x[:BLOCK] for x in packed])
    queries = [(x, BLOCK, HALF) for x in packed]
    kv_c = swapped(kv, "core")
    state = (shape_of(4, 128, BLOCK, kind=WIDE), shape_of(4, 8, BLOCK, kind=WIDE))
    acc, peak = kernel_call(
        functools.partial(forward_kernel, (0, 1), True, False),
        state,
        (kv, kv_c, *queries, begin),
        scalars=(place,),
        scratch=(pltpu.VMEM((2, 4, 128, BLOCK), LOW), pltpu.VMEM((BLOCK, 128), LOW), four),
        flops=20 * 4 * BLOCK * BLOCK * 128,
        exps=20 * BLOCK * BLOCK,
        mib=24,
    )
    acc, peak, kv_z = tied((acc, peak, swapped(kv, "zl")))
    kv_zc = swapped(kv_z, "core")
    *heads, out_t, total = kernel_call(
        functools.partial(forward_kernel, (2, 3), False, True),
        (*[quarter] * 4, *state),
        (kv_z, kv_zc, *queries, begin, acc, peak),
        scalars=(place,),
        scratch=(pltpu.VMEM((2, 4, 128, BLOCK), LOW), pltpu.VMEM((BLOCK, 128), LOW), four, four),
        flops=20 * 4 * BLOCK * BLOCK * 128,
        exps=20 * BLOCK * BLOCK,
        mib=24,
    )
    heads = across(heads)
    share, low_share = shape_of(64, 2048, kind=WIDE), shape_of(64, 2048)
    attended_low, *partial_branch = kernel_call(
        branch_kernel,
        (shape_of(BLOCK, 256), *[shape_of(128, 2048)] * 2, *[low_share] * 4),
        (*heads, w_out),
        scalars=(place,),
        scratch=(pltpu.VMEM((BLOCK, 2048), LOW), four),
        late=1,
        flops=2 * 512 * 256 * 2048,
    )
    to_above, to_below, to_other, own_part, other_part, far_part = partial_branch
    from_below, from_above = y_moved(to_above, 1), y_moved(to_below, 3)
    other_part, far_part = kernel_call(
        meet_kernel,
        (low_share, low_share),
        (from_below, from_above, swapped(to_other, "xl"), other_part, far_part),
        scalars=(place,),
        quick=True,
    )
    other_part, far_part = swapped(other_part, "xl"), y_moved(far_part, 2)
    second_share, middle, second_rows, stats2 = kernel_call(
        second_norm_kernel,
        (low_share, share, share, shape_of(64, 128, kind=WIDE)),
        (from_below, from_above, own_part, other_part, far_part, tok_share),
        scalars=(place,),
        small=(second_gain[None], second_shift[None]),
    )
    second_low = gathered(second_share)
    strip = shape_of(BLOCK, 704)
    hidden_low, grad_gate, grad_up, partial_second = kernel_call(
        feed_kernel,
        (strip, strip, strip, shape_of(BLOCK, 2048)),
        (second_low, (w2, 0, 1), (w2, 1, 1), grad_hidden),
        scalars=(place,),
        late=2,
        leaving=True,
        flops=8 * 512 * 2048 * 704,
        mib=24,
    )
    second_parts = tp_parts(partial_second)

    feed_mine, feed_theirs = weight_grads(
        ((grad_gate, second_low), (grad_up, second_low), (hidden_low, cotangent)), place
    )
    second_parts, feed_mine, feed_theirs = tied((second_parts, feed_mine, feed_theirs))
    copies, grad_middle, second_sums = kernel_call(
        second_gradient_kernel,
        (shape_of(8, 64, 2048), share),
        (second_parts, cot_share, second_rows, stats2),
        moved=1,
        small=(second_gain[None],),
        small_outs=(shape_of(2, 2048, kind=WIDE),),
    )
    grad_branch = dealt(copies, TP).reshape(BLOCK, 2048)
    partial_feed = jnp.dot(hidden_low, w_down, preferred_element_type=WIDE).astype(LOW)
    grad_branch, partial_feed = tied((grad_branch, partial_feed))
    feed_z = z_parts(feed_mine, swapped(feed_theirs, "core"))
    feed_1, feed_3 = z_permute(feed_z[1], 1), z_permute(feed_z[3], 3)
    grads = kernel_call(
        grad_attended_kernel,
        (*[quarter] * 4,),
        (grad_branch, w_out),
        moved=1,
        scalars=(place,),
        scratch=(four,),
        flops=2 * 512 * 256 * 2048,
    )
    feed_1, feed_3, partial_feed, *grads = tied((feed_1, feed_3, partial_feed, *grads))
    feed_parts = dealt(partial_feed.reshape(4, 128, 2048), "y")
    *grads, feed_2 = tied((*across(grads), feed_z[2]))
    feed_2 = z_permute(feed_2, 2)
    scratch = (
        pltpu.VMEM((2, 4, 128, BLOCK), LOW),
        pltpu.VMEM((BLOCK, 128), LOW),
        pltpu.VMEM((BLOCK, 128), LOW),
        pltpu.VMEM((1, BLOCK), WIDE),
        pltpu.VMEM((2, 4, BLOCK, 128), WIDE),
        four,
        four,
    )
    blocks = shape_of(4, BLOCK, 128)
    acc, keep1, send1 = kernel_call(
        functools.partial(backward_kernel, (2, 3), True),
        (state[0], blocks, blocks),
        (kv_z, kv_zc, *queries, *grads, out_t, total, begin),
        scalars=(place,),
        scratch=scratch,
        flops=20 * 10 * BLOCK * BLOCK * 128,
        exps=20 * BLOCK * BLOCK,
        mib=28,
    )
    acc, send1, feed_parts, feed_2 = tied((acc, send1, feed_parts, feed_2))
    (feed_half,) = kernel_call(
        feed_sum_kernel,
        (shape_of(128, 2048),),
        (feed_parts, middle),
        scalars=(place,),
        moved=1,
    )
    far = (keep1.astype(WIDE) + swapped(send1, "core").astype(WIDE)).astype(LOW)
    acc, far, feed_half = tied((acc, far, feed_half))
    near = kernel_call(
        functools.partial(backward_kernel, (0, 1), False),
        (*[quarter] * 4, blocks, blocks),
        (kv, kv_c, *queries, *grads, out_t, total, begin, acc),
        scalars=(place,),
        scratch=(*scratch, pltpu.VMEM((4, 128, BLOCK), WIDE), four),
        flops=20 * 10 * BLOCK * BLOCK * 128,
        exps=20 * BLOCK * BLOCK,
        mib=28,
    )
    *near, far, feed_other = tied((*near, swapped(far, "zl"), swapped(feed_half, "xl")))
    *grad_queries, keep0, send0 = near
    pieces = kernel_call(
        join_kernel,
        (*[piece] * 4,),
        (keep0, swapped(send0, "core"), far, *grad_queries),
    )
    (copies4,) = kernel_call(layer_out_kernel, (shape_of(4, 128, 2048),), (feed_half, feed_other))
    *pieces, copies4, feed_0, feed_1, feed_2, feed_3 = tied(
        (*pieces, copies4, feed_z[0], feed_1, feed_2, feed_3)
    )
    feed_keep, feed_send = xh_halves([feed_0, feed_1, feed_2, feed_3])
    *pieces, feed_send = tied((*across(pieces), feed_send))
    feed_received = swapped(feed_send, "xh")
    layer_out = dealt(copies4, "y")
    grad_mixed, partial_normed, gain_sum, shift_sum, bias_sum = kernel_call(
        grad_project_kernel,
        (shape_of(BLOCK, 768), shape_of(BLOCK, 2048)),
        (*pieces, cosine, sine, tokens, stats1, w3),
        small_outs=(
            shape_of(1, 2048, kind=WIDE),
            shape_of(1, 2048, kind=WIDE),
            shape_of(3, 256, kind=WIDE),
        ),
        scalars=(place,),
        scratch=(pltpu.VMEM((4, BLOCK, 128), LOW), four),
        late=3,
        flops=2 * 512 * 2048 * 768,
    )
    partial_normed, layer_out = tied((partial_normed, layer_out))
    layer_out = settled(layer_out)
    normed_parts = tp_parts(partial_normed)

    rest_mine, rest_theirs = weight_grads(
        ((grad_mixed, normed_low), (attended_low, grad_branch)), place
    )
    rest_mine, rest_theirs, feed_received = tied((rest_mine, rest_theirs, feed_received))
    rest_z = z_parts(rest_mine, swapped(rest_theirs, "core"))
    vectors = jnp.concatenate([gain_sum, shift_sum, second_sums], axis=0).reshape(32, 256)
    vectors = jnp.concatenate([vectors, bias_sum], axis=0)
    vectors = summed_by_pairs(vectors, (("core", 2, 1), ("zl", 2, 1), ("zh", 2, 1)))
    vectors, *rest_z = tied((vectors, *rest_z))
    vectors = summed_by_pairs(vectors, (("xh", 2, 1),))
    rest_1, rest_3 = z_permute(rest_z[1], 1), z_permute(rest_z[3], 3)
    feed_w = feed_keep + feed_received.astype(WIDE)
    normed_parts, vectors, layer_out, feed_w = tied((normed_parts, vectors, layer_out, feed_w))
    bias_grad = vectors[32:]
    (last_share,) = kernel_call(
        first_gradient_kernel,
        (shape_of(64, 2048 + 128),),
        (normed_parts, grad_middle, tok_share, my_share(stats1), vectors[:32].reshape(64, 128)),
        moved=1,
        small=(first_gain[None],),
    )
    last_share, rest_2 = tied((last_share, rest_z[2]))
    last_shares, rest_1, rest_3 = gathered(last_share, rest_1, rest_3)
    grad_tokens, vectors = last_call(last_shares, place)
    vectors = vectors.reshape(4, 2048)
    rest_z = (rest_z[0], rest_1, z_permute(rest_2, 2), rest_3)
    rest_keep, rest_send = xh_halves(rest_z)
    rest_w = rest_keep + swapped(rest_send, "xh").astype(WIDE)
    return (
        layer_out,
        grad_tokens,
        vectors[0],
        vectors[1],
        vectors[2],
        vectors[3],
        jnp.transpose(rest_w[:768].reshape(3, 256, 128), (2, 0, 1)),
        bias_grad,
        rest_w[768:],
        jnp.transpose(feed_w[:1408].reshape(2, 704, 128), (2, 0, 1)),
        feed_w[1408:],
    )


def solution(mesh):
    fine = Mesh(
        mesh.devices.reshape(2, 2, 2, 2, 4, 2), ("xh", "zh", "zl", "core", "y", "xl")
    )
    rows = P(CTX, None)
    return jax.shard_map(
        body,
        mesh=fine,
        in_specs=(
            rows, rows, P(), P(), P(), P(), P(),
            P(None, None, TP), P(None, TP), P(TP, None), P(None, None, TP), P(TP, None),
        ),
        out_specs=(
            rows, rows, P(), P(), P(), P(),
            P(CTX, None, TP), P(None, TP), P(TP, CTX), P(CTX, None, TP), P(TP, CTX),
        ),
        check_vma=False,
    )
```

```python
import functools

import jax
import jax.numpy as jnp
from jax import lax
from jax.experimental import pallas as pl
from jax.experimental.pallas import tpu as pltpu
from jax.sharding import Mesh
from jax.sharding import PartitionSpec as P

HDIM = 64
DOCS = 3
BLOCK = 512
HALF = 256
LOW = jnp.bfloat16
WIDE = jnp.float32
CTX = ("xh", "zh", "zl", "core")
TP = ("y", "xl")
SPREAD = ("xh", "zh")
Z = ("zh", "zl")


def size_of(a):
    return a.size * jnp.dtype(a.dtype).itemsize


def gathered_order(place):
    x, y = place[3], place[4]
    row = [lax.rem(y + k, 4) * 2 for k in range(4)]
    other = 1 - x
    return [
        row[0] + x, row[0] + other,
        row[3] + x, row[1] + x, row[2] + x,
        row[3] + other, row[1] + other, row[2] + other,
    ]


def deal_rows(place, rows, outs):
    x, y = place[3], place[4]
    far = lax.rem(y + 2, 4)
    firsts = [
        lax.rem(y + 1, 4) * 2, lax.rem(y + 3, 4) * 2,
        far * 2 + 1 - x, y * 2 + x, y * 2 + 1 - x, far * 2 + x,
    ]
    for first, out in zip(firsts, outs):
        out[...] = rows[pl.ds(pl.multiple_of(first * 64, 64), out.shape[0]), :]


def meet_kernel(place, below, above, crossed, other, far, out_other, out_far):
    column = pl.multiple_of((1 - place[3]) * 64, 64)

    def work(at):
        there = pl.ds(pl.multiple_of(column + at.start, 16), at.size)
        total = other[at, :].astype(WIDE) + below[there, :].astype(WIDE) + above[there, :].astype(WIDE)
        out_other[at, :] = total.astype(LOW)
        out_far[at, :] = (far[at, :].astype(WIDE) + crossed[at, :].astype(WIDE)).astype(LOW)

    for_rows(work)


def kernel_call(
    body, outs, inputs, *, small=(), small_outs=(), scalars=(), scratch=(), late=0, flops=0, exps=0, mib=12, quick=False, moved=0,
    leaving=False,
):
    inputs = [a if isinstance(a, (tuple, list)) else (a, 0, a.shape[0]) for a in inputs]
    flat = [x for a in inputs for x in (a if isinstance(a, list) else a[:1])]
    counts = [len(x) for x in (scalars, flat, small, outs, small_outs, inputs, outs)]

    def run(*refs):
        groups, at = [], 0
        for n in counts:
            groups.append(refs[at : at + n])
            at += n
        scalar_refs, far_in, near_in, far_out, near_out, held_in, held_out = groups
        arrived, left, *rest = refs[at:]
        pairs, ends = [], []
        for a, held in zip(inputs, held_in):
            if isinstance(a, list):
                rows = a[0].shape[0]
                for index in gathered_order(scalar_refs[0]):
                    pairs.append((None, held.at[pl.ds(pl.multiple_of(index * rows, rows), rows)]))
            else:
                pairs.append((pl.ds(a[1], a[2]), held))
            ends.append(len(pairs))
        moves = [
            pltpu.make_async_copy(x if part is None else x.at[part], held, arrived.at[k])
            for k, (x, (part, held)) in enumerate(zip(far_in, pairs))
        ]
        for move in moves:
            move.start()
        early = ends[len(inputs) - late - 1]
        for move in moves[:early]:
            move.wait()

        def arrive():
            for move in moves[early:]:
                move.wait()

        outward = [
            pltpu.make_async_copy(a, b, left.at[k]) for k, (a, b) in enumerate(zip(held_out, far_out))
        ]
        gone = []

        def leave(*which):
            for k in which:
                outward[k].start()
                gone.append(k)

        body(
            *([arrive] if late else []),
            *([leave] if leaving else []),
            *scalar_refs, *held_in, *near_in, *held_out, *near_out, *rest,
        )
        leave(*[k for k in range(len(outward)) if k not in gone])
        for move in outward:
            move.wait()

    vmem, hbm = pl.BlockSpec(memory_space=pltpu.VMEM), pl.BlockSpec(memory_space=pltpu.HBM)
    taken = [
        shape_of(8 * a[0].shape[0], a[0].shape[1], kind=a[0].dtype)
        if isinstance(a, list)
        else shape_of(a[2], *a[0].shape[1:], kind=a[0].dtype)
        for a in inputs
    ]
    held = [pltpu.VMEM(a.shape, a.dtype) for a in (*taken, *outs)]
    limit = sum(size_of(a) for a in (*taken, *outs, *small, *small_outs)) + mib * 1024 * 1024
    return pl.pallas_call(
        run,
        out_shape=(*[pltpu.HBM(a.shape, a.dtype) for a in outs], *small_outs),
        in_specs=[pl.BlockSpec(memory_space=pltpu.SMEM)] * len(scalars)
        + [pl.BlockSpec(memory_space=pl.ANY)] * moved
        + [hbm] * (len(flat) - moved)
        + [vmem] * len(small),
        out_specs=(*[hbm] * len(outs), *[vmem] * len(small_outs)),
        scratch_shapes=[
            *held,
            pltpu.SemaphoreType.DMA((len(flat),)),
            pltpu.SemaphoreType.DMA((max(1, len(outs)),)),
            *scratch,
        ],
        compiler_params=pltpu.CompilerParams(vmem_limit_bytes=limit),
        cost_estimate=pl.CostEstimate(
            flops=flops,
            bytes_accessed=0 if quick else sum(size_of(a) for a in (*taken, *outs)),
            transcendentals=exps,
        ),
    )(
        *scalars,
        *flat[:moved],
        *[pltpu.with_memory_space_constraint(a, pltpu.HBM) for a in flat[moved:]],
        *small,
    )


def lane_of(shape):
    return lax.broadcasted_iota(jnp.int32, shape, len(shape) - 1)


def exchange_halves(a, b):
    front = lane_of(a.shape) < HDIM
    return (
        jnp.where(front, a, pltpu.roll(b, HDIM, 1)),
        jnp.where(front, pltpu.roll(a, HDIM, 1), b),
    )


def nt(a, b):
    return lax.dot_general(a, b, (((1,), (1,)), ((), ())), preferred_element_type=WIDE)


def nn(a, b):
    return lax.dot_general(a, b, (((1,), (0,)), ((), ())), preferred_element_type=WIDE)


def turn(x, cosine, sine, sign):
    lane = lax.rem(lane_of(x.shape), HDIM)
    ahead = pltpu.roll(x, x.shape[1] - 8, 1)
    behind = pltpu.roll(x, 8, 1)
    swapped = jnp.where(lane < 8, -ahead, behind) * sign
    return x * cosine + swapped * sine


def rotation_table(angles_table):
    tokens = angles_table.shape[1]
    rest = jnp.zeros((112, tokens), WIDE)
    x = jnp.concatenate([angles_table, rest], axis=0).T
    lane = lane_of(x.shape)
    c = jnp.where(lane < 8, x, 0.0)
    c = c + pltpu.roll(c, 8, 1)
    c = c + pltpu.roll(c, HDIM, 1) + jnp.where(lax.rem(lane, HDIM) < 16, 0.0, 1.0)
    s = jnp.where((lane >= 8) & (lane < 16), x, 0.0)
    s = s + pltpu.roll(s, 120, 1)
    s = s + pltpu.roll(s, HDIM, 1)
    return c, s


def project_kernel(
    arrive, leave, place, tok, table, w, gain, shift, bias,
    normed, stats, x0, x1, x2, x3, cosine_out, sine_out, kept,
):
    rows = 64

    def norm_rows(i, carry):
        at = pl.ds(pl.multiple_of(i * rows, rows), rows)
        x = tok[at, :].astype(WIDE)
        mean = jnp.mean(x, axis=-1, keepdims=True)
        center = x - mean
        scale = lax.rsqrt(jnp.mean(center * center, axis=-1, keepdims=True) + 1e-05)
        normed[at, :] = (center * scale * gain[...] + shift[...]).astype(LOW)
        stats[at, :] = jnp.where(lane_of((rows, 128)) < HDIM, mean, scale)
        return carry

    lax.fori_loop(0, BLOCK // rows, norm_rows, 0)
    cosine, sine = rotation_table(table[...])
    cosine_out[...] = cosine
    sine_out[...] = sine
    leave(0, 1, 6, 7)
    arrive()
    mixed = [nn(normed[...], w[c]) + bias[c : c + 1, :] for c in range(3)]
    for pair in range(2):
        lanes = slice(pair * 128, pair * 128 + 128)
        q = turn(mixed[0][:, lanes], cosine, sine, 1.0) * 0.125
        k = turn(mixed[1][:, lanes], cosine, sine, 1.0)
        kv = exchange_halves(k, mixed[2][:, lanes])
        qq = exchange_halves(q[:HALF], q[HALF:])
        for one in range(2):
            kept[2 * pair + one, :BLOCK, :] = kv[one].astype(LOW)
            kept[2 * pair + one, BLOCK:, :] = qq[one].astype(LOW)
    for k, out in enumerate((x0, x1, x2, x3)):
        out[...] = kept[place[1] ^ k]


def padded_queries(q2):
    x = q2.astype(WIDE)
    front = lane_of(x.shape) < HDIM
    return (
        jnp.where(front, x, 0.0).astype(LOW),
        jnp.where(front, pltpu.roll(x, HDIM, 1), 0.0).astype(LOW),
    )


def padded_behind(d2):
    x = d2.astype(WIDE)
    front = lane_of(x.shape) < HDIM
    return (
        jnp.where(front, 0.0, pltpu.roll(x, HDIM, 1)).astype(LOW),
        jnp.where(front, 0.0, x).astype(LOW),
    )


def allowed_keys(key_block, first_query, begin):
    shape = (BLOCK, begin.shape[1])
    key_at = key_block * BLOCK + lax.broadcasted_iota(jnp.int32, shape, 0)
    query_at = first_query + lax.broadcasted_iota(jnp.int32, shape, 1)
    return (key_at <= query_at) & (key_at >= begin)


def for_steps(count, work):
    def pair(i, carry):
        work([2 * i, 2 * i + 1])
        return carry

    lax.fori_loop(0, count // 2, pair, 0)

    @pl.when(lax.rem(count, 2) == 1)
    def _():
        work([count - 1])


def key_blocks(place, rels, t):
    return [4 * t + (place[0] ^ rel) for rel in rels], place[1] ^ t


def forward_kernel(rels, first, last, *refs):
    place, kv0, kv1, q0, q1, q2, q3, begin = refs[:8]
    if first:
        acc_out, peak_out, kvt, queries, kept_q = refs[8:]
    else:
        acc_in, peak_in, o0, o1, o2, o3, out_t, total, kvt, queries, kept_q, kept_o = refs[8:]
        acc_out, peak_out = out_t, total
    me = place[1]
    front = lane_of((BLOCK, 128)) < HDIM
    for k, q in enumerate((q0, q1, q2, q3)):
        kept_q[me ^ k] = q[...]
    for i, kv in enumerate((kv0, kv1)):
        for t in range(4):
            kvt[i, t] = jnp.where(front, 1.0, kv[t].astype(WIDE)).T.astype(LOW)

    def one_query_block(j, carry):
        first_query = (4 * j + place[0]) * BLOCK
        queries[:HALF, :], queries[HALF:, :] = padded_queries(kept_q[j])
        if first:
            peak_out[j] = jnp.full((8, BLOCK), -1e30, WIDE)
            acc_out[j] = jnp.zeros((128, BLOCK), WIDE)
        else:
            peak_out[j] = peak_in[j]
            acc_out[j] = acc_in[j]

        def some_blocks(steps):
            scores, sources = [], []
            for t in steps:
                blocks, at = key_blocks(place, rels, t)
                for i, kv in enumerate((kv0, kv1)):
                    ok = allowed_keys(blocks[i], first_query, begin[j, :1])
                    scores.append(jnp.where(ok, nt(kv[at], queries[...]), -1e30))
                    sources.append((i, at))
            old = peak_out[j, :1]
            new = old
            for one in scores:
                new = jnp.maximum(new, jnp.max(one, axis=0, keepdims=True))
            done = acc_out[j] * jnp.exp(old - new)
            for one, (i, at) in zip(scores, sources):
                done += nn(kvt[i, at], jnp.exp(one - new).astype(LOW))
            acc_out[j] = done
            peak_out[j, :1] = new

        for_steps(j + 1, some_blocks)
        if last:
            weight_sum = acc_out[j, :1]
            done = acc_out[j] / weight_sum
            out_t[j] = done
            total[j, :1] = peak_out[j, :1] + jnp.log(weight_sum)
            rows = done.T
            x, y = rows[:HALF], rows[HALF:]
            kept_o[j] = jnp.where(lane_of(x.shape) < HDIM, pltpu.roll(x, HDIM, 1), y).astype(LOW)
        return carry

    lax.fori_loop(0, 4, one_query_block, 0)
    if last:
        for k, out in enumerate((o0, o1, o2, o3)):
            out[...] = kept_o[me ^ k]


def backward_kernel(rels, first, *refs):
    place, kv0, kv1, q0, q1, q2, q3, d0, d1, d2, d3, out_t, total, begin = refs[:14]
    if first:
        acc, keep, send, kvt, queries, grads, dot_rows, dkv, kept_q, kept_d = refs[14:]
    else:
        (
            acc_in, g0, g1, g2, g3, keep, send,
            kvt, queries, grads, dot_rows, dkv, kept_q, kept_d, acc, kept_g,
        ) = refs[14:]
    me = place[1]
    for k in range(4):
        kept_q[me ^ k] = (q0, q1, q2, q3)[k][...]
        kept_d[me ^ k] = (d0, d1, d2, d3)[k][...]
    for i, kv in enumerate((kv0, kv1)):
        for t in range(4):
            kvt[i, t] = kv[t].astype(WIDE).T.astype(LOW)
    dkv[...] = jnp.zeros(dkv.shape, WIDE)

    def one_query_block(j, carry):
        first_query = (4 * j + place[0]) * BLOCK
        queries[:HALF, :], queries[HALF:, :] = padded_queries(kept_q[j])
        grads[:HALF, :], grads[HALF:, :] = padded_behind(kept_d[j])
        dot_rows[...] = jnp.sum(grads[...].astype(WIDE).T * out_t[j], axis=0, keepdims=True)
        acc[j] = jnp.zeros((128, BLOCK), WIDE) if first else acc_in[j]

        def some_blocks(steps):
            for t in steps:
                blocks, at = key_blocks(place, rels, t)
                for i, kv in enumerate((kv0, kv1)):
                    term = 0.0
                    for half in range(2):
                        some = slice(half * HALF, half * HALF + HALF)
                        ok = allowed_keys(blocks[i], first_query + half * HALF, begin[j, :1, some])
                        scores = nt(kv[at], queries[some, :])
                        probs = jnp.where(ok, jnp.exp(scores - total[j, :1, some]), 0.0)
                        grad_probs = nt(kv[at], grads[some, :])
                        grad_scores = (probs * (grad_probs - dot_rows[:, some])).astype(LOW)
                        term += nn(grad_scores, queries[some, :])
                        term += nn(probs.astype(LOW), grads[some, :])
                        acc[j, :, some] += nn(kvt[i, at], grad_scores)
                    dkv[i, at] += term

        for_steps(j + 1, some_blocks)
        if not first:
            rows = acc[j].T
            x, y = rows[:HALF], rows[HALF:]
            kept_g[j] = jnp.where(lane_of(x.shape) < HDIM, x, pltpu.roll(y, HDIM, 1)).astype(LOW)
        return carry

    lax.fori_loop(0, 4, one_query_block, 0)
    if not first:
        for k, out in enumerate((g0, g1, g2, g3)):
            out[...] = kept_g[me ^ k]
    for t in range(4):
        keep[t] = dkv[0, t].astype(LOW)
        send[t] = dkv[1, t].astype(LOW)


def branch_kernel(arrive, place, h0, h1, h2, h3, w, attended, *refs):
    outs, (partial, kept) = refs[:6], refs[6:]
    for k, h in enumerate((h0, h1, h2, h3)):
        kept[place[1] ^ k] = h[...]
    for pair in range(2):
        lanes = slice(pair * 128, pair * 128 + 128)
        x, y = exchange_halves(kept[2 * pair].astype(WIDE), kept[2 * pair + 1].astype(WIDE))
        attended[:HALF, lanes] = x.astype(LOW)
        attended[HALF:, lanes] = y.astype(LOW)
    arrive()
    for n in range(4):
        at = slice(n * 512, n * 512 + 512)
        partial[:, at] = nn(attended[...], w[:, at]).astype(LOW)
    deal_rows(place, partial, outs)


def grad_attended_kernel(place, grad, w, d0, d1, d2, d3, kept):
    g = nt(grad[...], w[...])
    for pair in range(2):
        lanes = slice(pair * 128, pair * 128 + 128)
        both = exchange_halves(g[:HALF, lanes], g[HALF:, lanes])
        for one in range(2):
            kept[2 * pair + one] = both[one].astype(LOW)
    for k, out in enumerate((d0, d1, d2, d3)):
        out[...] = kept[place[1] ^ k]


def join_kernel(keep, received, far, g0, g1, g2, g3, x0, x1, x2, x3):
    for k in range(4):
        total = keep[k].astype(WIDE) + received[k].astype(WIDE) + far[k].astype(WIDE)
        out = (x0, x1, x2, x3)[k]
        out[:BLOCK, :] = total.astype(LOW)
        out[BLOCK:, :] = (g0, g1, g2, g3)[k][...]


def grad_project_kernel(
    arrive, place, x0, x1, x2, x3, cosine, sine, tok, stats, w,
    grad_mixed, partial, gain_sum, shift_sum, bias_sum, parts, kept,
):
    for k, x in enumerate((x0, x1, x2, x3)):
        parts[place[1] ^ k] = x[:BLOCK, :]
        kept[place[1] ^ k] = x[BLOCK:, :]
    for pair in range(2):
        lanes = slice(pair * 128, pair * 128 + 128)
        k, v = exchange_halves(parts[2 * pair].astype(WIDE), parts[2 * pair + 1].astype(WIDE))
        q = exchange_halves(kept[2 * pair].astype(WIDE), kept[2 * pair + 1].astype(WIDE))
        q = jnp.concatenate(q, axis=0)
        q = turn(q, cosine[...], sine[...], -1.0) * 0.125
        k = turn(k, cosine[...], sine[...], -1.0)
        for c, part in enumerate((q, k, v)):
            start = c * 256 + pair * 128
            low = part.astype(LOW)
            grad_mixed[:, start : start + 128] = low
            bias_sum[c : c + 1, lanes] = jnp.sum(low.astype(WIDE), axis=0, keepdims=True)
    arrive()
    mean, scale = stats[:, 0:1], stats[:, 64:65]
    for n in range(4):
        at = slice(n * 512, n * 512 + 512)
        total = nt(grad_mixed[:, :256], w[0, at, :])
        total += nt(grad_mixed[:, 256:512], w[1, at, :])
        total += nt(grad_mixed[:, 512:], w[2, at, :])
        partial[:, at] = total.astype(LOW)
        normal = (tok[:, at].astype(WIDE) - mean) * scale
        gain_sum[:, at] = jnp.sum(total * normal, axis=0, keepdims=True)
        shift_sum[:, at] = jnp.sum(total, axis=0, keepdims=True)


def hidden_gradient_kernel(cot, w, grad_hidden):
    grad_hidden[...] = nt(cot[...], w[...])


def feed_kernel(arrive, leave, place, second, w_gate, w_up, grad_hidden, hidden, grad_gate, grad_up, partial):
    gate = nt(second[...], w_gate[0])
    arrive()
    up = nt(second[...], w_up[0])
    sigmoid = 1.0 / (1.0 + jnp.exp(-gate))
    activated = gate * sigmoid
    hidden[...] = (activated * up).astype(LOW)
    grad = grad_hidden[...]
    grad_up[...] = (grad * activated).astype(LOW)
    grad_gate[...] = (grad * up * sigmoid * (1.0 + gate * (1.0 - sigmoid))).astype(LOW)
    leave(0, 1, 2)
    for n in range(4):
        at = slice(n * 512, n * 512 + 512)
        partial[:, at] = (nn(grad_gate[...], w_gate[0, :, at]) + nn(grad_up[...], w_up[0, :, at])).astype(LOW)


def for_rows(work):
    rows = 16

    def one(i, carry):
        work(pl.ds(pl.multiple_of(i * rows, rows), rows))
        return carry

    lax.fori_loop(0, 64 // rows, one, 0)


def summed(parts, at):
    total = parts[0, at, :].astype(WIDE)
    for k in range(1, 8):
        total += parts[k, at, :].astype(WIDE)
    return total


def second_norm_kernel(
    place, below, above, own, other, far, tok, gain, shift, low, middle, normal, stats
):
    column = pl.multiple_of(place[3] * 64, 64)

    def work(at):
        there = pl.ds(pl.multiple_of(column + at.start, 16), at.size)
        x = tok[at, :].astype(WIDE) + own[at, :].astype(WIDE)
        x += below[there, :].astype(WIDE) + above[there, :].astype(WIDE)
        x += other[at, :].astype(WIDE) + far[at, :].astype(WIDE)
        center = x - jnp.mean(x, axis=-1, keepdims=True)
        scale = lax.rsqrt(jnp.mean(center * center, axis=-1, keepdims=True) + 1e-05)
        rows = center * scale
        low[at, :] = (rows * gain[...] + shift[...]).astype(LOW)
        middle[at, :] = x
        normal[at, :] = rows
        stats[at, :] = jnp.broadcast_to(scale, (scale.shape[0], 128))

    for_rows(work)


def norm_gradient(grad, rows, scale, gain):
    scaled = grad * gain
    return scale * (
        scaled
        - jnp.mean(scaled, axis=-1, keepdims=True)
        - rows * jnp.mean(scaled * rows, axis=-1, keepdims=True)
    )


def second_gradient_kernel(parts, cot, normal, stats, gain, copies, grad_middle, sums):
    sums[...] = jnp.zeros(sums.shape, WIDE)

    def work(at):
        grad, rows = summed(parts, at), normal[at, :]
        done = cot[at, :].astype(WIDE) + norm_gradient(grad, rows, stats[at, 0:1], gain[...])
        low = done.astype(LOW)
        for k in range(8):
            copies[k, at, :] = low
        grad_middle[at, :] = done
        sums[0:1, :] += jnp.sum(grad * rows, axis=0, keepdims=True)
        sums[1:2, :] += jnp.sum(grad, axis=0, keepdims=True)

    for_rows(work)


def feed_sum_kernel(place, parts, middle, out):
    rows = 16
    mine = place[3]

    def one(i, carry):
        at = pl.ds(pl.multiple_of(i * rows, rows), rows)
        total = parts[0, at, :].astype(WIDE)
        for k in range(1, 4):
            total += parts[k, at, :].astype(WIDE)
        here = i * rows - mine * 64
        own = pl.ds(pl.multiple_of(jnp.clip(here, 0, 64 - rows), rows), rows)
        inside = (here >= 0) & (here < 64)
        out[at, :] = (total + jnp.where(inside, middle[own, :], 0.0)).astype(LOW)
        return carry

    lax.fori_loop(0, 128 // rows, one, 0)


def layer_out_kernel(a, b, copies):
    rows = 16

    def one(i, carry):
        at = pl.ds(pl.multiple_of(i * rows, rows), rows)
        low = (a[at, :].astype(WIDE) + b[at, :].astype(WIDE)).astype(LOW)
        for k in range(4):
            copies[k, at, :] = low
        return carry

    lax.fori_loop(0, 128 // rows, one, 0)


def first_gradient_kernel(parts, grad_middle, tok, stats, vectors, gain, low):
    def work(at):
        mean, scale = stats[at, 0:1], stats[at, 64:65]
        rows = (tok[at, :].astype(WIDE) - mean) * scale
        done = norm_gradient(summed(parts, at), rows, scale, gain[...])
        low[at, :2048] = (grad_middle[at, :] + done).astype(LOW)
        low[at, 2048:] = vectors[at, :].astype(LOW)

    for_rows(work)


def last_kernel(place, *refs):
    shares, (out, total, held, came, went) = refs[:8], refs[8:]
    moves = []
    for k, (x, index) in enumerate(zip(shares, gathered_order(place))):
        at = pl.ds(pl.multiple_of(index * 64, 64), 64)
        moves.append(
            (
                pltpu.make_async_copy(x, held.at[k], came.at[k]),
                pltpu.make_async_copy(held.at[k, :, pl.ds(0, 2048)], out.at[at], went.at[k]),
            )
        )
    for come, _ in moves:
        come.start()
    for come, go in moves:
        come.wait()
        go.start()
    done = held[0, :, 2048:].astype(WIDE)
    for k in range(1, 8):
        done += held[k, :, 2048:].astype(WIDE)
    total[...] = done
    for _, go in moves:
        go.wait()


def last_call(shares, place):
    hbm = pl.BlockSpec(memory_space=pltpu.HBM)
    return pl.pallas_call(
        last_kernel,
        out_shape=(pltpu.HBM((BLOCK, 2048), LOW), shape_of(64, 128, kind=WIDE)),
        in_specs=[pl.BlockSpec(memory_space=pltpu.SMEM), *[hbm] * 8],
        out_specs=(hbm, pl.BlockSpec(memory_space=pltpu.VMEM)),
        scratch_shapes=[
            pltpu.VMEM((8, 64, 2048 + 128), LOW),
            pltpu.SemaphoreType.DMA((8,)),
            pltpu.SemaphoreType.DMA((8,)),
        ],
        compiler_params=pltpu.CompilerParams(vmem_limit_bytes=8 * 1024 * 1024),
        cost_estimate=pl.CostEstimate(flops=0, bytes_accessed=0, transcendentals=0),
    )(place, *[pltpu.with_memory_space_constraint(a, pltpu.HBM) for a in shares])


def weight_kernel(widths, sources, arrive, place, *refs):
    count = max(max(pair) for pair in sources) + 1
    inputs = refs[:count]
    mine, theirs, turned = refs[count:]
    first_core = place[2] == 0
    start = 0
    for n, ((left, right), width) in enumerate(zip(sources, widths)):
        if n == 1:
            arrive()
        left, right = inputs[left], inputs[right]
        turned[:width, :] = left[...].astype(WIDE).T.astype(LOW)

        def one(n, carry, start=start, right=right, width=width):
            columns = right[:, pl.ds(pl.multiple_of(n * 256, 256), 256)]
            both = nn(turned[:width, :], columns)
            first, second = both[:, :128], both[:, 128:]
            at = pl.ds(start, width)
            mine[n, at, :] = jnp.where(first_core, first, second).astype(LOW)
            theirs[n, at, :] = jnp.where(first_core, second, first).astype(LOW)
            return carry

        lax.fori_loop(0, 8, one, 0, unroll=8)
        start += width


def weight_grads(pairs, place):
    inputs, sources = [], []
    for pair in pairs:
        for a in pair:
            if not any(a is b for b in inputs):
                inputs.append(a)
        sources.append(tuple(next(k for k, b in enumerate(inputs) if b is a) for a in pair))
    widths = tuple(a.shape[1] for a, _ in pairs)
    out = jax.ShapeDtypeStruct((8, sum(widths), 128), LOW)
    return kernel_call(
        functools.partial(weight_kernel, widths, sources),
        (out, out),
        inputs,
        scalars=(place,),
        scratch=(pltpu.VMEM((max(widths), BLOCK), LOW),),
        late=len(inputs) - 2,
        quick=True,
    )


def swapped(x, axis):
    return lax.ppermute(x, axis, [(0, 1), (1, 0)])


def across(pieces):
    moved = [
        lax.ppermute(pieces[k], SPREAD, [(i, i ^ k) for i in range(4)]) for k in range(1, 4)
    ]
    return (pieces[0], *moved)


def z_parts_kernel(place, mine, received, *refs):
    outs, (held_a, held_b, done, came, went) = refs[:4], refs[4:]
    z = place[0]
    order = [(k, xh) for k in (1, 3, 2, 0) for xh in range(2)]
    moves = []
    for n, (k, xh) in enumerate(order):
        at = xh * 4 + lax.rem(z + k, 4)
        moves.append(
            (
                pltpu.make_async_copy(mine.at[at], held_a.at[n], came.at[2 * n]),
                pltpu.make_async_copy(received.at[at], held_b.at[n], came.at[2 * n + 1]),
                pltpu.make_async_copy(done.at[n], outs[k].at[xh], went.at[n]),
            )
        )
    for a, b, _ in moves:
        a.start()
        b.start()
    for n, (a, b, out) in enumerate(moves):
        a.wait()
        b.wait()
        done[n] = (held_a[n].astype(WIDE) + held_b[n].astype(WIDE)).astype(LOW)
        out.start()
    for _, _, out in moves:
        out.wait()


def z_parts(mine, received):
    rows = mine.shape[1]
    hbm = pl.BlockSpec(memory_space=pltpu.HBM)
    held = pltpu.VMEM((8, rows, 128), LOW)
    return pl.pallas_call(
        z_parts_kernel,
        in_specs=[pl.BlockSpec(memory_space=pltpu.SMEM), hbm, hbm],
        out_specs=[hbm] * 4,
        out_shape=[pltpu.HBM((2, rows, 128), LOW)] * 4,
        scratch_shapes=[
            held,
            held,
            held,
            pltpu.SemaphoreType.DMA((16,)),
            pltpu.SemaphoreType.DMA((8,)),
        ],
        compiler_params=pltpu.CompilerParams(vmem_limit_bytes=24 * 1024 * 1024),
        cost_estimate=pl.CostEstimate(flops=0, bytes_accessed=0, transcendentals=0),
    )(
        lax.axis_index(Z).reshape(1),
        *[pltpu.with_memory_space_constraint(a, pltpu.HBM) for a in (mine, received)],
    )


def settled_kernel(x, out, held, came, went):
    rows = x.shape[1]
    moves = []
    for k in range(x.shape[0]):
        at = pl.ds(k * rows, rows)
        moves.append(
            (
                pltpu.make_async_copy(x.at[k], held.at[k], came.at[k]),
                pltpu.make_async_copy(held.at[k, :, pl.ds(0, 2048)], out.at[at], went.at[k]),
            )
        )
    for come, _ in moves:
        come.start()
    for come, go in moves:
        come.wait()
        go.start()
    for _, go in moves:
        go.wait()


def settled(x):
    hbm = pl.BlockSpec(memory_space=pltpu.HBM)
    parts, rows = x.shape[:2]
    return pl.pallas_call(
        settled_kernel,
        out_shape=pltpu.HBM((parts * rows, 2048), x.dtype),
        in_specs=[pl.BlockSpec(memory_space=pl.ANY)],
        out_specs=hbm,
        scratch_shapes=[
            pltpu.VMEM(x.shape, x.dtype),
            pltpu.SemaphoreType.DMA((parts,)),
            pltpu.SemaphoreType.DMA((parts,)),
        ],
        compiler_params=pltpu.CompilerParams(vmem_limit_bytes=8 * 1024 * 1024),
        cost_estimate=pl.CostEstimate(flops=0, bytes_accessed=0, transcendentals=0),
    )(x)


def z_permute(part, distance):
    return lax.ppermute(part, Z, [(i, (i + distance) % 4) for i in range(4)])


def xh_halves(moved):
    xh = lax.axis_index("xh")

    def added(at):
        return sum(lax.dynamic_index_in_dim(x, at, 0, False).astype(WIDE) for x in moved)

    return added(xh), added(1 - xh).astype(LOW)


def dealt(x, axis):
    return lax.all_to_all(x, axis, split_axis=0, concat_axis=0, tiled=True)


def tp_parts(partial):
    return dealt(partial.reshape(8, -1, partial.shape[1]), TP)


def y_moved(x, distance):
    return lax.ppermute(x, "y", [(i, (i + distance) % 4) for i in range(4)])


def gathered(share, *beside):
    across_x, *beside = lax.optimization_barrier((swapped(share, "xl"), *beside))
    back, ahead, far = (y_moved(share, k) for k in (1, 3, 2))
    shares = [
        share, across_x, back, ahead, far,
        y_moved(across_x, 1), y_moved(across_x, 3), swapped(far, "xl"),
    ]
    return (shares, *beside) if beside else shares


def summed_by_pairs(x, pairs):
    for axis, size, distance in pairs:
        x = x + lax.ppermute(x, axis, [(i, i ^ distance) for i in range(size)])
    return x


def shape_of(*dims, kind=LOW):
    return jax.ShapeDtypeStruct(dims, kind)


def body(
    tokens, cotangent, segment_ids, first_gain, first_shift, second_gain, second_shift,
    w_qkv, qkv_bias, w_out, w_gate_up, w_down,
):
    ctx = lax.axis_index(CTX)
    tp = lax.axis_index(TP)
    group = lax.axis_index(("zl", "core"))
    place = jnp.stack(
        [group, lax.axis_index(SPREAD), lax.axis_index("core"), lax.axis_index("xl"), lax.axis_index("y")]
    )
    tied = lax.optimization_barrier

    def my_share(array):
        return lax.dynamic_slice_in_dim(array, tp * 64, 64)

    labels = jnp.arange(DOCS, dtype=jnp.int32)
    starts = jnp.sum((segment_ids[None, :] < labels[:, None]).astype(jnp.int32), axis=1)
    begins = jnp.sum(
        jnp.where(segment_ids[None, :] == labels[:, None], starts[:, None], 0), axis=0
    )
    begin = lax.dynamic_index_in_dim(begins.reshape(4, 4, 1, BLOCK), group, 1, False)
    begin = jnp.broadcast_to(begin, (4, 8, BLOCK))
    own = lax.dynamic_slice_in_dim(begins, ctx * BLOCK, BLOCK)
    places = ctx * BLOCK + jnp.arange(BLOCK, dtype=jnp.int32) - own
    frequency = 10000.0 ** (-jnp.arange(8, dtype=WIDE) / 8.0)
    angles = frequency[:, None] * places.astype(WIDE)[None, :]
    table = jnp.concatenate([jnp.cos(angles), jnp.sin(angles)], axis=0)

    w3 = jnp.transpose(w_qkv, (1, 0, 2))
    w2 = jnp.transpose(w_gate_up, (1, 2, 0))
    quarter, piece = shape_of(HALF, 128), shape_of(BLOCK + HALF, 128)
    wide_block = shape_of(BLOCK, 128, kind=WIDE)
    four = pltpu.VMEM((4, HALF, 128), LOW)
    normed_low, stats1, *packed, cosine, sine = kernel_call(
        project_kernel,
        (shape_of(BLOCK, 2048), wide_block, *[piece] * 4, wide_block, wide_block),
        (tokens, table, w3),
        small=(first_gain[None], first_shift[None], qkv_bias),
        scalars=(place,),
        scratch=(pltpu.VMEM((4, BLOCK + HALF, 128), LOW),),
        late=1,
        leaving=True,
        flops=2 * 512 * 2048 * 768,
    )
    (grad_hidden,) = kernel_call(
        hidden_gradient_kernel,
        (shape_of(BLOCK, 704, kind=WIDE),),
        (cotangent, w_down),
        flops=2 * 512 * 2048 * 704,
    )
    *packed, grad_hidden, tok_share, cot_share = tied(
        (*across(packed), grad_hidden, my_share(tokens), my_share(cotangent))
    )
    kv = jnp.stack([x[:BLOCK] for x in packed])
    queries = [(x, BLOCK, HALF) for x in packed]
    kv_c = swapped(kv, "core")
    state = (shape_of(4, 128, BLOCK, kind=WIDE), shape_of(4, 8, BLOCK, kind=WIDE))
    acc, peak = kernel_call(
        functools.partial(forward_kernel, (0, 1), True, False),
        state,
        (kv, kv_c, *queries, begin),
        scalars=(place,),
        scratch=(pltpu.VMEM((2, 4, 128, BLOCK), LOW), pltpu.VMEM((BLOCK, 128), LOW), four),
        flops=20 * 4 * BLOCK * BLOCK * 128,
        exps=20 * BLOCK * BLOCK,
        mib=24,
    )
    acc, peak, kv_z = tied((acc, peak, swapped(kv, "zl")))
    kv_zc = swapped(kv_z, "core")
    *heads, out_t, total = kernel_call(
        functools.partial(forward_kernel, (2, 3), False, True),
        (*[quarter] * 4, *state),
        (kv_z, kv_zc, *queries, begin, acc, peak),
        scalars=(place,),
        scratch=(pltpu.VMEM((2, 4, 128, BLOCK), LOW), pltpu.VMEM((BLOCK, 128), LOW), four, four),
        flops=20 * 4 * BLOCK * BLOCK * 128,
        exps=20 * BLOCK * BLOCK,
        mib=24,
    )
    heads = across(heads)
    share, low_share = shape_of(64, 2048, kind=WIDE), shape_of(64, 2048)
    attended_low, *partial_branch = kernel_call(
        branch_kernel,
        (shape_of(BLOCK, 256), *[shape_of(128, 2048)] * 2, *[low_share] * 4),
        (*heads, w_out),
        scalars=(place,),
        scratch=(pltpu.VMEM((BLOCK, 2048), LOW), four),
        late=1,
        flops=2 * 512 * 256 * 2048,
    )
    to_above, to_below, to_other, own_part, other_part, far_part = partial_branch
    from_below, from_above = y_moved(to_above, 1), y_moved(to_below, 3)
    other_part, far_part = kernel_call(
        meet_kernel,
        (low_share, low_share),
        (from_below, from_above, swapped(to_other, "xl"), other_part, far_part),
        scalars=(place,),
        quick=True,
    )
    other_part, far_part = swapped(other_part, "xl"), y_moved(far_part, 2)
    second_share, middle, second_rows, stats2 = kernel_call(
        second_norm_kernel,
        (low_share, share, share, shape_of(64, 128, kind=WIDE)),
        (from_below, from_above, own_part, other_part, far_part, tok_share),
        scalars=(place,),
        small=(second_gain[None], second_shift[None]),
    )
    second_low = gathered(second_share)
    strip = shape_of(BLOCK, 704)
    hidden_low, grad_gate, grad_up, partial_second = kernel_call(
        feed_kernel,
        (strip, strip, strip, shape_of(BLOCK, 2048)),
        (second_low, (w2, 0, 1), (w2, 1, 1), grad_hidden),
        scalars=(place,),
        late=2,
        leaving=True,
        flops=8 * 512 * 2048 * 704,
        mib=24,
    )
    second_parts = tp_parts(partial_second)

    feed_mine, feed_theirs = weight_grads(
        ((grad_gate, second_low), (grad_up, second_low), (hidden_low, cotangent)), place
    )
    second_parts, feed_mine, feed_theirs = tied((second_parts, feed_mine, feed_theirs))
    copies, grad_middle, second_sums = kernel_call(
        second_gradient_kernel,
        (shape_of(8, 64, 2048), share),
        (second_parts, cot_share, second_rows, stats2),
        moved=1,
        small=(second_gain[None],),
        small_outs=(shape_of(2, 2048, kind=WIDE),),
    )
    grad_branch = dealt(copies, TP).reshape(BLOCK, 2048)
    partial_feed = jnp.dot(hidden_low, w_down, preferred_element_type=WIDE).astype(LOW)
    grad_branch, partial_feed = tied((grad_branch, partial_feed))
    feed_z = z_parts(feed_mine, swapped(feed_theirs, "core"))
    feed_1, feed_3 = z_permute(feed_z[1], 1), z_permute(feed_z[3], 3)
    grads = kernel_call(
        grad_attended_kernel,
        (*[quarter] * 4,),
        (grad_branch, w_out),
        moved=1,
        scalars=(place,),
        scratch=(four,),
        flops=2 * 512 * 256 * 2048,
    )
    feed_1, feed_3, partial_feed, *grads = tied((feed_1, feed_3, partial_feed, *grads))
    feed_parts = dealt(partial_feed.reshape(4, 128, 2048), "y")
    *grads, feed_2 = tied((*across(grads), feed_z[2]))
    feed_2 = z_permute(feed_2, 2)
    scratch = (
        pltpu.VMEM((2, 4, 128, BLOCK), LOW),
        pltpu.VMEM((BLOCK, 128), LOW),
        pltpu.VMEM((BLOCK, 128), LOW),
        pltpu.VMEM((1, BLOCK), WIDE),
        pltpu.VMEM((2, 4, BLOCK, 128), WIDE),
        four,
        four,
    )
    blocks = shape_of(4, BLOCK, 128)
    acc, keep1, send1 = kernel_call(
        functools.partial(backward_kernel, (2, 3), True),
        (state[0], blocks, blocks),
        (kv_z, kv_zc, *queries, *grads, out_t, total, begin),
        scalars=(place,),
        scratch=scratch,
        flops=20 * 10 * BLOCK * BLOCK * 128,
        exps=20 * BLOCK * BLOCK,
        mib=28,
    )
    acc, send1, feed_parts = tied((acc, send1, feed_parts))
    (feed_half,) = kernel_call(
        feed_sum_kernel,
        (shape_of(128, 2048),),
        (feed_parts, middle),
        scalars=(place,),
        moved=1,
    )
    far = (keep1.astype(WIDE) + swapped(send1, "core").astype(WIDE)).astype(LOW)
    acc, far, feed_half, feed_2 = tied((acc, far, feed_half, feed_2))
    near = kernel_call(
        functools.partial(backward_kernel, (0, 1), False),
        (*[quarter] * 4, blocks, blocks),
        (kv, kv_c, *queries, *grads, out_t, total, begin, acc),
        scalars=(place,),
        scratch=(*scratch, pltpu.VMEM((4, 128, BLOCK), WIDE), four),
        flops=20 * 10 * BLOCK * BLOCK * 128,
        exps=20 * BLOCK * BLOCK,
        mib=28,
    )
    *near, far, feed_other = tied((*near, swapped(far, "zl"), swapped(feed_half, "xl")))
    *grad_queries, keep0, send0 = near
    pieces = kernel_call(
        join_kernel,
        (*[piece] * 4,),
        (keep0, swapped(send0, "core"), far, *grad_queries),
    )
    (copies4,) = kernel_call(layer_out_kernel, (shape_of(4, 128, 2048),), (feed_half, feed_other))
    *pieces, copies4, feed_0, feed_1, feed_2, feed_3 = tied(
        (*pieces, copies4, feed_z[0], feed_1, feed_2, feed_3)
    )
    feed_keep, feed_send = xh_halves([feed_0, feed_1, feed_2, feed_3])
    *pieces, feed_send = tied((*across(pieces), feed_send))
    feed_received = swapped(feed_send, "xh")
    layer_out = dealt(copies4, "y")
    grad_mixed, partial_normed, gain_sum, shift_sum, bias_sum = kernel_call(
        grad_project_kernel,
        (shape_of(BLOCK, 768), shape_of(BLOCK, 2048)),
        (*pieces, cosine, sine, tokens, stats1, w3),
        small_outs=(
            shape_of(1, 2048, kind=WIDE),
            shape_of(1, 2048, kind=WIDE),
            shape_of(3, 256, kind=WIDE),
        ),
        scalars=(place,),
        scratch=(pltpu.VMEM((4, BLOCK, 128), LOW), four),
        late=3,
        flops=2 * 512 * 2048 * 768,
    )
    partial_normed, layer_out = tied((partial_normed, layer_out))
    layer_out = settled(layer_out)
    normed_parts = tp_parts(partial_normed)

    rest_mine, rest_theirs = weight_grads(
        ((grad_mixed, normed_low), (attended_low, grad_branch)), place
    )
    rest_mine, rest_theirs, feed_received = tied((rest_mine, rest_theirs, feed_received))
    rest_z = z_parts(rest_mine, swapped(rest_theirs, "core"))
    vectors = jnp.concatenate([gain_sum, shift_sum, second_sums], axis=0).reshape(32, 256)
    vectors = jnp.concatenate([vectors, bias_sum], axis=0)
    vectors = summed_by_pairs(vectors, (("core", 2, 1), ("zl", 2, 1), ("zh", 2, 1)))
    vectors, *rest_z = tied((vectors, *rest_z))
    vectors = summed_by_pairs(vectors, (("xh", 2, 1),))
    rest_1, rest_3 = z_permute(rest_z[1], 1), z_permute(rest_z[3], 3)
    feed_w = feed_keep + feed_received.astype(WIDE)
    normed_parts, vectors, layer_out, feed_w = tied((normed_parts, vectors, layer_out, feed_w))
    bias_grad = vectors[32:]
    (last_share,) = kernel_call(
        first_gradient_kernel,
        (shape_of(64, 2048 + 128),),
        (normed_parts, grad_middle, tok_share, my_share(stats1), vectors[:32].reshape(64, 128)),
        moved=1,
        small=(first_gain[None],),
    )
    last_shares, rest_1, rest_3 = gathered(last_share, rest_1, rest_3)
    grad_tokens, vectors = last_call(last_shares, place)
    vectors = vectors.reshape(4, 2048)
    rest_z = (rest_z[0], rest_1, z_permute(rest_z[2], 2), rest_3)
    rest_keep, rest_send = xh_halves(rest_z)
    rest_w = rest_keep + swapped(rest_send, "xh").astype(WIDE)
    return (
        layer_out,
        grad_tokens,
        vectors[0],
        vectors[1],
        vectors[2],
        vectors[3],
        jnp.transpose(rest_w[:768].reshape(3, 256, 128), (2, 0, 1)),
        bias_grad,
        rest_w[768:],
        jnp.transpose(feed_w[:1408].reshape(2, 704, 128), (2, 0, 1)),
        feed_w[1408:],
    )


def solution(mesh):
    fine = Mesh(
        mesh.devices.reshape(2, 2, 2, 2, 4, 2), ("xh", "zh", "zl", "core", "y", "xl")
    )
    rows = P(CTX, None)
    return jax.shard_map(
        body,
        mesh=fine,
        in_specs=(
            rows, rows, P(), P(), P(), P(), P(),
            P(None, None, TP), P(None, TP), P(TP, None), P(None, None, TP), P(TP, None),
        ),
        out_specs=(
            rows, rows, P(), P(), P(), P(),
            P(CTX, None, TP), P(None, TP), P(TP, CTX), P(CTX, None, TP), P(TP, CTX),
        ),
        check_vma=False,
    )
```
